32 devices in a mesh: groups: 2 (over x), row: 8 (over z, y), col: 2 (over core).
Axes of the slice: x: 2, y: 2, z: 4, core: 2. Of those that a mesh axis runs over, the one named last changes fastest.
Arguments:
- pair: bfloat16 [192, 96, 128], P(('groups', 'row'), 'col'), parts along dimension 0, may hold values from -6 to 6
- token_mask: int32 [192], P('groups'), parts along dimension 0, may hold values 0 or 1
- gain_in: float32 [128], replicated, may hold values from 0.1 to 1.9
- bias_in: float32 [128], replicated, may hold values from -3 to 3
- w_in: bfloat16 [128, 512], replicated, may hold values from -0.5 to 0.5
- w_gate: bfloat16 [128, 128], replicated, may hold values from -0.5 to 0.5
- gain_out: float32 [128], replicated, may hold values from 0.1 to 1.9
- bias_out: float32 [128], replicated, may hold values from -3 to 3
- w_out: bfloat16 [128, 128], replicated, may hold values from -0.5 to 0.5
Outputs:
- update: bfloat16 [192, 96, 128], P(('groups', 'row'), 'col'), parts along dimension 0
The draws below stay inside these ranges and needn't reach their ends.
There are 2 independent parts, one for each index of `groups`. The reference program is written for one: setup_inputs(seed, part) draws one part's arguments, and reference() takes and returns one part's arrays. A program takes and returns all parts, laid end to end along the dimension named above; an argument that names none is the same for every part. Nothing has to cross between parts.
All inputs are finite; a program needn't handle non-finite values.
Results may differ from the reference program's by a relative error of at most 0.0059.
Values may be sent and summed in bfloat16 or wider, within the bound.
No kernel may reach another device: no remote copies, remote signals or barrier semaphores. Data moves between devices by JAX's collectives and lax.ppermute only.
A program may use at most 128 MiB of HBM per device.

```python
import jax
import jax.numpy as jnp
from jax import lax

CZ = 128
CH = 128
TOKENS = 96


def set_ends(values, own_key, smallest, high):
    longest = values.shape.index(max(values.shape))
    spots = []
    for shift in (0, 1):
        where = [jax.random.randint(jax.random.fold_in(own_key, axis), (), 0, length) for axis, length in enumerate(values.shape)]
        where[longest] = (where[longest] + shift) % values.shape[longest]
        spots.append(tuple(where))
    return values.at[spots[0]].set(smallest).at[spots[1]].set(high)


def shard_levels(stream_key, extent, pieces, low, top_value):
    def one(axis_at, shards_of):
        draws = jax.random.uniform(jax.random.fold_in(jax.random.fold_in(stream_key, 6), axis_at), (shards_of,), jnp.float32, low / len(pieces), top_value / len(pieces))
        return jnp.repeat(jnp.exp(draws), extent[axis_at] // shards_of).reshape((-1,) + (1,) * (len(extent) - axis_at - 1))

    factor_of = one(*pieces[0])
    for cut in pieces[1:]:
        factor_of = factor_of * one(*cut)
    return factor_of


def bell_draw(stream_key, extent, spread, limit, cuts=(), dtype=jnp.bfloat16):
    factor_of = shard_levels(stream_key, extent, cuts, -0.22, 0.18) if cuts else 1.0
    result = jax.random.normal(stream_key, extent, jnp.float32) * spread * factor_of
    return jnp.minimum(jnp.maximum(result, -limit), limit).astype(dtype)


def setup_inputs(seed: int = 0, part: int = 0) -> dict:
    streams_of = jax.random.split(jax.random.key(seed), 10)
    part_splits = jax.random.split(jax.random.fold_in(streams_of[9], part), 10)
    pair = bell_draw(part_splits[0], (TOKENS, TOKENS, CZ), 1.0, 6.0, ((0, 8), (1, 2)))
    token_mask = set_ends((jax.random.randint(part_splits[1], (TOKENS,), 0, 8) < 7).astype(jnp.int32), jax.random.fold_in(part_splits[1], 1), 0, 1)
    gain_in = jnp.clip(1.0 + 0.18 * jax.random.normal(streams_of[2], (CZ,), jnp.float32), 0.1, 1.9)
    bias_in = bell_draw(streams_of[3], (CZ,), 0.5, 3.0, (), jnp.float32)
    w_in = bell_draw(streams_of[4], (CZ, 4 * CH), CZ ** -0.5, 0.5)
    w_gate = bell_draw(streams_of[5], (CZ, CZ), CZ ** -0.5, 0.5)
    gain_out = jnp.clip(1.0 + 0.18 * jax.random.normal(streams_of[6], (CH,), jnp.float32), 0.1, 1.9)
    bias_out = bell_draw(streams_of[7], (CH,), 0.5, 3.0, (), jnp.float32)
    w_out = bell_draw(streams_of[8], (CH, CZ), CH ** -0.5, 0.5)
    return {"pair": pair, "token_mask": token_mask, "gain_in": gain_in, "bias_in": bias_in, "w_in": w_in, "w_gate": w_gate, "gain_out": gain_out, "bias_out": bias_out, "w_out": w_out}


epsilon = 1e-05

def layer_norm(values, gain, bias):
    mean = lax.optimization_barrier(jnp.mean(values, axis=-1, keepdims=True))
    centred = values - mean
    variance = lax.optimization_barrier(jnp.mean(centred * centred, axis=-1, keepdims=True))
    return centred * lax.rsqrt(variance + epsilon) * gain + bias

def reference(pair, token_mask, gain_in, bias_in, w_in, w_gate, gain_out, bias_out, w_out):
    normed = layer_norm(pair.astype(jnp.float32), gain_in, bias_in).astype(jnp.bfloat16)
    flat = normed.reshape(TOKENS * TOKENS, CZ)
    projected = jnp.dot(flat, w_in, preferred_element_type=jnp.float32).reshape(TOKENS, TOKENS, 4 * CH)
    mask_float = token_mask.astype(jnp.float32)
    pair_mask = (mask_float[:, None] * mask_float[None, :])[:, :, None]
    left = (pair_mask * jax.nn.sigmoid(projected[:, :, 0:CH]) * projected[:, :, CH:2 * CH]).astype(jnp.bfloat16)
    right = (pair_mask * jax.nn.sigmoid(projected[:, :, 2 * CH:3 * CH]) * projected[:, :, 3 * CH:4 * CH]).astype(jnp.bfloat16)
    gate = jax.nn.sigmoid(jnp.dot(flat, w_gate, preferred_element_type=jnp.float32)).reshape(TOKENS, TOKENS, CZ)
    total = jnp.einsum('kic,kjc->ijc', left.astype(jnp.float32), right.astype(jnp.float32), precision=lax.Precision.HIGHEST)
    summed_norm = layer_norm(total, gain_out, bias_out).astype(jnp.bfloat16)
    output = jnp.dot(summed_norm.reshape(TOKENS * TOKENS, CH), w_out, preferred_element_type=jnp.float32).reshape(TOKENS, TOKENS, CZ)
    return (gate * output).astype(jnp.bfloat16)
```

```python
import jax
import jax.numpy as jnp
from jax import lax
from jax.sharding import PartitionSpec as P

epsilon = 1e-05
AXES = ("row", "col")


def layer_norm(values, gain, bias, axis):
    mean = jnp.mean(values, axis=axis, keepdims=True)
    centred = values - mean
    variance = jnp.mean(centred * centred, axis=axis, keepdims=True)
    return centred * lax.rsqrt(variance + epsilon) * gain + bias


def exchange(pieces, me, devices):
    got = [lax.dynamic_index_in_dim(pieces, me, 0, False)]
    for step in range(1, devices):
        piece = lax.dynamic_index_in_dim(pieces, me ^ step, 0, False)
        got.append(lax.ppermute(piece, AXES, [(i, i ^ step) for i in range(devices)]))
    return got


def per_device(rows, cols, pair, token_mask, gain_in, bias_in, w_in, w_gate, gain_out, bias_out, w_out):
    row_count, col_count, channels = pair.shape
    hidden = w_out.shape[0]
    devices = rows * cols
    share = hidden // devices
    tokens = row_count * col_count
    row_start = lax.axis_index("row") * row_count
    col_start = lax.axis_index("col") * col_count
    mask_float = token_mask.astype(jnp.float32)
    mask_rows = lax.dynamic_slice_in_dim(mask_float, row_start, row_count)
    mask_cols = lax.dynamic_slice_in_dim(mask_float, col_start, col_count)
    pair_mask = (mask_rows[:, None] * mask_cols[None, :]).reshape(1, tokens)
    flat = pair.reshape(tokens, channels).astype(jnp.float32)
    normed = layer_norm(flat, gain_in, bias_in, -1).astype(jnp.bfloat16)
    projected = lax.dot_general(w_in, normed, (((0,), (1,)), ((), ())), preferred_element_type=jnp.float32)
    projected = projected.reshape(2, 2, hidden, tokens)
    sides = (pair_mask * jax.nn.sigmoid(projected[:, 0]) * projected[:, 1]).astype(jnp.bfloat16)
    sides = sides.reshape(2, devices, share, tokens).transpose(1, 0, 2, 3)
    gate = jax.nn.sigmoid(jnp.dot(normed, w_gate, preferred_element_type=jnp.float32))
    me = lax.axis_index("row") * cols + lax.axis_index("col")
    got = exchange(sides, me, devices)
    got = jnp.stack(got).reshape(rows, cols, 2, share, row_count, col_count).transpose(2, 3, 0, 4, 1, 5)
    got = jnp.where(lax.axis_index("col") == 0, got, got[:, :, :, :, ::-1])
    got = got.reshape(2, share, rows * row_count, cols * col_count)
    total = jnp.einsum("cki,ckj->cij", got[0], got[1], preferred_element_type=jnp.float32).astype(jnp.bfloat16)
    total = total.reshape(share, rows, row_count, cols, col_count).transpose(1, 3, 0, 2, 4)
    total = total.reshape(devices, share, tokens)
    total = jnp.stack(exchange(total, me, devices))
    order = jnp.arange(devices) ^ me
    gain_out = gain_out.reshape(devices, share)[order].reshape(hidden)
    bias_out = bias_out.reshape(devices, share)[order].reshape(hidden)
    w_out = w_out.reshape(devices, share, channels)[order].reshape(hidden, channels)
    total = total.reshape(hidden, tokens).astype(jnp.float32)
    summed_norm = layer_norm(total, gain_out[:, None], bias_out[:, None], 0).astype(jnp.bfloat16)
    output = lax.dot_general(summed_norm, w_out, (((0,), (0,)), ((), ())), preferred_element_type=jnp.float32)
    return (gate * output).astype(jnp.bfloat16).reshape(row_count, col_count, channels)


def solution(mesh):
    import functools

    in_specs = (P(("groups", "row"), "col", None), P("groups"), P(), P(), P(), P(), P(), P(), P())
    out_specs = P(("groups", "row"), "col", None)
    body = functools.partial(per_device, mesh.shape["row"], mesh.shape["col"])
    return jax.shard_map(body, mesh=mesh, in_specs=in_specs, out_specs=out_specs, check_vma=False)
```

```python
import jax
import jax.numpy as jnp
from jax import lax
from jax.sharding import PartitionSpec as P

epsilon = 1e-05


def layer_norm(values, gain, bias, axis):
    mean = jnp.mean(values, axis=axis, keepdims=True)
    centred = values - mean
    variance = jnp.mean(centred * centred, axis=axis, keepdims=True)
    return centred * lax.rsqrt(variance + epsilon) * gain + bias


def per_device(rows, cols, pair, token_mask, gain_in, bias_in, w_in, w_gate, gain_out, bias_out, w_out):
    row_count, col_count, channels = pair.shape
    hidden = w_out.shape[0]
    share = hidden // rows
    tokens = row_count * col_count
    row_start = lax.axis_index("row") * row_count
    col_start = lax.axis_index("col") * col_count
    mask_float = token_mask.astype(jnp.float32)
    mask_rows = lax.dynamic_slice_in_dim(mask_float, row_start, row_count)
    mask_cols = lax.dynamic_slice_in_dim(mask_float, col_start, col_count)
    pair_mask = (mask_rows[:, None] * mask_cols[None, :]).reshape(1, tokens)
    flat = pair.reshape(tokens, channels).astype(jnp.float32)
    normed = layer_norm(flat, gain_in, bias_in, -1).astype(jnp.bfloat16)
    projected = lax.dot_general(w_in, normed, (((0,), (1,)), ((), ())), preferred_element_type=jnp.float32)
    projected = projected.reshape(2, 2, hidden, tokens)
    sides = (pair_mask * jax.nn.sigmoid(projected[:, 0]) * projected[:, 1]).astype(jnp.bfloat16)
    sides = sides.reshape(2, rows, share, tokens).transpose(1, 0, 2, 3)
    gate = jax.nn.sigmoid(jnp.dot(normed, w_gate, preferred_element_type=jnp.float32))
    got = lax.all_to_all(sides, "row", split_axis=0, concat_axis=0, tiled=True)
    left = lax.all_gather(got[:, 0], "col")
    left = left.reshape(cols, rows, share, row_count, col_count).transpose(2, 1, 3, 0, 4)
    left = left.reshape(share, rows * row_count, cols * col_count)
    right = got[:, 1].reshape(rows, share, row_count, col_count).transpose(1, 0, 2, 3)
    right = right.reshape(share, rows * row_count, col_count)
    total = jnp.einsum("cki,ckj->cij", left, right, preferred_element_type=jnp.float32).astype(jnp.bfloat16)
    total = total.reshape(share, rows, row_count, col_count).transpose(1, 0, 2, 3)
    total = total.reshape(rows, share, tokens)
    total = lax.all_to_all(total, "row", split_axis=0, concat_axis=0, tiled=True)
    total = total.reshape(hidden, tokens).astype(jnp.float32)
    summed_norm = layer_norm(total, gain_out[:, None], bias_out[:, None], 0).astype(jnp.bfloat16)
    output = lax.dot_general(summed_norm, w_out, (((0,), (0,)), ((), ())), preferred_element_type=jnp.float32)
    return (gate * output).astype(jnp.bfloat16).reshape(row_count, col_count, channels)


def solution(mesh):
    import functools

    in_specs = (P(("groups", "row"), "col", None), P("groups"), P(), P(), P(), P(), P(), P(), P())
    out_specs = P(("groups", "row"), "col", None)
    body = functools.partial(per_device, mesh.shape["row"], mesh.shape["col"])
    return jax.shard_map(body, mesh=mesh, in_specs=in_specs, out_specs=out_specs, check_vma=False)
```

```python
import functools

import jax
import jax.numpy as jnp
from jax import lax
from jax.experimental import pallas as pl
from jax.experimental.pallas import tpu as pltpu
from jax.sharding import PartitionSpec as P

epsilon = 1e-05
AXES = ("row", "col")
VMEM = pl.BlockSpec(memory_space=pltpu.VMEM)
LIMIT = pltpu.CompilerParams(vmem_limit_bytes=32 * 1024 * 1024)


def sigmoid(x):
    return 0.5 * jnp.tanh(0.5 * x) + 0.5


def layer_norm(values, gain, bias, axis):
    mean = jnp.mean(values, axis=axis, keepdims=True)
    centred = values - mean
    variance = jnp.mean(centred * centred, axis=axis, keepdims=True)
    return centred * lax.rsqrt(variance + epsilon) * gain + bias


def column(row):
    n = row.shape[1]
    eye = lax.broadcasted_iota(jnp.int32, (n, n), 0) == lax.broadcasted_iota(jnp.int32, (n, n), 1)
    return jnp.sum(jnp.where(eye, row, 0.0), axis=1, keepdims=True)


def project_kernel(pair_ref, gain_ref, bias_ref, w_ref, sides_ref, normed_ref):
    devices, both, tokens = sides_ref.shape
    channels = pair_ref.shape[2]
    hidden = w_ref.shape[1] // 4
    share = both // 2
    flat = pair_ref[...].reshape(tokens, channels).astype(jnp.float32)
    normed = layer_norm(flat, gain_ref[...], bias_ref[...], -1).astype(jnp.bfloat16)
    normed_ref[...] = normed
    projected = lax.dot_general(w_ref[...], normed, (((0,), (1,)), ((), ())), preferred_element_type=jnp.float32)
    left = sigmoid(projected[:hidden]) * projected[hidden : 2 * hidden]
    right = sigmoid(projected[2 * hidden : 3 * hidden]) * projected[3 * hidden :]
    sides = jnp.concatenate([left.reshape(devices, share, tokens), right.reshape(devices, share, tokens)], axis=1)
    sides_ref[...] = sides.astype(jnp.bfloat16)


def triangle_kernel(rows, cols, row_count, col_count, got_ref, mask_ref, total_ref, wide_ref, sum_ref, flat_ref):
    both = got_ref.shape[1]
    share = both // 2
    length = rows * row_count
    for source in range(rows * cols):
        row, col = divmod(source, cols)
        piece = got_ref[source].astype(jnp.float32)
        for k in range(row_count):
            at = (row * row_count + k) * both
            wide_ref[at : at + both, col * col_count : (col + 1) * col_count] = piece[:, k * col_count : (k + 1) * col_count]
    mask_row = mask_ref[...].astype(jnp.float32)
    mask = column(mask_row) * mask_row
    for c in range(share):
        left = (wide_ref[pl.ds(c, length, stride=both), 0:length] * mask).astype(jnp.bfloat16)
        right = (wide_ref[pl.ds(share + c, length, stride=both), 0:length] * mask).astype(jnp.bfloat16)
        sum_ref[pl.ds(c, length, stride=share), 0:length] = lax.dot_general(
            left, right, (((0,), (0,)), ((), ())), preferred_element_type=jnp.float32
        )
    for target in range(rows * cols):
        row, col = divmod(target, cols)
        for i in range(row_count):
            at = (row * row_count + i) * share
            flat_ref[target * share : (target + 1) * share, i * col_count : (i + 1) * col_count] = sum_ref[
                at : at + share, col * col_count : (col + 1) * col_count
            ]
        total_ref[target] = flat_ref[target * share : (target + 1) * share, :].astype(jnp.bfloat16)


def output_kernel(total_ref, gate_ref, gain_ref, bias_ref, w_ref, out_ref):
    devices, share, tokens = total_ref.shape
    total = total_ref[...].astype(jnp.float32).reshape(devices * share, tokens)
    normed = layer_norm(total, column(gain_ref[...]), column(bias_ref[...]), 0).astype(jnp.bfloat16)
    output = lax.dot_general(normed, w_ref[...], (((0,), (0,)), ((), ())), preferred_element_type=jnp.float32)
    out_ref[...] = (sigmoid(gate_ref[...]) * output).astype(jnp.bfloat16).reshape(out_ref.shape)


def per_device(rows, cols, pair, token_mask, gain_in, bias_in, w_in, w_gate, gain_out, bias_out, w_out):
    row_count, col_count, channels = pair.shape
    hidden = w_out.shape[0]
    devices = rows * cols
    share = hidden // devices
    tokens = row_count * col_count
    length = rows * row_count
    sides, normed = pl.pallas_call(
        project_kernel,
        out_shape=(
            jax.ShapeDtypeStruct((devices, 2 * share, tokens), jnp.bfloat16),
            jax.ShapeDtypeStruct((tokens, channels), jnp.bfloat16),
        ),
        in_specs=[VMEM] * 4,
        out_specs=(VMEM, VMEM),
        compiler_params=LIMIT,
    )(pair, gain_in.reshape(1, channels), bias_in.reshape(1, channels), w_in)
    got = lax.all_to_all(sides, AXES, split_axis=0, concat_axis=0, tiled=True)
    total = pl.pallas_call(
        functools.partial(triangle_kernel, rows, cols, row_count, col_count),
        out_shape=jax.ShapeDtypeStruct((devices, share, tokens), jnp.bfloat16),
        in_specs=[VMEM] * 2,
        out_specs=VMEM,
        scratch_shapes=[
            pltpu.VMEM((length * 2 * share, 128), jnp.float32),
            pltpu.VMEM((length * share, 128), jnp.float32),
            pltpu.VMEM((hidden, tokens), jnp.float32),
        ],
        compiler_params=LIMIT,
    )(got, token_mask.reshape(1, length))
    gate = jnp.dot(normed, w_gate, preferred_element_type=jnp.float32)
    total = lax.all_to_all(total, AXES, split_axis=0, concat_axis=0, tiled=True)
    return pl.pallas_call(
        output_kernel,
        out_shape=jax.ShapeDtypeStruct(pair.shape, jnp.bfloat16),
        in_specs=[VMEM] * 5,
        out_specs=VMEM,
        compiler_params=LIMIT,
    )(total, gate, gain_out.reshape(1, hidden), bias_out.reshape(1, hidden), w_out)


def plain_per_device(rows, cols, pair, token_mask, gain_in, bias_in, w_in, w_gate, gain_out, bias_out, w_out):
    row_count, col_count, channels = pair.shape
    hidden = w_out.shape[0]
    devices = rows * cols
    share = hidden // devices
    tokens = row_count * col_count
    row_start = lax.axis_index("row") * row_count
    col_start = lax.axis_index("col") * col_count
    mask_float = token_mask.astype(jnp.float32)
    mask_rows = lax.dynamic_slice_in_dim(mask_float, row_start, row_count)
    mask_cols = lax.dynamic_slice_in_dim(mask_float, col_start, col_count)
    pair_mask = (mask_rows[:, None] * mask_cols[None, :]).reshape(1, tokens)
    flat = pair.reshape(tokens, channels).astype(jnp.float32)
    normed = layer_norm(flat, gain_in, bias_in, -1).astype(jnp.bfloat16)
    projected = lax.dot_general(w_in, normed, (((0,), (1,)), ((), ())), preferred_element_type=jnp.float32)
    projected = projected.reshape(2, 2, hidden, tokens)
    sides = (pair_mask * jax.nn.sigmoid(projected[:, 0]) * projected[:, 1]).astype(jnp.bfloat16)
    sides = sides.reshape(2, devices, share, tokens).transpose(1, 0, 2, 3)
    gate = jax.nn.sigmoid(jnp.dot(normed, w_gate, preferred_element_type=jnp.float32))
    got = lax.all_to_all(sides, AXES, split_axis=0, concat_axis=0, tiled=True)
    got = got.reshape(rows, cols, 2, share, row_count, col_count).transpose(2, 3, 0, 4, 1, 5)
    got = got.reshape(2, share, rows * row_count, cols * col_count)
    total = jnp.einsum("cki,ckj->cij", got[0], got[1], preferred_element_type=jnp.float32).astype(jnp.bfloat16)
    total = total.reshape(share, rows, row_count, cols, col_count).transpose(1, 3, 0, 2, 4)
    total = total.reshape(devices, share, tokens)
    total = lax.all_to_all(total, AXES, split_axis=0, concat_axis=0, tiled=True)
    total = total.reshape(hidden, tokens).astype(jnp.float32)
    summed_norm = layer_norm(total, gain_out[:, None], bias_out[:, None], 0).astype(jnp.bfloat16)
    output = lax.dot_general(summed_norm, w_out, (((0,), (0,)), ((), ())), preferred_element_type=jnp.float32)
    return (gate * output).astype(jnp.bfloat16).reshape(row_count, col_count, channels)


def solution(mesh):
    in_specs = (P(("groups", "row"), "col", None), P("groups"), P(), P(), P(), P(), P(), P(), P())
    out_specs = P(("groups", "row"), "col", None)
    rows, cols = mesh.shape["row"], mesh.shape["col"]

    def per_shard(*args):
        hidden = args[-1].shape[0]
        length = args[1].shape[0]
        fits = hidden % (8 * rows * cols) == 0 and length <= 128
        return (per_device if fits else plain_per_device)(rows, cols, *args)

    return jax.shard_map(per_shard, mesh=mesh, in_specs=in_specs, out_specs=out_specs, check_vma=False)
```

```python
import functools

import jax
import jax.numpy as jnp
from jax import lax
from jax.experimental import pallas as pl
from jax.experimental.pallas import tpu as pltpu
from jax.sharding import PartitionSpec as P

epsilon = 1e-05
AXES = ("half", "quad", "col")
VMEM = pl.BlockSpec(memory_space=pltpu.VMEM)
HBM = pl.BlockSpec(memory_space=pltpu.HBM)
LIMIT = pltpu.CompilerParams(vmem_limit_bytes=32 * 1024 * 1024)


def sigmoid(x):
    return 0.5 * jnp.tanh(0.5 * x) + 0.5


def layer_norm(values, gain, bias, axis):
    mean = jnp.mean(values, axis=axis, keepdims=True)
    centred = values - mean
    variance = jnp.mean(centred * centred, axis=axis, keepdims=True)
    return centred * lax.rsqrt(variance + epsilon) * gain + bias


def column(row):
    n = row.shape[1]
    eye = lax.broadcasted_iota(jnp.int32, (n, n), 0) == lax.broadcasted_iota(jnp.int32, (n, n), 1)
    return jnp.sum(jnp.where(eye, row, 0.0), axis=1, keepdims=True)


def project_kernel(pair_hbm, gain_hbm, bias_hbm, w_hbm, mask_hbm, sides_ref, normed_ref, left_mask_ref, pair_ref, gain_ref, bias_ref, w_ref, mask_ref, column_ref, sems):
    copies = [
        pltpu.make_async_copy(source, target, sems.at[n])
        for n, (source, target) in enumerate(
            [(mask_hbm, mask_ref), (pair_hbm, pair_ref), (gain_hbm, gain_ref), (bias_hbm, bias_ref), (w_hbm, w_ref)]
        )
    ]
    for copy in copies:
        copy.start()
    devices, both, tokens = sides_ref.shape
    channels = pair_ref.shape[2]
    hidden = w_ref.shape[1] // 4
    share = both // 2
    depth, length = left_mask_ref.shape
    copies[0].wait()
    mask_row = mask_ref[...].astype(jnp.float32)
    column_ref[...] = jnp.broadcast_to(column(mask_row), column_ref.shape)
    start = pl.multiple_of(lax.axis_index("half") * depth, depth)
    left_mask_ref[...] = column_ref[pl.ds(start, depth), 0:length] * mask_row
    for copy in copies[1:4]:
        copy.wait()
    flat = pair_ref[...].reshape(tokens, channels).astype(jnp.float32)
    normed = layer_norm(flat, gain_ref[...], bias_ref[...], -1).astype(jnp.bfloat16)
    normed_ref[...] = normed
    copies[4].wait()
    projected = lax.dot_general(w_ref[...], normed, (((0,), (1,)), ((), ())), preferred_element_type=jnp.float32)
    left = sigmoid(projected[:hidden]) * projected[hidden : 2 * hidden]
    right = sigmoid(projected[2 * hidden : 3 * hidden]) * projected[3 * hidden :]
    sides = jnp.concatenate([left.reshape(devices, share, tokens), right.reshape(devices, share, tokens)], axis=1)
    sides_ref[...] = sides.astype(jnp.bfloat16)


def triangle_kernel(rows, cols, row_count, col_count, got_ref, left_mask_ref, mask_ref, total_ref, wide_ref, sum_ref, flat_ref):
    sources, both, _ = got_ref.shape
    share = both // 2
    depth, length = left_mask_ref.shape
    for source in range(sources):
        row, col = divmod(source, cols)
        piece = got_ref[source].astype(jnp.float32)
        for k in range(row_count):
            at = (row * row_count + k) * both
            wide_ref[at : at + both, col * col_count : (col + 1) * col_count] = piece[:, k * col_count : (k + 1) * col_count]
    left_mask = left_mask_ref[...]
    right_mask = mask_ref[...].astype(jnp.float32)
    for c in range(share):
        left = (wide_ref[pl.ds(c, depth, stride=both), 0:length] * left_mask).astype(jnp.bfloat16)
        right = (wide_ref[pl.ds(share + c, depth, stride=both), 0:length] * right_mask).astype(jnp.bfloat16)
        sum_ref[pl.ds(c, length, stride=share), 0:length] = lax.dot_general(
            left, right, (((0,), (0,)), ((), ())), preferred_element_type=jnp.float32
        )
    for target in range(rows * cols):
        row, col = divmod(target, cols)
        for i in range(row_count):
            at = (row * row_count + i) * share
            flat_ref[target * share : (target + 1) * share, i * col_count : (i + 1) * col_count] = sum_ref[
                at : at + share, col * col_count : (col + 1) * col_count
            ]
        total_ref[target] = flat_ref[target * share : (target + 1) * share, :].astype(jnp.bfloat16)


def gate_kernel(normed_ref, w_ref, gain_ref, bias_ref, gate_ref, gain_out_ref, bias_out_ref):
    gate_ref[...] = sigmoid(jnp.dot(normed_ref[...], w_ref[...], preferred_element_type=jnp.float32))
    gain_out_ref[...] = column(gain_ref[...])
    bias_out_ref[...] = column(bias_ref[...])


def output_kernel(total_ref, gate_ref, gain_ref, bias_ref, w_ref, out_ref):
    sources, share, tokens = total_ref.shape
    hidden = w_ref.shape[0]
    parts = total_ref[...].astype(jnp.float32).reshape(sources * share // hidden, hidden, tokens)
    total = jnp.sum(parts, axis=0)
    normed = layer_norm(total, gain_ref[...], bias_ref[...], 0).astype(jnp.bfloat16)
    output = lax.dot_general(normed, w_ref[...], (((0,), (0,)), ((), ())), preferred_element_type=jnp.float32)
    out_ref[...] = (gate_ref[...] * output).astype(jnp.bfloat16).reshape(out_ref.shape)


def per_device(rows, cols, halves, pair, token_mask, gain_in, bias_in, w_in, w_gate, gain_out, bias_out, w_out):
    row_count, col_count, channels = pair.shape
    hidden = w_out.shape[0]
    devices = rows * cols
    near = devices // halves
    share = hidden // near
    tokens = row_count * col_count
    length = rows * row_count
    depth = length // halves
    token_mask = token_mask.reshape(1, length)
    sides, normed, left_mask = pl.pallas_call(
        project_kernel,
        out_shape=(
            jax.ShapeDtypeStruct((near, 2 * share, tokens), jnp.bfloat16),
            jax.ShapeDtypeStruct((tokens, channels), jnp.bfloat16),
            jax.ShapeDtypeStruct((depth, length), jnp.float32),
        ),
        in_specs=[HBM] * 5,
        out_specs=(VMEM, VMEM, VMEM),
        scratch_shapes=[
            pltpu.VMEM(pair.shape, pair.dtype),
            pltpu.VMEM((1, channels), jnp.float32),
            pltpu.VMEM((1, channels), jnp.float32),
            pltpu.VMEM(w_in.shape, w_in.dtype),
            pltpu.VMEM((1, length), jnp.int32),
            pltpu.VMEM((length, 128), jnp.float32),
            pltpu.SemaphoreType.DMA((5,)),
        ],
        compiler_params=LIMIT,
    )(pair, gain_in.reshape(1, channels), bias_in.reshape(1, channels), w_in, token_mask)
    got = lax.all_to_all(sides, ("quad", "col"), split_axis=0, concat_axis=0, tiled=True)
    total = pl.pallas_call(
        functools.partial(triangle_kernel, rows, cols, row_count, col_count),
        out_shape=jax.ShapeDtypeStruct((devices, share, tokens), jnp.bfloat16),
        in_specs=[VMEM] * 3,
        out_specs=VMEM,
        scratch_shapes=[
            pltpu.VMEM((depth * 2 * share, 128), jnp.float32),
            pltpu.VMEM((length * share, 128), jnp.float32),
            pltpu.VMEM((devices * share, tokens), jnp.float32),
        ],
        compiler_params=LIMIT,
    )(got, left_mask, token_mask)
    gate, gain_out, bias_out = pl.pallas_call(
        gate_kernel,
        out_shape=(
            jax.ShapeDtypeStruct((tokens, channels), jnp.float32),
            jax.ShapeDtypeStruct((hidden, 1), jnp.float32),
            jax.ShapeDtypeStruct((hidden, 1), jnp.float32),
        ),
        in_specs=[VMEM] * 4,
        out_specs=(VMEM, VMEM, VMEM),
        compiler_params=LIMIT,
        cost_estimate=pl.CostEstimate(flops=2 * tokens * channels * channels, bytes_accessed=4 * tokens * channels, transcendentals=0),
    )(normed, w_gate, gain_out.reshape(1, hidden), bias_out.reshape(1, hidden))
    total = lax.all_to_all(total, ("half", "quad", "col"), split_axis=0, concat_axis=0, tiled=True)
    return pl.pallas_call(
        output_kernel,
        out_shape=jax.ShapeDtypeStruct(pair.shape, jnp.bfloat16),
        in_specs=[VMEM] * 5,
        out_specs=VMEM,
        compiler_params=LIMIT,
    )(total, gate, gain_out, bias_out, w_out)


def plain_per_device(rows, cols, pair, token_mask, gain_in, bias_in, w_in, w_gate, gain_out, bias_out, w_out):
    row_count, col_count, channels = pair.shape
    hidden = w_out.shape[0]
    devices = rows * cols
    share = hidden // devices
    tokens = row_count * col_count
    row_start = lax.axis_index(("half", "quad")) * row_count
    col_start = lax.axis_index("col") * col_count
    mask_float = token_mask.astype(jnp.float32)
    mask_rows = lax.dynamic_slice_in_dim(mask_float, row_start, row_count)
    mask_cols = lax.dynamic_slice_in_dim(mask_float, col_start, col_count)
    pair_mask = (mask_rows[:, None] * mask_cols[None, :]).reshape(1, tokens)
    flat = pair.reshape(tokens, channels).astype(jnp.float32)
    normed = layer_norm(flat, gain_in, bias_in, -1).astype(jnp.bfloat16)
    projected = lax.dot_general(w_in, normed, (((0,), (1,)), ((), ())), preferred_element_type=jnp.float32)
    projected = projected.reshape(2, 2, hidden, tokens)
    sides = (pair_mask * jax.nn.sigmoid(projected[:, 0]) * projected[:, 1]).astype(jnp.bfloat16)
    sides = sides.reshape(2, devices, share, tokens).transpose(1, 0, 2, 3)
    gate = jax.nn.sigmoid(jnp.dot(normed, w_gate, preferred_element_type=jnp.float32))
    got = lax.all_to_all(sides, AXES, split_axis=0, concat_axis=0, tiled=True)
    got = got.reshape(rows, cols, 2, share, row_count, col_count).transpose(2, 3, 0, 4, 1, 5)
    got = got.reshape(2, share, rows * row_count, cols * col_count)
    total = jnp.einsum("cki,ckj->cij", got[0], got[1], preferred_element_type=jnp.float32).astype(jnp.bfloat16)
    total = total.reshape(share, rows, row_count, cols, col_count).transpose(1, 3, 0, 2, 4)
    total = total.reshape(devices, share, tokens)
    total = lax.all_to_all(total, AXES, split_axis=0, concat_axis=0, tiled=True)
    total = total.reshape(hidden, tokens).astype(jnp.float32)
    summed_norm = layer_norm(total, gain_out[:, None], bias_out[:, None], 0).astype(jnp.bfloat16)
    output = lax.dot_general(summed_norm, w_out, (((0,), (0,)), ((), ())), preferred_element_type=jnp.float32)
    return (gate * output).astype(jnp.bfloat16).reshape(row_count, col_count, channels)


def solution(mesh):
    rows, cols = mesh.shape["row"], mesh.shape["col"]
    halves = 2
    parts = (mesh.shape["groups"], halves, rows // halves, cols)
    finer = jax.sharding.Mesh(mesh.devices.reshape(parts), ("groups", "half", "quad", "col"))

    def per_shard(*args):
        near, hidden, length = rows * cols // halves, args[-1].shape[0], args[1].shape[0]
        if hidden % (16 * near) == 0 and length <= 128:
            return per_device(rows, cols, halves, *args)
        return plain_per_device(rows, cols, *args)

    tokens = P(("groups", "half", "quad"), "col", None)
    in_specs = (tokens, P("groups"), P(), P(), P(), P(), P(), P(), P())
    return jax.shard_map(per_shard, mesh=finer, in_specs=in_specs, out_specs=tokens, check_vma=False)
```

```python
import functools

import jax
import jax.numpy as jnp
from jax import lax
from jax.experimental import pallas as pl
from jax.experimental.pallas import tpu as pltpu
from jax.sharding import PartitionSpec as P

epsilon = 1e-05
AXES = ("half", "quad", "col")
VMEM = pl.BlockSpec(memory_space=pltpu.VMEM)
HBM = pl.BlockSpec(memory_space=pltpu.HBM)
LIMIT = pltpu.CompilerParams(vmem_limit_bytes=32 * 1024 * 1024)


def sigmoid(x):
    return 0.5 * jnp.tanh(0.5 * x) + 0.5


def layer_norm(values, gain, bias, axis):
    mean = jnp.mean(values, axis=axis, keepdims=True)
    centred = values - mean
    variance = jnp.mean(centred * centred, axis=axis, keepdims=True)
    return centred * lax.rsqrt(variance + epsilon) * gain + bias


def column(row):
    n = row.shape[1]
    eye = lax.broadcasted_iota(jnp.int32, (n, n), 0) == lax.broadcasted_iota(jnp.int32, (n, n), 1)
    return jnp.sum(jnp.where(eye, row, 0.0), axis=1, keepdims=True)


def project_kernel(pair_hbm, gain_hbm, bias_hbm, w_hbm, mask_hbm, sides_ref, normed_ref, left_mask_ref, pair_ref, gain_ref, bias_ref, w_ref, mask_ref, column_ref, sems):
    copies = [
        pltpu.make_async_copy(source, target, sems.at[n])
        for n, (source, target) in enumerate(
            [(mask_hbm, mask_ref), (pair_hbm, pair_ref), (gain_hbm, gain_ref), (bias_hbm, bias_ref), (w_hbm, w_ref)]
        )
    ]
    for copy in copies:
        copy.start()
    devices, both, tokens = sides_ref.shape
    channels = pair_ref.shape[2]
    hidden = w_ref.shape[1] // 4
    share = both // 2
    depth, length = left_mask_ref.shape
    copies[0].wait()
    mask_row = mask_ref[...].astype(jnp.float32)
    column_ref[...] = jnp.broadcast_to(column(mask_row), column_ref.shape)
    start = pl.multiple_of(lax.axis_index("half") * depth, depth)
    left_mask_ref[...] = column_ref[pl.ds(start, depth), 0:length] * mask_row
    for copy in copies[1:4]:
        copy.wait()
    flat = pair_ref[...].reshape(tokens, channels).astype(jnp.float32)
    normed = layer_norm(flat, gain_ref[...], bias_ref[...], -1).astype(jnp.bfloat16)
    normed_ref[...] = normed
    copies[4].wait()
    projected = lax.dot_general(w_ref[...], normed, (((0,), (1,)), ((), ())), preferred_element_type=jnp.float32)
    left = sigmoid(projected[:hidden]) * projected[hidden : 2 * hidden]
    right = sigmoid(projected[2 * hidden : 3 * hidden]) * projected[3 * hidden :]
    sides = jnp.concatenate([left.reshape(devices, share, tokens), right.reshape(devices, share, tokens)], axis=1)
    sides_ref[...] = sides.astype(jnp.bfloat16)


def triangle_kernel(halves, cols, row_count, col_count, got_ref, left_mask_ref, mask_ref, total_ref, wide_ref, sum_ref, flat_ref):
    sources, both, _ = got_ref.shape
    share = both // 2
    depth, length = left_mask_ref.shape
    quads = sources // cols
    for source in range(sources):
        col, row = divmod(source, quads)
        piece = got_ref[source].astype(jnp.float32)
        for k in range(row_count):
            at = (row * row_count + k) * both
            wide_ref[at : at + both, col * col_count : (col + 1) * col_count] = piece[:, k * col_count : (k + 1) * col_count]
    left_mask = left_mask_ref[...]
    right_mask = mask_ref[...].astype(jnp.float32)
    for c in range(share):
        left = (wide_ref[pl.ds(c, depth, stride=both), 0:length] * left_mask).astype(jnp.bfloat16)
        right = (wide_ref[pl.ds(share + c, depth, stride=both), 0:length] * right_mask).astype(jnp.bfloat16)
        sum_ref[pl.ds(c, length, stride=share), 0:length] = lax.dot_general(
            left, right, (((0,), (0,)), ((), ())), preferred_element_type=jnp.float32
        )
    for target in range(sources * halves):
        col, row = divmod(target // halves, quads)
        row += target % halves * quads
        for i in range(row_count):
            at = (row * row_count + i) * share
            flat_ref[target * share : (target + 1) * share, i * col_count : (i + 1) * col_count] = sum_ref[
                at : at + share, col * col_count : (col + 1) * col_count
            ]
        total_ref[target] = flat_ref[target * share : (target + 1) * share, :].astype(jnp.bfloat16)


def gate_kernel(normed_ref, w_ref, gain_ref, bias_ref, gate_ref, gain_out_ref, bias_out_ref):
    gate_ref[...] = sigmoid(jnp.dot(normed_ref[...], w_ref[...], preferred_element_type=jnp.float32))
    gain_out_ref[...] = column(gain_ref[...])
    bias_out_ref[...] = column(bias_ref[...])


def output_kernel(total_ref, gate_ref, gain_ref, bias_ref, w_ref, out_ref):
    sources, share, tokens = total_ref.shape
    hidden = w_ref.shape[0]
    halves = sources * share // hidden
    parts = total_ref[...].astype(jnp.float32).reshape(sources // halves, halves, share, tokens)
    total = jnp.sum(parts, axis=1).reshape(hidden, tokens)
    normed = layer_norm(total, gain_ref[...], bias_ref[...], 0).astype(jnp.bfloat16)
    output = lax.dot_general(normed, w_ref[...], (((0,), (0,)), ((), ())), preferred_element_type=jnp.float32)
    out_ref[...] = (gate_ref[...] * output).astype(jnp.bfloat16).reshape(out_ref.shape)


def per_device(rows, cols, halves, pair, token_mask, gain_in, bias_in, w_in, w_gate, gain_out, bias_out, w_out):
    row_count, col_count, channels = pair.shape
    hidden = w_out.shape[0]
    devices = rows * cols
    near = devices // halves
    share = hidden // near
    tokens = row_count * col_count
    length = rows * row_count
    depth = length // halves
    token_mask = token_mask.reshape(1, length)
    arguments = (pair, gain_in.reshape(1, channels), bias_in.reshape(1, channels), w_in, token_mask)
    sides, normed, left_mask = pl.pallas_call(
        project_kernel,
        out_shape=(
            jax.ShapeDtypeStruct((near, 2 * share, tokens), jnp.bfloat16),
            jax.ShapeDtypeStruct((tokens, channels), jnp.bfloat16),
            jax.ShapeDtypeStruct((depth, length), jnp.float32),
        ),
        in_specs=[HBM] * 5,
        out_specs=(VMEM, VMEM, VMEM),
        scratch_shapes=[
            pltpu.VMEM(pair.shape, pair.dtype),
            pltpu.VMEM((1, channels), jnp.float32),
            pltpu.VMEM((1, channels), jnp.float32),
            pltpu.VMEM(w_in.shape, w_in.dtype),
            pltpu.VMEM((1, length), jnp.int32),
            pltpu.VMEM((length, 128), jnp.float32),
            pltpu.SemaphoreType.DMA((5,)),
        ],
        compiler_params=LIMIT,
    )(*(pltpu.with_memory_space_constraint(x, pltpu.HBM) for x in arguments))
    got = lax.all_to_all(sides, ("col", "quad"), split_axis=0, concat_axis=0, tiled=True)
    total = pl.pallas_call(
        functools.partial(triangle_kernel, halves, cols, row_count, col_count),
        out_shape=jax.ShapeDtypeStruct((devices, share, tokens), jnp.bfloat16),
        in_specs=[VMEM] * 3,
        out_specs=VMEM,
        scratch_shapes=[
            pltpu.VMEM((depth * 2 * share, 128), jnp.float32),
            pltpu.VMEM((length * share, 128), jnp.float32),
            pltpu.VMEM((devices * share, tokens), jnp.float32),
        ],
        compiler_params=LIMIT,
    )(got, left_mask, token_mask)
    gate, gain_out, bias_out = pl.pallas_call(
        gate_kernel,
        out_shape=(
            jax.ShapeDtypeStruct((tokens, channels), jnp.float32),
            jax.ShapeDtypeStruct((hidden, 1), jnp.float32),
            jax.ShapeDtypeStruct((hidden, 1), jnp.float32),
        ),
        in_specs=[VMEM] * 4,
        out_specs=(VMEM, VMEM, VMEM),
        compiler_params=LIMIT,
        cost_estimate=pl.CostEstimate(flops=2 * tokens * channels * channels, bytes_accessed=4 * tokens * channels, transcendentals=0),
    )(normed, w_gate, gain_out.reshape(1, hidden), bias_out.reshape(1, hidden))
    total = lax.all_to_all(total, ("col", "quad", "half"), split_axis=0, concat_axis=0, tiled=True)
    return pl.pallas_call(
        output_kernel,
        out_shape=jax.ShapeDtypeStruct(pair.shape, jnp.bfloat16),
        in_specs=[VMEM] * 5,
        out_specs=VMEM,
        compiler_params=LIMIT,
    )(total, gate, gain_out, bias_out, w_out)


def plain_per_device(rows, cols, pair, token_mask, gain_in, bias_in, w_in, w_gate, gain_out, bias_out, w_out):
    row_count, col_count, channels = pair.shape
    hidden = w_out.shape[0]
    devices = rows * cols
    share = hidden // devices
    tokens = row_count * col_count
    row_start = lax.axis_index(("half", "quad")) * row_count
    col_start = lax.axis_index("col") * col_count
    mask_float = token_mask.astype(jnp.float32)
    mask_rows = lax.dynamic_slice_in_dim(mask_float, row_start, row_count)
    mask_cols = lax.dynamic_slice_in_dim(mask_float, col_start, col_count)
    pair_mask = (mask_rows[:, None] * mask_cols[None, :]).reshape(1, tokens)
    flat = pair.reshape(tokens, channels).astype(jnp.float32)
    normed = layer_norm(flat, gain_in, bias_in, -1).astype(jnp.bfloat16)
    projected = lax.dot_general(w_in, normed, (((0,), (1,)), ((), ())), preferred_element_type=jnp.float32)
    projected = projected.reshape(2, 2, hidden, tokens)
    sides = (pair_mask * jax.nn.sigmoid(projected[:, 0]) * projected[:, 1]).astype(jnp.bfloat16)
    sides = sides.reshape(2, devices, share, tokens).transpose(1, 0, 2, 3)
    gate = jax.nn.sigmoid(jnp.dot(normed, w_gate, preferred_element_type=jnp.float32))
    got = lax.all_to_all(sides, AXES, split_axis=0, concat_axis=0, tiled=True)
    got = got.reshape(rows, cols, 2, share, row_count, col_count).transpose(2, 3, 0, 4, 1, 5)
    got = got.reshape(2, share, rows * row_count, cols * col_count)
    total = jnp.einsum("cki,ckj->cij", got[0], got[1], preferred_element_type=jnp.float32).astype(jnp.bfloat16)
    total = total.reshape(share, rows, row_count, cols, col_count).transpose(1, 3, 0, 2, 4)
    total = total.reshape(devices, share, tokens)
    total = lax.all_to_all(total, AXES, split_axis=0, concat_axis=0, tiled=True)
    total = total.reshape(hidden, tokens).astype(jnp.float32)
    summed_norm = layer_norm(total, gain_out[:, None], bias_out[:, None], 0).astype(jnp.bfloat16)
    output = lax.dot_general(summed_norm, w_out, (((0,), (0,)), ((), ())), preferred_element_type=jnp.float32)
    return (gate * output).astype(jnp.bfloat16).reshape(row_count, col_count, channels)


def solution(mesh):
    rows, cols = mesh.shape["row"], mesh.shape["col"]
    halves = 2
    parts = (mesh.shape["groups"], halves, rows // halves, cols)
    finer = jax.sharding.Mesh(mesh.devices.reshape(parts), ("groups", "half", "quad", "col"))

    def per_shard(*args):
        near, hidden, length = rows * cols // halves, args[-1].shape[0], args[1].shape[0]
        if hidden % (16 * near) == 0 and length <= 128:
            return per_device(rows, cols, halves, *args)
        return plain_per_device(rows, cols, *args)

    tokens = P(("groups", "half", "quad"), "col", None)
    in_specs = (tokens, P("groups"), P(), P(), P(), P(), P(), P(), P())
    return jax.shard_map(per_shard, mesh=finer, in_specs=in_specs, out_specs=tokens, check_vma=False)
```

```python
import functools

import jax
import jax.numpy as jnp
from jax import lax
from jax.experimental import pallas as pl
from jax.experimental.pallas import tpu as pltpu
from jax.sharding import PartitionSpec as P

epsilon = 1e-05
AXES = ("half", "quad", "col")
VMEM = pl.BlockSpec(memory_space=pltpu.VMEM)
HBM = pl.BlockSpec(memory_space=pltpu.HBM)
LIMIT = pltpu.CompilerParams(vmem_limit_bytes=32 * 1024 * 1024)


def sigmoid(x):
    return 0.5 * jnp.tanh(0.5 * x) + 0.5


def layer_norm(values, gain, bias, axis):
    mean = jnp.mean(values, axis=axis, keepdims=True)
    centred = values - mean
    variance = jnp.mean(centred * centred, axis=axis, keepdims=True)
    return centred * lax.rsqrt(variance + epsilon) * gain + bias


def column(row):
    n = row.shape[1]
    eye = lax.broadcasted_iota(jnp.int32, (n, n), 0) == lax.broadcasted_iota(jnp.int32, (n, n), 1)
    return jnp.sum(jnp.where(eye, row, 0.0), axis=1, keepdims=True)


def project_kernel(pair_hbm, gain_hbm, bias_hbm, w_hbm, mask_hbm, sides_ref, normed_ref, left_mask_ref, right_mask_ref, pair_ref, gain_ref, bias_ref, w_ref, mask_ref, column_ref, sems):
    copies = [
        pltpu.make_async_copy(source, target, sems.at[n])
        for n, (source, target) in enumerate(
            [(mask_hbm, mask_ref), (pair_hbm, pair_ref), (gain_hbm, gain_ref), (bias_hbm, bias_ref), (w_hbm, w_ref)]
        )
    ]
    for copy in copies:
        copy.start()
    devices, both, tokens = sides_ref.shape
    channels = pair_ref.shape[2]
    hidden = w_ref.shape[1] // 4
    share = both // 2
    depth, length = left_mask_ref.shape
    copies[0].wait()
    mask_row = mask_ref[...].astype(jnp.float32)
    right_mask_ref[...] = mask_row
    column_ref[...] = jnp.broadcast_to(column(mask_row), column_ref.shape)
    start = pl.multiple_of(lax.axis_index("half") * depth, depth)
    left_mask_ref[...] = column_ref[pl.ds(start, depth), 0:length] * mask_row
    for copy in copies[1:4]:
        copy.wait()
    flat = pair_ref[...].reshape(tokens, channels).astype(jnp.float32)
    normed = layer_norm(flat, gain_ref[...], bias_ref[...], -1).astype(jnp.bfloat16)
    normed_ref[...] = normed
    copies[4].wait()
    projected = lax.dot_general(w_ref[...], normed, (((0,), (1,)), ((), ())), preferred_element_type=jnp.float32)
    left = sigmoid(projected[:hidden]) * projected[hidden : 2 * hidden]
    right = sigmoid(projected[2 * hidden : 3 * hidden]) * projected[3 * hidden :]
    sides = jnp.concatenate([left.reshape(devices, share, tokens), right.reshape(devices, share, tokens)], axis=1)
    sides_ref[...] = sides.astype(jnp.bfloat16)


def triangle_kernel(halves, cols, row_count, col_count, got_ref, left_mask_ref, right_mask_ref, total_ref, wide_ref, sum_ref, flat_ref):
    sources, both, _ = got_ref.shape
    share = both // 2
    depth, length = left_mask_ref.shape
    quads = sources // cols
    for source in range(sources):
        col, row = divmod(source, quads)
        piece = got_ref[source].astype(jnp.float32)
        for k in range(row_count):
            at = (row * row_count + k) * both
            wide_ref[at : at + both, col * col_count : (col + 1) * col_count] = piece[:, k * col_count : (k + 1) * col_count]
    left_mask = left_mask_ref[...]
    right_mask = right_mask_ref[...]
    for c in range(share):
        left = (wide_ref[pl.ds(c, depth, stride=both), 0:length] * left_mask).astype(jnp.bfloat16)
        right = (wide_ref[pl.ds(share + c, depth, stride=both), 0:length] * right_mask).astype(jnp.bfloat16)
        sum_ref[pl.ds(c, length, stride=share), 0:length] = lax.dot_general(
            left, right, (((0,), (0,)), ((), ())), preferred_element_type=jnp.float32
        )
    for target in range(sources * halves):
        col, row = divmod(target // halves, quads)
        row += (halves - 1 - target % halves) * quads
        for i in range(row_count):
            at = (row * row_count + i) * share
            flat_ref[target * share : (target + 1) * share, i * col_count : (i + 1) * col_count] = sum_ref[
                at : at + share, col * col_count : (col + 1) * col_count
            ]
        total_ref[target] = flat_ref[target * share : (target + 1) * share, :].astype(jnp.bfloat16)


def gate_kernel(normed_ref, w_ref, gain_ref, bias_ref, gate_ref, gain_out_ref, bias_out_ref):
    gate_ref[...] = sigmoid(jnp.dot(normed_ref[...], w_ref[...], preferred_element_type=jnp.float32))
    gain_out_ref[...] = column(gain_ref[...])
    bias_out_ref[...] = column(bias_ref[...])


def output_kernel(total_ref, gate_ref, gain_ref, bias_ref, w_ref, out_ref):
    sources, share, tokens = total_ref.shape
    hidden = w_ref.shape[0]
    halves = sources * share // hidden
    parts = total_ref[...].astype(jnp.float32).reshape(sources // halves, halves, share, tokens)
    total = jnp.sum(parts, axis=1).reshape(hidden, tokens)
    normed = layer_norm(total, gain_ref[...], bias_ref[...], 0).astype(jnp.bfloat16)
    output = lax.dot_general(normed, w_ref[...], (((0,), (0,)), ((), ())), preferred_element_type=jnp.float32)
    out_ref[...] = (gate_ref[...] * output).astype(jnp.bfloat16).reshape(out_ref.shape)


def per_device(rows, cols, halves, pair, token_mask, gain_in, bias_in, w_in, w_gate, gain_out, bias_out, w_out):
    row_count, col_count, channels = pair.shape
    hidden = w_out.shape[0]
    devices = rows * cols
    near = devices // halves
    quads = rows // halves
    far_order = [half * near + quad * cols + col for col in range(cols) for quad in range(quads) for half in reversed(range(halves))]
    share = hidden // near
    tokens = row_count * col_count
    length = rows * row_count
    depth = length // halves
    token_mask = token_mask.reshape(1, length)
    arguments = (pair, gain_in.reshape(1, channels), bias_in.reshape(1, channels), w_in, token_mask)
    sides, normed, left_mask, right_mask = pl.pallas_call(
        project_kernel,
        out_shape=(
            jax.ShapeDtypeStruct((near, 2 * share, tokens), jnp.bfloat16),
            jax.ShapeDtypeStruct((tokens, channels), jnp.bfloat16),
            jax.ShapeDtypeStruct((depth, length), jnp.float32),
            jax.ShapeDtypeStruct((1, length), jnp.float32),
        ),
        in_specs=[HBM] * 5,
        out_specs=(VMEM, VMEM, VMEM, VMEM),
        scratch_shapes=[
            pltpu.VMEM(pair.shape, pair.dtype),
            pltpu.VMEM((1, channels), jnp.float32),
            pltpu.VMEM((1, channels), jnp.float32),
            pltpu.VMEM(w_in.shape, w_in.dtype),
            pltpu.VMEM((1, length), jnp.int32),
            pltpu.VMEM((length, 128), jnp.float32),
            pltpu.SemaphoreType.DMA((5,)),
        ],
        compiler_params=LIMIT,
    )(*(pltpu.with_memory_space_constraint(x, pltpu.HBM) for x in arguments))
    got = lax.all_to_all(sides, ("col", "quad"), split_axis=0, concat_axis=0, tiled=True)
    total = pl.pallas_call(
        functools.partial(triangle_kernel, halves, cols, row_count, col_count),
        out_shape=jax.ShapeDtypeStruct((devices, share, tokens), jnp.bfloat16),
        in_specs=[VMEM] * 3,
        out_specs=VMEM,
        scratch_shapes=[
            pltpu.VMEM((depth * 2 * share, 128), jnp.float32),
            pltpu.VMEM((length * share, 128), jnp.float32),
            pltpu.VMEM((devices * share, tokens), jnp.float32),
        ],
        compiler_params=LIMIT,
    )(got, left_mask, right_mask)
    gate, gain_out, bias_out = pl.pallas_call(
        gate_kernel,
        out_shape=(
            jax.ShapeDtypeStruct((tokens, channels), jnp.float32),
            jax.ShapeDtypeStruct((hidden, 1), jnp.float32),
            jax.ShapeDtypeStruct((hidden, 1), jnp.float32),
        ),
        in_specs=[VMEM] * 4,
        out_specs=(VMEM, VMEM, VMEM),
        compiler_params=LIMIT,
        cost_estimate=pl.CostEstimate(flops=2 * tokens * channels * channels, bytes_accessed=4 * tokens * channels, transcendentals=0),
    )(normed, w_gate, gain_out.reshape(1, hidden), bias_out.reshape(1, hidden))
    total = lax.all_to_all(total, ("half", "quad", "col"), split_axis=0, concat_axis=0, tiled=True, axis_index_groups=[far_order])
    return pl.pallas_call(
        output_kernel,
        out_shape=jax.ShapeDtypeStruct(pair.shape, jnp.bfloat16),
        in_specs=[VMEM] * 5,
        out_specs=VMEM,
        compiler_params=LIMIT,
    )(total, gate, gain_out, bias_out, w_out)


def plain_per_device(rows, cols, pair, token_mask, gain_in, bias_in, w_in, w_gate, gain_out, bias_out, w_out):
    row_count, col_count, channels = pair.shape
    hidden = w_out.shape[0]
    devices = rows * cols
    share = hidden // devices
    tokens = row_count * col_count
    row_start = lax.axis_index(("half", "quad")) * row_count
    col_start = lax.axis_index("col") * col_count
    mask_float = token_mask.astype(jnp.float32)
    mask_rows = lax.dynamic_slice_in_dim(mask_float, row_start, row_count)
    mask_cols = lax.dynamic_slice_in_dim(mask_float, col_start, col_count)
    pair_mask = (mask_rows[:, None] * mask_cols[None, :]).reshape(1, tokens)
    flat = pair.reshape(tokens, channels).astype(jnp.float32)
    normed = layer_norm(flat, gain_in, bias_in, -1).astype(jnp.bfloat16)
    projected = lax.dot_general(w_in, normed, (((0,), (1,)), ((), ())), preferred_element_type=jnp.float32)
    projected = projected.reshape(2, 2, hidden, tokens)
    sides = (pair_mask * jax.nn.sigmoid(projected[:, 0]) * projected[:, 1]).astype(jnp.bfloat16)
    sides = sides.reshape(2, devices, share, tokens).transpose(1, 0, 2, 3)
    gate = jax.nn.sigmoid(jnp.dot(normed, w_gate, preferred_element_type=jnp.float32))
    got = lax.all_to_all(sides, AXES, split_axis=0, concat_axis=0, tiled=True)
    got = got.reshape(rows, cols, 2, share, row_count, col_count).transpose(2, 3, 0, 4, 1, 5)
    got = got.reshape(2, share, rows * row_count, cols * col_count)
    total = jnp.einsum("cki,ckj->cij", got[0], got[1], preferred_element_type=jnp.float32).astype(jnp.bfloat16)
    total = total.reshape(share, rows, row_count, cols, col_count).transpose(1, 3, 0, 2, 4)
    total = total.reshape(devices, share, tokens)
    total = lax.all_to_all(total, AXES, split_axis=0, concat_axis=0, tiled=True)
    total = total.reshape(hidden, tokens).astype(jnp.float32)
    summed_norm = layer_norm(total, gain_out[:, None], bias_out[:, None], 0).astype(jnp.bfloat16)
    output = lax.dot_general(summed_norm, w_out, (((0,), (0,)), ((), ())), preferred_element_type=jnp.float32)
    return (gate * output).astype(jnp.bfloat16).reshape(row_count, col_count, channels)


def solution(mesh):
    rows, cols = mesh.shape["row"], mesh.shape["col"]
    halves = 2
    parts = (mesh.shape["groups"], halves, rows // halves, cols)
    finer = jax.sharding.Mesh(mesh.devices.reshape(parts), ("groups", "half", "quad", "col"))

    def per_shard(*args):
        near, hidden, length = rows * cols // halves, args[-1].shape[0], args[1].shape[0]
        if hidden % (16 * near) == 0 and length <= 128:
            return per_device(rows, cols, halves, *args)
        return plain_per_device(rows, cols, *args)

    tokens = P(("groups", "half", "quad"), "col", None)
    in_specs = (tokens, P("groups"), P(), P(), P(), P(), P(), P(), P())
    return jax.shard_map(per_shard, mesh=finer, in_specs=in_specs, out_specs=tokens, check_vma=False)
```

```python
import functools

import jax
import jax.numpy as jnp
from jax import lax
from jax.experimental import pallas as pl
from jax.experimental.pallas import tpu as pltpu
from jax.sharding import PartitionSpec as P

epsilon = 1e-05
AXES = ("half", "quad", "col")
VMEM = pl.BlockSpec(memory_space=pltpu.VMEM)
HBM = pl.BlockSpec(memory_space=pltpu.HBM)
LIMIT = pltpu.CompilerParams(vmem_limit_bytes=32 * 1024 * 1024)


def sigmoid(x):
    return 0.5 * jnp.tanh(0.5 * x) + 0.5


def layer_norm(values, gain, bias, axis):
    mean = jnp.mean(values, axis=axis, keepdims=True)
    centred = values - mean
    variance = jnp.mean(centred * centred, axis=axis, keepdims=True)
    return centred * lax.rsqrt(variance + epsilon) * gain + bias


def column(row):
    n = row.shape[1]
    eye = lax.broadcasted_iota(jnp.int32, (n, n), 0) == lax.broadcasted_iota(jnp.int32, (n, n), 1)
    return jnp.sum(jnp.where(eye, row, 0.0), axis=1, keepdims=True)


def project_kernel(pair_hbm, gain_hbm, bias_hbm, w_hbm, mask_hbm, sides_ref, normed_ref, left_mask_ref, right_mask_ref, pair_ref, gain_ref, bias_ref, w_ref, mask_ref, column_ref, sems):
    copies = [
        pltpu.make_async_copy(source, target, sems.at[n])
        for n, (source, target) in enumerate(
            [(mask_hbm, mask_ref), (pair_hbm, pair_ref), (gain_hbm, gain_ref), (bias_hbm, bias_ref), (w_hbm, w_ref)]
        )
    ]
    for copy in copies:
        copy.start()
    devices, both, tokens = sides_ref.shape
    channels = pair_ref.shape[2]
    hidden = w_ref.shape[1] // 4
    share = both // 2
    depth, length = left_mask_ref.shape
    copies[0].wait()
    mask_row = mask_ref[...].astype(jnp.float32)
    right_mask_ref[...] = mask_row
    column_ref[...] = jnp.broadcast_to(column(mask_row), column_ref.shape)
    start = pl.multiple_of(lax.axis_index("half") * depth, depth)
    left_mask_ref[...] = column_ref[pl.ds(start, depth), 0:length] * mask_row
    for copy in copies[1:4]:
        copy.wait()
    flat = pair_ref[...].reshape(tokens, channels).astype(jnp.float32)
    normed = layer_norm(flat, gain_ref[...], bias_ref[...], -1).astype(jnp.bfloat16)
    normed_ref[...] = normed
    copies[4].wait()
    projected = lax.dot_general(w_ref[...], normed, (((0,), (1,)), ((), ())), preferred_element_type=jnp.float32)
    left = sigmoid(projected[:hidden]) * projected[hidden : 2 * hidden]
    right = sigmoid(projected[2 * hidden : 3 * hidden]) * projected[3 * hidden :]
    sides = jnp.concatenate([left.reshape(devices, share, tokens), right.reshape(devices, share, tokens)], axis=1)
    sides_ref[...] = sides.astype(jnp.bfloat16)


def triangle_kernel(halves, cols, row_count, col_count, got_ref, left_mask_ref, right_mask_ref, total_ref, wide_ref, sum_ref, flat_ref):
    sources, both, _ = got_ref.shape
    share = both // 2
    depth, length = left_mask_ref.shape
    quads = sources // cols
    for source in range(sources):
        col, row = divmod(sources - 1 - source, quads)
        piece = got_ref[source].astype(jnp.float32)
        for k in range(row_count):
            at = (row * row_count + k) * both
            wide_ref[at : at + both, col * col_count : (col + 1) * col_count] = piece[:, k * col_count : (k + 1) * col_count]
    left_mask = left_mask_ref[...]
    right_mask = right_mask_ref[...]
    for c in range(share):
        left = (wide_ref[pl.ds(c, depth, stride=both), 0:length] * left_mask).astype(jnp.bfloat16)
        right = (wide_ref[pl.ds(share + c, depth, stride=both), 0:length] * right_mask).astype(jnp.bfloat16)
        sum_ref[pl.ds(c, length, stride=share), 0:length] = lax.dot_general(
            left, right, (((0,), (0,)), ((), ())), preferred_element_type=jnp.float32
        )
    for target in range(sources * halves):
        col, row = divmod(sources - 1 - target // halves, quads)
        row += (halves - 1 - target % halves) * quads
        for i in range(row_count):
            at = (row * row_count + i) * share
            flat_ref[target * share : (target + 1) * share, i * col_count : (i + 1) * col_count] = sum_ref[
                at : at + share, col * col_count : (col + 1) * col_count
            ]
        total_ref[target] = flat_ref[target * share : (target + 1) * share, :].astype(jnp.bfloat16)


def gate_kernel(normed_ref, w_ref, gain_ref, bias_ref, gate_ref, gain_out_ref, bias_out_ref):
    gate_ref[...] = sigmoid(jnp.dot(normed_ref[...], w_ref[...], preferred_element_type=jnp.float32))
    gain_out_ref[...] = column(gain_ref[...])
    bias_out_ref[...] = column(bias_ref[...])


def output_kernel(total_ref, gate_ref, gain_ref, bias_ref, w_ref, out_ref):
    sources, share, tokens = total_ref.shape
    hidden = w_ref.shape[0]
    halves = sources * share // hidden
    parts = total_ref[...].astype(jnp.float32).reshape(sources // halves, halves, share, tokens)
    total = jnp.sum(parts, axis=1).reshape(hidden, tokens)
    normed = layer_norm(total, gain_ref[...], bias_ref[...], 0).astype(jnp.bfloat16)
    output = lax.dot_general(normed, w_ref[...], (((0,), (0,)), ((), ())), preferred_element_type=jnp.float32)
    out_ref[...] = (gate_ref[...] * output).astype(jnp.bfloat16).reshape(out_ref.shape)


def per_device(rows, cols, halves, pair, token_mask, gain_in, bias_in, w_in, w_gate, gain_out, bias_out, w_out):
    row_count, col_count, channels = pair.shape
    hidden = w_out.shape[0]
    devices = rows * cols
    near = devices // halves
    quads = rows // halves
    near_order = [quad * cols + col for col in reversed(range(cols)) for quad in reversed(range(quads))]
    far_order = [half * near + index for index in near_order for half in reversed(range(halves))]
    share = hidden // near
    tokens = row_count * col_count
    length = rows * row_count
    depth = length // halves
    token_mask = token_mask.reshape(1, length)
    arguments = (pair, gain_in.reshape(1, channels), bias_in.reshape(1, channels), w_in, token_mask)
    sides, normed, left_mask, right_mask = pl.pallas_call(
        project_kernel,
        out_shape=(
            jax.ShapeDtypeStruct((near, 2 * share, tokens), jnp.bfloat16),
            jax.ShapeDtypeStruct((tokens, channels), jnp.bfloat16),
            jax.ShapeDtypeStruct((depth, length), jnp.float32),
            jax.ShapeDtypeStruct((1, length), jnp.float32),
        ),
        in_specs=[HBM] * 5,
        out_specs=(VMEM, VMEM, VMEM, VMEM),
        scratch_shapes=[
            pltpu.VMEM(pair.shape, pair.dtype),
            pltpu.VMEM((1, channels), jnp.float32),
            pltpu.VMEM((1, channels), jnp.float32),
            pltpu.VMEM(w_in.shape, w_in.dtype),
            pltpu.VMEM((1, length), jnp.int32),
            pltpu.VMEM((length, 128), jnp.float32),
            pltpu.SemaphoreType.DMA((5,)),
        ],
        compiler_params=LIMIT,
    )(*(pltpu.with_memory_space_constraint(x, pltpu.HBM) for x in arguments))
    got = lax.all_to_all(sides, ("quad", "col"), split_axis=0, concat_axis=0, tiled=True, axis_index_groups=[near_order])
    total = pl.pallas_call(
        functools.partial(triangle_kernel, halves, cols, row_count, col_count),
        out_shape=jax.ShapeDtypeStruct((devices, share, tokens), jnp.bfloat16),
        in_specs=[VMEM] * 3,
        out_specs=VMEM,
        scratch_shapes=[
            pltpu.VMEM((depth * 2 * share, 128), jnp.float32),
            pltpu.VMEM((length * share, 128), jnp.float32),
            pltpu.VMEM((devices * share, tokens), jnp.float32),
        ],
        compiler_params=LIMIT,
    )(got, left_mask, right_mask)
    gate, gain_out, bias_out = pl.pallas_call(
        gate_kernel,
        out_shape=(
            jax.ShapeDtypeStruct((tokens, channels), jnp.float32),
            jax.ShapeDtypeStruct((hidden, 1), jnp.float32),
            jax.ShapeDtypeStruct((hidden, 1), jnp.float32),
        ),
        in_specs=[VMEM] * 4,
        out_specs=(VMEM, VMEM, VMEM),
        compiler_params=LIMIT,
        cost_estimate=pl.CostEstimate(flops=2 * tokens * channels * channels, bytes_accessed=4 * tokens * channels, transcendentals=0),
    )(normed, w_gate, gain_out.reshape(1, hidden), bias_out.reshape(1, hidden))
    total = lax.all_to_all(total, ("half", "quad", "col"), split_axis=0, concat_axis=0, tiled=True, axis_index_groups=[far_order])
    return pl.pallas_call(
        output_kernel,
        out_shape=jax.ShapeDtypeStruct(pair.shape, jnp.bfloat16),
        in_specs=[VMEM] * 5,
        out_specs=VMEM,
        compiler_params=LIMIT,
    )(total, gate, gain_out, bias_out, w_out)


def plain_per_device(rows, cols, pair, token_mask, gain_in, bias_in, w_in, w_gate, gain_out, bias_out, w_out):
    row_count, col_count, channels = pair.shape
    hidden = w_out.shape[0]
    devices = rows * cols
    share = hidden // devices
    tokens = row_count * col_count
    row_start = lax.axis_index(("half", "quad")) * row_count
    col_start = lax.axis_index("col") * col_count
    mask_float = token_mask.astype(jnp.float32)
    mask_rows = lax.dynamic_slice_in_dim(mask_float, row_start, row_count)
    mask_cols = lax.dynamic_slice_in_dim(mask_float, col_start, col_count)
    pair_mask = (mask_rows[:, None] * mask_cols[None, :]).reshape(1, tokens)
    flat = pair.reshape(tokens, channels).astype(jnp.float32)
    normed = layer_norm(flat, gain_in, bias_in, -1).astype(jnp.bfloat16)
    projected = lax.dot_general(w_in, normed, (((0,), (1,)), ((), ())), preferred_element_type=jnp.float32)
    projected = projected.reshape(2, 2, hidden, tokens)
    sides = (pair_mask * jax.nn.sigmoid(projected[:, 0]) * projected[:, 1]).astype(jnp.bfloat16)
    sides = sides.reshape(2, devices, share, tokens).transpose(1, 0, 2, 3)
    gate = jax.nn.sigmoid(jnp.dot(normed, w_gate, preferred_element_type=jnp.float32))
    got = lax.all_to_all(sides, AXES, split_axis=0, concat_axis=0, tiled=True)
    got = got.reshape(rows, cols, 2, share, row_count, col_count).transpose(2, 3, 0, 4, 1, 5)
    got = got.reshape(2, share, rows * row_count, cols * col_count)
    total = jnp.einsum("cki,ckj->cij", got[0], got[1], preferred_element_type=jnp.float32).astype(jnp.bfloat16)
    total = total.reshape(share, rows, row_count, cols, col_count).transpose(1, 3, 0, 2, 4)
    total = total.reshape(devices, share, tokens)
    total = lax.all_to_all(total, AXES, split_axis=0, concat_axis=0, tiled=True)
    total = total.reshape(hidden, tokens).astype(jnp.float32)
    summed_norm = layer_norm(total, gain_out[:, None], bias_out[:, None], 0).astype(jnp.bfloat16)
    output = lax.dot_general(summed_norm, w_out, (((0,), (0,)), ((), ())), preferred_element_type=jnp.float32)
    return (gate * output).astype(jnp.bfloat16).reshape(row_count, col_count, channels)


def solution(mesh):
    rows, cols = mesh.shape["row"], mesh.shape["col"]
    halves = 2
    parts = (mesh.shape["groups"], halves, rows // halves, cols)
    finer = jax.sharding.Mesh(mesh.devices.reshape(parts), ("groups", "half", "quad", "col"))

    def per_shard(*args):
        near, hidden, length = rows * cols // halves, args[-1].shape[0], args[1].shape[0]
        if hidden % (16 * near) == 0 and length <= 128:
            return per_device(rows, cols, halves, *args)
        return plain_per_device(rows, cols, *args)

    tokens = P(("groups", "half", "quad"), "col", None)
    in_specs = (tokens, P("groups"), P(), P(), P(), P(), P(), P(), P())
    return jax.shard_map(per_shard, mesh=finer, in_specs=in_specs, out_specs=tokens, check_vma=False)
```

```python
import functools

import jax
import jax.numpy as jnp
from jax import lax
from jax.experimental import pallas as pl
from jax.experimental.pallas import tpu as pltpu
from jax.sharding import PartitionSpec as P

epsilon = 1e-05
LANES = 128
AXES = ("half", "quad", "col")
VMEM = pl.BlockSpec(memory_space=pltpu.VMEM)
HBM = pl.BlockSpec(memory_space=pltpu.HBM)
LIMIT = pltpu.CompilerParams(vmem_limit_bytes=32 * 1024 * 1024)


def sigmoid(x):
    return 0.5 * jnp.tanh(0.5 * x) + 0.5


def layer_norm(values, gain, bias, axis):
    mean = jnp.mean(values, axis=axis, keepdims=True)
    centred = values - mean
    variance = jnp.mean(centred * centred, axis=axis, keepdims=True)
    return centred * lax.rsqrt(variance + epsilon) * gain + bias


def column(row):
    n = row.shape[1]
    eye = lax.broadcasted_iota(jnp.int32, (n, n), 0) == lax.broadcasted_iota(jnp.int32, (n, n), 1)
    return jnp.sum(jnp.where(eye, row, 0.0), axis=1, keepdims=True)


def pack(x):
    rows, tokens = x.shape[-2:]
    whole, rest = divmod(tokens, LANES)
    blocks = [x[..., t * LANES : (t + 1) * LANES] for t in range(whole)]
    if rest:
        tail = x[..., whole * LANES :]
        blocks.append(jnp.concatenate([tail[..., : rows // 2, :], tail[..., rows // 2 :, :]], axis=-1))
    return jnp.concatenate(blocks, axis=-2)


def unpack(x, rows):
    whole, rest = divmod(x.shape[-2], rows)
    blocks = [x[..., t * rows : (t + 1) * rows, :] for t in range(whole)]
    if rest:
        tail = x[..., whole * rows :, :]
        blocks.append(jnp.concatenate([tail[..., : LANES // 2], tail[..., LANES // 2 :]], axis=-2))
    return jnp.concatenate(blocks, axis=-1)


def project_kernel(pair_hbm, gain_hbm, bias_hbm, w_hbm, mask_hbm, sides_ref, normed_ref, left_mask_ref, right_mask_ref, pair_ref, gain_ref, bias_ref, w_ref, mask_ref, column_ref, sems):
    copies = [
        pltpu.make_async_copy(source, target, sems.at[n])
        for n, (source, target) in enumerate(
            [(mask_hbm, mask_ref), (pair_hbm, pair_ref), (gain_hbm, gain_ref), (bias_hbm, bias_ref), (w_hbm, w_ref)]
        )
    ]
    for copy in copies:
        copy.start()
    devices = sides_ref.shape[0]
    tokens, channels = normed_ref.shape
    hidden = w_ref.shape[1] // 4
    share = hidden // devices
    depth, length = left_mask_ref.shape
    copies[0].wait()
    mask_row = mask_ref[...].astype(jnp.float32)
    right_mask_ref[...] = mask_row
    column_ref[...] = jnp.broadcast_to(column(mask_row), column_ref.shape)
    start = pl.multiple_of(lax.axis_index("half") * depth, depth)
    left_mask_ref[...] = column_ref[pl.ds(start, depth), 0:length] * mask_row
    for copy in copies[1:4]:
        copy.wait()
    flat = pair_ref[...].reshape(tokens, channels).astype(jnp.float32)
    normed = layer_norm(flat, gain_ref[...], bias_ref[...], -1).astype(jnp.bfloat16)
    normed_ref[...] = normed
    copies[4].wait()
    projected = lax.dot_general(w_ref[...], normed, (((0,), (1,)), ((), ())), preferred_element_type=jnp.float32)
    left = sigmoid(projected[:hidden]) * projected[hidden : 2 * hidden]
    right = sigmoid(projected[2 * hidden : 3 * hidden]) * projected[3 * hidden :]
    sides = jnp.concatenate([left.reshape(devices, share, tokens), right.reshape(devices, share, tokens)], axis=1)
    sides_ref[...] = pack(sides).astype(jnp.bfloat16)


def triangle_kernel(halves, cols, row_count, col_count, share, got_ref, left_mask_ref, right_mask_ref, total_ref, wide_ref, sum_ref, flat_ref):
    sources = got_ref.shape[0]
    both = 2 * share
    depth, length = left_mask_ref.shape
    wide_step, sum_step = wide_ref.shape[0] // depth, sum_ref.shape[0] // length
    quads = sources // cols
    for source in range(sources):
        col, row = divmod(sources - 1 - source, quads)
        piece = unpack(got_ref[source].astype(jnp.float32), both)
        for k in range(row_count):
            at = (row * row_count + k) * wide_step
            wide_ref[at : at + both, col * col_count : (col + 1) * col_count] = piece[:, k * col_count : (k + 1) * col_count]
    left_mask = left_mask_ref[...]
    right_mask = right_mask_ref[...]
    for c in range(share):
        left = (wide_ref[pl.ds(c, depth, stride=wide_step), 0:length] * left_mask).astype(jnp.bfloat16)
        right = (wide_ref[pl.ds(share + c, depth, stride=wide_step), 0:length] * right_mask).astype(jnp.bfloat16)
        sum_ref[pl.ds(c, length, stride=sum_step), 0:length] = lax.dot_general(
            left, right, (((0,), (0,)), ((), ())), preferred_element_type=jnp.float32
        )
    for target in range(sources * halves):
        col, row = divmod(sources - 1 - target // halves, quads)
        row += (halves - 1 - target % halves) * quads
        for i in range(row_count):
            at = (row * row_count + i) * sum_step
            flat_ref[target * share : (target + 1) * share, i * col_count : (i + 1) * col_count] = sum_ref[
                at : at + share, col * col_count : (col + 1) * col_count
            ]
        total_ref[target] = pack(flat_ref[target * share : (target + 1) * share, :]).astype(jnp.bfloat16)


def gate_kernel(normed_ref, w_ref, gain_ref, bias_ref, gate_ref, gain_out_ref, bias_out_ref):
    gate_ref[...] = sigmoid(jnp.dot(normed_ref[...], w_ref[...], preferred_element_type=jnp.float32))
    gain_out_ref[...] = column(gain_ref[...])
    bias_out_ref[...] = column(bias_ref[...])


def output_kernel(total_ref, gate_ref, gain_ref, bias_ref, w_ref, out_ref):
    sources, packed, _ = total_ref.shape
    tokens = gate_ref.shape[0]
    hidden = w_ref.shape[0]
    share = packed * LANES // tokens
    near = hidden // share
    parts = total_ref[...].astype(jnp.float32).reshape(near, sources // near, packed, LANES)
    total = unpack(jnp.sum(parts, axis=1), share).reshape(hidden, tokens)
    normed = layer_norm(total, gain_ref[...], bias_ref[...], 0).astype(jnp.bfloat16)
    output = lax.dot_general(normed, w_ref[...], (((0,), (0,)), ((), ())), preferred_element_type=jnp.float32)
    out_ref[...] = (gate_ref[...] * output).astype(jnp.bfloat16).reshape(out_ref.shape)


def per_device(rows, cols, halves, pair, token_mask, gain_in, bias_in, w_in, w_gate, gain_out, bias_out, w_out):
    row_count, col_count, channels = pair.shape
    hidden = w_out.shape[0]
    devices = rows * cols
    near = devices // halves
    quads = rows // halves
    near_order = [quad * cols + col for col in reversed(range(cols)) for quad in reversed(range(quads))]
    far_order = [half * near + index for index in near_order for half in reversed(range(halves))]
    share = hidden // near
    tokens = row_count * col_count
    length = rows * row_count
    depth = length // halves
    token_mask = token_mask.reshape(1, length)
    arguments = (pair, gain_in.reshape(1, channels), bias_in.reshape(1, channels), w_in, token_mask)
    sides, normed, left_mask, right_mask = pl.pallas_call(
        project_kernel,
        out_shape=(
            jax.ShapeDtypeStruct((near, 2 * share * tokens // LANES, LANES), jnp.bfloat16),
            jax.ShapeDtypeStruct((tokens, channels), jnp.bfloat16),
            jax.ShapeDtypeStruct((depth, length), jnp.float32),
            jax.ShapeDtypeStruct((1, length), jnp.float32),
        ),
        in_specs=[HBM] * 5,
        out_specs=(VMEM, VMEM, VMEM, VMEM),
        scratch_shapes=[
            pltpu.VMEM(pair.shape, pair.dtype),
            pltpu.VMEM((1, channels), jnp.float32),
            pltpu.VMEM((1, channels), jnp.float32),
            pltpu.VMEM(w_in.shape, w_in.dtype),
            pltpu.VMEM((1, length), jnp.int32),
            pltpu.VMEM((length, LANES), jnp.float32),
            pltpu.SemaphoreType.DMA((5,)),
        ],
        compiler_params=LIMIT,
    )(*(pltpu.with_memory_space_constraint(x, pltpu.HBM) for x in arguments))
    got = lax.all_to_all(sides, ("quad", "col"), split_axis=0, concat_axis=0, tiled=True, axis_index_groups=[near_order])
    total = pl.pallas_call(
        functools.partial(triangle_kernel, halves, cols, row_count, col_count, share),
        out_shape=jax.ShapeDtypeStruct((devices, share * tokens // LANES, LANES), jnp.bfloat16),
        in_specs=[VMEM] * 3,
        out_specs=VMEM,
        scratch_shapes=[
            pltpu.VMEM((depth * (2 * share + 8), LANES), jnp.float32),
            pltpu.VMEM((length * (share + 8), LANES), jnp.float32),
            pltpu.VMEM((devices * share, tokens), jnp.float32),
        ],
        compiler_params=LIMIT,
    )(got, left_mask, right_mask)
    gate, gain_out, bias_out = pl.pallas_call(
        gate_kernel,
        out_shape=(
            jax.ShapeDtypeStruct((tokens, channels), jnp.float32),
            jax.ShapeDtypeStruct((hidden, 1), jnp.float32),
            jax.ShapeDtypeStruct((hidden, 1), jnp.float32),
        ),
        in_specs=[VMEM] * 4,
        out_specs=(VMEM, VMEM, VMEM),
        compiler_params=LIMIT,
        cost_estimate=pl.CostEstimate(flops=2 * tokens * channels * channels, bytes_accessed=4 * tokens * channels, transcendentals=0),
    )(normed, w_gate, gain_out.reshape(1, hidden), bias_out.reshape(1, hidden))
    total = lax.all_to_all(total, ("half", "quad", "col"), split_axis=0, concat_axis=0, tiled=True, axis_index_groups=[far_order])
    return pl.pallas_call(
        output_kernel,
        out_shape=jax.ShapeDtypeStruct(pair.shape, jnp.bfloat16),
        in_specs=[VMEM] * 5,
        out_specs=VMEM,
        compiler_params=LIMIT,
    )(total, gate, gain_out, bias_out, w_out)


def plain_per_device(rows, cols, pair, token_mask, gain_in, bias_in, w_in, w_gate, gain_out, bias_out, w_out):
    row_count, col_count, channels = pair.shape
    hidden = w_out.shape[0]
    devices = rows * cols
    share = hidden // devices
    tokens = row_count * col_count
    row_start = lax.axis_index(("half", "quad")) * row_count
    col_start = lax.axis_index("col") * col_count
    mask_float = token_mask.astype(jnp.float32)
    mask_rows = lax.dynamic_slice_in_dim(mask_float, row_start, row_count)
    mask_cols = lax.dynamic_slice_in_dim(mask_float, col_start, col_count)
    pair_mask = (mask_rows[:, None] * mask_cols[None, :]).reshape(1, tokens)
    flat = pair.reshape(tokens, channels).astype(jnp.float32)
    normed = layer_norm(flat, gain_in, bias_in, -1).astype(jnp.bfloat16)
    projected = lax.dot_general(w_in, normed, (((0,), (1,)), ((), ())), preferred_element_type=jnp.float32)
    projected = projected.reshape(2, 2, hidden, tokens)
    sides = (pair_mask * jax.nn.sigmoid(projected[:, 0]) * projected[:, 1]).astype(jnp.bfloat16)
    sides = sides.reshape(2, devices, share, tokens).transpose(1, 0, 2, 3)
    gate = jax.nn.sigmoid(jnp.dot(normed, w_gate, preferred_element_type=jnp.float32))
    got = lax.all_to_all(sides, AXES, split_axis=0, concat_axis=0, tiled=True)
    got = got.reshape(rows, cols, 2, share, row_count, col_count).transpose(2, 3, 0, 4, 1, 5)
    got = got.reshape(2, share, rows * row_count, cols * col_count)
    total = jnp.einsum("cki,ckj->cij", got[0], got[1], preferred_element_type=jnp.float32).astype(jnp.bfloat16)
    total = total.reshape(share, rows, row_count, cols, col_count).transpose(1, 3, 0, 2, 4)
    total = total.reshape(devices, share, tokens)
    total = lax.all_to_all(total, AXES, split_axis=0, concat_axis=0, tiled=True)
    total = total.reshape(hidden, tokens).astype(jnp.float32)
    summed_norm = layer_norm(total, gain_out[:, None], bias_out[:, None], 0).astype(jnp.bfloat16)
    output = lax.dot_general(summed_norm, w_out, (((0,), (0,)), ((), ())), preferred_element_type=jnp.float32)
    return (gate * output).astype(jnp.bfloat16).reshape(row_count, col_count, channels)


def solution(mesh):
    rows, cols = mesh.shape["row"], mesh.shape["col"]
    halves = 2
    parts = (mesh.shape["groups"], halves, rows // halves, cols)
    finer = jax.sharding.Mesh(mesh.devices.reshape(parts), ("groups", "half", "quad", "col"))

    def per_shard(*args):
        near, hidden, length = rows * cols // halves, args[-1].shape[0], args[1].shape[0]
        tokens = args[0].shape[0] * args[0].shape[1]
        if hidden % (16 * near) == 0 and length <= LANES and tokens % (LANES // 2) == 0:
            return per_device(rows, cols, halves, *args)
        return plain_per_device(rows, cols, *args)

    tokens = P(("groups", "half", "quad"), "col", None)
    in_specs = (tokens, P("groups"), P(), P(), P(), P(), P(), P(), P())
    return jax.shard_map(per_shard, mesh=finer, in_specs=in_specs, out_specs=tokens, check_vma=False)
```

```python
import functools

import jax
import jax.numpy as jnp
from jax import lax
from jax.experimental import pallas as pl
from jax.experimental.pallas import tpu as pltpu
from jax.sharding import PartitionSpec as P

epsilon = 1e-05
LANES = 128
GROUP = 8
AXES = ("half", "quad", "col")
VMEM = pl.BlockSpec(memory_space=pltpu.VMEM)
HBM = pl.BlockSpec(memory_space=pltpu.HBM)
LIMIT = pltpu.CompilerParams(vmem_limit_bytes=32 * 1024 * 1024)


def sigmoid(x):
    return 0.5 * jnp.tanh(0.5 * x) + 0.5


def layer_norm(values, gain, bias, axis):
    mean = jnp.mean(values, axis=axis, keepdims=True)
    centred = values - mean
    variance = jnp.mean(centred * centred, axis=axis, keepdims=True)
    return centred * lax.rsqrt(variance + epsilon) * gain + bias


def column(row):
    n = row.shape[1]
    eye = lax.broadcasted_iota(jnp.int32, (n, n), 0) == lax.broadcasted_iota(jnp.int32, (n, n), 1)
    return jnp.sum(jnp.where(eye, row, 0.0), axis=1, keepdims=True)


def pack(x):
    rows, tokens = x.shape[-2:]
    whole, rest = divmod(tokens, LANES)
    blocks = [x[..., t * LANES : (t + 1) * LANES] for t in range(whole)]
    if rest:
        tail = x[..., whole * LANES :]
        blocks.append(jnp.concatenate([tail[..., : rows // 2, :], tail[..., rows // 2 :, :]], axis=-1))
    return jnp.concatenate(blocks, axis=-2)


def unpack(x, rows):
    whole, rest = divmod(x.shape[-2], rows)
    blocks = [x[..., t * rows : (t + 1) * rows, :] for t in range(whole)]
    if rest:
        tail = x[..., whole * rows :, :]
        blocks.append(jnp.concatenate([tail[..., : LANES // 2], tail[..., LANES // 2 :]], axis=-2))
    return jnp.concatenate(blocks, axis=-1)


def project_kernel(pair_hbm, gain_hbm, bias_hbm, w_hbm, mask_hbm, sides_ref, normed_ref, spread_ref, row_mask_ref, column_mask_ref, pair_ref, gain_ref, bias_ref, w_ref, mask_ref, sems):
    copies = [
        pltpu.make_async_copy(source, target, sems.at[n])
        for n, (source, target) in enumerate(
            [(mask_hbm, mask_ref), (pair_hbm, pair_ref), (gain_hbm, gain_ref), (bias_hbm, bias_ref), (w_hbm, w_ref)]
        )
    ]
    for copy in copies:
        copy.start()
    devices = sides_ref.shape[0]
    tokens, channels = normed_ref.shape
    hidden = w_ref.shape[1] // 4
    share = hidden // devices
    group, lanes = spread_ref.shape
    copies[0].wait()
    mask_row = mask_ref[...].astype(jnp.float32)
    row_mask_ref[...] = mask_row
    column_mask_ref[...] = column(mask_row)
    start = lax.axis_index("half") * (lanes // group)
    token = lax.broadcasted_iota(jnp.int32, (mask_row.shape[1], lanes), 0)
    lane = lax.broadcasted_iota(jnp.int32, (mask_row.shape[1], lanes), 1)
    pick = jnp.where(lane // group + start == token, 1.0, 0.0)
    kept = jnp.dot(mask_row.astype(jnp.bfloat16), pick.astype(jnp.bfloat16), preferred_element_type=jnp.float32)
    channel = lax.broadcasted_iota(jnp.int32, (group, lanes), 0)
    lane = lax.broadcasted_iota(jnp.int32, (group, lanes), 1)
    spread_ref[...] = jnp.where(lane % group == channel, kept, 0.0)
    for copy in copies[1:4]:
        copy.wait()
    flat = pair_ref[...].reshape(tokens, channels).astype(jnp.float32)
    normed = layer_norm(flat, gain_ref[...], bias_ref[...], -1).astype(jnp.bfloat16)
    normed_ref[...] = normed
    copies[4].wait()
    projected = lax.dot_general(w_ref[...], normed, (((0,), (1,)), ((), ())), preferred_element_type=jnp.float32)
    left = sigmoid(projected[:hidden]) * projected[hidden : 2 * hidden]
    right = sigmoid(projected[2 * hidden : 3 * hidden]) * projected[3 * hidden :]
    sides = jnp.concatenate([left.reshape(devices, share, tokens), right.reshape(devices, share, tokens)], axis=1)
    sides_ref[...] = pack(sides).astype(jnp.bfloat16)


def triangle_kernel(halves, cols, row_count, col_count, share, got_ref, spread_ref, row_mask_ref, column_mask_ref, total_ref, wide_ref, sum_ref):
    sources = got_ref.shape[0]
    both = 2 * share
    group, lanes = spread_ref.shape
    depth = lanes // group
    length = row_mask_ref.shape[1]
    quads = sources // cols
    for source in range(sources):
        col, row = divmod(sources - 1 - source, quads)
        piece = unpack(got_ref[source].astype(jnp.float32), both)
        for k in range(row_count):
            wide_ref[row * row_count + k, :, col * col_count : (col + 1) * col_count] = piece[:, k * col_count : (k + 1) * col_count]
    for part in range(share // group):
        at = part * group
        left = wide_ref[:, at : at + group, :].reshape(lanes, LANES).T[0:length] * column_mask_ref[...]
        left = (left[:, None, :] * spread_ref[...][None]).reshape(length * group, lanes).astype(jnp.bfloat16)
        right = wide_ref[:, share + at : share + at + group, :].reshape(lanes, LANES)[:, 0:length]
        right = (right * row_mask_ref[...]).astype(jnp.bfloat16)
        sums = jnp.dot(left, right, preferred_element_type=jnp.float32)
        sum_ref[:, at : at + group, 0:length] = sums.reshape(length, group, length)
    for target in range(sources * halves):
        col, row = divmod(sources - 1 - target // halves, quads)
        row += (halves - 1 - target % halves) * quads
        pieces = [sum_ref[row * row_count + i, :, col * col_count : (col + 1) * col_count] for i in range(row_count)]
        total_ref[target] = pack(jnp.concatenate(pieces, axis=1)).astype(jnp.bfloat16)


def gate_kernel(normed_ref, w_ref, gain_ref, bias_ref, gate_ref, gain_out_ref, bias_out_ref):
    gate_ref[...] = sigmoid(jnp.dot(normed_ref[...], w_ref[...], preferred_element_type=jnp.float32))
    gain_out_ref[...] = column(gain_ref[...])
    bias_out_ref[...] = column(bias_ref[...])


def output_kernel(total_ref, gate_ref, gain_ref, bias_ref, w_ref, out_ref):
    sources, packed, _ = total_ref.shape
    tokens = gate_ref.shape[0]
    hidden = w_ref.shape[0]
    share = packed * LANES // tokens
    near = hidden // share
    parts = total_ref[...].astype(jnp.float32).reshape(near, sources // near, packed, LANES)
    total = unpack(jnp.sum(parts, axis=1), share).reshape(hidden, tokens)
    normed = layer_norm(total, gain_ref[...], bias_ref[...], 0).astype(jnp.bfloat16)
    output = lax.dot_general(normed, w_ref[...], (((0,), (0,)), ((), ())), preferred_element_type=jnp.float32)
    out_ref[...] = (gate_ref[...] * output).astype(jnp.bfloat16).reshape(out_ref.shape)


def per_device(rows, cols, halves, pair, token_mask, gain_in, bias_in, w_in, w_gate, gain_out, bias_out, w_out):
    row_count, col_count, channels = pair.shape
    hidden = w_out.shape[0]
    devices = rows * cols
    near = devices // halves
    quads = rows // halves
    near_order = [quad * cols + col for col in reversed(range(cols)) for quad in reversed(range(quads))]
    far_order = [half * near + index for index in near_order for half in reversed(range(halves))]
    share = hidden // near
    tokens = row_count * col_count
    length = rows * row_count
    depth = length // halves
    token_mask = token_mask.reshape(1, length)
    arguments = (pair, gain_in.reshape(1, channels), bias_in.reshape(1, channels), w_in, token_mask)
    sides, normed, *masks = pl.pallas_call(
        project_kernel,
        out_shape=(
            jax.ShapeDtypeStruct((near, 2 * share * tokens // LANES, LANES), jnp.bfloat16),
            jax.ShapeDtypeStruct((tokens, channels), jnp.bfloat16),
            jax.ShapeDtypeStruct((GROUP, GROUP * depth), jnp.float32),
            jax.ShapeDtypeStruct((1, length), jnp.float32),
            jax.ShapeDtypeStruct((length, 1), jnp.float32),
        ),
        in_specs=[HBM] * 5,
        out_specs=(VMEM,) * 5,
        scratch_shapes=[
            pltpu.VMEM(pair.shape, pair.dtype),
            pltpu.VMEM((1, channels), jnp.float32),
            pltpu.VMEM((1, channels), jnp.float32),
            pltpu.VMEM(w_in.shape, w_in.dtype),
            pltpu.VMEM((1, length), jnp.int32),
            pltpu.SemaphoreType.DMA((5,)),
        ],
        compiler_params=LIMIT,
    )(*(pltpu.with_memory_space_constraint(x, pltpu.HBM) for x in arguments))
    got = lax.all_to_all(sides, ("quad", "col"), split_axis=0, concat_axis=0, tiled=True, axis_index_groups=[near_order])
    total = pl.pallas_call(
        functools.partial(triangle_kernel, halves, cols, row_count, col_count, share),
        out_shape=jax.ShapeDtypeStruct((devices, share * tokens // LANES, LANES), jnp.bfloat16),
        in_specs=[VMEM] * 4,
        out_specs=VMEM,
        scratch_shapes=[
            pltpu.VMEM((depth, 2 * share, LANES), jnp.float32),
            pltpu.VMEM((length, share, LANES), jnp.float32),
        ],
        compiler_params=LIMIT,
    )(got, *masks)
    gate, gain_out, bias_out = pl.pallas_call(
        gate_kernel,
        out_shape=(
            jax.ShapeDtypeStruct((tokens, channels), jnp.float32),
            jax.ShapeDtypeStruct((hidden, 1), jnp.float32),
            jax.ShapeDtypeStruct((hidden, 1), jnp.float32),
        ),
        in_specs=[VMEM] * 4,
        out_specs=(VMEM, VMEM, VMEM),
        compiler_params=LIMIT,
        cost_estimate=pl.CostEstimate(flops=2 * tokens * channels * channels, bytes_accessed=4 * tokens * channels, transcendentals=0),
    )(normed, w_gate, gain_out.reshape(1, hidden), bias_out.reshape(1, hidden))
    total = lax.all_to_all(total, ("half", "quad", "col"), split_axis=0, concat_axis=0, tiled=True, axis_index_groups=[far_order])
    return pl.pallas_call(
        output_kernel,
        out_shape=jax.ShapeDtypeStruct(pair.shape, jnp.bfloat16),
        in_specs=[VMEM] * 5,
        out_specs=VMEM,
        compiler_params=LIMIT,
    )(total, gate, gain_out, bias_out, w_out)


def plain_per_device(rows, cols, pair, token_mask, gain_in, bias_in, w_in, w_gate, gain_out, bias_out, w_out):
    row_count, col_count, channels = pair.shape
    hidden = w_out.shape[0]
    devices = rows * cols
    share = hidden // devices
    tokens = row_count * col_count
    row_start = lax.axis_index(("half", "quad")) * row_count
    col_start = lax.axis_index("col") * col_count
    mask_float = token_mask.astype(jnp.float32)
    mask_rows = lax.dynamic_slice_in_dim(mask_float, row_start, row_count)
    mask_cols = lax.dynamic_slice_in_dim(mask_float, col_start, col_count)
    pair_mask = (mask_rows[:, None] * mask_cols[None, :]).reshape(1, tokens)
    flat = pair.reshape(tokens, channels).astype(jnp.float32)
    normed = layer_norm(flat, gain_in, bias_in, -1).astype(jnp.bfloat16)
    projected = lax.dot_general(w_in, normed, (((0,), (1,)), ((), ())), preferred_element_type=jnp.float32)
    projected = projected.reshape(2, 2, hidden, tokens)
    sides = (pair_mask * jax.nn.sigmoid(projected[:, 0]) * projected[:, 1]).astype(jnp.bfloat16)
    sides = sides.reshape(2, devices, share, tokens).transpose(1, 0, 2, 3)
    gate = jax.nn.sigmoid(jnp.dot(normed, w_gate, preferred_element_type=jnp.float32))
    got = lax.all_to_all(sides, AXES, split_axis=0, concat_axis=0, tiled=True)
    got = got.reshape(rows, cols, 2, share, row_count, col_count).transpose(2, 3, 0, 4, 1, 5)
    got = got.reshape(2, share, rows * row_count, cols * col_count)
    total = jnp.einsum("cki,ckj->cij", got[0], got[1], preferred_element_type=jnp.float32).astype(jnp.bfloat16)
    total = total.reshape(share, rows, row_count, cols, col_count).transpose(1, 3, 0, 2, 4)
    total = total.reshape(devices, share, tokens)
    total = lax.all_to_all(total, AXES, split_axis=0, concat_axis=0, tiled=True)
    total = total.reshape(hidden, tokens).astype(jnp.float32)
    summed_norm = layer_norm(total, gain_out[:, None], bias_out[:, None], 0).astype(jnp.bfloat16)
    output = lax.dot_general(summed_norm, w_out, (((0,), (0,)), ((), ())), preferred_element_type=jnp.float32)
    return (gate * output).astype(jnp.bfloat16).reshape(row_count, col_count, channels)


def solution(mesh):
    rows, cols = mesh.shape["row"], mesh.shape["col"]
    halves = 2
    parts = (mesh.shape["groups"], halves, rows // halves, cols)
    finer = jax.sharding.Mesh(mesh.devices.reshape(parts), ("groups", "half", "quad", "col"))

    def per_shard(*args):
        near, hidden, length = rows * cols // halves, args[-1].shape[0], args[1].shape[0]
        tokens = args[0].shape[0] * args[0].shape[1]
        if hidden % (16 * near) == 0 and length <= LANES and tokens % (LANES // 2) == 0:
            return per_device(rows, cols, halves, *args)
        return plain_per_device(rows, cols, *args)

    tokens = P(("groups", "half", "quad"), "col", None)
    in_specs = (tokens, P("groups"), P(), P(), P(), P(), P(), P(), P())
    return jax.shard_map(per_shard, mesh=finer, in_specs=in_specs, out_specs=tokens, check_vma=False)
```

```python
import functools

import jax
import jax.numpy as jnp
from jax import lax
from jax.experimental import pallas as pl
from jax.experimental.pallas import tpu as pltpu
from jax.sharding import PartitionSpec as P

epsilon = 1e-05
LANES = 128
GROUP = 8
AXES = ("half", "quad", "col")
VMEM = pl.BlockSpec(memory_space=pltpu.VMEM)
HBM = pl.BlockSpec(memory_space=pltpu.HBM)
LIMIT = pltpu.CompilerParams(vmem_limit_bytes=32 * 1024 * 1024)


def sigmoid(x):
    return 0.5 * jnp.tanh(0.5 * x) + 0.5


def layer_norm(values, gain, bias, axis):
    mean = jnp.mean(values, axis=axis, keepdims=True)
    centred = values - mean
    variance = jnp.mean(centred * centred, axis=axis, keepdims=True)
    return centred * lax.rsqrt(variance + epsilon) * gain + bias


def column(row):
    n = row.shape[1]
    eye = lax.broadcasted_iota(jnp.int32, (n, n), 0) == lax.broadcasted_iota(jnp.int32, (n, n), 1)
    return jnp.sum(jnp.where(eye, row, 0.0), axis=1, keepdims=True)


def pack(x):
    rows, tokens = x.shape[-2:]
    whole, rest = divmod(tokens, LANES)
    blocks = [x[..., t * LANES : (t + 1) * LANES] for t in range(whole)]
    if rest:
        tail = x[..., whole * LANES :]
        blocks.append(jnp.concatenate([tail[..., : rows // 2, :], tail[..., rows // 2 :, :]], axis=-1))
    return jnp.concatenate(blocks, axis=-2)


def unpack(x, rows):
    whole, rest = divmod(x.shape[-2], rows)
    blocks = [x[..., t * rows : (t + 1) * rows, :] for t in range(whole)]
    if rest:
        tail = x[..., whole * rows :, :]
        blocks.append(jnp.concatenate([tail[..., : LANES // 2], tail[..., LANES // 2 :]], axis=-2))
    return jnp.concatenate(blocks, axis=-1)


def project_kernel(pair_hbm, gain_hbm, bias_hbm, w_hbm, mask_hbm, sides_ref, normed_ref, spread_ref, row_mask_ref, column_mask_ref, pair_ref, gain_ref, bias_ref, w_ref, mask_ref, sems):
    copies = [
        pltpu.make_async_copy(source, target, sems.at[n])
        for n, (source, target) in enumerate(
            [(mask_hbm, mask_ref), (pair_hbm, pair_ref), (gain_hbm, gain_ref), (bias_hbm, bias_ref), (w_hbm, w_ref)]
        )
    ]
    for copy in copies:
        copy.start()
    devices = sides_ref.shape[0]
    tokens, channels = normed_ref.shape
    hidden = w_ref.shape[1] // 4
    share = hidden // devices
    group, lanes = spread_ref.shape
    copies[0].wait()
    mask_row = mask_ref[...].astype(jnp.float32)
    row_mask_ref[...] = mask_row
    column_mask_ref[...] = column(mask_row)
    start = lax.axis_index("half") * (lanes // group)
    token = lax.broadcasted_iota(jnp.int32, (mask_row.shape[1], lanes), 0)
    lane = lax.broadcasted_iota(jnp.int32, (mask_row.shape[1], lanes), 1)
    pick = jnp.where(lane // group + start == token, 1.0, 0.0)
    kept = jnp.dot(mask_row.astype(jnp.bfloat16), pick.astype(jnp.bfloat16), preferred_element_type=jnp.float32)
    channel = lax.broadcasted_iota(jnp.int32, (group, lanes), 0)
    lane = lax.broadcasted_iota(jnp.int32, (group, lanes), 1)
    spread_ref[...] = jnp.where(lane % group == channel, kept, 0.0)
    for copy in copies[1:4]:
        copy.wait()
    flat = pair_ref[...].reshape(tokens, channels).astype(jnp.float32)
    normed = layer_norm(flat, gain_ref[...], bias_ref[...], -1).astype(jnp.bfloat16)
    normed_ref[...] = normed
    copies[4].wait()
    projected = lax.dot_general(w_ref[...], normed, (((0,), (1,)), ((), ())), preferred_element_type=jnp.float32)
    left = sigmoid(projected[:hidden]) * projected[hidden : 2 * hidden]
    right = sigmoid(projected[2 * hidden : 3 * hidden]) * projected[3 * hidden :]
    sides = jnp.concatenate([left.reshape(devices, share, tokens), right.reshape(devices, share, tokens)], axis=1)
    sides_ref[...] = pack(sides).astype(jnp.bfloat16)


def triangle_kernel(halves, cols, row_count, col_count, share, got_ref, spread_ref, row_mask_ref, column_mask_ref, total_ref, wide_ref, sum_ref):
    sources = got_ref.shape[0]
    both = 2 * share
    group, lanes = spread_ref.shape
    depth = lanes // group
    length = row_mask_ref.shape[1]
    quads = sources // cols
    for source in range(sources):
        col, row = divmod(sources - 1 - source, quads)
        piece = unpack(got_ref[source], both)
        for k in range(row_count):
            wide_ref[row * row_count + k, :, col * col_count : (col + 1) * col_count] = piece[:, k * col_count : (k + 1) * col_count]
    wide = wide_ref[...].astype(jnp.float32)
    parts = []
    for part in range(share // group):
        at = part * group
        left = wide[:, at : at + group, :].reshape(lanes, LANES).T[0:length] * column_mask_ref[...]
        left = (left[:, None, :] * spread_ref[...][None]).reshape(length * group, lanes).astype(jnp.bfloat16)
        right = wide[:, share + at : share + at + group, :].reshape(lanes, LANES)[:, 0:length]
        right = (right * row_mask_ref[...]).astype(jnp.bfloat16)
        sums = jnp.dot(left, right, preferred_element_type=jnp.float32)
        parts.append(sums.reshape(length, group, length))
    sum_ref[:, :, 0:length] = jnp.concatenate(parts, axis=1).astype(jnp.bfloat16)
    for target in range(sources * halves):
        col, row = divmod(sources - 1 - target // halves, quads)
        row += (halves - 1 - target % halves) * quads
        pieces = [sum_ref[row * row_count + i, :, col * col_count : (col + 1) * col_count] for i in range(row_count)]
        total_ref[target] = pack(jnp.concatenate(pieces, axis=1))


def gate_kernel(normed_ref, w_ref, gain_ref, bias_ref, gate_ref, gain_out_ref, bias_out_ref):
    gate_ref[...] = sigmoid(jnp.dot(normed_ref[...], w_ref[...], preferred_element_type=jnp.float32))
    gain_out_ref[...] = column(gain_ref[...])
    bias_out_ref[...] = column(bias_ref[...])


def output_kernel(total_ref, gate_ref, gain_ref, bias_ref, w_ref, out_ref):
    sources, packed, _ = total_ref.shape
    tokens = gate_ref.shape[0]
    hidden = w_ref.shape[0]
    share = packed * LANES // tokens
    near = hidden // share
    parts = total_ref[...].astype(jnp.float32).reshape(near, sources // near, packed, LANES)
    total = unpack(jnp.sum(parts, axis=1), share).reshape(hidden, tokens)
    normed = layer_norm(total, gain_ref[...], bias_ref[...], 0).astype(jnp.bfloat16)
    output = lax.dot_general(normed, w_ref[...], (((0,), (0,)), ((), ())), preferred_element_type=jnp.float32)
    out_ref[...] = (gate_ref[...] * output).astype(jnp.bfloat16).reshape(out_ref.shape)


def per_device(rows, cols, halves, pair, token_mask, gain_in, bias_in, w_in, w_gate, gain_out, bias_out, w_out):
    row_count, col_count, channels = pair.shape
    hidden = w_out.shape[0]
    devices = rows * cols
    near = devices // halves
    quads = rows // halves
    near_order = [quad * cols + col for col in reversed(range(cols)) for quad in reversed(range(quads))]
    far_order = [half * near + index for index in near_order for half in reversed(range(halves))]
    share = hidden // near
    tokens = row_count * col_count
    length = rows * row_count
    depth = length // halves
    token_mask = token_mask.reshape(1, length)
    arguments = (pair, gain_in.reshape(1, channels), bias_in.reshape(1, channels), w_in, token_mask)
    sides, normed, *masks = pl.pallas_call(
        project_kernel,
        out_shape=(
            jax.ShapeDtypeStruct((near, 2 * share * tokens // LANES, LANES), jnp.bfloat16),
            jax.ShapeDtypeStruct((tokens, channels), jnp.bfloat16),
            jax.ShapeDtypeStruct((GROUP, GROUP * depth), jnp.float32),
            jax.ShapeDtypeStruct((1, length), jnp.float32),
            jax.ShapeDtypeStruct((length, 1), jnp.float32),
        ),
        in_specs=[HBM] * 5,
        out_specs=(VMEM,) * 5,
        scratch_shapes=[
            pltpu.VMEM(pair.shape, pair.dtype),
            pltpu.VMEM((1, channels), jnp.float32),
            pltpu.VMEM((1, channels), jnp.float32),
            pltpu.VMEM(w_in.shape, w_in.dtype),
            pltpu.VMEM((1, length), jnp.int32),
            pltpu.SemaphoreType.DMA((5,)),
        ],
        compiler_params=LIMIT,
    )(*(pltpu.with_memory_space_constraint(x, pltpu.HBM) for x in arguments))
    got = lax.all_to_all(sides, ("quad", "col"), split_axis=0, concat_axis=0, tiled=True, axis_index_groups=[near_order])
    total = pl.pallas_call(
        functools.partial(triangle_kernel, halves, cols, row_count, col_count, share),
        out_shape=jax.ShapeDtypeStruct((devices, share * tokens // LANES, LANES), jnp.bfloat16),
        in_specs=[VMEM] * 4,
        out_specs=VMEM,
        scratch_shapes=[
            pltpu.VMEM((depth, 2 * share, LANES), jnp.bfloat16),
            pltpu.VMEM((length, share, LANES), jnp.bfloat16),
        ],
        compiler_params=LIMIT,
    )(got, *masks)
    gate, gain_out, bias_out = pl.pallas_call(
        gate_kernel,
        out_shape=(
            jax.ShapeDtypeStruct((tokens, channels), jnp.float32),
            jax.ShapeDtypeStruct((hidden, 1), jnp.float32),
            jax.ShapeDtypeStruct((hidden, 1), jnp.float32),
        ),
        in_specs=[VMEM] * 4,
        out_specs=(VMEM, VMEM, VMEM),
        compiler_params=LIMIT,
        cost_estimate=pl.CostEstimate(flops=2 * tokens * channels * channels, bytes_accessed=4 * tokens * channels, transcendentals=0),
    )(normed, w_gate, gain_out.reshape(1, hidden), bias_out.reshape(1, hidden))
    total = lax.all_to_all(total, ("half", "quad", "col"), split_axis=0, concat_axis=0, tiled=True, axis_index_groups=[far_order])
    return pl.pallas_call(
        output_kernel,
        out_shape=jax.ShapeDtypeStruct(pair.shape, jnp.bfloat16),
        in_specs=[VMEM] * 5,
        out_specs=VMEM,
        compiler_params=LIMIT,
    )(total, gate, gain_out, bias_out, w_out)


def plain_per_device(rows, cols, pair, token_mask, gain_in, bias_in, w_in, w_gate, gain_out, bias_out, w_out):
    row_count, col_count, channels = pair.shape
    hidden = w_out.shape[0]
    devices = rows * cols
    share = hidden // devices
    tokens = row_count * col_count
    row_start = lax.axis_index(("half", "quad")) * row_count
    col_start = lax.axis_index("col") * col_count
    mask_float = token_mask.astype(jnp.float32)
    mask_rows = lax.dynamic_slice_in_dim(mask_float, row_start, row_count)
    mask_cols = lax.dynamic_slice_in_dim(mask_float, col_start, col_count)
    pair_mask = (mask_rows[:, None] * mask_cols[None, :]).reshape(1, tokens)
    flat = pair.reshape(tokens, channels).astype(jnp.float32)
    normed = layer_norm(flat, gain_in, bias_in, -1).astype(jnp.bfloat16)
    projected = lax.dot_general(w_in, normed, (((0,), (1,)), ((), ())), preferred_element_type=jnp.float32)
    projected = projected.reshape(2, 2, hidden, tokens)
    sides = (pair_mask * jax.nn.sigmoid(projected[:, 0]) * projected[:, 1]).astype(jnp.bfloat16)
    sides = sides.reshape(2, devices, share, tokens).transpose(1, 0, 2, 3)
    gate = jax.nn.sigmoid(jnp.dot(normed, w_gate, preferred_element_type=jnp.float32))
    got = lax.all_to_all(sides, AXES, split_axis=0, concat_axis=0, tiled=True)
    got = got.reshape(rows, cols, 2, share, row_count, col_count).transpose(2, 3, 0, 4, 1, 5)
    got = got.reshape(2, share, rows * row_count, cols * col_count)
    total = jnp.einsum("cki,ckj->cij", got[0], got[1], preferred_element_type=jnp.float32).astype(jnp.bfloat16)
    total = total.reshape(share, rows, row_count, cols, col_count).transpose(1, 3, 0, 2, 4)
    total = total.reshape(devices, share, tokens)
    total = lax.all_to_all(total, AXES, split_axis=0, concat_axis=0, tiled=True)
    total = total.reshape(hidden, tokens).astype(jnp.float32)
    summed_norm = layer_norm(total, gain_out[:, None], bias_out[:, None], 0).astype(jnp.bfloat16)
    output = lax.dot_general(summed_norm, w_out, (((0,), (0,)), ((), ())), preferred_element_type=jnp.float32)
    return (gate * output).astype(jnp.bfloat16).reshape(row_count, col_count, channels)


def solution(mesh):
    rows, cols = mesh.shape["row"], mesh.shape["col"]
    halves = 2
    parts = (mesh.shape["groups"], halves, rows // halves, cols)
    finer = jax.sharding.Mesh(mesh.devices.reshape(parts), ("groups", "half", "quad", "col"))

    def per_shard(*args):
        near, hidden, length = rows * cols // halves, args[-1].shape[0], args[1].shape[0]
        tokens = args[0].shape[0] * args[0].shape[1]
        if hidden % (16 * near) == 0 and length <= LANES and tokens % (LANES // 2) == 0:
            return per_device(rows, cols, halves, *args)
        return plain_per_device(rows, cols, *args)

    tokens = P(("groups", "half", "quad"), "col", None)
    in_specs = (tokens, P("groups"), P(), P(), P(), P(), P(), P(), P())
    return jax.shard_map(per_shard, mesh=finer, in_specs=in_specs, out_specs=tokens, check_vma=False)
```

```python
import functools

import jax
import jax.numpy as jnp
from jax import lax
from jax.experimental import pallas as pl
from jax.experimental.pallas import tpu as pltpu
from jax.sharding import PartitionSpec as P

epsilon = 1e-05
LANES = 128
GROUP = 8
AXES = ("half", "quad", "col")
VMEM = pl.BlockSpec(memory_space=pltpu.VMEM)
HBM = pl.BlockSpec(memory_space=pltpu.HBM)
LIMIT = pltpu.CompilerParams(vmem_limit_bytes=32 * 1024 * 1024)


def sigmoid(x):
    return 0.5 * jnp.tanh(0.5 * x) + 0.5


def layer_norm(values, gain, bias, axis):
    mean = jnp.mean(values, axis=axis, keepdims=True)
    centred = values - mean
    variance = jnp.mean(centred * centred, axis=axis, keepdims=True)
    return centred * lax.rsqrt(variance + epsilon) * gain + bias


def column(row):
    n = row.shape[1]
    eye = lax.broadcasted_iota(jnp.int32, (n, n), 0) == lax.broadcasted_iota(jnp.int32, (n, n), 1)
    return jnp.sum(jnp.where(eye, row, 0.0), axis=1, keepdims=True)


def pack(x):
    rows, tokens = x.shape[-2:]
    whole, rest = divmod(tokens, LANES)
    blocks = [x[..., t * LANES : (t + 1) * LANES] for t in range(whole)]
    if rest:
        tail = x[..., whole * LANES :]
        blocks.append(jnp.concatenate([tail[..., : rows // 2, :], tail[..., rows // 2 :, :]], axis=-1))
    return jnp.concatenate(blocks, axis=-2)


def unpack(x, rows):
    whole, rest = divmod(x.shape[-2], rows)
    blocks = [x[..., t * rows : (t + 1) * rows, :] for t in range(whole)]
    if rest:
        tail = x[..., whole * rows :, :]
        blocks.append(jnp.concatenate([tail[..., : LANES // 2], tail[..., LANES // 2 :]], axis=-2))
    return jnp.concatenate(blocks, axis=-1)


def arrange(x):
    row_count, col_count, _ = x.shape
    whole, spare = row_count // 3, LANES - 2 * col_count
    blocks = []
    for t in range(whole):
        blocks += [x[2 * t], x[2 * t + 1], x[2 * whole + t, :spare]]
    return jnp.concatenate(blocks + [x[2 * whole + t, spare:] for t in range(whole)], axis=0)


def restore(x, row_count, col_count):
    whole, spare = row_count // 3, LANES - 2 * col_count
    rest = col_count - spare
    rows = []
    for t in range(whole):
        rows += [x[t * LANES : t * LANES + col_count], x[t * LANES + col_count : t * LANES + 2 * col_count]]
    for t in range(whole):
        tail = whole * LANES + t * rest
        rows += [x[t * LANES + 2 * col_count : (t + 1) * LANES], x[tail : tail + rest]]
    return jnp.concatenate(rows, axis=0)


def project_kernel(pair_hbm, gain_hbm, bias_hbm, w_hbm, mask_hbm, sides_ref, normed_ref, spread_ref, column_mask_ref, pair_ref, gain_ref, bias_ref, w_ref, mask_ref, sems):
    copies = [
        pltpu.make_async_copy(source, target, sems.at[n])
        for n, (source, target) in enumerate(
            [(mask_hbm, mask_ref), (pair_hbm, pair_ref), (gain_hbm, gain_ref), (bias_hbm, bias_ref), (w_hbm, w_ref)]
        )
    ]
    for copy in copies:
        copy.start()
    devices = sides_ref.shape[0]
    tokens, channels = normed_ref.shape
    hidden = w_ref.shape[1] // 4
    share = hidden // devices
    group, lanes = spread_ref.shape
    copies[0].wait()
    mask_row = mask_ref[...].astype(jnp.float32)
    column_mask_ref[...] = column(mask_row)
    start = lax.axis_index("half") * (lanes // group)
    token = lax.broadcasted_iota(jnp.int32, (mask_row.shape[1], lanes), 0)
    lane = lax.broadcasted_iota(jnp.int32, (mask_row.shape[1], lanes), 1)
    row_count = pair_ref.shape[0]
    whole = row_count // 3
    quads = lanes // group // row_count
    block, t, row = lane // LANES, lane // (quads * group) % whole, lane // group % quads
    k = row * row_count + jnp.where(block < 2, 2 * t + block, 2 * whole + t)
    pick = jnp.where(k + start == token, 1.0, 0.0)
    kept = jnp.dot(mask_row.astype(jnp.bfloat16), pick.astype(jnp.bfloat16), preferred_element_type=jnp.float32)
    channel = lax.broadcasted_iota(jnp.int32, (group, lanes), 0)
    lane = lax.broadcasted_iota(jnp.int32, (group, lanes), 1)
    spread_ref[...] = jnp.where(lane % group == channel, kept, 0.0)
    for copy in copies[1:4]:
        copy.wait()
    flat = pair_ref[...].reshape(tokens, channels).astype(jnp.float32)
    normed = layer_norm(flat, gain_ref[...], bias_ref[...], -1).astype(jnp.bfloat16)
    normed_ref[...] = normed
    copies[4].wait()
    arranged = arrange(normed.reshape(pair_ref.shape))
    projected = lax.dot_general(w_ref[...], arranged, (((0,), (1,)), ((), ())), preferred_element_type=jnp.float32)
    left = sigmoid(projected[:hidden]) * projected[hidden : 2 * hidden]
    right = sigmoid(projected[2 * hidden : 3 * hidden]) * projected[3 * hidden :]
    sides = jnp.concatenate([left.reshape(devices, share, tokens), right.reshape(devices, share, tokens)], axis=1)
    sides_ref[...] = pack(sides).astype(jnp.bfloat16)


def triangle_kernel(halves, cols, row_count, col_count, share, got_ref, spread_ref, mask_ref, total_ref):
    sources = got_ref.shape[0]
    both = 2 * share
    group, lanes = spread_ref.shape
    length = mask_ref.shape[0]
    rows, quads, parts = length // row_count, sources // cols, share // group
    whole, spare = row_count // 3, LANES - 2 * col_count
    rest = col_count - spare
    blocks = [[got_ref[sources - 1 - (col * quads + row)].astype(jnp.float32) for row in range(quads)] for col in range(cols)]

    def turned(picks):
        return jnp.concatenate([blocks[col][row][at : at + group] for col, row, at in picks], axis=0).T

    tail = turned([(col, row, whole * both + part * group) for col in range(cols) for part in range(parts) for row in range(quads)])

    def side(which, part):
        even, odd, third = [], [], []
        for col in range(cols):
            at = which * share + part * group
            block = turned([(col, row, t * both + at) for t in range(whole) for row in range(quads)])
            even.append(block[:col_count])
            odd.append(block[col_count : 2 * col_count])
            lane = (col * parts + part) * quads * group
            at = which * LANES // 2
            last = [tail[at + t * rest : at + (t + 1) * rest, lane : lane + quads * group] for t in range(whole)]
            third += [block[2 * col_count :], jnp.concatenate(last, axis=1)]
        tokens = [jnp.concatenate(pieces, axis=0) for pieces in (even, odd, third)]
        return jnp.concatenate(tokens, axis=1) * mask_ref[...]

    def placed(pieces):
        return jnp.concatenate([jnp.zeros((piece, lanes), jnp.bfloat16) if isinstance(piece, int) else piece for piece in pieces], axis=0)

    contract = (((1,), (1,)), ((), ()))
    mains, lasts = [], []
    for part in range(parts):
        left, right = side(0, part), side(1, part).astype(jnp.bfloat16)
        left = (left[:, None, :] * spread_ref[...][None]).reshape(rows, row_count, group, lanes)
        pairs = left[:, : 2 * whole].reshape(rows, whole, 2, group, lanes)
        left = jnp.concatenate([pairs[:, :, 0], pairs[:, :, 1], left[:, 2 * whole :]], axis=-1)
        left = left.reshape(rows * whole * group, 3 * lanes).astype(jnp.bfloat16)
        ours = [right[col * col_count : (col + 1) * col_count] for col in range(cols)]
        weights = [
            placed([p for mine in ours for p in (mine, LANES - col_count)]),
            placed([p for mine in ours for p in (col_count, mine, spare)]),
            placed([p for mine in ours for p in (2 * col_count, mine[:spare])]),
        ]
        weights = jnp.concatenate(weights, axis=1)
        mains.append(lax.dot_general(left, weights, contract, preferred_element_type=jnp.float32))
        weights = jnp.concatenate([mine[spare:] for mine in ours], axis=0)
        lasts.append(lax.dot_general(left[:, 2 * lanes :], weights, contract, preferred_element_type=jnp.float32))
    for target in range(sources * halves):
        col, row = divmod(sources - 1 - target // halves, quads)
        row += (halves - 1 - target % halves) * quads
        spots = [(row * whole + t) * group for t in range(whole)]
        tiles = [main[at : at + group, col * LANES : (col + 1) * LANES] for at in spots for main in mains]
        last = [part[at : at + group, col * rest : (col + 1) * rest] for part in lasts for at in spots]
        tiles.append(jnp.concatenate(last, axis=1))
        total_ref[target] = jnp.concatenate(tiles, axis=0).astype(jnp.bfloat16)


def gate_kernel(normed_ref, w_ref, gain_ref, bias_ref, gate_ref, gain_out_ref, bias_out_ref):
    gate_ref[...] = sigmoid(jnp.dot(normed_ref[...], w_ref[...], preferred_element_type=jnp.float32))
    gain_out_ref[...] = column(gain_ref[...])
    bias_out_ref[...] = column(bias_ref[...])


def output_kernel(total_ref, gate_ref, gain_ref, bias_ref, w_ref, out_ref):
    sources, packed, _ = total_ref.shape
    tokens = gate_ref.shape[0]
    hidden = w_ref.shape[0]
    share = packed * LANES // tokens
    near = hidden // share
    parts = total_ref[...].astype(jnp.float32).reshape(near, sources // near, packed, LANES)
    total = unpack(jnp.sum(parts, axis=1), share).reshape(hidden, tokens)
    normed = layer_norm(total, gain_ref[...], bias_ref[...], 0).astype(jnp.bfloat16)
    output = lax.dot_general(normed, w_ref[...], (((0,), (0,)), ((), ())), preferred_element_type=jnp.float32)
    output = restore(output, out_ref.shape[0], out_ref.shape[1])
    out_ref[...] = (gate_ref[...] * output).astype(jnp.bfloat16).reshape(out_ref.shape)


def per_device(rows, cols, halves, pair, token_mask, gain_in, bias_in, w_in, w_gate, gain_out, bias_out, w_out):
    row_count, col_count, channels = pair.shape
    hidden = w_out.shape[0]
    devices = rows * cols
    near = devices // halves
    quads = rows // halves
    near_order = [quad * cols + col for col in reversed(range(cols)) for quad in reversed(range(quads))]
    far_order = [half * near + index for index in near_order for half in reversed(range(halves))]
    share = hidden // near
    tokens = row_count * col_count
    length = rows * row_count
    depth = length // halves
    token_mask = token_mask.reshape(1, length)
    arguments = (pair, gain_in.reshape(1, channels), bias_in.reshape(1, channels), w_in, token_mask)
    sides, normed, *masks = pl.pallas_call(
        project_kernel,
        out_shape=(
            jax.ShapeDtypeStruct((near, 2 * share * tokens // LANES, LANES), jnp.bfloat16),
            jax.ShapeDtypeStruct((tokens, channels), jnp.bfloat16),
            jax.ShapeDtypeStruct((GROUP, GROUP * depth), jnp.float32),
            jax.ShapeDtypeStruct((length, 1), jnp.float32),
        ),
        in_specs=[HBM] * 5,
        out_specs=(VMEM,) * 4,
        scratch_shapes=[
            pltpu.VMEM(pair.shape, pair.dtype),
            pltpu.VMEM((1, channels), jnp.float32),
            pltpu.VMEM((1, channels), jnp.float32),
            pltpu.VMEM(w_in.shape, w_in.dtype),
            pltpu.VMEM((1, length), jnp.int32),
            pltpu.SemaphoreType.DMA((5,)),
        ],
        compiler_params=LIMIT,
    )(*(pltpu.with_memory_space_constraint(x, pltpu.HBM) for x in arguments))
    got = lax.all_to_all(sides, ("quad", "col"), split_axis=0, concat_axis=0, tiled=True, axis_index_groups=[near_order])
    total = pl.pallas_call(
        functools.partial(triangle_kernel, halves, cols, row_count, col_count, share),
        out_shape=jax.ShapeDtypeStruct((devices, share * tokens // LANES, LANES), jnp.bfloat16),
        in_specs=[VMEM] * 3,
        out_specs=VMEM,
        compiler_params=LIMIT,
    )(got, *masks)
    gate, gain_out, bias_out = pl.pallas_call(
        gate_kernel,
        out_shape=(
            jax.ShapeDtypeStruct((tokens, channels), jnp.float32),
            jax.ShapeDtypeStruct((hidden, 1), jnp.float32),
            jax.ShapeDtypeStruct((hidden, 1), jnp.float32),
        ),
        in_specs=[VMEM] * 4,
        out_specs=(VMEM, VMEM, VMEM),
        compiler_params=LIMIT,
        cost_estimate=pl.CostEstimate(flops=2 * tokens * channels * channels, bytes_accessed=4 * tokens * channels, transcendentals=0),
    )(normed, w_gate, gain_out.reshape(1, hidden), bias_out.reshape(1, hidden))
    total = lax.all_to_all(total, ("half", "quad", "col"), split_axis=0, concat_axis=0, tiled=True, axis_index_groups=[far_order])
    return pl.pallas_call(
        output_kernel,
        out_shape=jax.ShapeDtypeStruct(pair.shape, jnp.bfloat16),
        in_specs=[VMEM] * 5,
        out_specs=VMEM,
        compiler_params=LIMIT,
    )(total, gate, gain_out, bias_out, w_out)


def plain_per_device(rows, cols, pair, token_mask, gain_in, bias_in, w_in, w_gate, gain_out, bias_out, w_out):
    row_count, col_count, channels = pair.shape
    hidden = w_out.shape[0]
    devices = rows * cols
    share = hidden // devices
    tokens = row_count * col_count
    row_start = lax.axis_index(("half", "quad")) * row_count
    col_start = lax.axis_index("col") * col_count
    mask_float = token_mask.astype(jnp.float32)
    mask_rows = lax.dynamic_slice_in_dim(mask_float, row_start, row_count)
    mask_cols = lax.dynamic_slice_in_dim(mask_float, col_start, col_count)
    pair_mask = (mask_rows[:, None] * mask_cols[None, :]).reshape(1, tokens)
    flat = pair.reshape(tokens, channels).astype(jnp.float32)
    normed = layer_norm(flat, gain_in, bias_in, -1).astype(jnp.bfloat16)
    projected = lax.dot_general(w_in, normed, (((0,), (1,)), ((), ())), preferred_element_type=jnp.float32)
    projected = projected.reshape(2, 2, hidden, tokens)
    sides = (pair_mask * jax.nn.sigmoid(projected[:, 0]) * projected[:, 1]).astype(jnp.bfloat16)
    sides = sides.reshape(2, devices, share, tokens).transpose(1, 0, 2, 3)
    gate = jax.nn.sigmoid(jnp.dot(normed, w_gate, preferred_element_type=jnp.float32))
    got = lax.all_to_all(sides, AXES, split_axis=0, concat_axis=0, tiled=True)
    got = got.reshape(rows, cols, 2, share, row_count, col_count).transpose(2, 3, 0, 4, 1, 5)
    got = got.reshape(2, share, rows * row_count, cols * col_count)
    total = jnp.einsum("cki,ckj->cij", got[0], got[1], preferred_element_type=jnp.float32).astype(jnp.bfloat16)
    total = total.reshape(share, rows, row_count, cols, col_count).transpose(1, 3, 0, 2, 4)
    total = total.reshape(devices, share, tokens)
    total = lax.all_to_all(total, AXES, split_axis=0, concat_axis=0, tiled=True)
    total = total.reshape(hidden, tokens).astype(jnp.float32)
    summed_norm = layer_norm(total, gain_out[:, None], bias_out[:, None], 0).astype(jnp.bfloat16)
    output = lax.dot_general(summed_norm, w_out, (((0,), (0,)), ((), ())), preferred_element_type=jnp.float32)
    return (gate * output).astype(jnp.bfloat16).reshape(row_count, col_count, channels)


def solution(mesh):
    rows, cols = mesh.shape["row"], mesh.shape["col"]
    halves = 2
    parts = (mesh.shape["groups"], halves, rows // halves, cols)
    finer = jax.sharding.Mesh(mesh.devices.reshape(parts), ("groups", "half", "quad", "col"))

    def per_shard(*args):
        near, hidden, length = rows * cols // halves, args[-1].shape[0], args[1].shape[0]
        row_count, col_count, _ = args[0].shape
        spare = LANES - 2 * col_count
        fits = hidden % (2 * GROUP * near) == 0 and cols == 2 and length <= LANES and row_count % 3 == 0
        fits = fits and 0 < spare < col_count and row_count // 3 * (col_count - spare) * 2 == LANES
        fits = fits and row_count // 3 * (rows // halves) * GROUP == LANES
        return per_device(rows, cols, halves, *args) if fits else plain_per_device(rows, cols, *args)

    tokens = P(("groups", "half", "quad"), "col", None)
    in_specs = (tokens, P("groups"), P(), P(), P(), P(), P(), P(), P())
    return jax.shard_map(per_shard, mesh=finer, in_specs=in_specs, out_specs=tokens, check_vma=False)
```

```python
import functools

import jax
import jax.numpy as jnp
from jax import lax
from jax.experimental import pallas as pl
from jax.experimental.pallas import tpu as pltpu
from jax.sharding import PartitionSpec as P

epsilon = 1e-05
LANES = 128
GROUP = 8
AXES = ("half", "quad", "col")
VMEM = pl.BlockSpec(memory_space=pltpu.VMEM)
HBM = pl.BlockSpec(memory_space=pltpu.HBM)
LIMIT = pltpu.CompilerParams(vmem_limit_bytes=32 * 1024 * 1024)


def sigmoid(x):
    return 0.5 * jnp.tanh(0.5 * x) + 0.5


def layer_norm(values, gain, bias, axis):
    mean = jnp.mean(values, axis=axis, keepdims=True)
    centred = values - mean
    variance = jnp.mean(centred * centred, axis=axis, keepdims=True)
    return centred * lax.rsqrt(variance + epsilon) * gain + bias


def column(row):
    n = row.shape[1]
    eye = lax.broadcasted_iota(jnp.int32, (n, n), 0) == lax.broadcasted_iota(jnp.int32, (n, n), 1)
    return jnp.sum(jnp.where(eye, row, 0.0), axis=1, keepdims=True)


def pack(x):
    rows, tokens = x.shape[-2:]
    whole, rest = divmod(tokens, LANES)
    blocks = [x[..., t * LANES : (t + 1) * LANES] for t in range(whole)]
    if rest:
        tail = x[..., whole * LANES :]
        blocks.append(jnp.concatenate([tail[..., : rows // 2, :], tail[..., rows // 2 :, :]], axis=-1))
    return jnp.concatenate(blocks, axis=-2)


def unpack(x, rows):
    whole, rest = divmod(x.shape[-2], rows)
    blocks = [x[..., t * rows : (t + 1) * rows, :] for t in range(whole)]
    if rest:
        tail = x[..., whole * rows :, :]
        blocks.append(jnp.concatenate([tail[..., : LANES // 2], tail[..., LANES // 2 :]], axis=-2))
    return jnp.concatenate(blocks, axis=-1)


def arrange(x):
    row_count, col_count, _ = x.shape
    whole, spare = row_count // 3, LANES - 2 * col_count
    blocks = []
    for t in range(whole):
        blocks += [x[2 * t], x[2 * t + 1], x[2 * whole + t, :spare]]
    return jnp.concatenate(blocks + [x[2 * whole + t, spare:] for t in range(whole)], axis=0)


def restore(x, row_count, col_count):
    whole, spare = row_count // 3, LANES - 2 * col_count
    rest = col_count - spare
    rows = []
    for t in range(whole):
        rows += [x[t * LANES : t * LANES + col_count], x[t * LANES + col_count : t * LANES + 2 * col_count]]
    for t in range(whole):
        tail = whole * LANES + t * rest
        rows += [x[t * LANES + 2 * col_count : (t + 1) * LANES], x[tail : tail + rest]]
    return jnp.concatenate(rows, axis=0)


def project_kernel(pair_hbm, gain_hbm, bias_hbm, w_hbm, mask_hbm, sides_ref, normed_ref, spread_ref, column_mask_ref, pair_ref, gain_ref, bias_ref, w_ref, mask_ref, sems):
    copies = [
        pltpu.make_async_copy(source, target, sems.at[n])
        for n, (source, target) in enumerate(
            [(mask_hbm, mask_ref), (pair_hbm, pair_ref), (gain_hbm, gain_ref), (bias_hbm, bias_ref), (w_hbm, w_ref)]
        )
    ]
    for copy in copies:
        copy.start()
    devices = sides_ref.shape[0]
    tokens, channels = normed_ref.shape
    hidden = w_ref.shape[1] // 4
    share = hidden // devices
    group, lanes = spread_ref.shape
    copies[0].wait()
    mask_row = mask_ref[...].astype(jnp.float32)
    column_mask_ref[...] = column(mask_row)
    start = lax.axis_index("half") * (lanes // group)
    token = lax.broadcasted_iota(jnp.int32, (mask_row.shape[1], lanes), 0)
    lane = lax.broadcasted_iota(jnp.int32, (mask_row.shape[1], lanes), 1)
    row_count = pair_ref.shape[0]
    whole = row_count // 3
    quads = lanes // group // row_count
    block, t, row = lane // LANES, lane // (quads * group) % whole, lane // group % quads
    k = row * row_count + jnp.where(block < 2, 2 * t + block, 2 * whole + t)
    pick = jnp.where(k + start == token, 1.0, 0.0)
    kept = jnp.dot(mask_row.astype(jnp.bfloat16), pick.astype(jnp.bfloat16), preferred_element_type=jnp.float32)
    channel = lax.broadcasted_iota(jnp.int32, (group, lanes), 0)
    lane = lax.broadcasted_iota(jnp.int32, (group, lanes), 1)
    spread_ref[...] = jnp.where(lane % group == channel, kept, 0.0)
    for copy in copies[1:4]:
        copy.wait()
    flat = pair_ref[...].reshape(tokens, channels).astype(jnp.float32)
    normed = layer_norm(flat, gain_ref[...], bias_ref[...], -1).astype(jnp.bfloat16)
    normed_ref[...] = normed
    copies[4].wait()
    arranged = arrange(normed.reshape(pair_ref.shape))
    projected = lax.dot_general(w_ref[...], arranged, (((0,), (1,)), ((), ())), preferred_element_type=jnp.float32)
    left = sigmoid(projected[:hidden]) * projected[hidden : 2 * hidden]
    right = sigmoid(projected[2 * hidden : 3 * hidden]) * projected[3 * hidden :]
    sides = jnp.concatenate([left.reshape(devices, share, tokens), right.reshape(devices, share, tokens)], axis=1)
    sides_ref[...] = pack(sides).astype(jnp.bfloat16)


def triangle_kernel(far_order, cols, row_count, col_count, share, got_ref, spread_ref, mask_ref, total_ref):
    sources = got_ref.shape[0]
    both = 2 * share
    group, lanes = spread_ref.shape
    length = mask_ref.shape[0]
    rows, quads, parts = length // row_count, sources // cols, share // group
    whole, spare = row_count // 3, LANES - 2 * col_count
    rest = col_count - spare
    blocks = [[got_ref[sources - 1 - (col * quads + row)].astype(jnp.float32) for row in range(quads)] for col in range(cols)]

    def turned(picks):
        return jnp.concatenate([blocks[col][row][at : at + group] for col, row, at in picks], axis=0).T

    tail = turned([(col, row, whole * both + part * group) for col in range(cols) for part in range(parts) for row in range(quads)])

    def side(which, part):
        even, odd, third = [], [], []
        for col in range(cols):
            at = which * share + part * group
            block = turned([(col, row, t * both + at) for t in range(whole) for row in range(quads)])
            even.append(block[:col_count])
            odd.append(block[col_count : 2 * col_count])
            lane = (col * parts + part) * quads * group
            at = which * LANES // 2
            last = [tail[at + t * rest : at + (t + 1) * rest, lane : lane + quads * group] for t in range(whole)]
            third += [block[2 * col_count :], jnp.concatenate(last, axis=1)]
        tokens = [jnp.concatenate(pieces, axis=0) for pieces in (even, odd, third)]
        return jnp.concatenate(tokens, axis=1) * mask_ref[...]

    def placed(pieces):
        return jnp.concatenate([jnp.zeros((piece, lanes), jnp.bfloat16) if isinstance(piece, int) else piece for piece in pieces], axis=0)

    contract = (((1,), (1,)), ((), ()))
    mains, lasts = [], []
    for part in range(parts):
        left, right = side(0, part), side(1, part).astype(jnp.bfloat16)
        left = (left[:, None, :] * spread_ref[...][None]).reshape(rows, row_count, group, lanes)
        pairs = left[:, : 2 * whole].reshape(rows, whole, 2, group, lanes)
        left = jnp.concatenate([pairs[:, :, 0], pairs[:, :, 1], left[:, 2 * whole :]], axis=-1)
        left = left.reshape(rows * whole * group, 3 * lanes).astype(jnp.bfloat16)
        ours = [right[col * col_count : (col + 1) * col_count] for col in range(cols)]
        weights = [
            placed([p for mine in ours for p in (mine, LANES - col_count)]),
            placed([p for mine in ours for p in (col_count, mine, spare)]),
            placed([p for mine in ours for p in (2 * col_count, mine[:spare])]),
        ]
        weights = jnp.concatenate(weights, axis=1)
        mains.append(lax.dot_general(left, weights, contract, preferred_element_type=jnp.float32))
        weights = jnp.concatenate([mine[spare:] for mine in ours], axis=0)
        lasts.append(lax.dot_general(left[:, 2 * lanes :], weights, contract, preferred_element_type=jnp.float32))
    for target, device in enumerate(far_order):
        row, col = divmod(device, cols)
        spots = [(row * whole + t) * group for t in range(whole)]
        tiles = [main[at : at + group, col * LANES : (col + 1) * LANES] for at in spots for main in mains]
        last = [part[at : at + group, col * rest : (col + 1) * rest] for part in lasts for at in spots]
        tiles.append(jnp.concatenate(last, axis=1))
        total_ref[target] = jnp.concatenate(tiles, axis=0).astype(jnp.bfloat16)


def gate_kernel(normed_ref, w_ref, gain_ref, bias_ref, gate_ref, gain_out_ref, bias_out_ref):
    gate_ref[...] = sigmoid(jnp.dot(normed_ref[...], w_ref[...], preferred_element_type=jnp.float32))
    gain_out_ref[...] = column(gain_ref[...])
    bias_out_ref[...] = column(bias_ref[...])


def output_kernel(far_order, near_order, total_ref, gate_ref, gain_ref, bias_ref, w_ref, out_ref):
    tokens = gate_ref.shape[0]
    hidden = w_ref.shape[0]
    near = len(near_order)
    share = hidden // near
    blocks = []
    for index in near_order:
        parts = [total_ref[source].astype(jnp.float32) for source, device in enumerate(far_order) if device % near == index]
        blocks.append(unpack(sum(parts[1:], parts[0]), share))
    total = jnp.concatenate(blocks, axis=0)
    normed = layer_norm(total, gain_ref[...], bias_ref[...], 0).astype(jnp.bfloat16)
    output = lax.dot_general(normed, w_ref[...], (((0,), (0,)), ((), ())), preferred_element_type=jnp.float32)
    output = restore(output, out_ref.shape[0], out_ref.shape[1])
    out_ref[...] = (gate_ref[...] * output).astype(jnp.bfloat16).reshape(out_ref.shape)


def per_device(rows, cols, halves, pair, token_mask, gain_in, bias_in, w_in, w_gate, gain_out, bias_out, w_out):
    row_count, col_count, channels = pair.shape
    hidden = w_out.shape[0]
    devices = rows * cols
    near = devices // halves
    quads = rows // halves
    near_order = [quad * cols + col for col in reversed(range(cols)) for quad in reversed(range(quads))]
    far_order = []
    for col in reversed(range(cols)):
        for quad in range(quads):
            for half in reversed(range(halves)):
                far_order.append(half * near + (quads - 1 - quad if half else quad) * cols + col)
    share = hidden // near
    tokens = row_count * col_count
    length = rows * row_count
    depth = length // halves
    token_mask = token_mask.reshape(1, length)
    arguments = (pair, gain_in.reshape(1, channels), bias_in.reshape(1, channels), w_in, token_mask)
    sides, normed, *masks = pl.pallas_call(
        project_kernel,
        out_shape=(
            jax.ShapeDtypeStruct((near, 2 * share * tokens // LANES, LANES), jnp.bfloat16),
            jax.ShapeDtypeStruct((tokens, channels), jnp.bfloat16),
            jax.ShapeDtypeStruct((GROUP, GROUP * depth), jnp.float32),
            jax.ShapeDtypeStruct((length, 1), jnp.float32),
        ),
        in_specs=[HBM] * 5,
        out_specs=(VMEM,) * 4,
        scratch_shapes=[
            pltpu.VMEM(pair.shape, pair.dtype),
            pltpu.VMEM((1, channels), jnp.float32),
            pltpu.VMEM((1, channels), jnp.float32),
            pltpu.VMEM(w_in.shape, w_in.dtype),
            pltpu.VMEM((1, length), jnp.int32),
            pltpu.SemaphoreType.DMA((5,)),
        ],
        compiler_params=LIMIT,
    )(*(pltpu.with_memory_space_constraint(x, pltpu.HBM) for x in arguments))
    got = lax.all_to_all(sides, ("quad", "col"), split_axis=0, concat_axis=0, tiled=True, axis_index_groups=[near_order])
    total = pl.pallas_call(
        functools.partial(triangle_kernel, far_order, cols, row_count, col_count, share),
        out_shape=jax.ShapeDtypeStruct((devices, share * tokens // LANES, LANES), jnp.bfloat16),
        in_specs=[VMEM] * 3,
        out_specs=VMEM,
        compiler_params=LIMIT,
    )(got, *masks)
    gate, gain_out, bias_out = pl.pallas_call(
        gate_kernel,
        out_shape=(
            jax.ShapeDtypeStruct((tokens, channels), jnp.float32),
            jax.ShapeDtypeStruct((hidden, 1), jnp.float32),
            jax.ShapeDtypeStruct((hidden, 1), jnp.float32),
        ),
        in_specs=[VMEM] * 4,
        out_specs=(VMEM, VMEM, VMEM),
        compiler_params=LIMIT,
        cost_estimate=pl.CostEstimate(flops=2 * tokens * channels * channels, bytes_accessed=4 * tokens * channels, transcendentals=0),
    )(normed, w_gate, gain_out.reshape(1, hidden), bias_out.reshape(1, hidden))
    total = lax.all_to_all(total, ("half", "quad", "col"), split_axis=0, concat_axis=0, tiled=True, axis_index_groups=[far_order])
    return pl.pallas_call(
        functools.partial(output_kernel, far_order, near_order),
        out_shape=jax.ShapeDtypeStruct(pair.shape, jnp.bfloat16),
        in_specs=[VMEM] * 5,
        out_specs=VMEM,
        compiler_params=LIMIT,
    )(total, gate, gain_out, bias_out, w_out)


def plain_per_device(rows, cols, pair, token_mask, gain_in, bias_in, w_in, w_gate, gain_out, bias_out, w_out):
    row_count, col_count, channels = pair.shape
    hidden = w_out.shape[0]
    devices = rows * cols
    share = hidden // devices
    tokens = row_count * col_count
    row_start = lax.axis_index(("half", "quad")) * row_count
    col_start = lax.axis_index("col") * col_count
    mask_float = token_mask.astype(jnp.float32)
    mask_rows = lax.dynamic_slice_in_dim(mask_float, row_start, row_count)
    mask_cols = lax.dynamic_slice_in_dim(mask_float, col_start, col_count)
    pair_mask = (mask_rows[:, None] * mask_cols[None, :]).reshape(1, tokens)
    flat = pair.reshape(tokens, channels).astype(jnp.float32)
    normed = layer_norm(flat, gain_in, bias_in, -1).astype(jnp.bfloat16)
    projected = lax.dot_general(w_in, normed, (((0,), (1,)), ((), ())), preferred_element_type=jnp.float32)
    projected = projected.reshape(2, 2, hidden, tokens)
    sides = (pair_mask * jax.nn.sigmoid(projected[:, 0]) * projected[:, 1]).astype(jnp.bfloat16)
    sides = sides.reshape(2, devices, share, tokens).transpose(1, 0, 2, 3)
    gate = jax.nn.sigmoid(jnp.dot(normed, w_gate, preferred_element_type=jnp.float32))
    got = lax.all_to_all(sides, AXES, split_axis=0, concat_axis=0, tiled=True)
    got = got.reshape(rows, cols, 2, share, row_count, col_count).transpose(2, 3, 0, 4, 1, 5)
    got = got.reshape(2, share, rows * row_count, cols * col_count)
    total = jnp.einsum("cki,ckj->cij", got[0], got[1], preferred_element_type=jnp.float32).astype(jnp.bfloat16)
    total = total.reshape(share, rows, row_count, cols, col_count).transpose(1, 3, 0, 2, 4)
    total = total.reshape(devices, share, tokens)
    total = lax.all_to_all(total, AXES, split_axis=0, concat_axis=0, tiled=True)
    total = total.reshape(hidden, tokens).astype(jnp.float32)
    summed_norm = layer_norm(total, gain_out[:, None], bias_out[:, None], 0).astype(jnp.bfloat16)
    output = lax.dot_general(summed_norm, w_out, (((0,), (0,)), ((), ())), preferred_element_type=jnp.float32)
    return (gate * output).astype(jnp.bfloat16).reshape(row_count, col_count, channels)


def solution(mesh):
    rows, cols = mesh.shape["row"], mesh.shape["col"]
    halves = 2
    parts = (mesh.shape["groups"], halves, rows // halves, cols)
    finer = jax.sharding.Mesh(mesh.devices.reshape(parts), ("groups", "half", "quad", "col"))

    def per_shard(*args):
        near, hidden, length = rows * cols // halves, args[-1].shape[0], args[1].shape[0]
        row_count, col_count, _ = args[0].shape
        spare = LANES - 2 * col_count
        fits = hidden % (2 * GROUP * near) == 0 and cols == 2 and length <= LANES and row_count % 3 == 0
        fits = fits and 0 < spare < col_count and row_count // 3 * (col_count - spare) * 2 == LANES
        fits = fits and row_count // 3 * (rows // halves) * GROUP == LANES
        return per_device(rows, cols, halves, *args) if fits else plain_per_device(rows, cols, *args)

    tokens = P(("groups", "half", "quad"), "col", None)
    in_specs = (tokens, P("groups"), P(), P(), P(), P(), P(), P(), P())
    return jax.shard_map(per_shard, mesh=finer, in_specs=in_specs, out_specs=tokens, check_vma=False)
```

```python
import functools

import jax
import jax.numpy as jnp
from jax import lax
from jax.experimental import pallas as pl
from jax.experimental.pallas import tpu as pltpu
from jax.sharding import PartitionSpec as P

epsilon = 1e-05
LANES = 128
GROUP = 8
AXES = ("half", "quad", "col")
VMEM = pl.BlockSpec(memory_space=pltpu.VMEM)
HBM = pl.BlockSpec(memory_space=pltpu.HBM)
LIMIT = pltpu.CompilerParams(vmem_limit_bytes=32 * 1024 * 1024)


def sigmoid(x):
    return 0.5 * jnp.tanh(0.5 * x) + 0.5


def layer_norm(values, gain, bias, axis):
    mean = jnp.mean(values, axis=axis, keepdims=True)
    centred = values - mean
    variance = jnp.mean(centred * centred, axis=axis, keepdims=True)
    return centred * lax.rsqrt(variance + epsilon) * gain + bias


def column(row):
    n = row.shape[1]
    eye = lax.broadcasted_iota(jnp.int32, (n, n), 0) == lax.broadcasted_iota(jnp.int32, (n, n), 1)
    return jnp.sum(jnp.where(eye, row, 0.0), axis=1, keepdims=True)


def pack(x):
    rows, tokens = x.shape[-2:]
    whole, rest = divmod(tokens, LANES)
    blocks = [x[..., t * LANES : (t + 1) * LANES] for t in range(whole)]
    if rest:
        tail = x[..., whole * LANES :]
        blocks.append(jnp.concatenate([tail[..., : rows // 2, :], tail[..., rows // 2 :, :]], axis=-1))
    return jnp.concatenate(blocks, axis=-2)


def unpack(x, rows):
    whole, rest = divmod(x.shape[-2], rows)
    blocks = [x[..., t * rows : (t + 1) * rows, :] for t in range(whole)]
    if rest:
        tail = x[..., whole * rows :, :]
        blocks.append(jnp.concatenate([tail[..., : LANES // 2], tail[..., LANES // 2 :]], axis=-2))
    return jnp.concatenate(blocks, axis=-1)


def arrange(x):
    row_count, col_count, _ = x.shape
    whole, spare = row_count // 3, LANES - 2 * col_count
    blocks = []
    for t in range(whole):
        blocks += [x[2 * t], x[2 * t + 1], x[2 * whole + t, :spare]]
    return jnp.concatenate(blocks + [x[2 * whole + t, spare:] for t in range(whole)], axis=0)


def restore(x, row_count, col_count):
    whole, spare = row_count // 3, LANES - 2 * col_count
    rest = col_count - spare
    rows = []
    for t in range(whole):
        rows += [x[t * LANES : t * LANES + col_count], x[t * LANES + col_count : t * LANES + 2 * col_count]]
    for t in range(whole):
        tail = whole * LANES + t * rest
        rows += [x[t * LANES + 2 * col_count : (t + 1) * LANES], x[tail : tail + rest]]
    return jnp.concatenate(rows, axis=0)


def project_kernel(pair_hbm, gain_hbm, bias_hbm, w_hbm, mask_hbm, sides_ref, normed_ref, spread_ref, column_mask_ref, pair_ref, gain_ref, bias_ref, w_ref, mask_ref, sems):
    copies = [
        pltpu.make_async_copy(source, target, sems.at[n])
        for n, (source, target) in enumerate(
            [(mask_hbm, mask_ref), (pair_hbm, pair_ref), (gain_hbm, gain_ref), (bias_hbm, bias_ref), (w_hbm, w_ref)]
        )
    ]
    for copy in copies:
        copy.start()
    devices = sides_ref.shape[0]
    tokens, channels = normed_ref.shape
    hidden = w_ref.shape[1] // 4
    share = hidden // devices
    group, lanes = spread_ref.shape
    copies[0].wait()
    mask_row = mask_ref[...].astype(jnp.float32)
    column_mask_ref[...] = column(mask_row)
    start = lax.axis_index("half") * (lanes // group)
    token = lax.broadcasted_iota(jnp.int32, (mask_row.shape[1], lanes), 0)
    lane = lax.broadcasted_iota(jnp.int32, (mask_row.shape[1], lanes), 1)
    row_count = pair_ref.shape[0]
    whole = row_count // 3
    quads = lanes // group // row_count
    block, t, row = lane // LANES, lane // (quads * group) % whole, lane // group % quads
    k = row * row_count + jnp.where(block < 2, 2 * t + block, 2 * whole + t)
    pick = jnp.where(k + start == token, 1.0, 0.0)
    kept = jnp.dot(mask_row.astype(jnp.bfloat16), pick.astype(jnp.bfloat16), preferred_element_type=jnp.float32)
    channel = lax.broadcasted_iota(jnp.int32, (group, lanes), 0)
    lane = lax.broadcasted_iota(jnp.int32, (group, lanes), 1)
    spread_ref[...] = jnp.where(lane % group == channel, kept, 0.0)
    for copy in copies[1:4]:
        copy.wait()
    flat = pair_ref[...].reshape(tokens, channels).astype(jnp.float32)
    normed = layer_norm(flat, gain_ref[...], bias_ref[...], -1).astype(jnp.bfloat16)
    normed_ref[...] = normed
    copies[4].wait()
    arranged = arrange(normed.reshape(pair_ref.shape))
    projected = lax.dot_general(w_ref[...], arranged, (((0,), (1,)), ((), ())), preferred_element_type=jnp.float32)
    left = sigmoid(projected[:hidden]) * projected[hidden : 2 * hidden]
    right = sigmoid(projected[2 * hidden : 3 * hidden]) * projected[3 * hidden :]
    sides = jnp.concatenate([left.reshape(devices, share, tokens), right.reshape(devices, share, tokens)], axis=1)
    sides_ref[...] = pack(sides).astype(jnp.bfloat16)


def triangle_kernel(far_order, cols, row_count, col_count, share, got_ref, spread_ref, mask_ref, total_ref):
    sources = got_ref.shape[0]
    both = 2 * share
    group, lanes = spread_ref.shape
    length = mask_ref.shape[0]
    rows, quads, parts = length // row_count, sources // cols, share // group
    whole, spare = row_count // 3, LANES - 2 * col_count
    rest = col_count - spare
    blocks = [[got_ref[sources - 1 - (col * quads + row)].astype(jnp.float32) for row in range(quads)] for col in range(cols)]

    def turned(picks):
        return jnp.concatenate([blocks[col][row][at : at + group] for col, row, at in picks], axis=0).T

    tail = turned([(col, row, whole * both + part * group) for col in range(cols) for part in range(parts) for row in range(quads)])

    def side(which, part):
        even, odd, third = [], [], []
        for col in range(cols):
            at = which * share + part * group
            block = turned([(col, row, t * both + at) for t in range(whole) for row in range(quads)])
            even.append(block[:col_count])
            odd.append(block[col_count : 2 * col_count])
            lane = (col * parts + part) * quads * group
            at = which * LANES // 2
            last = [tail[at + t * rest : at + (t + 1) * rest, lane : lane + quads * group] for t in range(whole)]
            third += [block[2 * col_count :], jnp.concatenate(last, axis=1)]
        tokens = [jnp.concatenate(pieces, axis=0) for pieces in (even, odd, third)]
        return jnp.concatenate(tokens, axis=1) * mask_ref[...]

    def placed(pieces):
        return jnp.concatenate([jnp.zeros((piece, lanes), jnp.bfloat16) if isinstance(piece, int) else piece for piece in pieces], axis=0)

    contract = (((1,), (1,)), ((), ()))
    mains, lasts = [], []
    for part in range(parts):
        left, right = side(0, part), side(1, part).astype(jnp.bfloat16)
        left = (left[:, None, :] * spread_ref[...][None]).reshape(rows, row_count, group, lanes)
        pairs = left[:, : 2 * whole].reshape(rows, whole, 2, group, lanes)
        left = jnp.concatenate([pairs[:, :, 0], pairs[:, :, 1], left[:, 2 * whole :]], axis=-1)
        left = left.reshape(rows * whole * group, 3 * lanes).astype(jnp.bfloat16)
        ours = [right[col * col_count : (col + 1) * col_count] for col in range(cols)]
        weights = [
            placed([p for mine in ours for p in (mine, LANES - col_count)]),
            placed([p for mine in ours for p in (col_count, mine, spare)]),
            placed([p for mine in ours for p in (2 * col_count, mine[:spare])]),
        ]
        weights = jnp.concatenate(weights, axis=1)
        mains.append(lax.dot_general(left, weights, contract, preferred_element_type=jnp.float32))
        weights = jnp.concatenate([mine[spare:] for mine in ours], axis=0)
        lasts.append(lax.dot_general(left[:, 2 * lanes :], weights, contract, preferred_element_type=jnp.float32))
    for target, device in enumerate(far_order):
        row, col = divmod(device, cols)
        spots = [(row * whole + t) * group for t in range(whole)]
        tiles = [main[at : at + group, col * LANES : (col + 1) * LANES] for at in spots for main in mains]
        last = [part[at : at + group, col * rest : (col + 1) * rest] for part in lasts for at in spots]
        tiles.append(jnp.concatenate(last, axis=1))
        total_ref[target] = jnp.concatenate(tiles, axis=0).astype(jnp.bfloat16)


def gate_kernel(normed_ref, w_ref, gain_ref, bias_ref, gate_ref, gain_out_ref, bias_out_ref):
    gate_ref[...] = sigmoid(jnp.dot(normed_ref[...], w_ref[...], preferred_element_type=jnp.float32))
    gain_out_ref[...] = column(gain_ref[...])
    bias_out_ref[...] = column(bias_ref[...])


def output_kernel(far_order, near_order, total_ref, gate_ref, gain_ref, bias_ref, w_ref, out_ref):
    tokens = gate_ref.shape[0]
    hidden = w_ref.shape[0]
    near = len(near_order)
    share = hidden // near
    blocks = []
    for index in near_order:
        parts = [total_ref[source].astype(jnp.float32) for source, device in enumerate(far_order) if device % near == index]
        blocks.append(unpack(sum(parts[1:], parts[0]), share))
    total = jnp.concatenate(blocks, axis=0)
    normed = layer_norm(total, gain_ref[...], bias_ref[...], 0).astype(jnp.bfloat16)
    output = lax.dot_general(normed, w_ref[...], (((0,), (0,)), ((), ())), preferred_element_type=jnp.float32)
    output = restore(output, out_ref.shape[0], out_ref.shape[1])
    out_ref[...] = (gate_ref[...] * output).astype(jnp.bfloat16).reshape(out_ref.shape)


def per_device(rows, cols, halves, pair, token_mask, gain_in, bias_in, w_in, w_gate, gain_out, bias_out, w_out):
    row_count, col_count, channels = pair.shape
    hidden = w_out.shape[0]
    devices = rows * cols
    near = devices // halves
    quads = rows // halves
    near_order = [quad * cols + col for col in reversed(range(cols)) for quad in reversed(range(quads))]
    far_order = []
    for col in reversed(range(cols)):
        ahead = list(range(quads)) if col else list(range(1, quads)) + [0]
        for quad, other in zip(ahead, reversed(range(quads))):
            far_order += [near + other * cols + col, quad * cols + col]
    share = hidden // near
    tokens = row_count * col_count
    length = rows * row_count
    depth = length // halves
    token_mask = token_mask.reshape(1, length)
    arguments = (pair, gain_in.reshape(1, channels), bias_in.reshape(1, channels), w_in, token_mask)
    sides, normed, *masks = pl.pallas_call(
        project_kernel,
        out_shape=(
            jax.ShapeDtypeStruct((near, 2 * share * tokens // LANES, LANES), jnp.bfloat16),
            jax.ShapeDtypeStruct((tokens, channels), jnp.bfloat16),
            jax.ShapeDtypeStruct((GROUP, GROUP * depth), jnp.float32),
            jax.ShapeDtypeStruct((length, 1), jnp.float32),
        ),
        in_specs=[HBM] * 5,
        out_specs=(VMEM,) * 4,
        scratch_shapes=[
            pltpu.VMEM(pair.shape, pair.dtype),
            pltpu.VMEM((1, channels), jnp.float32),
            pltpu.VMEM((1, channels), jnp.float32),
            pltpu.VMEM(w_in.shape, w_in.dtype),
            pltpu.VMEM((1, length), jnp.int32),
            pltpu.SemaphoreType.DMA((5,)),
        ],
        compiler_params=LIMIT,
    )(*(pltpu.with_memory_space_constraint(x, pltpu.HBM) for x in arguments))
    got = lax.all_to_all(sides, ("quad", "col"), split_axis=0, concat_axis=0, tiled=True, axis_index_groups=[near_order])
    total = pl.pallas_call(
        functools.partial(triangle_kernel, far_order, cols, row_count, col_count, share),
        out_shape=jax.ShapeDtypeStruct((devices, share * tokens // LANES, LANES), jnp.bfloat16),
        in_specs=[VMEM] * 3,
        out_specs=VMEM,
        compiler_params=LIMIT,
    )(got, *masks)
    gate, gain_out, bias_out = pl.pallas_call(
        gate_kernel,
        out_shape=(
            jax.ShapeDtypeStruct((tokens, channels), jnp.float32),
            jax.ShapeDtypeStruct((hidden, 1), jnp.float32),
            jax.ShapeDtypeStruct((hidden, 1), jnp.float32),
        ),
        in_specs=[VMEM] * 4,
        out_specs=(VMEM, VMEM, VMEM),
        compiler_params=LIMIT,
        cost_estimate=pl.CostEstimate(flops=2 * tokens * channels * channels, bytes_accessed=4 * tokens * channels, transcendentals=0),
    )(normed, w_gate, gain_out.reshape(1, hidden), bias_out.reshape(1, hidden))
    total = lax.all_to_all(total, ("half", "quad", "col"), split_axis=0, concat_axis=0, tiled=True, axis_index_groups=[far_order])
    return pl.pallas_call(
        functools.partial(output_kernel, far_order, near_order),
        out_shape=jax.ShapeDtypeStruct(pair.shape, jnp.bfloat16),
        in_specs=[VMEM] * 5,
        out_specs=VMEM,
        compiler_params=LIMIT,
    )(total, gate, gain_out, bias_out, w_out)


def plain_per_device(rows, cols, pair, token_mask, gain_in, bias_in, w_in, w_gate, gain_out, bias_out, w_out):
    row_count, col_count, channels = pair.shape
    hidden = w_out.shape[0]
    devices = rows * cols
    share = hidden // devices
    tokens = row_count * col_count
    row_start = lax.axis_index(("half", "quad")) * row_count
    col_start = lax.axis_index("col") * col_count
    mask_float = token_mask.astype(jnp.float32)
    mask_rows = lax.dynamic_slice_in_dim(mask_float, row_start, row_count)
    mask_cols = lax.dynamic_slice_in_dim(mask_float, col_start, col_count)
    pair_mask = (mask_rows[:, None] * mask_cols[None, :]).reshape(1, tokens)
    flat = pair.reshape(tokens, channels).astype(jnp.float32)
    normed = layer_norm(flat, gain_in, bias_in, -1).astype(jnp.bfloat16)
    projected = lax.dot_general(w_in, normed, (((0,), (1,)), ((), ())), preferred_element_type=jnp.float32)
    projected = projected.reshape(2, 2, hidden, tokens)
    sides = (pair_mask * jax.nn.sigmoid(projected[:, 0]) * projected[:, 1]).astype(jnp.bfloat16)
    sides = sides.reshape(2, devices, share, tokens).transpose(1, 0, 2, 3)
    gate = jax.nn.sigmoid(jnp.dot(normed, w_gate, preferred_element_type=jnp.float32))
    got = lax.all_to_all(sides, AXES, split_axis=0, concat_axis=0, tiled=True)
    got = got.reshape(rows, cols, 2, share, row_count, col_count).transpose(2, 3, 0, 4, 1, 5)
    got = got.reshape(2, share, rows * row_count, cols * col_count)
    total = jnp.einsum("cki,ckj->cij", got[0], got[1], preferred_element_type=jnp.float32).astype(jnp.bfloat16)
    total = total.reshape(share, rows, row_count, cols, col_count).transpose(1, 3, 0, 2, 4)
    total = total.reshape(devices, share, tokens)
    total = lax.all_to_all(total, AXES, split_axis=0, concat_axis=0, tiled=True)
    total = total.reshape(hidden, tokens).astype(jnp.float32)
    summed_norm = layer_norm(total, gain_out[:, None], bias_out[:, None], 0).astype(jnp.bfloat16)
    output = lax.dot_general(summed_norm, w_out, (((0,), (0,)), ((), ())), preferred_element_type=jnp.float32)
    return (gate * output).astype(jnp.bfloat16).reshape(row_count, col_count, channels)


def solution(mesh):
    rows, cols = mesh.shape["row"], mesh.shape["col"]
    halves = 2
    parts = (mesh.shape["groups"], halves, rows // halves, cols)
    finer = jax.sharding.Mesh(mesh.devices.reshape(parts), ("groups", "half", "quad", "col"))

    def per_shard(*args):
        near, hidden, length = rows * cols // halves, args[-1].shape[0], args[1].shape[0]
        row_count, col_count, _ = args[0].shape
        spare = LANES - 2 * col_count
        fits = hidden % (2 * GROUP * near) == 0 and cols == 2 and length <= LANES and row_count % 3 == 0
        fits = fits and 0 < spare < col_count and row_count // 3 * (col_count - spare) * 2 == LANES
        fits = fits and row_count // 3 * (rows // halves) * GROUP == LANES
        return per_device(rows, cols, halves, *args) if fits else plain_per_device(rows, cols, *args)

    tokens = P(("groups", "half", "quad"), "col", None)
    in_specs = (tokens, P("groups"), P(), P(), P(), P(), P(), P(), P())
    return jax.shard_map(per_shard, mesh=finer, in_specs=in_specs, out_specs=tokens, check_vma=False)
```

```python
import functools

import jax
import jax.numpy as jnp
from jax import lax
from jax.experimental import pallas as pl
from jax.experimental.pallas import tpu as pltpu
from jax.sharding import PartitionSpec as P

epsilon = 1e-05
LANES = 128
GROUP = 8
AXES = ("half", "quad", "col")
VMEM = pl.BlockSpec(memory_space=pltpu.VMEM)
HBM = pl.BlockSpec(memory_space=pltpu.HBM)
LIMIT = pltpu.CompilerParams(vmem_limit_bytes=32 * 1024 * 1024)


def sigmoid(x):
    return 0.5 * jnp.tanh(0.5 * x) + 0.5


def layer_norm(values, gain, bias, axis):
    mean = jnp.mean(values, axis=axis, keepdims=True)
    centred = values - mean
    variance = jnp.mean(centred * centred, axis=axis, keepdims=True)
    return centred * lax.rsqrt(variance + epsilon) * gain + bias


def column(row):
    n = row.shape[1]
    eye = lax.broadcasted_iota(jnp.int32, (n, n), 0) == lax.broadcasted_iota(jnp.int32, (n, n), 1)
    return jnp.sum(jnp.where(eye, row, 0.0), axis=1, keepdims=True)


def pack(x):
    rows, tokens = x.shape[-2:]
    whole, rest = divmod(tokens, LANES)
    blocks = [x[..., t * LANES : (t + 1) * LANES] for t in range(whole)]
    if rest:
        tail = x[..., whole * LANES :]
        blocks.append(jnp.concatenate([tail[..., : rows // 2, :], tail[..., rows // 2 :, :]], axis=-1))
    return jnp.concatenate(blocks, axis=-2)


def unpack(x, rows):
    whole, rest = divmod(x.shape[-2], rows)
    blocks = [x[..., t * rows : (t + 1) * rows, :] for t in range(whole)]
    if rest:
        tail = x[..., whole * rows :, :]
        blocks.append(jnp.concatenate([tail[..., : LANES // 2], tail[..., LANES // 2 :]], axis=-2))
    return jnp.concatenate(blocks, axis=-1)


def arrange(x):
    row_count, col_count, _ = x.shape
    whole, spare = row_count // 3, LANES - 2 * col_count
    blocks = []
    for t in range(whole):
        blocks += [x[2 * t], x[2 * t + 1], x[2 * whole + t, :spare]]
    return jnp.concatenate(blocks + [x[2 * whole + t, spare:] for t in range(whole)], axis=0)


def restore(x, row_count, col_count):
    whole, spare = row_count // 3, LANES - 2 * col_count
    rest = col_count - spare
    rows = []
    for t in range(whole):
        rows += [x[t * LANES : t * LANES + col_count], x[t * LANES + col_count : t * LANES + 2 * col_count]]
    for t in range(whole):
        tail = whole * LANES + t * rest
        rows += [x[t * LANES + 2 * col_count : (t + 1) * LANES], x[tail : tail + rest]]
    return jnp.concatenate(rows, axis=0)


def project_kernel(pair_hbm, gain_hbm, bias_hbm, w_hbm, mask_hbm, sides_ref, normed_ref, spread_ref, column_mask_ref, pair_ref, gain_ref, bias_ref, w_ref, mask_ref, sems):
    copies = [
        pltpu.make_async_copy(source, target, sems.at[n])
        for n, (source, target) in enumerate(
            [(mask_hbm, mask_ref), (pair_hbm, pair_ref), (gain_hbm, gain_ref), (bias_hbm, bias_ref), (w_hbm, w_ref)]
        )
    ]
    for copy in copies:
        copy.start()
    devices = sides_ref.shape[0]
    tokens, channels = normed_ref.shape
    hidden = w_ref.shape[1] // 4
    share = hidden // devices
    group, lanes = spread_ref.shape
    copies[0].wait()
    mask_row = mask_ref[...].astype(jnp.float32)
    column_mask_ref[...] = column(mask_row)
    start = lax.axis_index("half") * (lanes // group)
    token = lax.broadcasted_iota(jnp.int32, (mask_row.shape[1], lanes), 0)
    lane = lax.broadcasted_iota(jnp.int32, (mask_row.shape[1], lanes), 1)
    row_count = pair_ref.shape[0]
    whole = row_count // 3
    quads = lanes // group // row_count
    block, t, row = lane // LANES, lane // (quads * group) % whole, lane // group % quads
    k = row * row_count + jnp.where(block < 2, 2 * t + block, 2 * whole + t)
    pick = jnp.where(k + start == token, 1.0, 0.0)
    kept = jnp.dot(mask_row.astype(jnp.bfloat16), pick.astype(jnp.bfloat16), preferred_element_type=jnp.float32)
    channel = lax.broadcasted_iota(jnp.int32, (group, lanes), 0)
    lane = lax.broadcasted_iota(jnp.int32, (group, lanes), 1)
    spread_ref[...] = jnp.where(lane % group == channel, kept, 0.0)
    for copy in copies[1:4]:
        copy.wait()
    flat = pair_ref[...].reshape(tokens, channels).astype(jnp.float32)
    normed = layer_norm(flat, gain_ref[...], bias_ref[...], -1).astype(jnp.bfloat16)
    normed_ref[...] = normed
    copies[4].wait()
    arranged = arrange(normed.reshape(pair_ref.shape))
    projected = lax.dot_general(w_ref[...], arranged, (((0,), (1,)), ((), ())), preferred_element_type=jnp.float32)
    left = sigmoid(projected[:hidden]) * projected[hidden : 2 * hidden]
    right = sigmoid(projected[2 * hidden : 3 * hidden]) * projected[3 * hidden :]
    sides = jnp.concatenate([left.reshape(devices, share, tokens), right.reshape(devices, share, tokens)], axis=1)
    sides_ref[...] = pack(sides).astype(jnp.bfloat16)


def triangle_kernel(far_order, cols, row_count, col_count, share, got_ref, spread_ref, mask_ref, total_ref):
    sources = got_ref.shape[0]
    both = 2 * share
    group, lanes = spread_ref.shape
    length = mask_ref.shape[0]
    rows, quads, parts = length // row_count, sources // cols, share // group
    whole, spare = row_count // 3, LANES - 2 * col_count
    rest = col_count - spare
    blocks = [[got_ref[sources - 1 - (col * quads + row)].astype(jnp.float32) for row in range(quads)] for col in range(cols)]

    def turned(picks):
        return jnp.concatenate([blocks[col][row][at : at + group] for col, row, at in picks], axis=0).T

    tail = turned([(col, row, whole * both + part * group) for col in range(cols) for part in range(parts) for row in range(quads)])

    def side(which, part):
        even, odd, third = [], [], []
        for col in range(cols):
            at = which * share + part * group
            block = turned([(col, row, t * both + at) for t in range(whole) for row in range(quads)])
            even.append(block[:col_count])
            odd.append(block[col_count : 2 * col_count])
            lane = (col * parts + part) * quads * group
            at = which * LANES // 2
            last = [tail[at + t * rest : at + (t + 1) * rest, lane : lane + quads * group] for t in range(whole)]
            third += [block[2 * col_count :], jnp.concatenate(last, axis=1)]
        tokens = [jnp.concatenate(pieces, axis=0) for pieces in (even, odd, third)]
        return jnp.concatenate(tokens, axis=1) * mask_ref[...]

    def placed(pieces):
        return jnp.concatenate([jnp.zeros((piece, lanes), jnp.bfloat16) if isinstance(piece, int) else piece for piece in pieces], axis=0)

    contract = (((1,), (1,)), ((), ()))
    mains, lasts = [], []
    for part in range(parts):
        left, right = side(0, part), side(1, part).astype(jnp.bfloat16)
        left = (left[:, None, :] * spread_ref[...][None]).reshape(rows, row_count, group, lanes)
        pairs = left[:, : 2 * whole].reshape(rows, whole, 2, group, lanes)
        left = jnp.concatenate([pairs[:, :, 0], pairs[:, :, 1], left[:, 2 * whole :]], axis=-1)
        left = left.reshape(rows * whole * group, 3 * lanes).astype(jnp.bfloat16)
        ours = [right[col * col_count : (col + 1) * col_count] for col in range(cols)]
        weights = [
            placed([p for mine in ours for p in (mine, LANES - col_count)]),
            placed([p for mine in ours for p in (col_count, mine, spare)]),
            placed([p for mine in ours for p in (2 * col_count, mine[:spare])]),
        ]
        weights = jnp.concatenate(weights, axis=1)
        mains.append(lax.dot_general(left, weights, contract, preferred_element_type=jnp.float32))
        weights = jnp.concatenate([mine[spare:] for mine in ours], axis=0)
        lasts.append(lax.dot_general(left[:, 2 * lanes :], weights, contract, preferred_element_type=jnp.float32))
    for target, device in enumerate(far_order):
        row, col = divmod(device, cols)
        spots = [(row * whole + t) * group for t in range(whole)]
        tiles = [main[at : at + group, col * LANES : (col + 1) * LANES] for at in spots for main in mains]
        last = [part[at : at + group, col * rest : (col + 1) * rest] for part in lasts for at in spots]
        tiles.append(jnp.concatenate(last, axis=1))
        total_ref[target] = jnp.concatenate(tiles, axis=0).astype(jnp.bfloat16)


def gate_kernel(normed_ref, w_ref, gain_ref, bias_ref, gate_ref, gain_out_ref, bias_out_ref):
    gate_ref[...] = sigmoid(jnp.dot(normed_ref[...], w_ref[...], preferred_element_type=jnp.float32))
    gain_out_ref[...] = column(gain_ref[...])
    bias_out_ref[...] = column(bias_ref[...])


def output_kernel(far_order, near_order, total_ref, gate_ref, gain_ref, bias_ref, w_ref, out_ref):
    tokens = gate_ref.shape[0]
    hidden = w_ref.shape[0]
    near = len(near_order)
    share = hidden // near
    blocks = []
    for index in near_order:
        parts = [total_ref[source].astype(jnp.float32) for source, device in enumerate(far_order) if device % near == index]
        blocks.append(unpack(sum(parts[1:], parts[0]), share))
    total = jnp.concatenate(blocks, axis=0)
    normed = layer_norm(total, gain_ref[...], bias_ref[...], 0).astype(jnp.bfloat16)
    output = lax.dot_general(normed, w_ref[...], (((0,), (0,)), ((), ())), preferred_element_type=jnp.float32)
    output = restore(output, out_ref.shape[0], out_ref.shape[1])
    out_ref[...] = (gate_ref[...] * output).astype(jnp.bfloat16).reshape(out_ref.shape)


def per_device(rows, cols, halves, pair, token_mask, gain_in, bias_in, w_in, w_gate, gain_out, bias_out, w_out):
    row_count, col_count, channels = pair.shape
    hidden = w_out.shape[0]
    devices = rows * cols
    near = devices // halves
    quads = rows // halves
    near_order = [quad * cols + col for col in reversed(range(cols)) for quad in reversed(range(quads))]
    far_order = []
    for col in reversed(range(cols)):
        ahead = list(range(quads)) if col else list(range(1, quads)) + [0]
        behind = [1] + [quad for quad in reversed(range(quads)) if quad != 1] if col else list(reversed(range(quads)))
        for quad, other in zip(ahead, behind):
            far_order += [near + other * cols + col, quad * cols + col]
    share = hidden // near
    tokens = row_count * col_count
    length = rows * row_count
    depth = length // halves
    token_mask = token_mask.reshape(1, length)
    arguments = (pair, gain_in.reshape(1, channels), bias_in.reshape(1, channels), w_in, token_mask)
    sides, normed, *masks = pl.pallas_call(
        project_kernel,
        out_shape=(
            jax.ShapeDtypeStruct((near, 2 * share * tokens // LANES, LANES), jnp.bfloat16),
            jax.ShapeDtypeStruct((tokens, channels), jnp.bfloat16),
            jax.ShapeDtypeStruct((GROUP, GROUP * depth), jnp.float32),
            jax.ShapeDtypeStruct((length, 1), jnp.float32),
        ),
        in_specs=[HBM] * 5,
        out_specs=(VMEM,) * 4,
        scratch_shapes=[
            pltpu.VMEM(pair.shape, pair.dtype),
            pltpu.VMEM((1, channels), jnp.float32),
            pltpu.VMEM((1, channels), jnp.float32),
            pltpu.VMEM(w_in.shape, w_in.dtype),
            pltpu.VMEM((1, length), jnp.int32),
            pltpu.SemaphoreType.DMA((5,)),
        ],
        compiler_params=LIMIT,
    )(*(pltpu.with_memory_space_constraint(x, pltpu.HBM) for x in arguments))
    got = lax.all_to_all(sides, ("quad", "col"), split_axis=0, concat_axis=0, tiled=True, axis_index_groups=[near_order])
    total = pl.pallas_call(
        functools.partial(triangle_kernel, far_order, cols, row_count, col_count, share),
        out_shape=jax.ShapeDtypeStruct((devices, share * tokens // LANES, LANES), jnp.bfloat16),
        in_specs=[VMEM] * 3,
        out_specs=VMEM,
        compiler_params=LIMIT,
    )(got, *masks)
    gate, gain_out, bias_out = pl.pallas_call(
        gate_kernel,
        out_shape=(
            jax.ShapeDtypeStruct((tokens, channels), jnp.float32),
            jax.ShapeDtypeStruct((hidden, 1), jnp.float32),
            jax.ShapeDtypeStruct((hidden, 1), jnp.float32),
        ),
        in_specs=[VMEM] * 4,
        out_specs=(VMEM, VMEM, VMEM),
        compiler_params=LIMIT,
        cost_estimate=pl.CostEstimate(flops=2 * tokens * channels * channels, bytes_accessed=4 * tokens * channels, transcendentals=0),
    )(normed, w_gate, gain_out.reshape(1, hidden), bias_out.reshape(1, hidden))
    total = lax.all_to_all(total, ("half", "quad", "col"), split_axis=0, concat_axis=0, tiled=True, axis_index_groups=[far_order])
    return pl.pallas_call(
        functools.partial(output_kernel, far_order, near_order),
        out_shape=jax.ShapeDtypeStruct(pair.shape, jnp.bfloat16),
        in_specs=[VMEM] * 5,
        out_specs=VMEM,
        compiler_params=LIMIT,
    )(total, gate, gain_out, bias_out, w_out)


def plain_per_device(rows, cols, pair, token_mask, gain_in, bias_in, w_in, w_gate, gain_out, bias_out, w_out):
    row_count, col_count, channels = pair.shape
    hidden = w_out.shape[0]
    devices = rows * cols
    share = hidden // devices
    tokens = row_count * col_count
    row_start = lax.axis_index(("half", "quad")) * row_count
    col_start = lax.axis_index("col") * col_count
    mask_float = token_mask.astype(jnp.float32)
    mask_rows = lax.dynamic_slice_in_dim(mask_float, row_start, row_count)
    mask_cols = lax.dynamic_slice_in_dim(mask_float, col_start, col_count)
    pair_mask = (mask_rows[:, None] * mask_cols[None, :]).reshape(1, tokens)
    flat = pair.reshape(tokens, channels).astype(jnp.float32)
    normed = layer_norm(flat, gain_in, bias_in, -1).astype(jnp.bfloat16)
    projected = lax.dot_general(w_in, normed, (((0,), (1,)), ((), ())), preferred_element_type=jnp.float32)
    projected = projected.reshape(2, 2, hidden, tokens)
    sides = (pair_mask * jax.nn.sigmoid(projected[:, 0]) * projected[:, 1]).astype(jnp.bfloat16)
    sides = sides.reshape(2, devices, share, tokens).transpose(1, 0, 2, 3)
    gate = jax.nn.sigmoid(jnp.dot(normed, w_gate, preferred_element_type=jnp.float32))
    got = lax.all_to_all(sides, AXES, split_axis=0, concat_axis=0, tiled=True)
    got = got.reshape(rows, cols, 2, share, row_count, col_count).transpose(2, 3, 0, 4, 1, 5)
    got = got.reshape(2, share, rows * row_count, cols * col_count)
    total = jnp.einsum("cki,ckj->cij", got[0], got[1], preferred_element_type=jnp.float32).astype(jnp.bfloat16)
    total = total.reshape(share, rows, row_count, cols, col_count).transpose(1, 3, 0, 2, 4)
    total = total.reshape(devices, share, tokens)
    total = lax.all_to_all(total, AXES, split_axis=0, concat_axis=0, tiled=True)
    total = total.reshape(hidden, tokens).astype(jnp.float32)
    summed_norm = layer_norm(total, gain_out[:, None], bias_out[:, None], 0).astype(jnp.bfloat16)
    output = lax.dot_general(summed_norm, w_out, (((0,), (0,)), ((), ())), preferred_element_type=jnp.float32)
    return (gate * output).astype(jnp.bfloat16).reshape(row_count, col_count, channels)


def solution(mesh):
    rows, cols = mesh.shape["row"], mesh.shape["col"]
    halves = 2
    parts = (mesh.shape["groups"], halves, rows // halves, cols)
    finer = jax.sharding.Mesh(mesh.devices.reshape(parts), ("groups", "half", "quad", "col"))

    def per_shard(*args):
        near, hidden, length = rows * cols // halves, args[-1].shape[0], args[1].shape[0]
        row_count, col_count, _ = args[0].shape
        spare = LANES - 2 * col_count
        fits = hidden % (2 * GROUP * near) == 0 and cols == 2 and length <= LANES and row_count % 3 == 0
        fits = fits and 0 < spare < col_count and row_count // 3 * (col_count - spare) * 2 == LANES
        fits = fits and row_count // 3 * (rows // halves) * GROUP == LANES
        return per_device(rows, cols, halves, *args) if fits else plain_per_device(rows, cols, *args)

    tokens = P(("groups", "half", "quad"), "col", None)
    in_specs = (tokens, P("groups"), P(), P(), P(), P(), P(), P(), P())
    return jax.shard_map(per_shard, mesh=finer, in_specs=in_specs, out_specs=tokens, check_vma=False)
```

```python
import functools

import jax
import jax.numpy as jnp
from jax import lax
from jax.experimental import pallas as pl
from jax.experimental.pallas import tpu as pltpu
from jax.sharding import PartitionSpec as P

epsilon = 1e-05
LANES = 128
GROUP = 8
PIECES = 3
AXES = ("half", "quad", "col")
VMEM = pl.BlockSpec(memory_space=pltpu.VMEM)
HBM = pl.BlockSpec(memory_space=pltpu.HBM)
LIMIT = pltpu.CompilerParams(vmem_limit_bytes=32 * 1024 * 1024)


def sigmoid(x):
    return 0.5 * jnp.tanh(0.5 * x) + 0.5


def layer_norm(values, gain, bias, axis):
    mean = jnp.mean(values, axis=axis, keepdims=True)
    centred = values - mean
    variance = jnp.mean(centred * centred, axis=axis, keepdims=True)
    return centred * lax.rsqrt(variance + epsilon) * gain + bias


def column(row):
    n = row.shape[1]
    eye = lax.broadcasted_iota(jnp.int32, (n, n), 0) == lax.broadcasted_iota(jnp.int32, (n, n), 1)
    return jnp.sum(jnp.where(eye, row, 0.0), axis=1, keepdims=True)


def pack(x):
    rows, tokens = x.shape[-2:]
    whole, rest = divmod(tokens, LANES)
    blocks = [x[..., t * LANES : (t + 1) * LANES] for t in range(whole)]
    if rest:
        tail = x[..., whole * LANES :]
        blocks.append(jnp.concatenate([tail[..., : rows // 2, :], tail[..., rows // 2 :, :]], axis=-1))
    return jnp.concatenate(blocks, axis=-2)


def arrange(x):
    row_count, col_count, _ = x.shape
    whole, spare = row_count // 3, LANES - 2 * col_count
    blocks = []
    for t in range(whole):
        blocks += [x[2 * t], x[2 * t + 1], x[2 * whole + t, :spare]]
    return jnp.concatenate(blocks + [x[2 * whole + t, spare:] for t in range(whole)], axis=0)


def project_kernel(pair_hbm, gain_hbm, bias_hbm, w_hbm, mask_hbm, sides_ref, normed_ref, spread_ref, column_mask_ref, pair_ref, gain_ref, bias_ref, w_ref, mask_ref, sems):
    step = pair_ref.shape[0] // PIECES
    pieces = [pl.ds(n * step, step) for n in range(PIECES)]
    moves = [(mask_hbm, mask_ref), (gain_hbm, gain_ref), (bias_hbm, bias_ref)]
    moves += [(pair_hbm.at[piece], pair_ref.at[piece]) for piece in pieces] + [(w_hbm, w_ref)]
    copies = [pltpu.make_async_copy(source, target, sems.at[n]) for n, (source, target) in enumerate(moves)]
    for copy in copies:
        copy.start()
    devices = sides_ref.shape[0]
    tokens, channels = normed_ref.shape
    hidden = w_ref.shape[1] // 4
    share = hidden // devices
    group, lanes = spread_ref.shape
    copies[0].wait()
    mask_row = mask_ref[...].astype(jnp.float32)
    column_mask_ref[...] = column(mask_row)
    start = lax.axis_index("half") * (lanes // group)
    token = lax.broadcasted_iota(jnp.int32, (mask_row.shape[1], lanes), 0)
    lane = lax.broadcasted_iota(jnp.int32, (mask_row.shape[1], lanes), 1)
    row_count = pair_ref.shape[0]
    whole = row_count // 3
    quads = lanes // group // row_count
    block, t, row = lane // LANES, lane // (quads * group) % whole, lane // group % quads
    k = row * row_count + jnp.where(block < 2, 2 * t + block, 2 * whole + t)
    pick = jnp.where(k + start == token, 1.0, 0.0)
    kept = jnp.dot(mask_row.astype(jnp.bfloat16), pick.astype(jnp.bfloat16), preferred_element_type=jnp.float32)
    channel = lax.broadcasted_iota(jnp.int32, (group, lanes), 0)
    lane = lax.broadcasted_iota(jnp.int32, (group, lanes), 1)
    spread_ref[...] = jnp.where(lane % group == channel, kept, 0.0)
    for copy in copies[1:3]:
        copy.wait()
    ones = jnp.ones((channels, channels), jnp.bfloat16)
    parts = []
    for piece, copy in zip(pieces, copies[3:]):
        copy.wait()
        flat = pair_ref[piece].reshape(tokens // PIECES, channels)
        mean = jnp.dot(flat, ones, preferred_element_type=jnp.float32) * (1.0 / channels)
        centred = flat.astype(jnp.float32) - mean
        square = centred * centred
        high = square.astype(jnp.bfloat16)
        low = (square - high.astype(jnp.float32)).astype(jnp.bfloat16)
        variance = jnp.dot(jnp.concatenate([high, low], axis=1), jnp.concatenate([ones, ones], axis=0), preferred_element_type=jnp.float32)
        scale = lax.rsqrt(variance * (1.0 / channels) + epsilon)
        parts.append((centred * scale * gain_ref[...] + bias_ref[...]).astype(jnp.bfloat16))
    normed = jnp.concatenate(parts, axis=0)
    normed_ref[...] = normed
    copies[-1].wait()
    arranged = arrange(normed.reshape(pair_ref.shape))
    projected = lax.dot_general(w_ref[...], arranged, (((0,), (1,)), ((), ())), preferred_element_type=jnp.float32)
    left = sigmoid(projected[:hidden]) * projected[hidden : 2 * hidden]
    right = sigmoid(projected[2 * hidden : 3 * hidden]) * projected[3 * hidden :]
    sides = jnp.concatenate([left.reshape(devices, share, tokens), right.reshape(devices, share, tokens)], axis=1)
    sides_ref[...] = pack(sides).astype(jnp.bfloat16)


def triangle_kernel(far_order, cols, row_count, col_count, share, got_ref, spread_ref, mask_ref, total_ref, left_ref):
    sources = got_ref.shape[0]
    both = 2 * share
    group, lanes = spread_ref.shape
    length = mask_ref.shape[0]
    rows, quads, parts = length // row_count, sources // cols, share // group
    whole, spare = row_count // 3, LANES - 2 * col_count
    rest = col_count - spare
    blocks = [[got_ref[sources - 1 - (col * quads + row)].astype(jnp.float32) for row in range(quads)] for col in range(cols)]

    def turned(picks):
        return jnp.concatenate([blocks[col][row][at : at + group] for col, row, at in picks], axis=0).T

    tail = turned([(col, row, whole * both + part * group) for col in range(cols) for part in range(parts) for row in range(quads)])

    def side(which, part):
        even, odd, third = [], [], []
        for col in range(cols):
            at = which * share + part * group
            block = turned([(col, row, t * both + at) for t in range(whole) for row in range(quads)])
            even.append(block[:col_count])
            odd.append(block[col_count : 2 * col_count])
            lane = (col * parts + part) * quads * group
            at = which * LANES // 2
            last = [tail[at + t * rest : at + (t + 1) * rest, lane : lane + quads * group] for t in range(whole)]
            third += [block[2 * col_count :], jnp.concatenate(last, axis=1)]
        tokens = [jnp.concatenate(pieces, axis=0) for pieces in (even, odd, third)]
        return jnp.concatenate(tokens, axis=1) * mask_ref[...]

    def placed(pieces):
        return jnp.concatenate([jnp.zeros((piece, lanes), jnp.bfloat16) if isinstance(piece, int) else piece for piece in pieces], axis=0)

    contract = (((1,), (1,)), ((), ()))
    mains, lasts = [], []
    for part in range(parts):
        left_ref[part] = side(0, part)
        right = side(1, part).astype(jnp.bfloat16)
        left = []
        for row in range(rows):
            for t in range(whole):
                at = row * row_count
                picks = [at + 2 * t, at + 2 * t + 1, at + 2 * whole + t]
                wide = [jnp.broadcast_to(left_ref[part, i : i + 1, :], (group, lanes)) * spread_ref[...] for i in picks]
                left.append(jnp.concatenate(wide, axis=1))
        left = jnp.concatenate(left, axis=0).astype(jnp.bfloat16)
        ours = [right[col * col_count : (col + 1) * col_count] for col in range(cols)]
        weights = [
            placed([p for mine in ours for p in (mine, LANES - col_count)]),
            placed([p for mine in ours for p in (col_count, mine, spare)]),
            placed([p for mine in ours for p in (2 * col_count, mine[:spare])]),
        ]
        weights = jnp.concatenate(weights, axis=1)
        mains.append(lax.dot_general(left, weights, contract, preferred_element_type=jnp.float32))
        weights = jnp.concatenate([mine[spare:] for mine in ours], axis=0)
        lasts.append(lax.dot_general(left[:, 2 * lanes :], weights, contract, preferred_element_type=jnp.float32))
    for target, device in enumerate(far_order):
        row, col = divmod(device, cols)
        spots = [(row * whole + t) * group for t in range(whole)]
        tiles = [main[at : at + group, col * LANES : (col + 1) * LANES] for at in spots for main in mains]
        last = [part[at : at + group, col * rest : (col + 1) * rest] for part in lasts for at in spots]
        tiles.append(jnp.concatenate(last, axis=1))
        total_ref[target] = jnp.concatenate(tiles, axis=0).astype(jnp.bfloat16)


def gate_kernel(normed_ref, w_ref, gain_ref, bias_ref, gate_ref, gain_out_ref, bias_out_ref):
    gate_ref[...] = sigmoid(jnp.dot(normed_ref[...], w_ref[...], preferred_element_type=jnp.float32))
    gain_out_ref[...] = column(gain_ref[...])
    bias_out_ref[...] = column(bias_ref[...])


def output_kernel(far_order, near_order, total_ref, gate_ref, gain_ref, bias_ref, w_ref, out_hbm, out_ref, sems):
    row_count, col_count, channels = out_ref.shape
    near = len(near_order)
    share = w_ref.shape[0] // near
    whole, spare = row_count // 3, LANES - 2 * col_count
    rest = col_count - spare
    blocks = []
    for index in near_order:
        parts = [total_ref[source].astype(jnp.float32) for source, device in enumerate(far_order) if device % near == index]
        blocks.append(sum(parts[1:], parts[0]))

    def project(total):
        normed = layer_norm(total, gain_ref[...], bias_ref[...], 0).astype(jnp.bfloat16)
        return lax.dot_general(normed, w_ref[...], (((0,), (0,)), ((), ())), preferred_element_type=jnp.float32)

    def store(row, at, values):
        spot = pl.ds(row * col_count + at, values.shape[0])
        out_ref[row, pl.ds(at, values.shape[0])] = (gate_ref[spot] * values).astype(jnp.bfloat16)

    tails = [block[whole * share :] for block in blocks]
    tails = [jnp.concatenate([tail[:, : LANES // 2], tail[:, LANES // 2 :]], axis=0) for tail in tails]
    last = project(jnp.concatenate(tails, axis=0))
    for t in range(whole):
        store(2 * whole + t, spare, last[t * rest : (t + 1) * rest])
    copies = []
    for t in range(whole):
        values = project(jnp.concatenate([block[t * share : (t + 1) * share] for block in blocks], axis=0))
        store(2 * t, 0, values[:col_count])
        store(2 * t + 1, 0, values[col_count : 2 * col_count])
        store(2 * whole + t, 0, values[2 * col_count :])
        for rows in (pl.ds(2 * t, 2), pl.ds(2 * whole + t, 1)):
            copy = pltpu.make_async_copy(out_ref.at[rows], out_hbm.at[rows], sems.at[len(copies)])
            copy.start()
            copies.append(copy)
    for copy in copies:
        copy.wait()


def per_device(rows, cols, halves, pair, token_mask, gain_in, bias_in, w_in, w_gate, gain_out, bias_out, w_out):
    row_count, col_count, channels = pair.shape
    hidden = w_out.shape[0]
    devices = rows * cols
    near = devices // halves
    quads = rows // halves
    near_order = [quad * cols + col for col in reversed(range(cols)) for quad in reversed(range(quads))]
    far_order = []
    for col in reversed(range(cols)):
        ahead = list(range(quads)) if col else list(range(1, quads)) + [0]
        behind = [1] + [quad for quad in reversed(range(quads)) if quad != 1] if col else list(reversed(range(quads)))
        for quad, other in zip(ahead, behind):
            far_order += [near + other * cols + col, quad * cols + col]
    share = hidden // near
    tokens = row_count * col_count
    length = rows * row_count
    depth = length // halves
    token_mask = token_mask.reshape(1, length)
    arguments = (pair, gain_in.reshape(1, channels), bias_in.reshape(1, channels), w_in, token_mask)
    sides, normed, *masks = pl.pallas_call(
        project_kernel,
        out_shape=(
            jax.ShapeDtypeStruct((near, 2 * share * tokens // LANES, LANES), jnp.bfloat16),
            jax.ShapeDtypeStruct((tokens, channels), jnp.bfloat16),
            jax.ShapeDtypeStruct((GROUP, GROUP * depth), jnp.float32),
            jax.ShapeDtypeStruct((length, 1), jnp.float32),
        ),
        in_specs=[HBM] * 5,
        out_specs=(VMEM,) * 4,
        scratch_shapes=[
            pltpu.VMEM(pair.shape, pair.dtype),
            pltpu.VMEM((1, channels), jnp.float32),
            pltpu.VMEM((1, channels), jnp.float32),
            pltpu.VMEM(w_in.shape, w_in.dtype),
            pltpu.VMEM((1, length), jnp.int32),
            pltpu.SemaphoreType.DMA((PIECES + 4,)),
        ],
        compiler_params=LIMIT,
    )(*(pltpu.with_memory_space_constraint(x, pltpu.HBM) for x in arguments))
    got = lax.all_to_all(sides, ("quad", "col"), split_axis=0, concat_axis=0, tiled=True, axis_index_groups=[near_order])
    total = pl.pallas_call(
        functools.partial(triangle_kernel, far_order, cols, row_count, col_count, share),
        out_shape=jax.ShapeDtypeStruct((devices, share * tokens // LANES, LANES), jnp.bfloat16),
        in_specs=[VMEM] * 3,
        out_specs=VMEM,
        scratch_shapes=[pltpu.VMEM((share // GROUP, length, GROUP * depth), jnp.float32)],
        compiler_params=LIMIT,
    )(got, *masks)
    gate, gain_out, bias_out = pl.pallas_call(
        gate_kernel,
        out_shape=(
            jax.ShapeDtypeStruct((tokens, channels), jnp.float32),
            jax.ShapeDtypeStruct((hidden, 1), jnp.float32),
            jax.ShapeDtypeStruct((hidden, 1), jnp.float32),
        ),
        in_specs=[VMEM] * 4,
        out_specs=(VMEM, VMEM, VMEM),
        compiler_params=LIMIT,
        cost_estimate=pl.CostEstimate(flops=2 * tokens * channels * channels, bytes_accessed=4 * tokens * channels, transcendentals=0),
    )(normed, w_gate, gain_out.reshape(1, hidden), bias_out.reshape(1, hidden))
    total = lax.all_to_all(total, ("half", "quad", "col"), split_axis=0, concat_axis=0, tiled=True, axis_index_groups=[far_order])
    return pl.pallas_call(
        functools.partial(output_kernel, far_order, near_order),
        out_shape=jax.ShapeDtypeStruct(pair.shape, jnp.bfloat16),
        in_specs=[VMEM] * 5,
        out_specs=HBM,
        scratch_shapes=[pltpu.VMEM(pair.shape, jnp.bfloat16), pltpu.SemaphoreType.DMA((2 * row_count // 3,))],
        compiler_params=LIMIT,
    )(total, gate, gain_out, bias_out, w_out)


def plain_per_device(rows, cols, pair, token_mask, gain_in, bias_in, w_in, w_gate, gain_out, bias_out, w_out):
    row_count, col_count, channels = pair.shape
    hidden = w_out.shape[0]
    devices = rows * cols
    share = hidden // devices
    tokens = row_count * col_count
    row_start = lax.axis_index(("half", "quad")) * row_count
    col_start = lax.axis_index("col") * col_count
    mask_float = token_mask.astype(jnp.float32)
    mask_rows = lax.dynamic_slice_in_dim(mask_float, row_start, row_count)
    mask_cols = lax.dynamic_slice_in_dim(mask_float, col_start, col_count)
    pair_mask = (mask_rows[:, None] * mask_cols[None, :]).reshape(1, tokens)
    flat = pair.reshape(tokens, channels).astype(jnp.float32)
    normed = layer_norm(flat, gain_in, bias_in, -1).astype(jnp.bfloat16)
    projected = lax.dot_general(w_in, normed, (((0,), (1,)), ((), ())), preferred_element_type=jnp.float32)
    projected = projected.reshape(2, 2, hidden, tokens)
    sides = (pair_mask * jax.nn.sigmoid(projected[:, 0]) * projected[:, 1]).astype(jnp.bfloat16)
    sides = sides.reshape(2, devices, share, tokens).transpose(1, 0, 2, 3)
    gate = jax.nn.sigmoid(jnp.dot(normed, w_gate, preferred_element_type=jnp.float32))
    got = lax.all_to_all(sides, AXES, split_axis=0, concat_axis=0, tiled=True)
    got = got.reshape(rows, cols, 2, share, row_count, col_count).transpose(2, 3, 0, 4, 1, 5)
    got = got.reshape(2, share, rows * row_count, cols * col_count)
    total = jnp.einsum("cki,ckj->cij", got[0], got[1], preferred_element_type=jnp.float32).astype(jnp.bfloat16)
    total = total.reshape(share, rows, row_count, cols, col_count).transpose(1, 3, 0, 2, 4)
    total = total.reshape(devices, share, tokens)
    total = lax.all_to_all(total, AXES, split_axis=0, concat_axis=0, tiled=True)
    total = total.reshape(hidden, tokens).astype(jnp.float32)
    summed_norm = layer_norm(total, gain_out[:, None], bias_out[:, None], 0).astype(jnp.bfloat16)
    output = lax.dot_general(summed_norm, w_out, (((0,), (0,)), ((), ())), preferred_element_type=jnp.float32)
    return (gate * output).astype(jnp.bfloat16).reshape(row_count, col_count, channels)


def solution(mesh):
    rows, cols = mesh.shape["row"], mesh.shape["col"]
    halves = 2
    parts = (mesh.shape["groups"], halves, rows // halves, cols)
    finer = jax.sharding.Mesh(mesh.devices.reshape(parts), ("groups", "half", "quad", "col"))

    def per_shard(*args):
        near, hidden, length = rows * cols // halves, args[-1].shape[0], args[1].shape[0]
        row_count, col_count, _ = args[0].shape
        spare = LANES - 2 * col_count
        fits = hidden % (2 * GROUP * near) == 0 and cols == 2 and length <= LANES and row_count % 3 == 0
        fits = fits and 0 < spare < col_count and row_count // 3 * (col_count - spare) * 2 == LANES
        fits = fits and row_count // 3 * (rows // halves) * GROUP == LANES
        return per_device(rows, cols, halves, *args) if fits else plain_per_device(rows, cols, *args)

    tokens = P(("groups", "half", "quad"), "col", None)
    in_specs = (tokens, P("groups"), P(), P(), P(), P(), P(), P(), P())
    return jax.shard_map(per_shard, mesh=finer, in_specs=in_specs, out_specs=tokens, check_vma=False)
```

```python
import functools

import jax
import jax.numpy as jnp
from jax import lax
from jax.experimental import pallas as pl
from jax.experimental.pallas import tpu as pltpu
from jax.sharding import PartitionSpec as P

epsilon = 1e-05
LANES = 128
GROUP = 8
AXES = ("half", "quad", "col")
VMEM = pl.BlockSpec(memory_space=pltpu.VMEM)
HBM = pl.BlockSpec(memory_space=pltpu.HBM)
LIMIT = pltpu.CompilerParams(vmem_limit_bytes=32 * 1024 * 1024)


def sigmoid(x):
    return 0.5 * jnp.tanh(0.5 * x) + 0.5


def layer_norm(values, gain, bias, axis):
    mean = jnp.mean(values, axis=axis, keepdims=True)
    centred = values - mean
    variance = jnp.mean(centred * centred, axis=axis, keepdims=True)
    return centred * lax.rsqrt(variance + epsilon) * gain + bias


def column(row):
    n = row.shape[1]
    eye = lax.broadcasted_iota(jnp.int32, (n, n), 0) == lax.broadcasted_iota(jnp.int32, (n, n), 1)
    return jnp.sum(jnp.where(eye, row, 0.0), axis=1, keepdims=True)


def pack(x):
    rows, tokens = x.shape[-2:]
    whole, rest = divmod(tokens, LANES)
    blocks = [x[..., t * LANES : (t + 1) * LANES] for t in range(whole)]
    if rest:
        tail = x[..., whole * LANES :]
        blocks.append(jnp.concatenate([tail[..., : rows // 2, :], tail[..., rows // 2 :, :]], axis=-1))
    return jnp.concatenate(blocks, axis=-2)


def unpack(x, rows):
    whole, rest = divmod(x.shape[-2], rows)
    blocks = [x[..., t * rows : (t + 1) * rows, :] for t in range(whole)]
    if rest:
        tail = x[..., whole * rows :, :]
        blocks.append(jnp.concatenate([tail[..., : LANES // 2], tail[..., LANES // 2 :]], axis=-2))
    return jnp.concatenate(blocks, axis=-1)


def arrange(x):
    row_count, col_count, _ = x.shape
    whole, spare = row_count // 3, LANES - 2 * col_count
    blocks = []
    for t in range(whole):
        blocks += [x[2 * t], x[2 * t + 1], x[2 * whole + t, :spare]]
    return jnp.concatenate(blocks + [x[2 * whole + t, spare:] for t in range(whole)], axis=0)


def restore(x, row_count, col_count):
    whole, spare = row_count // 3, LANES - 2 * col_count
    rest = col_count - spare
    rows = []
    for t in range(whole):
        rows += [x[t * LANES : t * LANES + col_count], x[t * LANES + col_count : t * LANES + 2 * col_count]]
    for t in range(whole):
        tail = whole * LANES + t * rest
        rows += [x[t * LANES + 2 * col_count : (t + 1) * LANES], x[tail : tail + rest]]
    return jnp.concatenate(rows, axis=0)


def project_kernel(quads, cols, pair_hbm, gain_hbm, bias_hbm, w_hbm, mask_hbm, *refs):
    piece_refs, refs = refs[: quads * cols], refs[quads * cols :]
    normed_ref, spread_ref, column_mask_ref, pair_ref, gain_ref, bias_ref, w_ref, mask_ref, sems, sides_ref = refs
    copies = [
        pltpu.make_async_copy(source, target, sems.at[n])
        for n, (source, target) in enumerate(
            [(mask_hbm, mask_ref), (pair_hbm, pair_ref), (gain_hbm, gain_ref), (bias_hbm, bias_ref), (w_hbm, w_ref)]
        )
    ]
    for copy in copies:
        copy.start()
    devices = sides_ref.shape[0]
    my_quad, my_col = lax.axis_index("quad"), lax.axis_index("col")
    tokens, channels = normed_ref.shape
    hidden = w_ref.shape[1] // 4
    share = hidden // devices
    group, lanes = spread_ref.shape
    copies[0].wait()
    mask_row = mask_ref[...].astype(jnp.float32)
    mask_column = column(mask_row)
    middle = mask_column.shape[0] // cols
    swapped = jnp.concatenate([mask_column[middle:], mask_column[:middle]], axis=0)
    column_mask_ref[...] = jnp.where(my_col == 0, mask_column, swapped)
    start = lax.axis_index("half") * (lanes // group)
    token = lax.broadcasted_iota(jnp.int32, (mask_row.shape[1], lanes), 0)
    lane = lax.broadcasted_iota(jnp.int32, (mask_row.shape[1], lanes), 1)
    row_count = pair_ref.shape[0]
    whole = row_count // 3
    block, t, row = lane // LANES, lane // (quads * group) % whole, lane // group % quads
    k = (row ^ my_quad) * row_count + jnp.where(block < 2, 2 * t + block, 2 * whole + t)
    pick = jnp.where(k + start == token, 1.0, 0.0)
    kept = jnp.dot(mask_row.astype(jnp.bfloat16), pick.astype(jnp.bfloat16), preferred_element_type=jnp.float32)
    channel = lax.broadcasted_iota(jnp.int32, (group, lanes), 0)
    lane = lax.broadcasted_iota(jnp.int32, (group, lanes), 1)
    spread_ref[...] = jnp.where(lane % group == channel, kept, 0.0)
    for copy in copies[1:4]:
        copy.wait()
    flat = pair_ref[...].reshape(tokens, channels).astype(jnp.float32)
    normed = layer_norm(flat, gain_ref[...], bias_ref[...], -1).astype(jnp.bfloat16)
    normed_ref[...] = normed
    copies[4].wait()
    arranged = arrange(normed.reshape(pair_ref.shape))
    projected = lax.dot_general(w_ref[...], arranged, (((0,), (1,)), ((), ())), preferred_element_type=jnp.float32)
    left = sigmoid(projected[:hidden]) * projected[hidden : 2 * hidden]
    right = sigmoid(projected[2 * hidden : 3 * hidden]) * projected[3 * hidden :]
    sides = jnp.concatenate([left.reshape(devices, share, tokens), right.reshape(devices, share, tokens)], axis=1)
    sides_ref[...] = pack(sides).astype(jnp.bfloat16)
    for step, piece_ref in enumerate(piece_refs):
        piece_ref[...] = sides_ref[(my_quad * cols + my_col) ^ step]


def triangle_kernel(far_order, cols, row_count, col_count, share, *refs):
    *got_refs, spread_ref, mask_ref, total_ref = refs
    sources = len(got_refs)
    my_col = lax.axis_index("col")
    both = 2 * share
    group, lanes = spread_ref.shape
    length = mask_ref.shape[0]
    rows, quads, parts = length // row_count, sources // cols, share // group
    whole, spare = row_count // 3, LANES - 2 * col_count
    rest = col_count - spare
    blocks = [[got_refs[row * cols + col][...].astype(jnp.float32) for row in range(quads)] for col in range(cols)]

    def turned(picks):
        return jnp.concatenate([blocks[col][row][at : at + group] for col, row, at in picks], axis=0).T

    tail = turned([(col, row, whole * both + part * group) for col in range(cols) for part in range(parts) for row in range(quads)])

    def side(which, part):
        even, odd, third = [], [], []
        for col in range(cols):
            at = which * share + part * group
            block = turned([(col, row, t * both + at) for t in range(whole) for row in range(quads)])
            even.append(block[:col_count])
            odd.append(block[col_count : 2 * col_count])
            lane = (col * parts + part) * quads * group
            at = which * LANES // 2
            last = [tail[at + t * rest : at + (t + 1) * rest, lane : lane + quads * group] for t in range(whole)]
            third += [block[2 * col_count :], jnp.concatenate(last, axis=1)]
        tokens = [jnp.concatenate(pieces, axis=0) for pieces in (even, odd, third)]
        return jnp.concatenate(tokens, axis=1) * mask_ref[...]

    def placed(pieces):
        return jnp.concatenate([jnp.zeros((piece, lanes), jnp.bfloat16) if isinstance(piece, int) else piece for piece in pieces], axis=0)

    contract = (((1,), (1,)), ((), ()))
    mains, lasts = [], []
    for part in range(parts):
        left, right = side(0, part), side(1, part).astype(jnp.bfloat16)
        left = (left[:, None, :] * spread_ref[...][None]).reshape(rows, row_count, group, lanes)
        pairs = left[:, : 2 * whole].reshape(rows, whole, 2, group, lanes)
        left = jnp.concatenate([pairs[:, :, 0], pairs[:, :, 1], left[:, 2 * whole :]], axis=-1)
        left = left.reshape(rows * whole * group, 3 * lanes).astype(jnp.bfloat16)
        ours = [right[col * col_count : (col + 1) * col_count] for col in range(cols)]
        weights = [
            placed([p for mine in ours for p in (mine, LANES - col_count)]),
            placed([p for mine in ours for p in (col_count, mine, spare)]),
            placed([p for mine in ours for p in (2 * col_count, mine[:spare])]),
        ]
        weights = jnp.concatenate(weights, axis=1)
        mains.append(lax.dot_general(left, weights, contract, preferred_element_type=jnp.float32))
        weights = jnp.concatenate([mine[spare:] for mine in ours], axis=0)
        lasts.append(lax.dot_general(left[:, 2 * lanes :], weights, contract, preferred_element_type=jnp.float32))
    for device in range(rows * cols):
        row, col = divmod(device, cols)
        other = (row + rows // 2) % rows * cols + 1 - col
        target = jnp.where(my_col == 0, far_order.index(device), far_order.index(other))
        spots = [(row * whole + t) * group for t in range(whole)]
        tiles = [main[at : at + group, col * LANES : (col + 1) * LANES] for at in spots for main in mains]
        last = [part[at : at + group, col * rest : (col + 1) * rest] for part in lasts for at in spots]
        tiles.append(jnp.concatenate(last, axis=1))
        total_ref[target] = jnp.concatenate(tiles, axis=0).astype(jnp.bfloat16)


def gate_kernel(normed_ref, w_ref, gain_ref, bias_ref, gate_ref, gain_out_ref, bias_out_ref):
    gate_ref[...] = sigmoid(jnp.dot(normed_ref[...], w_ref[...], preferred_element_type=jnp.float32))
    gain_out_ref[...] = column(gain_ref[...])
    bias_out_ref[...] = column(bias_ref[...])


def output_kernel(far_order, near, total_ref, gate_ref, gain_ref, bias_ref, w_ref, out_ref):
    tokens = gate_ref.shape[0]
    hidden = w_ref.shape[0]
    share = hidden // near
    blocks = []
    for index in range(near):
        parts = [total_ref[source].astype(jnp.float32) for source, device in enumerate(far_order) if device % near == index]
        blocks.append(unpack(sum(parts[1:], parts[0]), share))
    total = jnp.concatenate(blocks, axis=0)
    normed = layer_norm(total, gain_ref[...], bias_ref[...], 0).astype(jnp.bfloat16)
    output = lax.dot_general(normed, w_ref[...], (((0,), (0,)), ((), ())), preferred_element_type=jnp.float32)
    output = restore(output, out_ref.shape[0], out_ref.shape[1])
    out_ref[...] = (gate_ref[...] * output).astype(jnp.bfloat16).reshape(out_ref.shape)


def per_device(rows, cols, halves, pair, token_mask, gain_in, bias_in, w_in, w_gate, gain_out, bias_out, w_out):
    row_count, col_count, channels = pair.shape
    hidden = w_out.shape[0]
    devices = rows * cols
    near = devices // halves
    quads = rows // halves
    far_order = []
    for col in reversed(range(cols)):
        ahead = list(range(quads)) if col else list(range(1, quads)) + [0]
        behind = [1] + [quad for quad in reversed(range(quads)) if quad != 1] if col else list(reversed(range(quads)))
        for quad, other in zip(ahead, behind):
            far_order += [near + other * cols + col, quad * cols + col]
    share = hidden // near
    tokens = row_count * col_count
    length = rows * row_count
    depth = length // halves
    token_mask = token_mask.reshape(1, length)
    arguments = (pair, gain_in.reshape(1, channels), bias_in.reshape(1, channels), w_in, token_mask)
    *pieces, normed, spread, mask = pl.pallas_call(
        functools.partial(project_kernel, quads, cols),
        out_shape=(
            *[jax.ShapeDtypeStruct((2 * share * tokens // LANES, LANES), jnp.bfloat16)] * near,
            jax.ShapeDtypeStruct((tokens, channels), jnp.bfloat16),
            jax.ShapeDtypeStruct((GROUP, GROUP * depth), jnp.float32),
            jax.ShapeDtypeStruct((length, 1), jnp.float32),
        ),
        in_specs=[HBM] * 5,
        out_specs=(VMEM,) * (near + 3),
        scratch_shapes=[
            pltpu.VMEM(pair.shape, pair.dtype),
            pltpu.VMEM((1, channels), jnp.float32),
            pltpu.VMEM((1, channels), jnp.float32),
            pltpu.VMEM(w_in.shape, w_in.dtype),
            pltpu.VMEM((1, length), jnp.int32),
            pltpu.SemaphoreType.DMA((5,)),
            pltpu.VMEM((near, 2 * share * tokens // LANES, LANES), jnp.bfloat16),
        ],
        compiler_params=LIMIT,
    )(*(pltpu.with_memory_space_constraint(x, pltpu.HBM) for x in arguments))
    got = pieces[:1] + [None] * (near - 1)
    for quad in reversed(range(quads)):
        for step in range(quad * cols, (quad + 1) * cols):
            if step:
                got[step] = lax.ppermute(pieces[step], ("quad", "col"), [(i, i ^ step) for i in range(near)])
    total = pl.pallas_call(
        functools.partial(triangle_kernel, far_order, cols, row_count, col_count, share),
        out_shape=jax.ShapeDtypeStruct((devices, share * tokens // LANES, LANES), jnp.bfloat16),
        in_specs=[VMEM] * (near + 2),
        out_specs=VMEM,
        compiler_params=LIMIT,
    )(*got, spread, mask)
    gate, gain_out, bias_out = pl.pallas_call(
        gate_kernel,
        out_shape=(
            jax.ShapeDtypeStruct((tokens, channels), jnp.float32),
            jax.ShapeDtypeStruct((hidden, 1), jnp.float32),
            jax.ShapeDtypeStruct((hidden, 1), jnp.float32),
        ),
        in_specs=[VMEM] * 4,
        out_specs=(VMEM, VMEM, VMEM),
        compiler_params=LIMIT,
        cost_estimate=pl.CostEstimate(flops=2 * tokens * channels * channels, bytes_accessed=4 * tokens * channels, transcendentals=0),
    )(normed, w_gate, gain_out.reshape(1, hidden), bias_out.reshape(1, hidden))
    total = lax.all_to_all(total, ("half", "quad", "col"), split_axis=0, concat_axis=0, tiled=True, axis_index_groups=[far_order])
    return pl.pallas_call(
        functools.partial(output_kernel, far_order, near),
        out_shape=jax.ShapeDtypeStruct(pair.shape, jnp.bfloat16),
        in_specs=[VMEM] * 5,
        out_specs=VMEM,
        compiler_params=LIMIT,
    )(total, gate, gain_out, bias_out, w_out)


def plain_per_device(rows, cols, pair, token_mask, gain_in, bias_in, w_in, w_gate, gain_out, bias_out, w_out):
    row_count, col_count, channels = pair.shape
    hidden = w_out.shape[0]
    devices = rows * cols
    share = hidden // devices
    tokens = row_count * col_count
    row_start = lax.axis_index(("half", "quad")) * row_count
    col_start = lax.axis_index("col") * col_count
    mask_float = token_mask.astype(jnp.float32)
    mask_rows = lax.dynamic_slice_in_dim(mask_float, row_start, row_count)
    mask_cols = lax.dynamic_slice_in_dim(mask_float, col_start, col_count)
    pair_mask = (mask_rows[:, None] * mask_cols[None, :]).reshape(1, tokens)
    flat = pair.reshape(tokens, channels).astype(jnp.float32)
    normed = layer_norm(flat, gain_in, bias_in, -1).astype(jnp.bfloat16)
    projected = lax.dot_general(w_in, normed, (((0,), (1,)), ((), ())), preferred_element_type=jnp.float32)
    projected = projected.reshape(2, 2, hidden, tokens)
    sides = (pair_mask * jax.nn.sigmoid(projected[:, 0]) * projected[:, 1]).astype(jnp.bfloat16)
    sides = sides.reshape(2, devices, share, tokens).transpose(1, 0, 2, 3)
    gate = jax.nn.sigmoid(jnp.dot(normed, w_gate, preferred_element_type=jnp.float32))
    got = lax.all_to_all(sides, AXES, split_axis=0, concat_axis=0, tiled=True)
    got = got.reshape(rows, cols, 2, share, row_count, col_count).transpose(2, 3, 0, 4, 1, 5)
    got = got.reshape(2, share, rows * row_count, cols * col_count)
    total = jnp.einsum("cki,ckj->cij", got[0], got[1], preferred_element_type=jnp.float32).astype(jnp.bfloat16)
    total = total.reshape(share, rows, row_count, cols, col_count).transpose(1, 3, 0, 2, 4)
    total = total.reshape(devices, share, tokens)
    total = lax.all_to_all(total, AXES, split_axis=0, concat_axis=0, tiled=True)
    total = total.reshape(hidden, tokens).astype(jnp.float32)
    summed_norm = layer_norm(total, gain_out[:, None], bias_out[:, None], 0).astype(jnp.bfloat16)
    output = lax.dot_general(summed_norm, w_out, (((0,), (0,)), ((), ())), preferred_element_type=jnp.float32)
    return (gate * output).astype(jnp.bfloat16).reshape(row_count, col_count, channels)


def solution(mesh):
    rows, cols = mesh.shape["row"], mesh.shape["col"]
    halves = 2
    parts = (mesh.shape["groups"], halves, rows // halves, cols)
    finer = jax.sharding.Mesh(mesh.devices.reshape(parts), ("groups", "half", "quad", "col"))

    def per_shard(*args):
        near, hidden, length = rows * cols // halves, args[-1].shape[0], args[1].shape[0]
        row_count, col_count, _ = args[0].shape
        spare = LANES - 2 * col_count
        fits = hidden % (2 * GROUP * near) == 0 and cols == 2 and length <= LANES and row_count % 3 == 0
        fits = fits and 0 < spare < col_count and row_count // 3 * (col_count - spare) * 2 == LANES
        fits = fits and row_count // 3 * (rows // halves) * GROUP == LANES
        return per_device(rows, cols, halves, *args) if fits else plain_per_device(rows, cols, *args)

    tokens = P(("groups", "half", "quad"), "col", None)
    in_specs = (tokens, P("groups"), P(), P(), P(), P(), P(), P(), P())
    return jax.shard_map(per_shard, mesh=finer, in_specs=in_specs, out_specs=tokens, check_vma=False)
```

```python
import functools

import jax
import jax.numpy as jnp
from jax import lax
from jax.experimental import pallas as pl
from jax.experimental.pallas import tpu as pltpu
from jax.sharding import PartitionSpec as P

epsilon = 1e-05
LANES = 128
GROUP = 8
AXES = ("half", "quad", "col")
VMEM = pl.BlockSpec(memory_space=pltpu.VMEM)
HBM = pl.BlockSpec(memory_space=pltpu.HBM)
LIMIT = pltpu.CompilerParams(vmem_limit_bytes=32 * 1024 * 1024)


def sigmoid(x):
    return 0.5 * jnp.tanh(0.5 * x) + 0.5


def layer_norm(values, gain, bias, axis):
    mean = jnp.mean(values, axis=axis, keepdims=True)
    centred = values - mean
    variance = jnp.mean(centred * centred, axis=axis, keepdims=True)
    return centred * lax.rsqrt(variance + epsilon) * gain + bias


def column(row):
    n = row.shape[1]
    eye = lax.broadcasted_iota(jnp.int32, (n, n), 0) == lax.broadcasted_iota(jnp.int32, (n, n), 1)
    return jnp.sum(jnp.where(eye, row, 0.0), axis=1, keepdims=True)


def pack(x):
    rows, tokens = x.shape[-2:]
    whole, rest = divmod(tokens, LANES)
    blocks = [x[..., t * LANES : (t + 1) * LANES] for t in range(whole)]
    if rest:
        tail = x[..., whole * LANES :]
        blocks.append(jnp.concatenate([tail[..., : rows // 2, :], tail[..., rows // 2 :, :]], axis=-1))
    return jnp.concatenate(blocks, axis=-2)


def unpack(x, rows):
    whole, rest = divmod(x.shape[-2], rows)
    blocks = [x[..., t * rows : (t + 1) * rows, :] for t in range(whole)]
    if rest:
        tail = x[..., whole * rows :, :]
        blocks.append(jnp.concatenate([tail[..., : LANES // 2], tail[..., LANES // 2 :]], axis=-2))
    return jnp.concatenate(blocks, axis=-1)


def arrange(x):
    row_count, col_count, _ = x.shape
    whole, spare = row_count // 3, LANES - 2 * col_count
    blocks = []
    for t in range(whole):
        blocks += [x[2 * t], x[2 * t + 1], x[2 * whole + t, :spare]]
    return jnp.concatenate(blocks + [x[2 * whole + t, spare:] for t in range(whole)], axis=0)


def restore(x, row_count, col_count):
    whole, spare = row_count // 3, LANES - 2 * col_count
    rest = col_count - spare
    rows = []
    for t in range(whole):
        rows += [x[t * LANES : t * LANES + col_count], x[t * LANES + col_count : t * LANES + 2 * col_count]]
    for t in range(whole):
        tail = whole * LANES + t * rest
        rows += [x[t * LANES + 2 * col_count : (t + 1) * LANES], x[tail : tail + rest]]
    return jnp.concatenate(rows, axis=0)


def project_kernel(quads, cols, pair_hbm, gain_hbm, bias_hbm, w_hbm, mask_hbm, *refs):
    piece_refs, refs = refs[: quads * cols], refs[quads * cols :]
    normed_ref, spread_ref, column_mask_ref, pair_ref, gain_ref, bias_ref, w_ref, mask_ref, sems, sides_ref = refs
    copies = [
        pltpu.make_async_copy(source, target, sems.at[n])
        for n, (source, target) in enumerate(
            [(mask_hbm, mask_ref), (pair_hbm, pair_ref), (gain_hbm, gain_ref), (bias_hbm, bias_ref), (w_hbm, w_ref)]
        )
    ]
    for copy in copies:
        copy.start()
    devices = sides_ref.shape[0]
    my_quad, my_col = lax.axis_index("quad"), lax.axis_index("col")
    tokens, channels = normed_ref.shape
    hidden = w_ref.shape[1] // 4
    share = hidden // devices
    group, lanes = spread_ref.shape
    copies[0].wait()
    mask_row = mask_ref[...].astype(jnp.float32)
    mask_column = column(mask_row)
    middle = mask_column.shape[0] // cols
    swapped = jnp.concatenate([mask_column[middle:], mask_column[:middle]], axis=0)
    column_mask_ref[...] = jnp.where(my_col == 0, mask_column, swapped)
    start = lax.axis_index("half") * (lanes // group)
    token = lax.broadcasted_iota(jnp.int32, (mask_row.shape[1], lanes), 0)
    lane = lax.broadcasted_iota(jnp.int32, (mask_row.shape[1], lanes), 1)
    row_count = pair_ref.shape[0]
    whole = row_count // 3
    block, t, row = lane // LANES, lane // (quads * group) % whole, lane // group % quads
    k = (row ^ my_quad) * row_count + jnp.where(block < 2, 2 * t + block, 2 * whole + t)
    pick = jnp.where(k + start == token, 1.0, 0.0)
    kept = jnp.dot(mask_row.astype(jnp.bfloat16), pick.astype(jnp.bfloat16), preferred_element_type=jnp.float32)
    channel = lax.broadcasted_iota(jnp.int32, (group, lanes), 0)
    lane = lax.broadcasted_iota(jnp.int32, (group, lanes), 1)
    spread_ref[...] = jnp.where(lane % group == channel, kept, 0.0)
    for copy in copies[1:4]:
        copy.wait()
    flat = pair_ref[...].reshape(tokens, channels).astype(jnp.float32)
    normed = layer_norm(flat, gain_ref[...], bias_ref[...], -1).astype(jnp.bfloat16)
    normed_ref[...] = normed
    copies[4].wait()
    arranged = arrange(normed.reshape(pair_ref.shape))
    projected = lax.dot_general(w_ref[...], arranged, (((0,), (1,)), ((), ())), preferred_element_type=jnp.float32)
    left = sigmoid(projected[:hidden]) * projected[hidden : 2 * hidden]
    right = sigmoid(projected[2 * hidden : 3 * hidden]) * projected[3 * hidden :]
    sides = jnp.concatenate([left.reshape(devices, share, tokens), right.reshape(devices, share, tokens)], axis=1)
    sides_ref[...] = pack(sides).astype(jnp.bfloat16)
    for step, piece_ref in enumerate(piece_refs):
        piece_ref[...] = sides_ref[(my_quad * cols + my_col) ^ step]


def triangle_kernel(far_order, steps, cols, row_count, col_count, share, *refs):
    *got_refs, spread_ref, mask_ref, total_ref = refs
    got_refs = {step: ref for step, ref in zip(steps, got_refs)}
    sources = len(steps)
    my_col = lax.axis_index("col")
    both = 2 * share
    group, lanes = spread_ref.shape
    length = mask_ref.shape[0]
    rows, quads, parts = length // row_count, sources // cols, share // group
    whole, spare = row_count // 3, LANES - 2 * col_count
    rest = col_count - spare
    blocks = [[got_refs[row * cols + col][...].astype(jnp.float32) for row in range(quads)] for col in range(cols)]

    def turned(picks):
        return jnp.concatenate([blocks[col][row][at : at + group] for col, row, at in picks], axis=0).T

    tail = turned([(col, row, whole * both + part * group) for col in range(cols) for part in range(parts) for row in range(quads)])

    def side(which, part):
        even, odd, third = [], [], []
        for col in range(cols):
            at = which * share + part * group
            block = turned([(col, row, t * both + at) for t in range(whole) for row in range(quads)])
            even.append(block[:col_count])
            odd.append(block[col_count : 2 * col_count])
            lane = (col * parts + part) * quads * group
            at = which * LANES // 2
            last = [tail[at + t * rest : at + (t + 1) * rest, lane : lane + quads * group] for t in range(whole)]
            third += [block[2 * col_count :], jnp.concatenate(last, axis=1)]
        tokens = [jnp.concatenate(pieces, axis=0) for pieces in (even, odd, third)]
        return jnp.concatenate(tokens, axis=1) * mask_ref[...]

    def placed(pieces):
        return jnp.concatenate([jnp.zeros((piece, lanes), jnp.bfloat16) if isinstance(piece, int) else piece for piece in pieces], axis=0)

    contract = (((1,), (1,)), ((), ()))
    mains, lasts = [], []
    for part in range(parts):
        left, right = side(0, part), side(1, part).astype(jnp.bfloat16)
        left = (left[:, None, :] * spread_ref[...][None]).reshape(rows, row_count, group, lanes)
        pairs = left[:, : 2 * whole].reshape(rows, whole, 2, group, lanes)
        left = jnp.concatenate([pairs[:, :, 0], pairs[:, :, 1], left[:, 2 * whole :]], axis=-1)
        left = left.reshape(rows * whole * group, 3 * lanes).astype(jnp.bfloat16)
        ours = [right[col * col_count : (col + 1) * col_count] for col in range(cols)]
        weights = [
            placed([p for mine in ours for p in (mine, LANES - col_count)]),
            placed([p for mine in ours for p in (col_count, mine, spare)]),
            placed([p for mine in ours for p in (2 * col_count, mine[:spare])]),
        ]
        weights = jnp.concatenate(weights, axis=1)
        mains.append(lax.dot_general(left, weights, contract, preferred_element_type=jnp.float32))
        weights = jnp.concatenate([mine[spare:] for mine in ours], axis=0)
        lasts.append(lax.dot_general(left[:, 2 * lanes :], weights, contract, preferred_element_type=jnp.float32))
    for device in range(rows * cols):
        row, col = divmod(device, cols)
        other = (row + rows // 2) % rows * cols + 1 - col
        target = jnp.where(my_col == 0, far_order.index(device), far_order.index(other))
        spots = [(row * whole + t) * group for t in range(whole)]
        tiles = [main[at : at + group, col * LANES : (col + 1) * LANES] for at in spots for main in mains]
        last = [part[at : at + group, col * rest : (col + 1) * rest] for part in lasts for at in spots]
        tiles.append(jnp.concatenate(last, axis=1))
        total_ref[target] = jnp.concatenate(tiles, axis=0).astype(jnp.bfloat16)


def gate_kernel(normed_ref, w_ref, gain_ref, bias_ref, gate_ref, gain_out_ref, bias_out_ref):
    gate_ref[...] = sigmoid(jnp.dot(normed_ref[...], w_ref[...], preferred_element_type=jnp.float32))
    gain_out_ref[...] = column(gain_ref[...])
    bias_out_ref[...] = column(bias_ref[...])


def output_kernel(far_order, near, total_ref, gate_ref, gain_ref, bias_ref, w_ref, out_ref):
    tokens = gate_ref.shape[0]
    hidden = w_ref.shape[0]
    share = hidden // near
    blocks = []
    for index in range(near):
        parts = [total_ref[source].astype(jnp.float32) for source, device in enumerate(far_order) if device % near == index]
        blocks.append(unpack(sum(parts[1:], parts[0]), share))
    total = jnp.concatenate(blocks, axis=0)
    normed = layer_norm(total, gain_ref[...], bias_ref[...], 0).astype(jnp.bfloat16)
    output = lax.dot_general(normed, w_ref[...], (((0,), (0,)), ((), ())), preferred_element_type=jnp.float32)
    output = restore(output, out_ref.shape[0], out_ref.shape[1])
    out_ref[...] = (gate_ref[...] * output).astype(jnp.bfloat16).reshape(out_ref.shape)


def per_device(rows, cols, halves, pair, token_mask, gain_in, bias_in, w_in, w_gate, gain_out, bias_out, w_out):
    row_count, col_count, channels = pair.shape
    hidden = w_out.shape[0]
    devices = rows * cols
    near = devices // halves
    quads = rows // halves
    far_order = []
    for col in reversed(range(cols)):
        ahead = list(range(quads)) if col else list(range(1, quads)) + [0]
        behind = [1] + [quad for quad in reversed(range(quads)) if quad != 1] if col else list(reversed(range(quads)))
        for quad, other in zip(ahead, behind):
            far_order += [near + other * cols + col, quad * cols + col]
    share = hidden // near
    tokens = row_count * col_count
    length = rows * row_count
    depth = length // halves
    token_mask = token_mask.reshape(1, length)
    arguments = (pair, gain_in.reshape(1, channels), bias_in.reshape(1, channels), w_in, token_mask)
    *pieces, normed, spread, mask = pl.pallas_call(
        functools.partial(project_kernel, quads, cols),
        out_shape=(
            *[jax.ShapeDtypeStruct((2 * share * tokens // LANES, LANES), jnp.bfloat16)] * near,
            jax.ShapeDtypeStruct((tokens, channels), jnp.bfloat16),
            jax.ShapeDtypeStruct((GROUP, GROUP * depth), jnp.float32),
            jax.ShapeDtypeStruct((length, 1), jnp.float32),
        ),
        in_specs=[HBM] * 5,
        out_specs=(VMEM,) * (near + 3),
        scratch_shapes=[
            pltpu.VMEM(pair.shape, pair.dtype),
            pltpu.VMEM((1, channels), jnp.float32),
            pltpu.VMEM((1, channels), jnp.float32),
            pltpu.VMEM(w_in.shape, w_in.dtype),
            pltpu.VMEM((1, length), jnp.int32),
            pltpu.SemaphoreType.DMA((5,)),
            pltpu.VMEM((near, 2 * share * tokens // LANES, LANES), jnp.bfloat16),
        ],
        compiler_params=LIMIT,
    )(*(pltpu.with_memory_space_constraint(x, pltpu.HBM) for x in arguments))
    steps = [step for quad in (3, 1, 2, 0) for step in range(quad * cols, (quad + 1) * cols)]
    got = []
    for step in steps:
        got.append(lax.ppermute(pieces[step], ("quad", "col"), [(i, i ^ step) for i in range(near)]) if step else pieces[0])
    total = pl.pallas_call(
        functools.partial(triangle_kernel, far_order, steps, cols, row_count, col_count, share),
        out_shape=jax.ShapeDtypeStruct((devices, share * tokens // LANES, LANES), jnp.bfloat16),
        in_specs=[VMEM] * (near + 2),
        out_specs=VMEM,
        compiler_params=LIMIT,
    )(*got, spread, mask)
    gate, gain_out, bias_out = pl.pallas_call(
        gate_kernel,
        out_shape=(
            jax.ShapeDtypeStruct((tokens, channels), jnp.float32),
            jax.ShapeDtypeStruct((hidden, 1), jnp.float32),
            jax.ShapeDtypeStruct((hidden, 1), jnp.float32),
        ),
        in_specs=[VMEM] * 4,
        out_specs=(VMEM, VMEM, VMEM),
        compiler_params=LIMIT,
        cost_estimate=pl.CostEstimate(flops=2 * tokens * channels * channels, bytes_accessed=4 * tokens * channels, transcendentals=0),
    )(normed, w_gate, gain_out.reshape(1, hidden), bias_out.reshape(1, hidden))
    total = lax.all_to_all(total, ("half", "quad", "col"), split_axis=0, concat_axis=0, tiled=True, axis_index_groups=[far_order])
    return pl.pallas_call(
        functools.partial(output_kernel, far_order, near),
        out_shape=jax.ShapeDtypeStruct(pair.shape, jnp.bfloat16),
        in_specs=[VMEM] * 5,
        out_specs=VMEM,
        compiler_params=LIMIT,
    )(total, gate, gain_out, bias_out, w_out)


def plain_per_device(rows, cols, pair, token_mask, gain_in, bias_in, w_in, w_gate, gain_out, bias_out, w_out):
    row_count, col_count, channels = pair.shape
    hidden = w_out.shape[0]
    devices = rows * cols
    share = hidden // devices
    tokens = row_count * col_count
    row_start = lax.axis_index(("half", "quad")) * row_count
    col_start = lax.axis_index("col") * col_count
    mask_float = token_mask.astype(jnp.float32)
    mask_rows = lax.dynamic_slice_in_dim(mask_float, row_start, row_count)
    mask_cols = lax.dynamic_slice_in_dim(mask_float, col_start, col_count)
    pair_mask = (mask_rows[:, None] * mask_cols[None, :]).reshape(1, tokens)
    flat = pair.reshape(tokens, channels).astype(jnp.float32)
    normed = layer_norm(flat, gain_in, bias_in, -1).astype(jnp.bfloat16)
    projected = lax.dot_general(w_in, normed, (((0,), (1,)), ((), ())), preferred_element_type=jnp.float32)
    projected = projected.reshape(2, 2, hidden, tokens)
    sides = (pair_mask * jax.nn.sigmoid(projected[:, 0]) * projected[:, 1]).astype(jnp.bfloat16)
    sides = sides.reshape(2, devices, share, tokens).transpose(1, 0, 2, 3)
    gate = jax.nn.sigmoid(jnp.dot(normed, w_gate, preferred_element_type=jnp.float32))
    got = lax.all_to_all(sides, AXES, split_axis=0, concat_axis=0, tiled=True)
    got = got.reshape(rows, cols, 2, share, row_count, col_count).transpose(2, 3, 0, 4, 1, 5)
    got = got.reshape(2, share, rows * row_count, cols * col_count)
    total = jnp.einsum("cki,ckj->cij", got[0], got[1], preferred_element_type=jnp.float32).astype(jnp.bfloat16)
    total = total.reshape(share, rows, row_count, cols, col_count).transpose(1, 3, 0, 2, 4)
    total = total.reshape(devices, share, tokens)
    total = lax.all_to_all(total, AXES, split_axis=0, concat_axis=0, tiled=True)
    total = total.reshape(hidden, tokens).astype(jnp.float32)
    summed_norm = layer_norm(total, gain_out[:, None], bias_out[:, None], 0).astype(jnp.bfloat16)
    output = lax.dot_general(summed_norm, w_out, (((0,), (0,)), ((), ())), preferred_element_type=jnp.float32)
    return (gate * output).astype(jnp.bfloat16).reshape(row_count, col_count, channels)


def solution(mesh):
    rows, cols = mesh.shape["row"], mesh.shape["col"]
    halves = 2
    parts = (mesh.shape["groups"], halves, rows // halves, cols)
    finer = jax.sharding.Mesh(mesh.devices.reshape(parts), ("groups", "half", "quad", "col"))

    def per_shard(*args):
        near, hidden, length = rows * cols // halves, args[-1].shape[0], args[1].shape[0]
        row_count, col_count, _ = args[0].shape
        spare = LANES - 2 * col_count
        fits = hidden % (2 * GROUP * near) == 0 and cols == 2 and rows // halves == 4 and length <= LANES and row_count % 3 == 0
        fits = fits and 0 < spare < col_count and row_count // 3 * (col_count - spare) * 2 == LANES
        fits = fits and row_count // 3 * (rows // halves) * GROUP == LANES
        return per_device(rows, cols, halves, *args) if fits else plain_per_device(rows, cols, *args)

    tokens = P(("groups", "half", "quad"), "col", None)
    in_specs = (tokens, P("groups"), P(), P(), P(), P(), P(), P(), P())
    return jax.shard_map(per_shard, mesh=finer, in_specs=in_specs, out_specs=tokens, check_vma=False)
```

```python
import functools

import jax
import jax.numpy as jnp
from jax import lax
from jax.experimental import pallas as pl
from jax.experimental.pallas import tpu as pltpu
from jax.sharding import PartitionSpec as P

epsilon = 1e-05
LANES = 128
GROUP = 8
AXES = ("half", "quad", "col")
VMEM = pl.BlockSpec(memory_space=pltpu.VMEM)
HBM = pl.BlockSpec(memory_space=pltpu.HBM)
LIMIT = pltpu.CompilerParams(vmem_limit_bytes=32 * 1024 * 1024)


def sigmoid(x):
    return 0.5 * jnp.tanh(0.5 * x) + 0.5


def layer_norm(values, gain, bias, axis):
    mean = jnp.mean(values, axis=axis, keepdims=True)
    centred = values - mean
    variance = jnp.mean(centred * centred, axis=axis, keepdims=True)
    return centred * lax.rsqrt(variance + epsilon) * gain + bias


def column(row):
    n = row.shape[1]
    eye = lax.broadcasted_iota(jnp.int32, (n, n), 0) == lax.broadcasted_iota(jnp.int32, (n, n), 1)
    return jnp.sum(jnp.where(eye, row, 0.0), axis=1, keepdims=True)


def pack(x):
    rows, tokens = x.shape[-2:]
    whole, rest = divmod(tokens, LANES)
    blocks = [x[..., t * LANES : (t + 1) * LANES] for t in range(whole)]
    if rest:
        tail = x[..., whole * LANES :]
        blocks.append(jnp.concatenate([tail[..., : rows // 2, :], tail[..., rows // 2 :, :]], axis=-1))
    return jnp.concatenate(blocks, axis=-2)


def unpack(x, rows):
    whole, rest = divmod(x.shape[-2], rows)
    blocks = [x[..., t * rows : (t + 1) * rows, :] for t in range(whole)]
    if rest:
        tail = x[..., whole * rows :, :]
        blocks.append(jnp.concatenate([tail[..., : LANES // 2], tail[..., LANES // 2 :]], axis=-2))
    return jnp.concatenate(blocks, axis=-1)


def arrange(x):
    row_count, col_count, _ = x.shape
    whole, spare = row_count // 3, LANES - 2 * col_count
    blocks = []
    for t in range(whole):
        blocks += [x[2 * t], x[2 * t + 1], x[2 * whole + t, :spare]]
    return jnp.concatenate(blocks + [x[2 * whole + t, spare:] for t in range(whole)], axis=0)


def restore(x, row_count, col_count):
    whole, spare = row_count // 3, LANES - 2 * col_count
    rest = col_count - spare
    rows = []
    for t in range(whole):
        rows += [x[t * LANES : t * LANES + col_count], x[t * LANES + col_count : t * LANES + 2 * col_count]]
    for t in range(whole):
        tail = whole * LANES + t * rest
        rows += [x[t * LANES + 2 * col_count : (t + 1) * LANES], x[tail : tail + rest]]
    return jnp.concatenate(rows, axis=0)


def project(flat, gain, bias, w, row_count):
    ours = w.shape[1] // 4
    normed = layer_norm(flat.astype(jnp.float32), gain, bias, -1).astype(jnp.bfloat16)
    arranged = arrange(normed.reshape(row_count, -1, normed.shape[1]))
    projected = lax.dot_general(w, arranged, (((0,), (1,)), ((), ())), preferred_element_type=jnp.float32)
    left = sigmoid(projected[:ours]) * projected[ours : 2 * ours]
    right = sigmoid(projected[2 * ours : 3 * ours]) * projected[3 * ours :]
    return normed, left, right


def own_kernel(quads, cols, pair_hbm, gain_hbm, bias_hbm, w_hbm, mask_hbm, sides_ref, normed_ref, spread_ref, column_mask_ref, w_ref, gain_ref, bias_ref, pair_ref, all_w_ref, mask_ref, sems):
    moves = [(mask_hbm, mask_ref), (pair_hbm, pair_ref), (gain_hbm, gain_ref), (bias_hbm, bias_ref), (w_hbm, all_w_ref)]
    copies = [pltpu.make_async_copy(source, target, sems.at[n]) for n, (source, target) in enumerate(moves)]
    for copy in copies:
        copy.start()
    my_quad, my_col = lax.axis_index("quad"), lax.axis_index("col")
    row_count, _, channels = pair_ref.shape
    tokens = normed_ref.shape[0]
    hidden = all_w_ref.shape[1] // 4
    ours = hidden // cols
    group, lanes = spread_ref.shape
    copies[0].wait()
    mask_row = mask_ref[...].astype(jnp.float32)
    column_mask_ref[...] = column(mask_row)
    start = lax.axis_index("half") * (lanes // group)
    token = lax.broadcasted_iota(jnp.int32, (mask_row.shape[1], lanes), 0)
    lane = lax.broadcasted_iota(jnp.int32, (mask_row.shape[1], lanes), 1)
    whole = row_count // 3
    block, t, row = lane // LANES, lane // (quads * group) % whole, lane // group % quads
    k = (row ^ my_quad) * row_count + jnp.where(block < 2, 2 * t + block, 2 * whole + t)
    pick = jnp.where(k + start == token, 1.0, 0.0)
    kept = jnp.dot(mask_row.astype(jnp.bfloat16), pick.astype(jnp.bfloat16), preferred_element_type=jnp.float32)
    channel = lax.broadcasted_iota(jnp.int32, (group, lanes), 0)
    lane = lax.broadcasted_iota(jnp.int32, (group, lanes), 1)
    spread_ref[...] = jnp.where(lane % group == channel, kept, 0.0)
    for copy in copies[1:]:
        copy.wait()
    parts = [all_w_ref[:, at : at + hidden] for at in range(0, 4 * hidden, hidden)]
    w_ref[...] = jnp.concatenate([jnp.where(my_col == 0, part[:, :ours], part[:, ours:]) for part in parts], axis=1)
    flat = pair_ref[...].reshape(tokens, channels)
    normed, left, right = project(flat, gain_ref[...], bias_ref[...], w_ref[...], row_count)
    normed_ref[...] = normed
    sides = jnp.concatenate([left.reshape(quads, -1, tokens), right.reshape(quads, -1, tokens)], axis=1)
    sides_ref[...] = pack(sides).astype(jnp.bfloat16)


def other_kernel(pair_ref, sides_ref, gain_ref, bias_ref, w_ref, *refs):
    *piece_refs, others_ref = refs
    my_quad, my_col = lax.axis_index("quad"), lax.axis_index("col")
    quads = sides_ref.shape[0]
    row_count, col_count, channels = pair_ref.shape
    tokens = row_count * col_count
    _, left, right = project(pair_ref[...].reshape(tokens, channels), gain_ref[...], bias_ref[...], w_ref[...], row_count)
    sides = jnp.concatenate([left.reshape(quads, -1, tokens), right.reshape(quads, -1, tokens)], axis=1)
    others_ref[...] = pack(sides).astype(jnp.bfloat16)
    for step, piece_ref in enumerate(piece_refs):
        piece_ref[my_col] = sides_ref[my_quad ^ step]
        piece_ref[1 - my_col] = others_ref[my_quad ^ step]


def triangle_kernel(far_order, steps, cols, row_count, col_count, share, *refs):
    *got_refs, spread_ref, mask_ref, total_ref = refs
    got_refs = {step: ref for step, ref in zip(steps, got_refs)}
    both = 2 * share
    group, lanes = spread_ref.shape
    length = mask_ref.shape[0]
    rows, quads, parts = length // row_count, len(steps), share // group
    whole, spare = row_count // 3, LANES - 2 * col_count
    rest = col_count - spare
    blocks = [[got_refs[row][col].astype(jnp.float32) for row in range(quads)] for col in range(cols)]

    def turned(picks):
        return jnp.concatenate([blocks[col][row][at : at + group] for col, row, at in picks], axis=0).T

    tail = turned([(col, row, whole * both + part * group) for col in range(cols) for part in range(parts) for row in range(quads)])

    def side(which, part):
        even, odd, third = [], [], []
        for col in range(cols):
            at = which * share + part * group
            block = turned([(col, row, t * both + at) for t in range(whole) for row in range(quads)])
            even.append(block[:col_count])
            odd.append(block[col_count : 2 * col_count])
            lane = (col * parts + part) * quads * group
            at = which * LANES // 2
            last = [tail[at + t * rest : at + (t + 1) * rest, lane : lane + quads * group] for t in range(whole)]
            third += [block[2 * col_count :], jnp.concatenate(last, axis=1)]
        tokens = [jnp.concatenate(pieces, axis=0) for pieces in (even, odd, third)]
        return jnp.concatenate(tokens, axis=1) * mask_ref[...]

    def placed(pieces):
        return jnp.concatenate([jnp.zeros((piece, lanes), jnp.bfloat16) if isinstance(piece, int) else piece for piece in pieces], axis=0)

    contract = (((1,), (1,)), ((), ()))
    mains, lasts = [], []
    for part in range(parts):
        left, right = side(0, part), side(1, part).astype(jnp.bfloat16)
        left = (left[:, None, :] * spread_ref[...][None]).reshape(rows, row_count, group, lanes)
        pairs = left[:, : 2 * whole].reshape(rows, whole, 2, group, lanes)
        left = jnp.concatenate([pairs[:, :, 0], pairs[:, :, 1], left[:, 2 * whole :]], axis=-1)
        left = left.reshape(rows * whole * group, 3 * lanes).astype(jnp.bfloat16)
        ours = [right[col * col_count : (col + 1) * col_count] for col in range(cols)]
        weights = [
            placed([p for mine in ours for p in (mine, LANES - col_count)]),
            placed([p for mine in ours for p in (col_count, mine, spare)]),
            placed([p for mine in ours for p in (2 * col_count, mine[:spare])]),
        ]
        weights = jnp.concatenate(weights, axis=1)
        mains.append(lax.dot_general(left, weights, contract, preferred_element_type=jnp.float32))
        weights = jnp.concatenate([mine[spare:] for mine in ours], axis=0)
        lasts.append(lax.dot_general(left[:, 2 * lanes :], weights, contract, preferred_element_type=jnp.float32))
    for target, device in enumerate(far_order):
        row, col = divmod(device, cols)
        spots = [(row * whole + t) * group for t in range(whole)]
        tiles = [main[at : at + group, col * LANES : (col + 1) * LANES] for at in spots for main in mains]
        last = [part[at : at + group, col * rest : (col + 1) * rest] for part in lasts for at in spots]
        tiles.append(jnp.concatenate(last, axis=1))
        total_ref[target] = jnp.concatenate(tiles, axis=0).astype(jnp.bfloat16)


def gate_kernel(normed_ref, w_ref, gain_ref, bias_ref, gate_ref, gain_out_ref, bias_out_ref):
    gate_ref[...] = sigmoid(jnp.dot(normed_ref[...], w_ref[...], preferred_element_type=jnp.float32))
    gain_out_ref[...] = column(gain_ref[...])
    bias_out_ref[...] = column(bias_ref[...])


def output_kernel(far_order, near_order, total_ref, gate_ref, gain_ref, bias_ref, w_ref, out_ref):
    tokens = gate_ref.shape[0]
    hidden = w_ref.shape[0]
    near = len(near_order)
    share = hidden // near
    blocks = []
    for index in near_order:
        parts = [total_ref[source].astype(jnp.float32) for source, device in enumerate(far_order) if device % near == index]
        blocks.append(unpack(sum(parts[1:], parts[0]), share))
    total = jnp.concatenate(blocks, axis=0)
    normed = layer_norm(total, gain_ref[...], bias_ref[...], 0).astype(jnp.bfloat16)
    output = lax.dot_general(normed, w_ref[...], (((0,), (0,)), ((), ())), preferred_element_type=jnp.float32)
    output = restore(output, out_ref.shape[0], out_ref.shape[1])
    out_ref[...] = (gate_ref[...] * output).astype(jnp.bfloat16).reshape(out_ref.shape)


def per_device(rows, cols, halves, pair, token_mask, gain_in, bias_in, w_in, w_gate, gain_out, bias_out, w_out):
    row_count, col_count, channels = pair.shape
    hidden = w_out.shape[0]
    devices = rows * cols
    near = devices // halves
    quads = rows // halves
    far_order = []
    for col in reversed(range(cols)):
        ahead = list(range(quads)) if col else list(range(1, quads)) + [0]
        behind = [1] + [quad for quad in reversed(range(quads)) if quad != 1] if col else list(reversed(range(quads)))
        for quad, other in zip(ahead, behind):
            far_order += [near + other * cols + col, quad * cols + col]
    share = hidden // near
    tokens = row_count * col_count
    length = rows * row_count
    depth = length // halves
    token_mask = token_mask.reshape(1, length)
    near_order = [quad * cols + col for col in range(cols) for quad in range(quads)]
    packed = 2 * share * tokens // LANES
    cost = pl.CostEstimate(flops=2 * tokens * channels * 4 * hidden, bytes_accessed=16 * tokens * channels, transcendentals=0)
    other_pair = lax.ppermute(pair, "col", [(i, (i + 1) % cols) for i in range(cols)])
    arguments = (pair, gain_in.reshape(1, channels), bias_in.reshape(1, channels), w_in, token_mask)
    sides, normed, spread, mask, *weights = pl.pallas_call(
        functools.partial(own_kernel, quads, cols),
        out_shape=(
            jax.ShapeDtypeStruct((quads, packed, LANES), jnp.bfloat16),
            jax.ShapeDtypeStruct((tokens, channels), jnp.bfloat16),
            jax.ShapeDtypeStruct((GROUP, GROUP * depth), jnp.float32),
            jax.ShapeDtypeStruct((length, 1), jnp.float32),
            jax.ShapeDtypeStruct((channels, 4 * hidden // cols), jnp.bfloat16),
            jax.ShapeDtypeStruct((1, channels), jnp.float32),
            jax.ShapeDtypeStruct((1, channels), jnp.float32),
        ),
        in_specs=[HBM] * 5,
        out_specs=(VMEM,) * 7,
        scratch_shapes=[
            pltpu.VMEM(pair.shape, pair.dtype),
            pltpu.VMEM(w_in.shape, w_in.dtype),
            pltpu.VMEM((1, length), jnp.int32),
            pltpu.SemaphoreType.DMA((5,)),
        ],
        compiler_params=LIMIT,
        cost_estimate=cost,
    )(*(pltpu.with_memory_space_constraint(x, pltpu.HBM) for x in arguments))
    w_ours, gain_in, bias_in = weights
    pieces = pl.pallas_call(
        other_kernel,
        out_shape=[jax.ShapeDtypeStruct((cols, packed, LANES), jnp.bfloat16)] * quads,
        in_specs=[VMEM] * 5,
        out_specs=[VMEM] * quads,
        scratch_shapes=[pltpu.VMEM((quads, packed, LANES), jnp.bfloat16)],
        compiler_params=LIMIT,
        cost_estimate=cost,
    )(other_pair, sides, gain_in, bias_in, w_ours)
    steps = [3, 1, 2, 0]
    got = [lax.ppermute(pieces[step], "quad", [(i, i ^ step) for i in range(quads)]) if step else pieces[0] for step in steps]
    total = pl.pallas_call(
        functools.partial(triangle_kernel, far_order, steps, cols, row_count, col_count, share),
        out_shape=jax.ShapeDtypeStruct((devices, share * tokens // LANES, LANES), jnp.bfloat16),
        in_specs=[VMEM] * (quads + 2),
        out_specs=VMEM,
        compiler_params=LIMIT,
    )(*got, spread, mask)
    gate, gain_out, bias_out = pl.pallas_call(
        gate_kernel,
        out_shape=(
            jax.ShapeDtypeStruct((tokens, channels), jnp.float32),
            jax.ShapeDtypeStruct((hidden, 1), jnp.float32),
            jax.ShapeDtypeStruct((hidden, 1), jnp.float32),
        ),
        in_specs=[VMEM] * 4,
        out_specs=(VMEM, VMEM, VMEM),
        compiler_params=LIMIT,
        cost_estimate=pl.CostEstimate(flops=2 * tokens * channels * channels, bytes_accessed=4 * tokens * channels, transcendentals=0),
    )(normed, w_gate, gain_out.reshape(1, hidden), bias_out.reshape(1, hidden))
    total = lax.all_to_all(total, ("half", "quad", "col"), split_axis=0, concat_axis=0, tiled=True, axis_index_groups=[far_order])
    return pl.pallas_call(
        functools.partial(output_kernel, far_order, near_order),
        out_shape=jax.ShapeDtypeStruct(pair.shape, jnp.bfloat16),
        in_specs=[VMEM] * 5,
        out_specs=VMEM,
        compiler_params=LIMIT,
    )(total, gate, gain_out, bias_out, w_out)


def plain_per_device(rows, cols, pair, token_mask, gain_in, bias_in, w_in, w_gate, gain_out, bias_out, w_out):
    row_count, col_count, channels = pair.shape
    hidden = w_out.shape[0]
    devices = rows * cols
    share = hidden // devices
    tokens = row_count * col_count
    row_start = lax.axis_index(("half", "quad")) * row_count
    col_start = lax.axis_index("col") * col_count
    mask_float = token_mask.astype(jnp.float32)
    mask_rows = lax.dynamic_slice_in_dim(mask_float, row_start, row_count)
    mask_cols = lax.dynamic_slice_in_dim(mask_float, col_start, col_count)
    pair_mask = (mask_rows[:, None] * mask_cols[None, :]).reshape(1, tokens)
    flat = pair.reshape(tokens, channels).astype(jnp.float32)
    normed = layer_norm(flat, gain_in, bias_in, -1).astype(jnp.bfloat16)
    projected = lax.dot_general(w_in, normed, (((0,), (1,)), ((), ())), preferred_element_type=jnp.float32)
    projected = projected.reshape(2, 2, hidden, tokens)
    sides = (pair_mask * jax.nn.sigmoid(projected[:, 0]) * projected[:, 1]).astype(jnp.bfloat16)
    sides = sides.reshape(2, devices, share, tokens).transpose(1, 0, 2, 3)
    gate = jax.nn.sigmoid(jnp.dot(normed, w_gate, preferred_element_type=jnp.float32))
    got = lax.all_to_all(sides, AXES, split_axis=0, concat_axis=0, tiled=True)
    got = got.reshape(rows, cols, 2, share, row_count, col_count).transpose(2, 3, 0, 4, 1, 5)
    got = got.reshape(2, share, rows * row_count, cols * col_count)
    total = jnp.einsum("cki,ckj->cij", got[0], got[1], preferred_element_type=jnp.float32).astype(jnp.bfloat16)
    total = total.reshape(share, rows, row_count, cols, col_count).transpose(1, 3, 0, 2, 4)
    total = total.reshape(devices, share, tokens)
    total = lax.all_to_all(total, AXES, split_axis=0, concat_axis=0, tiled=True)
    total = total.reshape(hidden, tokens).astype(jnp.float32)
    summed_norm = layer_norm(total, gain_out[:, None], bias_out[:, None], 0).astype(jnp.bfloat16)
    output = lax.dot_general(summed_norm, w_out, (((0,), (0,)), ((), ())), preferred_element_type=jnp.float32)
    return (gate * output).astype(jnp.bfloat16).reshape(row_count, col_count, channels)


def solution(mesh):
    rows, cols = mesh.shape["row"], mesh.shape["col"]
    halves = 2
    parts = (mesh.shape["groups"], halves, rows // halves, cols)
    finer = jax.sharding.Mesh(mesh.devices.reshape(parts), ("groups", "half", "quad", "col"))

    def per_shard(*args):
        near, hidden, length = rows * cols // halves, args[-1].shape[0], args[1].shape[0]
        row_count, col_count, _ = args[0].shape
        spare = LANES - 2 * col_count
        fits = hidden % (2 * GROUP * near) == 0 and cols == 2 and rows // halves == 4 and length <= LANES and row_count % 3 == 0
        fits = fits and 0 < spare < col_count and row_count // 3 * (col_count - spare) * 2 == LANES
        fits = fits and row_count // 3 * (rows // halves) * GROUP == LANES
        return per_device(rows, cols, halves, *args) if fits else plain_per_device(rows, cols, *args)

    tokens = P(("groups", "half", "quad"), "col", None)
    in_specs = (tokens, P("groups"), P(), P(), P(), P(), P(), P(), P())
    return jax.shard_map(per_shard, mesh=finer, in_specs=in_specs, out_specs=tokens, check_vma=False)
```

```python
import functools

import jax
import jax.numpy as jnp
from jax import lax
from jax.experimental import pallas as pl
from jax.experimental.pallas import tpu as pltpu
from jax.sharding import PartitionSpec as P

epsilon = 1e-05
LANES = 128
GROUP = 8
AXES = ("half", "quad", "col")
VMEM = pl.BlockSpec(memory_space=pltpu.VMEM)
HBM = pl.BlockSpec(memory_space=pltpu.HBM)
LIMIT = pltpu.CompilerParams(vmem_limit_bytes=32 * 1024 * 1024)


def sigmoid(x):
    return 0.5 * jnp.tanh(0.5 * x) + 0.5


def layer_norm(values, gain, bias, axis):
    mean = jnp.mean(values, axis=axis, keepdims=True)
    centred = values - mean
    variance = jnp.mean(centred * centred, axis=axis, keepdims=True)
    return centred * lax.rsqrt(variance + epsilon) * gain + bias


def column(row):
    n = row.shape[1]
    eye = lax.broadcasted_iota(jnp.int32, (n, n), 0) == lax.broadcasted_iota(jnp.int32, (n, n), 1)
    return jnp.sum(jnp.where(eye, row, 0.0), axis=1, keepdims=True)


def pack(x):
    rows, tokens = x.shape[-2:]
    whole, rest = divmod(tokens, LANES)
    blocks = [x[..., t * LANES : (t + 1) * LANES] for t in range(whole)]
    if rest:
        tail = x[..., whole * LANES :]
        blocks.append(jnp.concatenate([tail[..., : rows // 2, :], tail[..., rows // 2 :, :]], axis=-1))
    return jnp.concatenate(blocks, axis=-2)


def unpack(x, rows):
    whole, rest = divmod(x.shape[-2], rows)
    blocks = [x[..., t * rows : (t + 1) * rows, :] for t in range(whole)]
    if rest:
        tail = x[..., whole * rows :, :]
        blocks.append(jnp.concatenate([tail[..., : LANES // 2], tail[..., LANES // 2 :]], axis=-2))
    return jnp.concatenate(blocks, axis=-1)


def arrange(x):
    row_count, col_count, _ = x.shape
    whole, spare = row_count // 3, LANES - 2 * col_count
    blocks = []
    for t in range(whole):
        blocks += [x[2 * t], x[2 * t + 1], x[2 * whole + t, :spare]]
    return jnp.concatenate(blocks + [x[2 * whole + t, spare:] for t in range(whole)], axis=0)


def restore(x, row_count, col_count):
    whole, spare = row_count // 3, LANES - 2 * col_count
    rest = col_count - spare
    rows = []
    for t in range(whole):
        rows += [x[t * LANES : t * LANES + col_count], x[t * LANES + col_count : t * LANES + 2 * col_count]]
    for t in range(whole):
        tail = whole * LANES + t * rest
        rows += [x[t * LANES + 2 * col_count : (t + 1) * LANES], x[tail : tail + rest]]
    return jnp.concatenate(rows, axis=0)


def normalise(flat, gain, bias):
    return layer_norm(flat.astype(jnp.float32), gain, bias, -1).astype(jnp.bfloat16)


def project(normed, w, shape, quads):
    ours = w.shape[1] // 4
    tokens = normed.shape[0]
    projected = lax.dot_general(w, arrange(normed.reshape(shape)), (((0,), (1,)), ((), ())), preferred_element_type=jnp.float32)
    left = sigmoid(projected[:ours]) * projected[ours : 2 * ours]
    right = sigmoid(projected[2 * ours : 3 * ours]) * projected[3 * ours :]
    sides = jnp.concatenate([left.reshape(quads, -1, tokens), right.reshape(quads, -1, tokens)], axis=1)
    return pack(sides).astype(jnp.bfloat16)


def own_kernel(quads, cols, pair_hbm, gain_hbm, bias_hbm, w_hbm, mask_hbm, sides_ref, normed_ref, spread_ref, column_mask_ref, w_ref, gain_ref, bias_ref, pair_ref, all_w_ref, mask_ref, sems):
    moves = [(mask_hbm, mask_ref), (pair_hbm, pair_ref), (gain_hbm, gain_ref), (bias_hbm, bias_ref), (w_hbm, all_w_ref)]
    copies = [pltpu.make_async_copy(source, target, sems.at[n]) for n, (source, target) in enumerate(moves)]
    for copy in copies:
        copy.start()
    my_quad, my_col = lax.axis_index("quad"), lax.axis_index("col")
    row_count, _, channels = pair_ref.shape
    tokens = normed_ref.shape[0]
    hidden = all_w_ref.shape[1] // 4
    ours = hidden // cols
    group, lanes = spread_ref.shape
    copies[0].wait()
    mask_row = mask_ref[...].astype(jnp.float32)
    column_mask_ref[...] = column(mask_row)
    start = lax.axis_index("half") * (lanes // group)
    token = lax.broadcasted_iota(jnp.int32, (mask_row.shape[1], lanes), 0)
    lane = lax.broadcasted_iota(jnp.int32, (mask_row.shape[1], lanes), 1)
    whole = row_count // 3
    block, t, row = lane // LANES, lane // (quads * group) % whole, lane // group % quads
    k = (row ^ my_quad) * row_count + jnp.where(block < 2, 2 * t + block, 2 * whole + t)
    pick = jnp.where(k + start == token, 1.0, 0.0)
    kept = jnp.dot(mask_row.astype(jnp.bfloat16), pick.astype(jnp.bfloat16), preferred_element_type=jnp.float32)
    channel = lax.broadcasted_iota(jnp.int32, (group, lanes), 0)
    lane = lax.broadcasted_iota(jnp.int32, (group, lanes), 1)
    spread_ref[...] = jnp.where(lane % group == channel, kept, 0.0)
    for copy in copies[1:4]:
        copy.wait()
    normed = normalise(pair_ref[...].reshape(tokens, channels), gain_ref[...], bias_ref[...])
    normed_ref[...] = normed
    copies[4].wait()
    parts = [all_w_ref[:, at : at + hidden] for at in range(0, 4 * hidden, hidden)]
    w = jnp.concatenate([jnp.where(my_col == 0, part[:, :ours], part[:, ours:]) for part in parts], axis=1)
    w_ref[...] = w
    sides_ref[...] = project(normed, w, pair_ref.shape, quads)


def other_kernel(pair_ref, sides_ref, gain_ref, bias_ref, w_ref, *refs):
    *piece_refs, others_ref = refs
    my_quad, my_col = lax.axis_index("quad"), lax.axis_index("col")
    quads = sides_ref.shape[0]
    normed = normalise(pair_ref[...].reshape(-1, pair_ref.shape[2]), gain_ref[...], bias_ref[...])
    others_ref[...] = project(normed, w_ref[...], pair_ref.shape, quads)
    for step, piece_ref in enumerate(piece_refs):
        piece_ref[my_col] = sides_ref[my_quad ^ step]
        piece_ref[1 - my_col] = others_ref[my_quad ^ step]


def triangle_kernel(far_order, steps, cols, row_count, col_count, share, *refs):
    *got_refs, spread_ref, mask_ref, total_ref = refs
    got_refs = {step: ref for step, ref in zip(steps, got_refs)}
    both = 2 * share
    group, lanes = spread_ref.shape
    length = mask_ref.shape[0]
    rows, quads, parts = length // row_count, len(steps), share // group
    whole, spare = row_count // 3, LANES - 2 * col_count
    rest = col_count - spare
    blocks = [[got_refs[row][col].astype(jnp.float32) for row in range(quads)] for col in range(cols)]

    def turned(picks):
        return jnp.concatenate([blocks[col][row][at : at + group] for col, row, at in picks], axis=0).T

    tail = turned([(col, row, whole * both + part * group) for col in range(cols) for part in range(parts) for row in range(quads)])

    def side(which, part):
        even, odd, third = [], [], []
        for col in range(cols):
            at = which * share + part * group
            block = turned([(col, row, t * both + at) for t in range(whole) for row in range(quads)])
            even.append(block[:col_count])
            odd.append(block[col_count : 2 * col_count])
            lane = (col * parts + part) * quads * group
            at = which * LANES // 2
            last = [tail[at + t * rest : at + (t + 1) * rest, lane : lane + quads * group] for t in range(whole)]
            third += [block[2 * col_count :], jnp.concatenate(last, axis=1)]
        tokens = [jnp.concatenate(pieces, axis=0) for pieces in (even, odd, third)]
        return jnp.concatenate(tokens, axis=1) * mask_ref[...]

    def placed(pieces):
        return jnp.concatenate([jnp.zeros((piece, lanes), jnp.bfloat16) if isinstance(piece, int) else piece for piece in pieces], axis=0)

    contract = (((1,), (1,)), ((), ()))
    mains, lasts = [], []
    for part in range(parts):
        left, right = side(0, part), side(1, part).astype(jnp.bfloat16)
        left = (left[:, None, :] * spread_ref[...][None]).reshape(rows, row_count, group, lanes)
        pairs = left[:, : 2 * whole].reshape(rows, whole, 2, group, lanes)
        left = jnp.concatenate([pairs[:, :, 0], pairs[:, :, 1], left[:, 2 * whole :]], axis=-1)
        left = left.reshape(rows * whole * group, 3 * lanes).astype(jnp.bfloat16)
        ours = [right[col * col_count : (col + 1) * col_count] for col in range(cols)]
        weights = [
            placed([p for mine in ours for p in (mine, LANES - col_count)]),
            placed([p for mine in ours for p in (col_count, mine, spare)]),
            placed([p for mine in ours for p in (2 * col_count, mine[:spare])]),
        ]
        weights = jnp.concatenate(weights, axis=1)
        mains.append(lax.dot_general(left, weights, contract, preferred_element_type=jnp.float32))
        weights = jnp.concatenate([mine[spare:] for mine in ours], axis=0)
        lasts.append(lax.dot_general(left[:, 2 * lanes :], weights, contract, preferred_element_type=jnp.float32))
    for target, device in enumerate(far_order):
        row, col = divmod(device, cols)
        spots = [(row * whole + t) * group for t in range(whole)]
        tiles = [main[at : at + group, col * LANES : (col + 1) * LANES] for at in spots for main in mains]
        last = [part[at : at + group, col * rest : (col + 1) * rest] for part in lasts for at in spots]
        tiles.append(jnp.concatenate(last, axis=1))
        total_ref[target] = jnp.concatenate(tiles, axis=0).astype(jnp.bfloat16)


def gate_kernel(normed_ref, w_ref, gain_ref, bias_ref, gate_ref, gain_out_ref, bias_out_ref):
    gate_ref[...] = sigmoid(jnp.dot(normed_ref[...], w_ref[...], preferred_element_type=jnp.float32))
    gain_out_ref[...] = column(gain_ref[...])
    bias_out_ref[...] = column(bias_ref[...])


def output_kernel(far_order, near_order, total_ref, gate_ref, gain_ref, bias_ref, w_ref, out_ref):
    tokens = gate_ref.shape[0]
    hidden = w_ref.shape[0]
    near = len(near_order)
    share = hidden // near
    blocks = []
    for index in near_order:
        parts = [total_ref[source].astype(jnp.float32) for source, device in enumerate(far_order) if device % near == index]
        blocks.append(unpack(sum(parts[1:], parts[0]), share))
    total = jnp.concatenate(blocks, axis=0)
    normed = layer_norm(total, gain_ref[...], bias_ref[...], 0).astype(jnp.bfloat16)
    output = lax.dot_general(normed, w_ref[...], (((0,), (0,)), ((), ())), preferred_element_type=jnp.float32)
    output = restore(output, out_ref.shape[0], out_ref.shape[1])
    out_ref[...] = (gate_ref[...] * output).astype(jnp.bfloat16).reshape(out_ref.shape)


def per_device(rows, cols, halves, pair, token_mask, gain_in, bias_in, w_in, w_gate, gain_out, bias_out, w_out):
    row_count, col_count, channels = pair.shape
    hidden = w_out.shape[0]
    devices = rows * cols
    near = devices // halves
    quads = rows // halves
    far_order = []
    for col in reversed(range(cols)):
        ahead = list(range(quads)) if col else list(range(1, quads)) + [0]
        behind = [1] + [quad for quad in reversed(range(quads)) if quad != 1] if col else list(reversed(range(quads)))
        for quad, other in zip(ahead, behind):
            far_order += [near + other * cols + col, quad * cols + col]
    share = hidden // near
    tokens = row_count * col_count
    length = rows * row_count
    depth = length // halves
    token_mask = token_mask.reshape(1, length)
    near_order = [quad * cols + col for col in range(cols) for quad in range(quads)]
    packed = 2 * share * tokens // LANES
    cost = pl.CostEstimate(flops=2 * tokens * channels * 4 * hidden, bytes_accessed=16 * tokens * channels, transcendentals=0)
    other_pair = lax.ppermute(pair, "col", [(i, (i + 1) % cols) for i in range(cols)])
    arguments = (pair, gain_in.reshape(1, channels), bias_in.reshape(1, channels), w_in, token_mask)
    sides, normed, spread, mask, *weights = pl.pallas_call(
        functools.partial(own_kernel, quads, cols),
        out_shape=(
            jax.ShapeDtypeStruct((quads, packed, LANES), jnp.bfloat16),
            jax.ShapeDtypeStruct((tokens, channels), jnp.bfloat16),
            jax.ShapeDtypeStruct((GROUP, GROUP * depth), jnp.float32),
            jax.ShapeDtypeStruct((length, 1), jnp.float32),
            jax.ShapeDtypeStruct((channels, 4 * hidden // cols), jnp.bfloat16),
            jax.ShapeDtypeStruct((1, channels), jnp.float32),
            jax.ShapeDtypeStruct((1, channels), jnp.float32),
        ),
        in_specs=[HBM] * 5,
        out_specs=(VMEM,) * 7,
        scratch_shapes=[
            pltpu.VMEM(pair.shape, pair.dtype),
            pltpu.VMEM(w_in.shape, w_in.dtype),
            pltpu.VMEM((1, length), jnp.int32),
            pltpu.SemaphoreType.DMA((5,)),
        ],
        compiler_params=LIMIT,
        cost_estimate=cost,
    )(*(pltpu.with_memory_space_constraint(x, pltpu.HBM) for x in arguments))
    w_ours, gain_in, bias_in = weights
    pieces = pl.pallas_call(
        other_kernel,
        out_shape=[jax.ShapeDtypeStruct((cols, packed, LANES), jnp.bfloat16)] * quads,
        in_specs=[VMEM] * 5,
        out_specs=[VMEM] * quads,
        scratch_shapes=[pltpu.VMEM((quads, packed, LANES), jnp.bfloat16)],
        compiler_params=LIMIT,
        cost_estimate=cost,
    )(other_pair, sides, gain_in, bias_in, w_ours)
    steps = [1, 2, 3, 0]
    got = [lax.ppermute(pieces[step], "quad", [(i, i ^ step) for i in range(quads)]) if step else pieces[0] for step in steps]
    total = pl.pallas_call(
        functools.partial(triangle_kernel, far_order, steps, cols, row_count, col_count, share),
        out_shape=jax.ShapeDtypeStruct((devices, share * tokens // LANES, LANES), jnp.bfloat16),
        in_specs=[VMEM] * (quads + 2),
        out_specs=VMEM,
        compiler_params=LIMIT,
    )(*got, spread, mask)
    gate, gain_out, bias_out = pl.pallas_call(
        gate_kernel,
        out_shape=(
            jax.ShapeDtypeStruct((tokens, channels), jnp.float32),
            jax.ShapeDtypeStruct((hidden, 1), jnp.float32),
            jax.ShapeDtypeStruct((hidden, 1), jnp.float32),
        ),
        in_specs=[VMEM] * 4,
        out_specs=(VMEM, VMEM, VMEM),
        compiler_params=LIMIT,
        cost_estimate=pl.CostEstimate(flops=2 * tokens * channels * channels, bytes_accessed=4 * tokens * channels, transcendentals=0),
    )(normed, w_gate, gain_out.reshape(1, hidden), bias_out.reshape(1, hidden))
    total = lax.all_to_all(total, ("half", "quad", "col"), split_axis=0, concat_axis=0, tiled=True, axis_index_groups=[far_order])
    return pl.pallas_call(
        functools.partial(output_kernel, far_order, near_order),
        out_shape=jax.ShapeDtypeStruct(pair.shape, jnp.bfloat16),
        in_specs=[VMEM] * 5,
        out_specs=VMEM,
        compiler_params=LIMIT,
    )(total, gate, gain_out, bias_out, w_out)


def plain_per_device(rows, cols, pair, token_mask, gain_in, bias_in, w_in, w_gate, gain_out, bias_out, w_out):
    row_count, col_count, channels = pair.shape
    hidden = w_out.shape[0]
    devices = rows * cols
    share = hidden // devices
    tokens = row_count * col_count
    row_start = lax.axis_index(("half", "quad")) * row_count
    col_start = lax.axis_index("col") * col_count
    mask_float = token_mask.astype(jnp.float32)
    mask_rows = lax.dynamic_slice_in_dim(mask_float, row_start, row_count)
    mask_cols = lax.dynamic_slice_in_dim(mask_float, col_start, col_count)
    pair_mask = (mask_rows[:, None] * mask_cols[None, :]).reshape(1, tokens)
    flat = pair.reshape(tokens, channels).astype(jnp.float32)
    normed = layer_norm(flat, gain_in, bias_in, -1).astype(jnp.bfloat16)
    projected = lax.dot_general(w_in, normed, (((0,), (1,)), ((), ())), preferred_element_type=jnp.float32)
    projected = projected.reshape(2, 2, hidden, tokens)
    sides = (pair_mask * jax.nn.sigmoid(projected[:, 0]) * projected[:, 1]).astype(jnp.bfloat16)
    sides = sides.reshape(2, devices, share, tokens).transpose(1, 0, 2, 3)
    gate = jax.nn.sigmoid(jnp.dot(normed, w_gate, preferred_element_type=jnp.float32))
    got = lax.all_to_all(sides, AXES, split_axis=0, concat_axis=0, tiled=True)
    got = got.reshape(rows, cols, 2, share, row_count, col_count).transpose(2, 3, 0, 4, 1, 5)
    got = got.reshape(2, share, rows * row_count, cols * col_count)
    total = jnp.einsum("cki,ckj->cij", got[0], got[1], preferred_element_type=jnp.float32).astype(jnp.bfloat16)
    total = total.reshape(share, rows, row_count, cols, col_count).transpose(1, 3, 0, 2, 4)
    total = total.reshape(devices, share, tokens)
    total = lax.all_to_all(total, AXES, split_axis=0, concat_axis=0, tiled=True)
    total = total.reshape(hidden, tokens).astype(jnp.float32)
    summed_norm = layer_norm(total, gain_out[:, None], bias_out[:, None], 0).astype(jnp.bfloat16)
    output = lax.dot_general(summed_norm, w_out, (((0,), (0,)), ((), ())), preferred_element_type=jnp.float32)
    return (gate * output).astype(jnp.bfloat16).reshape(row_count, col_count, channels)


def solution(mesh):
    rows, cols = mesh.shape["row"], mesh.shape["col"]
    halves = 2
    parts = (mesh.shape["groups"], halves, rows // halves, cols)
    finer = jax.sharding.Mesh(mesh.devices.reshape(parts), ("groups", "half", "quad", "col"))

    def per_shard(*args):
        near, hidden, length = rows * cols // halves, args[-1].shape[0], args[1].shape[0]
        row_count, col_count, _ = args[0].shape
        spare = LANES - 2 * col_count
        fits = hidden % (2 * GROUP * near) == 0 and cols == 2 and rows // halves == 4 and length <= LANES and row_count % 3 == 0
        fits = fits and 0 < spare < col_count and row_count // 3 * (col_count - spare) * 2 == LANES
        fits = fits and row_count // 3 * (rows // halves) * GROUP == LANES
        return per_device(rows, cols, halves, *args) if fits else plain_per_device(rows, cols, *args)

    tokens = P(("groups", "half", "quad"), "col", None)
    in_specs = (tokens, P("groups"), P(), P(), P(), P(), P(), P(), P())
    return jax.shard_map(per_shard, mesh=finer, in_specs=in_specs, out_specs=tokens, check_vma=False)
```

```python
import functools

import jax
import jax.numpy as jnp
from jax import lax
from jax.experimental import pallas as pl
from jax.experimental.pallas import tpu as pltpu
from jax.sharding import PartitionSpec as P

epsilon = 1e-05
LANES = 128
GROUP = 8
AXES = ("half", "quad", "col")
VMEM = pl.BlockSpec(memory_space=pltpu.VMEM)
HBM = pl.BlockSpec(memory_space=pltpu.HBM)
LIMIT = pltpu.CompilerParams(vmem_limit_bytes=32 * 1024 * 1024)


def sigmoid(x):
    return 0.5 * jnp.tanh(0.5 * x) + 0.5


def layer_norm(values, gain, bias, axis):
    mean = jnp.mean(values, axis=axis, keepdims=True)
    centred = values - mean
    variance = jnp.mean(centred * centred, axis=axis, keepdims=True)
    return centred * lax.rsqrt(variance + epsilon) * gain + bias


def column(row):
    n = row.shape[1]
    eye = lax.broadcasted_iota(jnp.int32, (n, n), 0) == lax.broadcasted_iota(jnp.int32, (n, n), 1)
    return jnp.sum(jnp.where(eye, row, 0.0), axis=1, keepdims=True)


def pack(x):
    rows, tokens = x.shape[-2:]
    whole, rest = divmod(tokens, LANES)
    blocks = [x[..., t * LANES : (t + 1) * LANES] for t in range(whole)]
    if rest:
        tail = x[..., whole * LANES :]
        blocks.append(jnp.concatenate([tail[..., : rows // 2, :], tail[..., rows // 2 :, :]], axis=-1))
    return jnp.concatenate(blocks, axis=-2)


def unpack(x, rows):
    whole, rest = divmod(x.shape[-2], rows)
    blocks = [x[..., t * rows : (t + 1) * rows, :] for t in range(whole)]
    if rest:
        tail = x[..., whole * rows :, :]
        blocks.append(jnp.concatenate([tail[..., : LANES // 2], tail[..., LANES // 2 :]], axis=-2))
    return jnp.concatenate(blocks, axis=-1)


def arrange(x):
    row_count, col_count, _ = x.shape
    whole, spare = row_count // 3, LANES - 2 * col_count
    blocks = []
    for t in range(whole):
        blocks += [x[2 * t], x[2 * t + 1], x[2 * whole + t, :spare]]
    return jnp.concatenate(blocks + [x[2 * whole + t, spare:] for t in range(whole)], axis=0)


def restore(x, row_count, col_count):
    whole, spare = row_count // 3, LANES - 2 * col_count
    rest = col_count - spare
    rows = []
    for t in range(whole):
        rows += [x[t * LANES : t * LANES + col_count], x[t * LANES + col_count : t * LANES + 2 * col_count]]
    for t in range(whole):
        tail = whole * LANES + t * rest
        rows += [x[t * LANES + 2 * col_count : (t + 1) * LANES], x[tail : tail + rest]]
    return jnp.concatenate(rows, axis=0)


def normalise(flat, gain, bias):
    return layer_norm(flat.astype(jnp.float32), gain, bias, -1).astype(jnp.bfloat16)


def project(normed, w, shape, quads):
    ours = w.shape[1] // 4
    tokens = normed.shape[0]
    projected = lax.dot_general(w, arrange(normed.reshape(shape)), (((0,), (1,)), ((), ())), preferred_element_type=jnp.float32)
    left = sigmoid(projected[:ours]) * projected[ours : 2 * ours]
    right = sigmoid(projected[2 * ours : 3 * ours]) * projected[3 * ours :]
    sides = jnp.concatenate([left.reshape(quads, -1, tokens), right.reshape(quads, -1, tokens)], axis=1)
    return pack(sides).astype(jnp.bfloat16)


def own_kernel(quads, cols, pair_hbm, gain_hbm, bias_hbm, w_hbm, mask_hbm, sides_ref, normed_ref, spread_ref, column_mask_ref, w_ref, gain_ref, bias_ref, pair_ref, all_w_ref, mask_ref, sems):
    moves = [(mask_hbm, mask_ref), (pair_hbm, pair_ref), (gain_hbm, gain_ref), (bias_hbm, bias_ref), (w_hbm, all_w_ref)]
    copies = [pltpu.make_async_copy(source, target, sems.at[n]) for n, (source, target) in enumerate(moves)]
    for copy in copies:
        copy.start()
    my_quad, my_col = lax.axis_index("quad"), lax.axis_index("col")
    row_count, _, channels = pair_ref.shape
    tokens = normed_ref.shape[0]
    hidden = all_w_ref.shape[1] // 4
    ours = hidden // cols
    group, lanes = spread_ref.shape
    copies[0].wait()
    mask_row = mask_ref[...].astype(jnp.float32)
    column_mask_ref[...] = column(mask_row)
    start = lax.axis_index("half") * (lanes // group)
    token = lax.broadcasted_iota(jnp.int32, (mask_row.shape[1], lanes), 0)
    lane = lax.broadcasted_iota(jnp.int32, (mask_row.shape[1], lanes), 1)
    whole = row_count // 3
    block, t, row = lane // LANES, lane // (quads * group) % whole, lane // group % quads
    k = (row ^ my_quad) * row_count + jnp.where(block < 2, 2 * t + block, 2 * whole + t)
    pick = jnp.where(k + start == token, 1.0, 0.0)
    kept = jnp.dot(mask_row.astype(jnp.bfloat16), pick.astype(jnp.bfloat16), preferred_element_type=jnp.float32)
    channel = lax.broadcasted_iota(jnp.int32, (group, lanes), 0)
    lane = lax.broadcasted_iota(jnp.int32, (group, lanes), 1)
    spread_ref[...] = jnp.where(lane % group == channel, kept, 0.0)
    for copy in copies[1:4]:
        copy.wait()
    normed = normalise(pair_ref[...].reshape(tokens, channels), gain_ref[...], bias_ref[...])
    normed_ref[...] = normed
    copies[4].wait()
    parts = [all_w_ref[:, at : at + hidden] for at in range(0, 4 * hidden, hidden)]
    w = jnp.concatenate([jnp.where(my_col == 0, part[:, :ours], part[:, ours:]) for part in parts], axis=1)
    w_ref[...] = w
    sides_ref[...] = project(normed, w, pair_ref.shape, quads)


def other_kernel(pair_ref, sides_ref, gain_ref, bias_ref, w_ref, *refs):
    *piece_refs, others_ref = refs
    my_quad, my_col = lax.axis_index("quad"), lax.axis_index("col")
    quads = sides_ref.shape[0]
    normed = normalise(pair_ref[...].reshape(-1, pair_ref.shape[2]), gain_ref[...], bias_ref[...])
    others_ref[...] = project(normed, w_ref[...], pair_ref.shape, quads)
    for step, piece_ref in enumerate(piece_refs):
        piece_ref[my_col] = sides_ref[my_quad ^ step]
        piece_ref[1 - my_col] = others_ref[my_quad ^ step]


def triangle_kernel(far_order, steps, cols, row_count, col_count, share, *refs):
    *got_refs, spread_ref, mask_ref, total_ref = refs
    got_refs = {step: ref for step, ref in zip(steps, got_refs)}
    both = 2 * share
    group, lanes = spread_ref.shape
    length = mask_ref.shape[0]
    rows, quads, parts = length // row_count, len(steps), share // group
    whole, spare = row_count // 3, LANES - 2 * col_count
    rest = col_count - spare
    blocks = [[got_refs[row][col].astype(jnp.float32) for row in range(quads)] for col in range(cols)]

    def turned(picks):
        return jnp.concatenate([blocks[col][row][at : at + group] for col, row, at in picks], axis=0).T

    tail = turned([(col, row, whole * both + part * group) for col in range(cols) for part in range(parts) for row in range(quads)])

    def side(which, part):
        even, odd, third = [], [], []
        for col in range(cols):
            at = which * share + part * group
            block = turned([(col, row, t * both + at) for t in range(whole) for row in range(quads)])
            even.append(block[:col_count])
            odd.append(block[col_count : 2 * col_count])
            lane = (col * parts + part) * quads * group
            at = which * LANES // 2
            last = [tail[at + t * rest : at + (t + 1) * rest, lane : lane + quads * group] for t in range(whole)]
            third += [block[2 * col_count :], jnp.concatenate(last, axis=1)]
        tokens = [jnp.concatenate(pieces, axis=0) for pieces in (even, odd, third)]
        return jnp.concatenate(tokens, axis=1) * mask_ref[...]

    def placed(pieces):
        return jnp.concatenate([jnp.zeros((piece, lanes), jnp.bfloat16) if isinstance(piece, int) else piece for piece in pieces], axis=0)

    contract = (((1,), (1,)), ((), ()))
    mains, lasts = [], []
    for part in range(parts):
        left, right = side(0, part), side(1, part).astype(jnp.bfloat16)
        left = (left[:, None, :] * spread_ref[...][None]).reshape(rows, row_count, group, lanes)
        pairs = left[:, : 2 * whole].reshape(rows, whole, 2, group, lanes)
        left = jnp.concatenate([pairs[:, :, 0], pairs[:, :, 1], left[:, 2 * whole :]], axis=-1)
        left = left.reshape(rows * whole * group, 3 * lanes).astype(jnp.bfloat16)
        ours = [right[col * col_count : (col + 1) * col_count] for col in range(cols)]
        weights = [
            placed([p for mine in ours for p in (mine, LANES - col_count)]),
            placed([p for mine in ours for p in (col_count, mine, spare)]),
            placed([p for mine in ours for p in (2 * col_count, mine[:spare])]),
        ]
        weights = jnp.concatenate(weights, axis=1)
        mains.append(lax.dot_general(left, weights, contract, preferred_element_type=jnp.float32))
        weights = jnp.concatenate([mine[spare:] for mine in ours], axis=0)
        lasts.append(lax.dot_general(left[:, 2 * lanes :], weights, contract, preferred_element_type=jnp.float32))
    for target, device in enumerate(far_order):
        row, col = divmod(device, cols)
        spots = [(row * whole + t) * group for t in range(whole)]
        tiles = [main[at : at + group, col * LANES : (col + 1) * LANES] for at in spots for main in mains]
        last = [part[at : at + group, col * rest : (col + 1) * rest] for part in lasts for at in spots]
        tiles.append(jnp.concatenate(last, axis=1))
        total_ref[target] = jnp.concatenate(tiles, axis=0).astype(jnp.bfloat16)


def gate_kernel(normed_ref, w_ref, gain_ref, bias_ref, gate_ref, gain_out_ref, bias_out_ref):
    gate_ref[...] = sigmoid(jnp.dot(normed_ref[...], w_ref[...], preferred_element_type=jnp.float32))
    gain_out_ref[...] = column(gain_ref[...])
    bias_out_ref[...] = column(bias_ref[...])


def output_kernel(far_order, near_order, total_ref, gate_ref, gain_ref, bias_ref, w_ref, out_ref):
    tokens = gate_ref.shape[0]
    hidden = w_ref.shape[0]
    near = len(near_order)
    share = hidden // near
    blocks = []
    for index in near_order:
        parts = [total_ref[source].astype(jnp.float32) for source, device in enumerate(far_order) if device % near == index]
        blocks.append(unpack(sum(parts[1:], parts[0]), share))
    total = jnp.concatenate(blocks, axis=0)
    normed = layer_norm(total, gain_ref[...], bias_ref[...], 0).astype(jnp.bfloat16)
    output = lax.dot_general(normed, w_ref[...], (((0,), (0,)), ((), ())), preferred_element_type=jnp.float32)
    output = restore(output, out_ref.shape[0], out_ref.shape[1])
    out_ref[...] = (gate_ref[...] * output).astype(jnp.bfloat16).reshape(out_ref.shape)


def per_device(rows, cols, halves, pair, token_mask, gain_in, bias_in, w_in, w_gate, gain_out, bias_out, w_out):
    row_count, col_count, channels = pair.shape
    hidden = w_out.shape[0]
    devices = rows * cols
    near = devices // halves
    quads = rows // halves
    far_order = []
    for col in reversed(range(cols)):
        ahead = list(range(quads)) if col else list(range(1, quads)) + [0]
        behind = [1] + [quad for quad in reversed(range(quads)) if quad != 1] if col else list(reversed(range(quads)))
        for quad, other in zip(ahead, behind):
            far_order += [near + other * cols + col, quad * cols + col]
    share = hidden // near
    tokens = row_count * col_count
    length = rows * row_count
    depth = length // halves
    token_mask = token_mask.reshape(1, length)
    near_order = [quad * cols + col for col in range(cols) for quad in range(quads)]
    packed = 2 * share * tokens // LANES
    cost = pl.CostEstimate(flops=2 * tokens * channels * 4 * hidden, bytes_accessed=16 * tokens * channels, transcendentals=0)
    other_pair = lax.ppermute(pair, "col", [(i, (i + 1) % cols) for i in range(cols)])
    arguments = (pair, gain_in.reshape(1, channels), bias_in.reshape(1, channels), w_in, token_mask)
    sides, normed, spread, mask, *weights = pl.pallas_call(
        functools.partial(own_kernel, quads, cols),
        out_shape=(
            jax.ShapeDtypeStruct((quads, packed, LANES), jnp.bfloat16),
            jax.ShapeDtypeStruct((tokens, channels), jnp.bfloat16),
            jax.ShapeDtypeStruct((GROUP, GROUP * depth), jnp.float32),
            jax.ShapeDtypeStruct((length, 1), jnp.float32),
            jax.ShapeDtypeStruct((channels, 4 * hidden // cols), jnp.bfloat16),
            jax.ShapeDtypeStruct((1, channels), jnp.float32),
            jax.ShapeDtypeStruct((1, channels), jnp.float32),
        ),
        in_specs=[HBM] * 5,
        out_specs=(VMEM,) * 7,
        scratch_shapes=[
            pltpu.VMEM(pair.shape, pair.dtype),
            pltpu.VMEM(w_in.shape, w_in.dtype),
            pltpu.VMEM((1, length), jnp.int32),
            pltpu.SemaphoreType.DMA((5,)),
        ],
        compiler_params=LIMIT,
        cost_estimate=cost,
    )(*(pltpu.with_memory_space_constraint(x, pltpu.HBM) for x in arguments))
    w_ours, gain_in, bias_in = weights
    pieces = pl.pallas_call(
        other_kernel,
        out_shape=[jax.ShapeDtypeStruct((cols, packed, LANES), jnp.bfloat16)] * quads,
        in_specs=[VMEM] * 5,
        out_specs=[VMEM] * quads,
        scratch_shapes=[pltpu.VMEM((quads, packed, LANES), jnp.bfloat16)],
        compiler_params=LIMIT,
        cost_estimate=cost,
    )(other_pair, sides, gain_in, bias_in, w_ours)
    steps = [3, 1, 2, 0]
    got = [lax.ppermute(pieces[step], "quad", [(i, i ^ step) for i in range(quads)]) if step else pieces[0] for step in steps]
    total = pl.pallas_call(
        functools.partial(triangle_kernel, far_order, steps, cols, row_count, col_count, share),
        out_shape=jax.ShapeDtypeStruct((devices, share * tokens // LANES, LANES), jnp.bfloat16),
        in_specs=[VMEM] * (quads + 2),
        out_specs=VMEM,
        compiler_params=LIMIT,
    )(*got, spread, mask)
    gate, gain_out, bias_out = pl.pallas_call(
        gate_kernel,
        out_shape=(
            jax.ShapeDtypeStruct((tokens, channels), jnp.float32),
            jax.ShapeDtypeStruct((hidden, 1), jnp.float32),
            jax.ShapeDtypeStruct((hidden, 1), jnp.float32),
        ),
        in_specs=[VMEM] * 4,
        out_specs=(VMEM, VMEM, VMEM),
        compiler_params=LIMIT,
        cost_estimate=pl.CostEstimate(flops=2 * tokens * channels * channels, bytes_accessed=4 * tokens * channels, transcendentals=0),
    )(normed, w_gate, gain_out.reshape(1, hidden), bias_out.reshape(1, hidden))
    total = lax.all_to_all(total, ("half", "quad", "col"), split_axis=0, concat_axis=0, tiled=True, axis_index_groups=[far_order])
    return pl.pallas_call(
        functools.partial(output_kernel, far_order, near_order),
        out_shape=jax.ShapeDtypeStruct(pair.shape, jnp.bfloat16),
        in_specs=[VMEM] * 5,
        out_specs=VMEM,
        compiler_params=LIMIT,
    )(total, gate, gain_out, bias_out, w_out)


def plain_per_device(rows, cols, pair, token_mask, gain_in, bias_in, w_in, w_gate, gain_out, bias_out, w_out):
    row_count, col_count, channels = pair.shape
    hidden = w_out.shape[0]
    devices = rows * cols
    share = hidden // devices
    tokens = row_count * col_count
    row_start = lax.axis_index(("half", "quad")) * row_count
    col_start = lax.axis_index("col") * col_count
    mask_float = token_mask.astype(jnp.float32)
    mask_rows = lax.dynamic_slice_in_dim(mask_float, row_start, row_count)
    mask_cols = lax.dynamic_slice_in_dim(mask_float, col_start, col_count)
    pair_mask = (mask_rows[:, None] * mask_cols[None, :]).reshape(1, tokens)
    flat = pair.reshape(tokens, channels).astype(jnp.float32)
    normed = layer_norm(flat, gain_in, bias_in, -1).astype(jnp.bfloat16)
    projected = lax.dot_general(w_in, normed, (((0,), (1,)), ((), ())), preferred_element_type=jnp.float32)
    projected = projected.reshape(2, 2, hidden, tokens)
    sides = (pair_mask * jax.nn.sigmoid(projected[:, 0]) * projected[:, 1]).astype(jnp.bfloat16)
    sides = sides.reshape(2, devices, share, tokens).transpose(1, 0, 2, 3)
    gate = jax.nn.sigmoid(jnp.dot(normed, w_gate, preferred_element_type=jnp.float32))
    got = lax.all_to_all(sides, AXES, split_axis=0, concat_axis=0, tiled=True)
    got = got.reshape(rows, cols, 2, share, row_count, col_count).transpose(2, 3, 0, 4, 1, 5)
    got = got.reshape(2, share, rows * row_count, cols * col_count)
    total = jnp.einsum("cki,ckj->cij", got[0], got[1], preferred_element_type=jnp.float32).astype(jnp.bfloat16)
    total = total.reshape(share, rows, row_count, cols, col_count).transpose(1, 3, 0, 2, 4)
    total = total.reshape(devices, share, tokens)
    total = lax.all_to_all(total, AXES, split_axis=0, concat_axis=0, tiled=True)
    total = total.reshape(hidden, tokens).astype(jnp.float32)
    summed_norm = layer_norm(total, gain_out[:, None], bias_out[:, None], 0).astype(jnp.bfloat16)
    output = lax.dot_general(summed_norm, w_out, (((0,), (0,)), ((), ())), preferred_element_type=jnp.float32)
    return (gate * output).astype(jnp.bfloat16).reshape(row_count, col_count, channels)


def solution(mesh):
    rows, cols = mesh.shape["row"], mesh.shape["col"]
    halves = 2
    parts = (mesh.shape["groups"], halves, rows // halves, cols)
    finer = jax.sharding.Mesh(mesh.devices.reshape(parts), ("groups", "half", "quad", "col"))

    def per_shard(*args):
        near, hidden, length = rows * cols // halves, args[-1].shape[0], args[1].shape[0]
        row_count, col_count, _ = args[0].shape
        spare = LANES - 2 * col_count
        fits = hidden % (2 * GROUP * near) == 0 and cols == 2 and rows // halves == 4 and length <= LANES and row_count % 3 == 0
        fits = fits and 0 < spare < col_count and row_count // 3 * (col_count - spare) * 2 == LANES
        fits = fits and row_count // 3 * (rows // halves) * GROUP == LANES
        return per_device(rows, cols, halves, *args) if fits else plain_per_device(rows, cols, *args)

    tokens = P(("groups", "half", "quad"), "col", None)
    in_specs = (tokens, P("groups"), P(), P(), P(), P(), P(), P(), P())
    return jax.shard_map(per_shard, mesh=finer, in_specs=in_specs, out_specs=tokens, check_vma=False)
```

```python
import functools

import jax
import jax.numpy as jnp
from jax import lax
from jax.experimental import pallas as pl
from jax.experimental.pallas import tpu as pltpu
from jax.sharding import PartitionSpec as P

epsilon = 1e-05
LANES = 128
GROUP = 8
AXES = ("half", "quad", "col")
VMEM = pl.BlockSpec(memory_space=pltpu.VMEM)
HBM = pl.BlockSpec(memory_space=pltpu.HBM)
LIMIT = pltpu.CompilerParams(vmem_limit_bytes=32 * 1024 * 1024)


def sigmoid(x):
    return 0.5 * jnp.tanh(0.5 * x) + 0.5


def layer_norm(values, gain, bias, axis):
    mean = jnp.mean(values, axis=axis, keepdims=True)
    centred = values - mean
    variance = jnp.mean(centred * centred, axis=axis, keepdims=True)
    return centred * lax.rsqrt(variance + epsilon) * gain + bias


def column(row):
    n = row.shape[1]
    eye = lax.broadcasted_iota(jnp.int32, (n, n), 0) == lax.broadcasted_iota(jnp.int32, (n, n), 1)
    return jnp.sum(jnp.where(eye, row, 0.0), axis=1, keepdims=True)


def pack(x):
    rows, tokens = x.shape[-2:]
    whole, rest = divmod(tokens, LANES)
    blocks = [x[..., t * LANES : (t + 1) * LANES] for t in range(whole)]
    if rest:
        tail = x[..., whole * LANES :]
        blocks.append(jnp.concatenate([tail[..., : rows // 2, :], tail[..., rows // 2 :, :]], axis=-1))
    return jnp.concatenate(blocks, axis=-2)


def unpack(x, rows):
    whole, rest = divmod(x.shape[-2], rows)
    blocks = [x[..., t * rows : (t + 1) * rows, :] for t in range(whole)]
    if rest:
        tail = x[..., whole * rows :, :]
        blocks.append(jnp.concatenate([tail[..., : LANES // 2], tail[..., LANES // 2 :]], axis=-2))
    return jnp.concatenate(blocks, axis=-1)


def arrange(x):
    row_count, col_count, _ = x.shape
    whole, spare = row_count // 3, LANES - 2 * col_count
    blocks = []
    for t in range(whole):
        blocks += [x[2 * t], x[2 * t + 1], x[2 * whole + t, :spare]]
    return jnp.concatenate(blocks + [x[2 * whole + t, spare:] for t in range(whole)], axis=0)


def restore(x, row_count, col_count):
    whole, spare = row_count // 3, LANES - 2 * col_count
    rest = col_count - spare
    rows = []
    for t in range(whole):
        rows += [x[t * LANES : t * LANES + col_count], x[t * LANES + col_count : t * LANES + 2 * col_count]]
    for t in range(whole):
        tail = whole * LANES + t * rest
        rows += [x[t * LANES + 2 * col_count : (t + 1) * LANES], x[tail : tail + rest]]
    return jnp.concatenate(rows, axis=0)


def normalise(flat, gain, bias):
    return layer_norm(flat.astype(jnp.float32), gain, bias, -1).astype(jnp.bfloat16)


def project(normed, w, shape, quads):
    ours = w.shape[1] // 4
    tokens = normed.shape[0]
    projected = lax.dot_general(w, arrange(normed.reshape(shape)), (((0,), (1,)), ((), ())), preferred_element_type=jnp.float32)
    left = sigmoid(projected[:ours]) * projected[ours : 2 * ours]
    right = sigmoid(projected[2 * ours : 3 * ours]) * projected[3 * ours :]
    sides = jnp.concatenate([left.reshape(quads, -1, tokens), right.reshape(quads, -1, tokens)], axis=1)
    return pack(sides).astype(jnp.bfloat16)


def own_kernel(quads, cols, pair_hbm, gain_hbm, bias_hbm, w_hbm, mask_hbm, sides_ref, normed_ref, spread_ref, column_mask_ref, w_ref, gain_ref, bias_ref, pair_ref, all_w_ref, mask_ref, sems):
    moves = [(mask_hbm, mask_ref), (pair_hbm, pair_ref), (gain_hbm, gain_ref), (bias_hbm, bias_ref), (w_hbm, all_w_ref)]
    copies = [pltpu.make_async_copy(source, target, sems.at[n]) for n, (source, target) in enumerate(moves)]
    for copy in copies:
        copy.start()
    my_quad, my_col = lax.axis_index("quad"), lax.axis_index("col")
    row_count, _, channels = pair_ref.shape
    tokens = normed_ref.shape[0]
    hidden = all_w_ref.shape[1] // 4
    ours = hidden // cols
    group, lanes = spread_ref.shape
    copies[0].wait()
    mask_row = mask_ref[...].astype(jnp.float32)
    column_mask_ref[...] = column(mask_row)
    start = lax.axis_index("half") * (lanes // group)
    token = lax.broadcasted_iota(jnp.int32, (mask_row.shape[1], lanes), 0)
    lane = lax.broadcasted_iota(jnp.int32, (mask_row.shape[1], lanes), 1)
    whole = row_count // 3
    block, t, row = lane // LANES, lane // (quads * group) % whole, lane // group % quads
    k = (row ^ my_quad) * row_count + jnp.where(block < 2, 2 * t + block, 2 * whole + t)
    pick = jnp.where(k + start == token, 1.0, 0.0)
    kept = jnp.dot(mask_row.astype(jnp.bfloat16), pick.astype(jnp.bfloat16), preferred_element_type=jnp.float32)
    channel = lax.broadcasted_iota(jnp.int32, (group, lanes), 0)
    lane = lax.broadcasted_iota(jnp.int32, (group, lanes), 1)
    spread_ref[...] = jnp.where(lane % group == channel, kept, 0.0)
    for copy in copies[1:4]:
        copy.wait()
    normed = normalise(pair_ref[...].reshape(tokens, channels), gain_ref[...], bias_ref[...])
    normed_ref[...] = normed
    copies[4].wait()
    parts = [all_w_ref[:, at : at + hidden] for at in range(0, 4 * hidden, hidden)]
    w = jnp.concatenate([jnp.where(my_col == 0, part[:, :ours], part[:, ours:]) for part in parts], axis=1)
    w_ref[...] = w
    sides_ref[...] = project(normed, w, pair_ref.shape, quads)


def other_kernel(pair_ref, sides_ref, gain_ref, bias_ref, w_ref, *refs):
    *piece_refs, others_ref = refs
    my_quad, my_col = lax.axis_index("quad"), lax.axis_index("col")
    quads = sides_ref.shape[0]
    normed = normalise(pair_ref[...].reshape(-1, pair_ref.shape[2]), gain_ref[...], bias_ref[...])
    others_ref[...] = project(normed, w_ref[...], pair_ref.shape, quads)
    for step, piece_ref in enumerate(piece_refs):
        piece_ref[my_col] = sides_ref[my_quad ^ step]
        piece_ref[1 - my_col] = others_ref[my_quad ^ step]


def triangle_kernel(far_order, steps, cols, row_count, col_count, share, *refs):
    *got_refs, spread_ref, mask_ref, total_ref = refs
    got_refs = {step: ref for step, ref in zip(steps, got_refs)}
    both = 2 * share
    group, lanes = spread_ref.shape
    length = mask_ref.shape[0]
    rows, quads, parts = length // row_count, len(steps), share // group
    whole, spare = row_count // 3, LANES - 2 * col_count
    rest = col_count - spare
    blocks = [[got_refs[row][col].astype(jnp.float32) for row in range(quads)] for col in range(cols)]

    def turned(picks):
        return jnp.concatenate([blocks[col][row][at : at + group] for col, row, at in picks], axis=0).T

    tail = turned([(col, row, whole * both + part * group) for col in range(cols) for part in range(parts) for row in range(quads)])

    def side(which, part):
        even, odd, third = [], [], []
        for col in range(cols):
            at = which * share + part * group
            block = turned([(col, row, t * both + at) for t in range(whole) for row in range(quads)])
            even.append(block[:col_count])
            odd.append(block[col_count : 2 * col_count])
            lane = (col * parts + part) * quads * group
            at = which * LANES // 2
            last = [tail[at + t * rest : at + (t + 1) * rest, lane : lane + quads * group] for t in range(whole)]
            third += [block[2 * col_count :], jnp.concatenate(last, axis=1)]
        tokens = [jnp.concatenate(pieces, axis=0) for pieces in (even, odd, third)]
        return jnp.concatenate(tokens, axis=1) * mask_ref[...]

    def placed(pieces):
        return jnp.concatenate([jnp.zeros((piece, lanes), jnp.bfloat16) if isinstance(piece, int) else piece for piece in pieces], axis=0)

    contract = (((1,), (1,)), ((), ()))
    mains, lasts = [], []
    for part in range(parts):
        left, right = side(0, part), side(1, part).astype(jnp.bfloat16)
        left = (left[:, None, :] * spread_ref[...][None]).reshape(rows, row_count, group, lanes)
        pairs = left[:, : 2 * whole].reshape(rows, whole, 2, group, lanes)
        left = jnp.concatenate([pairs[:, :, 0], pairs[:, :, 1], left[:, 2 * whole :]], axis=-1)
        left = left.reshape(rows * whole * group, 3 * lanes).astype(jnp.bfloat16)
        ours = [right[col * col_count : (col + 1) * col_count] for col in range(cols)]
        weights = [
            placed([p for mine in ours for p in (mine, LANES - col_count)]),
            placed([p for mine in ours for p in (col_count, mine, spare)]),
            placed([p for mine in ours for p in (2 * col_count, mine[:spare])]),
        ]
        weights = jnp.concatenate(weights, axis=1)
        mains.append(lax.dot_general(left, weights, contract, preferred_element_type=jnp.float32))
        weights = jnp.concatenate([mine[spare:] for mine in ours], axis=0)
        lasts.append(lax.dot_general(left[:, 2 * lanes :], weights, contract, preferred_element_type=jnp.float32))
    for target, device in enumerate(far_order):
        row, col = divmod(device, cols)
        spots = [(row * whole + t) * group for t in range(whole)]
        tiles = [main[at : at + group, col * LANES : (col + 1) * LANES] for at in spots for main in mains]
        last = [part[at : at + group, col * rest : (col + 1) * rest] for part in lasts for at in spots]
        tiles.append(jnp.concatenate(last, axis=1))
        total_ref[target] = jnp.concatenate(tiles, axis=0).astype(jnp.bfloat16)


def gate_kernel(normed_ref, w_ref, gain_ref, bias_ref, gate_ref, gain_out_ref, bias_out_ref):
    gate_ref[...] = sigmoid(jnp.dot(normed_ref[...], w_ref[...], preferred_element_type=jnp.float32))
    gain_out_ref[...] = column(gain_ref[...])
    bias_out_ref[...] = column(bias_ref[...])


def output_kernel(far_order, near_order, total_ref, gate_ref, gain_ref, bias_ref, w_ref, out_ref):
    tokens = gate_ref.shape[0]
    hidden = w_ref.shape[0]
    near = len(near_order)
    share = hidden // near
    blocks = []
    for index in near_order:
        parts = [total_ref[source].astype(jnp.float32) for source, device in enumerate(far_order) if device % near == index]
        blocks.append(unpack(sum(parts[1:], parts[0]), share))
    total = jnp.concatenate(blocks, axis=0)
    normed = layer_norm(total, gain_ref[...], bias_ref[...], 0).astype(jnp.bfloat16)
    output = lax.dot_general(normed, w_ref[...], (((0,), (0,)), ((), ())), preferred_element_type=jnp.float32)
    output = restore(output, out_ref.shape[0], out_ref.shape[1])
    out_ref[...] = (gate_ref[...] * output).astype(jnp.bfloat16).reshape(out_ref.shape)


def per_device(rows, cols, halves, pair, token_mask, gain_in, bias_in, w_in, w_gate, gain_out, bias_out, w_out):
    row_count, col_count, channels = pair.shape
    hidden = w_out.shape[0]
    devices = rows * cols
    near = devices // halves
    quads = rows // halves
    far_order = []
    for col in reversed(range(cols)):
        ahead = list(range(quads)) if col else list(range(1, quads)) + [0]
        behind = [0] + list(reversed(range(1, quads))) if col else list(reversed(range(quads)))
        for quad, other in zip(ahead, behind):
            far_order += [near + other * cols + col, quad * cols + col]
    share = hidden // near
    tokens = row_count * col_count
    length = rows * row_count
    depth = length // halves
    token_mask = token_mask.reshape(1, length)
    near_order = [quad * cols + col for col in range(cols) for quad in range(quads)]
    packed = 2 * share * tokens // LANES
    cost = pl.CostEstimate(flops=2 * tokens * channels * 4 * hidden, bytes_accessed=16 * tokens * channels, transcendentals=0)
    other_pair = lax.ppermute(pair, "col", [(i, (i + 1) % cols) for i in range(cols)])
    arguments = (pair, gain_in.reshape(1, channels), bias_in.reshape(1, channels), w_in, token_mask)
    sides, normed, spread, mask, *weights = pl.pallas_call(
        functools.partial(own_kernel, quads, cols),
        out_shape=(
            jax.ShapeDtypeStruct((quads, packed, LANES), jnp.bfloat16),
            jax.ShapeDtypeStruct((tokens, channels), jnp.bfloat16),
            jax.ShapeDtypeStruct((GROUP, GROUP * depth), jnp.float32),
            jax.ShapeDtypeStruct((length, 1), jnp.float32),
            jax.ShapeDtypeStruct((channels, 4 * hidden // cols), jnp.bfloat16),
            jax.ShapeDtypeStruct((1, channels), jnp.float32),
            jax.ShapeDtypeStruct((1, channels), jnp.float32),
        ),
        in_specs=[HBM] * 5,
        out_specs=(VMEM,) * 7,
        scratch_shapes=[
            pltpu.VMEM(pair.shape, pair.dtype),
            pltpu.VMEM(w_in.shape, w_in.dtype),
            pltpu.VMEM((1, length), jnp.int32),
            pltpu.SemaphoreType.DMA((5,)),
        ],
        compiler_params=LIMIT,
        cost_estimate=cost,
    )(*(pltpu.with_memory_space_constraint(x, pltpu.HBM) for x in arguments))
    w_ours, gain_in, bias_in = weights
    pieces = pl.pallas_call(
        other_kernel,
        out_shape=[jax.ShapeDtypeStruct((cols, packed, LANES), jnp.bfloat16)] * quads,
        in_specs=[VMEM] * 5,
        out_specs=[VMEM] * quads,
        scratch_shapes=[pltpu.VMEM((quads, packed, LANES), jnp.bfloat16)],
        compiler_params=LIMIT,
        cost_estimate=cost,
    )(other_pair, sides, gain_in, bias_in, w_ours)
    steps = [3, 1, 2, 0]
    got = [lax.ppermute(pieces[step], "quad", [(i, i ^ step) for i in range(quads)]) if step else pieces[0] for step in steps]
    total = pl.pallas_call(
        functools.partial(triangle_kernel, far_order, steps, cols, row_count, col_count, share),
        out_shape=jax.ShapeDtypeStruct((devices, share * tokens // LANES, LANES), jnp.bfloat16),
        in_specs=[VMEM] * (quads + 2),
        out_specs=VMEM,
        compiler_params=LIMIT,
    )(*got, spread, mask)
    gate, gain_out, bias_out = pl.pallas_call(
        gate_kernel,
        out_shape=(
            jax.ShapeDtypeStruct((tokens, channels), jnp.float32),
            jax.ShapeDtypeStruct((hidden, 1), jnp.float32),
            jax.ShapeDtypeStruct((hidden, 1), jnp.float32),
        ),
        in_specs=[VMEM] * 4,
        out_specs=(VMEM, VMEM, VMEM),
        compiler_params=LIMIT,
        cost_estimate=pl.CostEstimate(flops=2 * tokens * channels * channels, bytes_accessed=4 * tokens * channels, transcendentals=0),
    )(normed, w_gate, gain_out.reshape(1, hidden), bias_out.reshape(1, hidden))
    total = lax.all_to_all(total, ("half", "quad", "col"), split_axis=0, concat_axis=0, tiled=True, axis_index_groups=[far_order])
    return pl.pallas_call(
        functools.partial(output_kernel, far_order, near_order),
        out_shape=jax.ShapeDtypeStruct(pair.shape, jnp.bfloat16),
        in_specs=[VMEM] * 5,
        out_specs=VMEM,
        compiler_params=LIMIT,
    )(total, gate, gain_out, bias_out, w_out)


def plain_per_device(rows, cols, pair, token_mask, gain_in, bias_in, w_in, w_gate, gain_out, bias_out, w_out):
    row_count, col_count, channels = pair.shape
    hidden = w_out.shape[0]
    devices = rows * cols
    share = hidden // devices
    tokens = row_count * col_count
    row_start = lax.axis_index(("half", "quad")) * row_count
    col_start = lax.axis_index("col") * col_count
    mask_float = token_mask.astype(jnp.float32)
    mask_rows = lax.dynamic_slice_in_dim(mask_float, row_start, row_count)
    mask_cols = lax.dynamic_slice_in_dim(mask_float, col_start, col_count)
    pair_mask = (mask_rows[:, None] * mask_cols[None, :]).reshape(1, tokens)
    flat = pair.reshape(tokens, channels).astype(jnp.float32)
    normed = layer_norm(flat, gain_in, bias_in, -1).astype(jnp.bfloat16)
    projected = lax.dot_general(w_in, normed, (((0,), (1,)), ((), ())), preferred_element_type=jnp.float32)
    projected = projected.reshape(2, 2, hidden, tokens)
    sides = (pair_mask * jax.nn.sigmoid(projected[:, 0]) * projected[:, 1]).astype(jnp.bfloat16)
    sides = sides.reshape(2, devices, share, tokens).transpose(1, 0, 2, 3)
    gate = jax.nn.sigmoid(jnp.dot(normed, w_gate, preferred_element_type=jnp.float32))
    got = lax.all_to_all(sides, AXES, split_axis=0, concat_axis=0, tiled=True)
    got = got.reshape(rows, cols, 2, share, row_count, col_count).transpose(2, 3, 0, 4, 1, 5)
    got = got.reshape(2, share, rows * row_count, cols * col_count)
    total = jnp.einsum("cki,ckj->cij", got[0], got[1], preferred_element_type=jnp.float32).astype(jnp.bfloat16)
    total = total.reshape(share, rows, row_count, cols, col_count).transpose(1, 3, 0, 2, 4)
    total = total.reshape(devices, share, tokens)
    total = lax.all_to_all(total, AXES, split_axis=0, concat_axis=0, tiled=True)
    total = total.reshape(hidden, tokens).astype(jnp.float32)
    summed_norm = layer_norm(total, gain_out[:, None], bias_out[:, None], 0).astype(jnp.bfloat16)
    output = lax.dot_general(summed_norm, w_out, (((0,), (0,)), ((), ())), preferred_element_type=jnp.float32)
    return (gate * output).astype(jnp.bfloat16).reshape(row_count, col_count, channels)


def solution(mesh):
    rows, cols = mesh.shape["row"], mesh.shape["col"]
    halves = 2
    parts = (mesh.shape["groups"], halves, rows // halves, cols)
    finer = jax.sharding.Mesh(mesh.devices.reshape(parts), ("groups", "half", "quad", "col"))

    def per_shard(*args):
        near, hidden, length = rows * cols // halves, args[-1].shape[0], args[1].shape[0]
        row_count, col_count, _ = args[0].shape
        spare = LANES - 2 * col_count
        fits = hidden % (2 * GROUP * near) == 0 and cols == 2 and rows // halves == 4 and length <= LANES and row_count % 3 == 0
        fits = fits and 0 < spare < col_count and row_count // 3 * (col_count - spare) * 2 == LANES
        fits = fits and row_count // 3 * (rows // halves) * GROUP == LANES
        return per_device(rows, cols, halves, *args) if fits else plain_per_device(rows, cols, *args)

    tokens = P(("groups", "half", "quad"), "col", None)
    in_specs = (tokens, P("groups"), P(), P(), P(), P(), P(), P(), P())
    return jax.shard_map(per_shard, mesh=finer, in_specs=in_specs, out_specs=tokens, check_vma=False)
```

```python
import functools

import jax
import jax.numpy as jnp
from jax import lax
from jax.experimental import pallas as pl
from jax.experimental.pallas import tpu as pltpu
from jax.sharding import PartitionSpec as P

epsilon = 1e-05
LANES = 128
GROUP = 8
AXES = ("half", "quad", "col")
VMEM = pl.BlockSpec(memory_space=pltpu.VMEM)
HBM = pl.BlockSpec(memory_space=pltpu.HBM)
LIMIT = pltpu.CompilerParams(vmem_limit_bytes=32 * 1024 * 1024)


def sigmoid(x):
    return 0.5 * jnp.tanh(0.5 * x) + 0.5


def layer_norm(values, gain, bias, axis):
    mean = jnp.mean(values, axis=axis, keepdims=True)
    centred = values - mean
    variance = jnp.mean(centred * centred, axis=axis, keepdims=True)
    return centred * lax.rsqrt(variance + epsilon) * gain + bias


def column(row):
    n = row.shape[1]
    eye = lax.broadcasted_iota(jnp.int32, (n, n), 0) == lax.broadcasted_iota(jnp.int32, (n, n), 1)
    return jnp.sum(jnp.where(eye, row, 0.0), axis=1, keepdims=True)


def pack(x):
    rows, tokens = x.shape[-2:]
    whole, rest = divmod(tokens, LANES)
    blocks = [x[..., t * LANES : (t + 1) * LANES] for t in range(whole)]
    if rest:
        tail = x[..., whole * LANES :]
        blocks.append(jnp.concatenate([tail[..., : rows // 2, :], tail[..., rows // 2 :, :]], axis=-1))
    return jnp.concatenate(blocks, axis=-2)


def unpack(x, rows):
    whole, rest = divmod(x.shape[-2], rows)
    blocks = [x[..., t * rows : (t + 1) * rows, :] for t in range(whole)]
    if rest:
        tail = x[..., whole * rows :, :]
        blocks.append(jnp.concatenate([tail[..., : LANES // 2], tail[..., LANES // 2 :]], axis=-2))
    return jnp.concatenate(blocks, axis=-1)


def arrange(x):
    row_count, col_count, _ = x.shape
    whole, spare = row_count // 3, LANES - 2 * col_count
    blocks = []
    for t in range(whole):
        blocks += [x[2 * t], x[2 * t + 1], x[2 * whole + t, :spare]]
    return jnp.concatenate(blocks + [x[2 * whole + t, spare:] for t in range(whole)], axis=0)


def restore(x, row_count, col_count):
    whole, spare = row_count // 3, LANES - 2 * col_count
    rest = col_count - spare
    rows = []
    for t in range(whole):
        rows += [x[t * LANES : t * LANES + col_count], x[t * LANES + col_count : t * LANES + 2 * col_count]]
    for t in range(whole):
        tail = whole * LANES + t * rest
        rows += [x[t * LANES + 2 * col_count : (t + 1) * LANES], x[tail : tail + rest]]
    return jnp.concatenate(rows, axis=0)


def normalise(flat, gain, bias):
    return layer_norm(flat.astype(jnp.float32), gain, bias, -1).astype(jnp.bfloat16)


def project(normed, w, shape, quads):
    ours = w.shape[1] // 4
    tokens = normed.shape[0]
    projected = lax.dot_general(w, arrange(normed.reshape(shape)), (((0,), (1,)), ((), ())), preferred_element_type=jnp.float32)
    left = sigmoid(projected[:ours]) * projected[ours : 2 * ours]
    right = sigmoid(projected[2 * ours : 3 * ours]) * projected[3 * ours :]
    sides = jnp.concatenate([left.reshape(quads, -1, tokens), right.reshape(quads, -1, tokens)], axis=1)
    return pack(sides).astype(jnp.bfloat16)


def own_kernel(quads, cols, pair_hbm, gain_hbm, bias_hbm, w_hbm, mask_hbm, sides_ref, normed_ref, spread_ref, column_mask_ref, w_ref, gain_ref, bias_ref, pair_ref, all_w_ref, mask_ref, sems):
    row_count, _, channels = pair_ref.shape
    pair_rows = [pl.ds(at, row_count // 3) for at in range(0, row_count, row_count // 3)]
    w_rows = [pl.ds(at, channels // 2) for at in range(0, channels, channels // 2)]
    moves = [(mask_hbm, mask_ref), (gain_hbm, gain_ref), (bias_hbm, bias_ref)]
    moves += [(pair_hbm.at[rows], pair_ref.at[rows]) for rows in pair_rows]
    moves += [(w_hbm.at[rows], all_w_ref.at[rows]) for rows in w_rows]
    copies = [pltpu.make_async_copy(source, target, sems.at[n]) for n, (source, target) in enumerate(moves)]
    for copy in copies:
        copy.start()
    my_quad, my_col = lax.axis_index("quad"), lax.axis_index("col")
    tokens = normed_ref.shape[0]
    hidden = all_w_ref.shape[1] // 4
    ours = hidden // cols
    group, lanes = spread_ref.shape
    copies[0].wait()
    mask_row = mask_ref[...].astype(jnp.float32)
    column_mask_ref[...] = column(mask_row)
    start = lax.axis_index("half") * (lanes // group)
    token = lax.broadcasted_iota(jnp.int32, (mask_row.shape[1], lanes), 0)
    lane = lax.broadcasted_iota(jnp.int32, (mask_row.shape[1], lanes), 1)
    whole = row_count // 3
    block, t, row = lane // LANES, lane // (quads * group) % whole, lane // group % quads
    k = (row ^ my_quad) * row_count + jnp.where(block < 2, 2 * t + block, 2 * whole + t)
    pick = jnp.where(k + start == token, 1.0, 0.0)
    kept = jnp.dot(mask_row.astype(jnp.bfloat16), pick.astype(jnp.bfloat16), preferred_element_type=jnp.float32)
    channel = lax.broadcasted_iota(jnp.int32, (group, lanes), 0)
    lane = lax.broadcasted_iota(jnp.int32, (group, lanes), 1)
    spread_ref[...] = jnp.where(lane % group == channel, kept, 0.0)
    for copy in copies[1:6]:
        copy.wait()
    normed = normalise(pair_ref[...].reshape(tokens, channels), gain_ref[...], bias_ref[...])
    normed_ref[...] = normed
    for copy in copies[6:]:
        copy.wait()
    parts = [all_w_ref[:, at : at + hidden] for at in range(0, 4 * hidden, hidden)]
    w = jnp.concatenate([jnp.where(my_col == 0, part[:, :ours], part[:, ours:]) for part in parts], axis=1)
    w_ref[...] = w
    sides_ref[...] = project(normed, w, pair_ref.shape, quads)


def other_kernel(pair_ref, sides_ref, gain_ref, bias_ref, w_ref, *refs):
    *piece_refs, others_ref = refs
    my_quad, my_col = lax.axis_index("quad"), lax.axis_index("col")
    quads = sides_ref.shape[0]
    normed = normalise(pair_ref[...].reshape(-1, pair_ref.shape[2]), gain_ref[...], bias_ref[...])
    others_ref[...] = project(normed, w_ref[...], pair_ref.shape, quads)
    for step, piece_ref in enumerate(piece_refs):
        piece_ref[my_col] = sides_ref[my_quad ^ step]
        piece_ref[1 - my_col] = others_ref[my_quad ^ step]


def triangle_kernel(far_order, steps, cols, row_count, col_count, share, *refs):
    *got_refs, spread_ref, mask_ref, total_ref = refs
    got_refs = {step: ref for step, ref in zip(steps, got_refs)}
    both = 2 * share
    group, lanes = spread_ref.shape
    length = mask_ref.shape[0]
    rows, quads, parts = length // row_count, len(steps), share // group
    whole, spare = row_count // 3, LANES - 2 * col_count
    rest = col_count - spare
    blocks = [[got_refs[row][col].astype(jnp.float32) for row in range(quads)] for col in range(cols)]

    def turned(picks):
        return jnp.concatenate([blocks[col][row][at : at + group] for col, row, at in picks], axis=0).T

    tail = turned([(col, row, whole * both + part * group) for col in range(cols) for part in range(parts) for row in range(quads)])

    def side(which, part):
        even, odd, third = [], [], []
        for col in range(cols):
            at = which * share + part * group
            block = turned([(col, row, t * both + at) for t in range(whole) for row in range(quads)])
            even.append(block[:col_count])
            odd.append(block[col_count : 2 * col_count])
            lane = (col * parts + part) * quads * group
            at = which * LANES // 2
            last = [tail[at + t * rest : at + (t + 1) * rest, lane : lane + quads * group] for t in range(whole)]
            third += [block[2 * col_count :], jnp.concatenate(last, axis=1)]
        tokens = [jnp.concatenate(pieces, axis=0) for pieces in (even, odd, third)]
        return jnp.concatenate(tokens, axis=1) * mask_ref[...]

    def placed(pieces):
        return jnp.concatenate([jnp.zeros((piece, lanes), jnp.bfloat16) if isinstance(piece, int) else piece for piece in pieces], axis=0)

    contract = (((1,), (1,)), ((), ()))
    mains, lasts = [], []
    for part in range(parts):
        left, right = side(0, part), side(1, part).astype(jnp.bfloat16)
        left = (left[:, None, :] * spread_ref[...][None]).reshape(rows, row_count, group, lanes)
        pairs = left[:, : 2 * whole].reshape(rows, whole, 2, group, lanes)
        left = jnp.concatenate([pairs[:, :, 0], pairs[:, :, 1], left[:, 2 * whole :]], axis=-1)
        left = left.reshape(rows * whole * group, 3 * lanes).astype(jnp.bfloat16)
        ours = [right[col * col_count : (col + 1) * col_count] for col in range(cols)]
        weights = [
            placed([p for mine in ours for p in (mine, LANES - col_count)]),
            placed([p for mine in ours for p in (col_count, mine, spare)]),
            placed([p for mine in ours for p in (2 * col_count, mine[:spare])]),
        ]
        weights = jnp.concatenate(weights, axis=1)
        mains.append(lax.dot_general(left, weights, contract, preferred_element_type=jnp.float32))
        weights = jnp.concatenate([mine[spare:] for mine in ours], axis=0)
        lasts.append(lax.dot_general(left[:, 2 * lanes :], weights, contract, preferred_element_type=jnp.float32))
    for target, device in enumerate(far_order):
        row, col = divmod(device, cols)
        spots = [(row * whole + t) * group for t in range(whole)]
        tiles = [main[at : at + group, col * LANES : (col + 1) * LANES] for at in spots for main in mains]
        last = [part[at : at + group, col * rest : (col + 1) * rest] for part in lasts for at in spots]
        tiles.append(jnp.concatenate(last, axis=1))
        total_ref[target] = jnp.concatenate(tiles, axis=0).astype(jnp.bfloat16)


def gate_kernel(normed_ref, w_ref, gain_ref, bias_ref, gate_ref, gain_out_ref, bias_out_ref):
    gate_ref[...] = sigmoid(jnp.dot(normed_ref[...], w_ref[...], preferred_element_type=jnp.float32))
    gain_out_ref[...] = column(gain_ref[...])
    bias_out_ref[...] = column(bias_ref[...])


def output_kernel(far_order, near_order, total_ref, gate_ref, gain_ref, bias_ref, w_ref, out_ref):
    tokens = gate_ref.shape[0]
    hidden = w_ref.shape[0]
    near = len(near_order)
    share = hidden // near
    blocks = []
    for index in near_order:
        parts = [total_ref[source].astype(jnp.float32) for source, device in enumerate(far_order) if device % near == index]
        blocks.append(unpack(sum(parts[1:], parts[0]), share))
    total = jnp.concatenate(blocks, axis=0)
    normed = layer_norm(total, gain_ref[...], bias_ref[...], 0).astype(jnp.bfloat16)
    output = lax.dot_general(normed, w_ref[...], (((0,), (0,)), ((), ())), preferred_element_type=jnp.float32)
    output = restore(output, out_ref.shape[0], out_ref.shape[1])
    out_ref[...] = (gate_ref[...] * output).astype(jnp.bfloat16).reshape(out_ref.shape)


def per_device(rows, cols, halves, pair, token_mask, gain_in, bias_in, w_in, w_gate, gain_out, bias_out, w_out):
    row_count, col_count, channels = pair.shape
    hidden = w_out.shape[0]
    devices = rows * cols
    near = devices // halves
    quads = rows // halves
    far_order = []
    for col in reversed(range(cols)):
        ahead = list(range(quads)) if col else list(range(1, quads)) + [0]
        behind = [0] + list(reversed(range(1, quads))) if col else list(reversed(range(quads)))
        for quad, other in zip(ahead, behind):
            far_order += [near + other * cols + col, quad * cols + col]
    share = hidden // near
    tokens = row_count * col_count
    length = rows * row_count
    depth = length // halves
    token_mask = token_mask.reshape(1, length)
    near_order = [quad * cols + col for col in range(cols) for quad in range(quads)]
    packed = 2 * share * tokens // LANES
    cost = pl.CostEstimate(flops=2 * tokens * channels * 4 * hidden, bytes_accessed=16 * tokens * channels, transcendentals=0)
    other_pair = lax.ppermute(pair, "col", [(i, (i + 1) % cols) for i in range(cols)])
    arguments = (pair, gain_in.reshape(1, channels), bias_in.reshape(1, channels), w_in, token_mask)
    sides, normed, spread, mask, *weights = pl.pallas_call(
        functools.partial(own_kernel, quads, cols),
        out_shape=(
            jax.ShapeDtypeStruct((quads, packed, LANES), jnp.bfloat16),
            jax.ShapeDtypeStruct((tokens, channels), jnp.bfloat16),
            jax.ShapeDtypeStruct((GROUP, GROUP * depth), jnp.float32),
            jax.ShapeDtypeStruct((length, 1), jnp.float32),
            jax.ShapeDtypeStruct((channels, 4 * hidden // cols), jnp.bfloat16),
            jax.ShapeDtypeStruct((1, channels), jnp.float32),
            jax.ShapeDtypeStruct((1, channels), jnp.float32),
        ),
        in_specs=[HBM] * 5,
        out_specs=(VMEM,) * 7,
        scratch_shapes=[
            pltpu.VMEM(pair.shape, pair.dtype),
            pltpu.VMEM(w_in.shape, w_in.dtype),
            pltpu.VMEM((1, length), jnp.int32),
            pltpu.SemaphoreType.DMA((8,)),
        ],
        compiler_params=LIMIT,
        cost_estimate=cost,
    )(*(pltpu.with_memory_space_constraint(x, pltpu.HBM) for x in arguments))
    w_ours, gain_in, bias_in = weights
    pieces = pl.pallas_call(
        other_kernel,
        out_shape=[jax.ShapeDtypeStruct((cols, packed, LANES), jnp.bfloat16)] * quads,
        in_specs=[VMEM] * 5,
        out_specs=[VMEM] * quads,
        scratch_shapes=[pltpu.VMEM((quads, packed, LANES), jnp.bfloat16)],
        compiler_params=LIMIT,
        cost_estimate=cost,
    )(other_pair, sides, gain_in, bias_in, w_ours)
    steps = [3, 1, 2, 0]
    got = [lax.ppermute(pieces[step], "quad", [(i, i ^ step) for i in range(quads)]) if step else pieces[0] for step in steps]
    total = pl.pallas_call(
        functools.partial(triangle_kernel, far_order, steps, cols, row_count, col_count, share),
        out_shape=jax.ShapeDtypeStruct((devices, share * tokens // LANES, LANES), jnp.bfloat16),
        in_specs=[VMEM] * (quads + 2),
        out_specs=VMEM,
        compiler_params=LIMIT,
    )(*got, spread, mask)
    gate, gain_out, bias_out = pl.pallas_call(
        gate_kernel,
        out_shape=(
            jax.ShapeDtypeStruct((tokens, channels), jnp.float32),
            jax.ShapeDtypeStruct((hidden, 1), jnp.float32),
            jax.ShapeDtypeStruct((hidden, 1), jnp.float32),
        ),
        in_specs=[VMEM] * 4,
        out_specs=(VMEM, VMEM, VMEM),
        compiler_params=LIMIT,
        cost_estimate=pl.CostEstimate(flops=2 * tokens * channels * channels, bytes_accessed=4 * tokens * channels, transcendentals=0),
    )(normed, w_gate, gain_out.reshape(1, hidden), bias_out.reshape(1, hidden))
    total = lax.all_to_all(total, ("half", "quad", "col"), split_axis=0, concat_axis=0, tiled=True, axis_index_groups=[far_order])
    return pl.pallas_call(
        functools.partial(output_kernel, far_order, near_order),
        out_shape=jax.ShapeDtypeStruct(pair.shape, jnp.bfloat16),
        in_specs=[VMEM] * 5,
        out_specs=VMEM,
        compiler_params=LIMIT,
    )(total, gate, gain_out, bias_out, w_out)


def plain_per_device(rows, cols, pair, token_mask, gain_in, bias_in, w_in, w_gate, gain_out, bias_out, w_out):
    row_count, col_count, channels = pair.shape
    hidden = w_out.shape[0]
    devices = rows * cols
    share = hidden // devices
    tokens = row_count * col_count
    row_start = lax.axis_index(("half", "quad")) * row_count
    col_start = lax.axis_index("col") * col_count
    mask_float = token_mask.astype(jnp.float32)
    mask_rows = lax.dynamic_slice_in_dim(mask_float, row_start, row_count)
    mask_cols = lax.dynamic_slice_in_dim(mask_float, col_start, col_count)
    pair_mask = (mask_rows[:, None] * mask_cols[None, :]).reshape(1, tokens)
    flat = pair.reshape(tokens, channels).astype(jnp.float32)
    normed = layer_norm(flat, gain_in, bias_in, -1).astype(jnp.bfloat16)
    projected = lax.dot_general(w_in, normed, (((0,), (1,)), ((), ())), preferred_element_type=jnp.float32)
    projected = projected.reshape(2, 2, hidden, tokens)
    sides = (pair_mask * jax.nn.sigmoid(projected[:, 0]) * projected[:, 1]).astype(jnp.bfloat16)
    sides = sides.reshape(2, devices, share, tokens).transpose(1, 0, 2, 3)
    gate = jax.nn.sigmoid(jnp.dot(normed, w_gate, preferred_element_type=jnp.float32))
    got = lax.all_to_all(sides, AXES, split_axis=0, concat_axis=0, tiled=True)
    got = got.reshape(rows, cols, 2, share, row_count, col_count).transpose(2, 3, 0, 4, 1, 5)
    got = got.reshape(2, share, rows * row_count, cols * col_count)
    total = jnp.einsum("cki,ckj->cij", got[0], got[1], preferred_element_type=jnp.float32).astype(jnp.bfloat16)
    total = total.reshape(share, rows, row_count, cols, col_count).transpose(1, 3, 0, 2, 4)
    total = total.reshape(devices, share, tokens)
    total = lax.all_to_all(total, AXES, split_axis=0, concat_axis=0, tiled=True)
    total = total.reshape(hidden, tokens).astype(jnp.float32)
    summed_norm = layer_norm(total, gain_out[:, None], bias_out[:, None], 0).astype(jnp.bfloat16)
    output = lax.dot_general(summed_norm, w_out, (((0,), (0,)), ((), ())), preferred_element_type=jnp.float32)
    return (gate * output).astype(jnp.bfloat16).reshape(row_count, col_count, channels)


def solution(mesh):
    rows, cols = mesh.shape["row"], mesh.shape["col"]
    halves = 2
    parts = (mesh.shape["groups"], halves, rows // halves, cols)
    finer = jax.sharding.Mesh(mesh.devices.reshape(parts), ("groups", "half", "quad", "col"))

    def per_shard(*args):
        near, hidden, length = rows * cols // halves, args[-1].shape[0], args[1].shape[0]
        row_count, col_count, _ = args[0].shape
        spare = LANES - 2 * col_count
        fits = hidden % (2 * GROUP * near) == 0 and cols == 2 and rows // halves == 4 and length <= LANES and row_count % 3 == 0
        fits = fits and 0 < spare < col_count and row_count // 3 * (col_count - spare) * 2 == LANES
        fits = fits and row_count // 3 * (rows // halves) * GROUP == LANES
        return per_device(rows, cols, halves, *args) if fits else plain_per_device(rows, cols, *args)

    tokens = P(("groups", "half", "quad"), "col", None)
    in_specs = (tokens, P("groups"), P(), P(), P(), P(), P(), P(), P())
    return jax.shard_map(per_shard, mesh=finer, in_specs=in_specs, out_specs=tokens, check_vma=False)
```

```python
import functools

import jax
import jax.numpy as jnp
from jax import lax
from jax.experimental import pallas as pl
from jax.experimental.pallas import tpu as pltpu
from jax.sharding import PartitionSpec as P

epsilon = 1e-05
LANES = 128
GROUP = 8
AXES = ("half", "quad", "col")
VMEM = pl.BlockSpec(memory_space=pltpu.VMEM)
HBM = pl.BlockSpec(memory_space=pltpu.HBM)
LIMIT = pltpu.CompilerParams(vmem_limit_bytes=32 * 1024 * 1024)


def sigmoid(x):
    return 0.5 * jnp.tanh(0.5 * x) + 0.5


def layer_norm(values, gain, bias, axis):
    mean = jnp.mean(values, axis=axis, keepdims=True)
    centred = values - mean
    variance = jnp.mean(centred * centred, axis=axis, keepdims=True)
    return centred * lax.rsqrt(variance + epsilon) * gain + bias


def column(row):
    n = row.shape[1]
    eye = lax.broadcasted_iota(jnp.int32, (n, n), 0) == lax.broadcasted_iota(jnp.int32, (n, n), 1)
    return jnp.sum(jnp.where(eye, row, 0.0), axis=1, keepdims=True)


def pack(x):
    rows, tokens = x.shape[-2:]
    whole, rest = divmod(tokens, LANES)
    blocks = [x[..., t * LANES : (t + 1) * LANES] for t in range(whole)]
    if rest:
        tail = x[..., whole * LANES :]
        blocks.append(jnp.concatenate([tail[..., : rows // 2, :], tail[..., rows // 2 :, :]], axis=-1))
    return jnp.concatenate(blocks, axis=-2)


def unpack(x, rows):
    whole, rest = divmod(x.shape[-2], rows)
    blocks = [x[..., t * rows : (t + 1) * rows, :] for t in range(whole)]
    if rest:
        tail = x[..., whole * rows :, :]
        blocks.append(jnp.concatenate([tail[..., : LANES // 2], tail[..., LANES // 2 :]], axis=-2))
    return jnp.concatenate(blocks, axis=-1)


def arrange(x):
    row_count, col_count, _ = x.shape
    whole, spare = row_count // 3, LANES - 2 * col_count
    blocks = []
    for t in range(whole):
        blocks += [x[2 * t], x[2 * t + 1], x[2 * whole + t, :spare]]
    return jnp.concatenate(blocks + [x[2 * whole + t, spare:] for t in range(whole)], axis=0)


def restore(x, row_count, col_count):
    whole, spare = row_count // 3, LANES - 2 * col_count
    rest = col_count - spare
    rows = []
    for t in range(whole):
        rows += [x[t * LANES : t * LANES + col_count], x[t * LANES + col_count : t * LANES + 2 * col_count]]
    for t in range(whole):
        tail = whole * LANES + t * rest
        rows += [x[t * LANES + 2 * col_count : (t + 1) * LANES], x[tail : tail + rest]]
    return jnp.concatenate(rows, axis=0)


def normalise(flat, gain, bias):
    return layer_norm(flat.astype(jnp.float32), gain, bias, -1).astype(jnp.bfloat16)


def project(normed, w, shape, quads):
    ours = w.shape[1] // 4
    tokens = normed.shape[0]
    projected = lax.dot_general(w, arrange(normed.reshape(shape)), (((0,), (1,)), ((), ())), preferred_element_type=jnp.float32)
    left = sigmoid(projected[:ours]) * projected[ours : 2 * ours]
    right = sigmoid(projected[2 * ours : 3 * ours]) * projected[3 * ours :]
    sides = jnp.concatenate([left.reshape(quads, -1, tokens), right.reshape(quads, -1, tokens)], axis=1)
    return pack(sides).astype(jnp.bfloat16)


def own_kernel(quads, cols, pair_hbm, gain_hbm, bias_hbm, w_hbm, sides_ref, normed_ref, w_ref, gain_ref, bias_ref, pair_ref, all_w_ref, sems):
    moves = [(pair_hbm, pair_ref), (gain_hbm, gain_ref), (bias_hbm, bias_ref), (w_hbm, all_w_ref)]
    copies = [pltpu.make_async_copy(source, target, sems.at[n]) for n, (source, target) in enumerate(moves)]
    for copy in copies:
        copy.start()
    my_col = lax.axis_index("col")
    hidden = all_w_ref.shape[1] // 4
    ours = hidden // cols
    for copy in copies[:3]:
        copy.wait()
    normed = normalise(pair_ref[...].reshape(normed_ref.shape), gain_ref[...], bias_ref[...])
    normed_ref[...] = normed
    copies[3].wait()
    parts = [all_w_ref[:, at : at + hidden] for at in range(0, 4 * hidden, hidden)]
    w = jnp.concatenate([jnp.where(my_col == 0, part[:, :ours], part[:, ours:]) for part in parts], axis=1)
    w_ref[...] = w
    sides_ref[...] = project(normed, w, pair_ref.shape, quads)


def mask_kernel(quads, row_count, mask_ref, after_ref, spread_ref, column_mask_ref):
    del after_ref
    group, lanes = spread_ref.shape
    mask_row = mask_ref[...].astype(jnp.float32)
    column_mask_ref[...] = column(mask_row)
    start = lax.axis_index("half") * (lanes // group)
    token = lax.broadcasted_iota(jnp.int32, (mask_row.shape[1], lanes), 0)
    lane = lax.broadcasted_iota(jnp.int32, (mask_row.shape[1], lanes), 1)
    whole = row_count // 3
    block, t, row = lane // LANES, lane // (quads * group) % whole, lane // group % quads
    k = (row ^ lax.axis_index("quad")) * row_count + jnp.where(block < 2, 2 * t + block, 2 * whole + t)
    pick = jnp.where(k + start == token, 1.0, 0.0)
    kept = jnp.dot(mask_row.astype(jnp.bfloat16), pick.astype(jnp.bfloat16), preferred_element_type=jnp.float32)
    channel = lax.broadcasted_iota(jnp.int32, (group, lanes), 0)
    lane = lax.broadcasted_iota(jnp.int32, (group, lanes), 1)
    spread_ref[...] = jnp.where(lane % group == channel, kept, 0.0)


def other_kernel(pair_ref, sides_ref, gain_ref, bias_ref, w_ref, *refs):
    *piece_refs, others_ref = refs
    my_quad, my_col = lax.axis_index("quad"), lax.axis_index("col")
    quads = sides_ref.shape[0]
    normed = normalise(pair_ref[...].reshape(-1, pair_ref.shape[2]), gain_ref[...], bias_ref[...])
    others_ref[...] = project(normed, w_ref[...], pair_ref.shape, quads)
    for step, piece_ref in enumerate(piece_refs):
        piece_ref[my_col] = sides_ref[my_quad ^ step]
        piece_ref[1 - my_col] = others_ref[my_quad ^ step]


def triangle_kernel(far_order, steps, cols, row_count, col_count, share, *refs):
    *got_refs, spread_ref, mask_ref, total_ref = refs
    got_refs = {step: ref for step, ref in zip(steps, got_refs)}
    both = 2 * share
    group, lanes = spread_ref.shape
    length = mask_ref.shape[0]
    rows, quads, parts = length // row_count, len(steps), share // group
    whole, spare = row_count // 3, LANES - 2 * col_count
    rest = col_count - spare
    blocks = [[got_refs[row][col].astype(jnp.float32) for row in range(quads)] for col in range(cols)]

    def turned(picks):
        return jnp.concatenate([blocks[col][row][at : at + group] for col, row, at in picks], axis=0).T

    tail = turned([(col, row, whole * both + part * group) for col in range(cols) for part in range(parts) for row in range(quads)])

    def side(which, part):
        even, odd, third = [], [], []
        for col in range(cols):
            at = which * share + part * group
            block = turned([(col, row, t * both + at) for t in range(whole) for row in range(quads)])
            even.append(block[:col_count])
            odd.append(block[col_count : 2 * col_count])
            lane = (col * parts + part) * quads * group
            at = which * LANES // 2
            last = [tail[at + t * rest : at + (t + 1) * rest, lane : lane + quads * group] for t in range(whole)]
            third += [block[2 * col_count :], jnp.concatenate(last, axis=1)]
        tokens = [jnp.concatenate(pieces, axis=0) for pieces in (even, odd, third)]
        return jnp.concatenate(tokens, axis=1) * mask_ref[...]

    def placed(pieces):
        return jnp.concatenate([jnp.zeros((piece, lanes), jnp.bfloat16) if isinstance(piece, int) else piece for piece in pieces], axis=0)

    contract = (((1,), (1,)), ((), ()))
    mains, lasts = [], []
    for part in range(parts):
        left, right = side(0, part), side(1, part).astype(jnp.bfloat16)
        left = (left[:, None, :] * spread_ref[...][None]).reshape(rows, row_count, group, lanes)
        pairs = left[:, : 2 * whole].reshape(rows, whole, 2, group, lanes)
        left = jnp.concatenate([pairs[:, :, 0], pairs[:, :, 1], left[:, 2 * whole :]], axis=-1)
        left = left.reshape(rows * whole * group, 3 * lanes).astype(jnp.bfloat16)
        ours = [right[col * col_count : (col + 1) * col_count] for col in range(cols)]
        weights = [
            placed([p for mine in ours for p in (mine, LANES - col_count)]),
            placed([p for mine in ours for p in (col_count, mine, spare)]),
            placed([p for mine in ours for p in (2 * col_count, mine[:spare])]),
        ]
        weights = jnp.concatenate(weights, axis=1)
        mains.append(lax.dot_general(left, weights, contract, preferred_element_type=jnp.float32))
        weights = jnp.concatenate([mine[spare:] for mine in ours], axis=0)
        lasts.append(lax.dot_general(left[:, 2 * lanes :], weights, contract, preferred_element_type=jnp.float32))
    for target, device in enumerate(far_order):
        row, col = divmod(device, cols)
        spots = [(row * whole + t) * group for t in range(whole)]
        tiles = [main[at : at + group, col * LANES : (col + 1) * LANES] for at in spots for main in mains]
        last = [part[at : at + group, col * rest : (col + 1) * rest] for part in lasts for at in spots]
        tiles.append(jnp.concatenate(last, axis=1))
        total_ref[target] = jnp.concatenate(tiles, axis=0).astype(jnp.bfloat16)


def gate_kernel(normed_ref, w_ref, gain_ref, bias_ref, gate_ref, gain_out_ref, bias_out_ref):
    gate_ref[...] = sigmoid(jnp.dot(normed_ref[...], w_ref[...], preferred_element_type=jnp.float32))
    gain_out_ref[...] = column(gain_ref[...])
    bias_out_ref[...] = column(bias_ref[...])


def output_kernel(far_order, near_order, total_ref, gate_ref, gain_ref, bias_ref, w_ref, out_ref):
    tokens = gate_ref.shape[0]
    hidden = w_ref.shape[0]
    near = len(near_order)
    share = hidden // near
    blocks = []
    for index in near_order:
        parts = [total_ref[source].astype(jnp.float32) for source, device in enumerate(far_order) if device % near == index]
        blocks.append(unpack(sum(parts[1:], parts[0]), share))
    total = jnp.concatenate(blocks, axis=0)
    normed = layer_norm(total, gain_ref[...], bias_ref[...], 0).astype(jnp.bfloat16)
    output = lax.dot_general(normed, w_ref[...], (((0,), (0,)), ((), ())), preferred_element_type=jnp.float32)
    output = restore(output, out_ref.shape[0], out_ref.shape[1])
    out_ref[...] = (gate_ref[...] * output).astype(jnp.bfloat16).reshape(out_ref.shape)


def per_device(rows, cols, halves, pair, token_mask, gain_in, bias_in, w_in, w_gate, gain_out, bias_out, w_out):
    row_count, col_count, channels = pair.shape
    hidden = w_out.shape[0]
    devices = rows * cols
    near = devices // halves
    quads = rows // halves
    far_order = []
    for col in reversed(range(cols)):
        ahead = list(range(quads)) if col else list(range(1, quads)) + [0]
        behind = [0] + list(reversed(range(1, quads))) if col else list(reversed(range(quads)))
        for quad, other in zip(ahead, behind):
            far_order += [near + other * cols + col, quad * cols + col]
    share = hidden // near
    tokens = row_count * col_count
    length = rows * row_count
    depth = length // halves
    token_mask = token_mask.reshape(1, length)
    near_order = [quad * cols + col for col in range(cols) for quad in range(quads)]
    packed = 2 * share * tokens // LANES
    cost = pl.CostEstimate(flops=2 * tokens * channels * 4 * hidden, bytes_accessed=16 * tokens * channels, transcendentals=0)
    other_pair = lax.ppermute(pair, "col", [(i, (i + 1) % cols) for i in range(cols)])
    arguments = (pair, gain_in.reshape(1, channels), bias_in.reshape(1, channels), w_in)
    sides, normed, *weights = pl.pallas_call(
        functools.partial(own_kernel, quads, cols),
        out_shape=(
            jax.ShapeDtypeStruct((quads, packed, LANES), jnp.bfloat16),
            jax.ShapeDtypeStruct((tokens, channels), jnp.bfloat16),
            jax.ShapeDtypeStruct((channels, 4 * hidden // cols), jnp.bfloat16),
            jax.ShapeDtypeStruct((1, channels), jnp.float32),
            jax.ShapeDtypeStruct((1, channels), jnp.float32),
        ),
        in_specs=[HBM] * 4,
        out_specs=(VMEM,) * 5,
        scratch_shapes=[
            pltpu.VMEM(pair.shape, pair.dtype),
            pltpu.VMEM(w_in.shape, w_in.dtype),
            pltpu.SemaphoreType.DMA((4,)),
        ],
        compiler_params=LIMIT,
        cost_estimate=cost,
    )(*(pltpu.with_memory_space_constraint(x, pltpu.HBM) for x in arguments))
    w_ours, gain_in, bias_in = weights
    pieces = pl.pallas_call(
        other_kernel,
        out_shape=[jax.ShapeDtypeStruct((cols, packed, LANES), jnp.bfloat16)] * quads,
        in_specs=[VMEM] * 5,
        out_specs=[VMEM] * quads,
        scratch_shapes=[pltpu.VMEM((quads, packed, LANES), jnp.bfloat16)],
        compiler_params=LIMIT,
        cost_estimate=cost,
    )(other_pair, sides, gain_in, bias_in, w_ours)
    spread, mask = pl.pallas_call(
        functools.partial(mask_kernel, quads, row_count),
        out_shape=(
            jax.ShapeDtypeStruct((GROUP, GROUP * depth), jnp.float32),
            jax.ShapeDtypeStruct((length, 1), jnp.float32),
        ),
        in_specs=[VMEM, VMEM],
        out_specs=(VMEM, VMEM),
        compiler_params=LIMIT,
    )(token_mask, pieces[0])
    steps = [3, 1, 2, 0]
    got = [lax.ppermute(pieces[step], "quad", [(i, i ^ step) for i in range(quads)]) if step else pieces[0] for step in steps]
    total = pl.pallas_call(
        functools.partial(triangle_kernel, far_order, steps, cols, row_count, col_count, share),
        out_shape=jax.ShapeDtypeStruct((devices, share * tokens // LANES, LANES), jnp.bfloat16),
        in_specs=[VMEM] * (quads + 2),
        out_specs=VMEM,
        compiler_params=LIMIT,
    )(*got, spread, mask)
    gate, gain_out, bias_out = pl.pallas_call(
        gate_kernel,
        out_shape=(
            jax.ShapeDtypeStruct((tokens, channels), jnp.float32),
            jax.ShapeDtypeStruct((hidden, 1), jnp.float32),
            jax.ShapeDtypeStruct((hidden, 1), jnp.float32),
        ),
        in_specs=[VMEM] * 4,
        out_specs=(VMEM, VMEM, VMEM),
        compiler_params=LIMIT,
        cost_estimate=pl.CostEstimate(flops=2 * tokens * channels * channels, bytes_accessed=4 * tokens * channels, transcendentals=0),
    )(normed, w_gate, gain_out.reshape(1, hidden), bias_out.reshape(1, hidden))
    total = lax.all_to_all(total, ("half", "quad", "col"), split_axis=0, concat_axis=0, tiled=True, axis_index_groups=[far_order])
    return pl.pallas_call(
        functools.partial(output_kernel, far_order, near_order),
        out_shape=jax.ShapeDtypeStruct(pair.shape, jnp.bfloat16),
        in_specs=[VMEM] * 5,
        out_specs=VMEM,
        compiler_params=LIMIT,
    )(total, gate, gain_out, bias_out, w_out)


def plain_per_device(rows, cols, pair, token_mask, gain_in, bias_in, w_in, w_gate, gain_out, bias_out, w_out):
    row_count, col_count, channels = pair.shape
    hidden = w_out.shape[0]
    devices = rows * cols
    share = hidden // devices
    tokens = row_count * col_count
    row_start = lax.axis_index(("half", "quad")) * row_count
    col_start = lax.axis_index("col") * col_count
    mask_float = token_mask.astype(jnp.float32)
    mask_rows = lax.dynamic_slice_in_dim(mask_float, row_start, row_count)
    mask_cols = lax.dynamic_slice_in_dim(mask_float, col_start, col_count)
    pair_mask = (mask_rows[:, None] * mask_cols[None, :]).reshape(1, tokens)
    flat = pair.reshape(tokens, channels).astype(jnp.float32)
    normed = layer_norm(flat, gain_in, bias_in, -1).astype(jnp.bfloat16)
    projected = lax.dot_general(w_in, normed, (((0,), (1,)), ((), ())), preferred_element_type=jnp.float32)
    projected = projected.reshape(2, 2, hidden, tokens)
    sides = (pair_mask * jax.nn.sigmoid(projected[:, 0]) * projected[:, 1]).astype(jnp.bfloat16)
    sides = sides.reshape(2, devices, share, tokens).transpose(1, 0, 2, 3)
    gate = jax.nn.sigmoid(jnp.dot(normed, w_gate, preferred_element_type=jnp.float32))
    got = lax.all_to_all(sides, AXES, split_axis=0, concat_axis=0, tiled=True)
    got = got.reshape(rows, cols, 2, share, row_count, col_count).transpose(2, 3, 0, 4, 1, 5)
    got = got.reshape(2, share, rows * row_count, cols * col_count)
    total = jnp.einsum("cki,ckj->cij", got[0], got[1], preferred_element_type=jnp.float32).astype(jnp.bfloat16)
    total = total.reshape(share, rows, row_count, cols, col_count).transpose(1, 3, 0, 2, 4)
    total = total.reshape(devices, share, tokens)
    total = lax.all_to_all(total, AXES, split_axis=0, concat_axis=0, tiled=True)
    total = total.reshape(hidden, tokens).astype(jnp.float32)
    summed_norm = layer_norm(total, gain_out[:, None], bias_out[:, None], 0).astype(jnp.bfloat16)
    output = lax.dot_general(summed_norm, w_out, (((0,), (0,)), ((), ())), preferred_element_type=jnp.float32)
    return (gate * output).astype(jnp.bfloat16).reshape(row_count, col_count, channels)


def solution(mesh):
    rows, cols = mesh.shape["row"], mesh.shape["col"]
    halves = 2
    parts = (mesh.shape["groups"], halves, rows // halves, cols)
    finer = jax.sharding.Mesh(mesh.devices.reshape(parts), ("groups", "half", "quad", "col"))

    def per_shard(*args):
        near, hidden, length = rows * cols // halves, args[-1].shape[0], args[1].shape[0]
        row_count, col_count, _ = args[0].shape
        spare = LANES - 2 * col_count
        fits = hidden % (2 * GROUP * near) == 0 and cols == 2 and rows // halves == 4 and length <= LANES and row_count % 3 == 0
        fits = fits and 0 < spare < col_count and row_count // 3 * (col_count - spare) * 2 == LANES
        fits = fits and row_count // 3 * (rows // halves) * GROUP == LANES
        return per_device(rows, cols, halves, *args) if fits else plain_per_device(rows, cols, *args)

    tokens = P(("groups", "half", "quad"), "col", None)
    in_specs = (tokens, P("groups"), P(), P(), P(), P(), P(), P(), P())
    return jax.shard_map(per_shard, mesh=finer, in_specs=in_specs, out_specs=tokens, check_vma=False)
```

```python
import functools

import jax
import jax.numpy as jnp
from jax import lax
from jax.experimental import pallas as pl
from jax.experimental.pallas import tpu as pltpu
from jax.sharding import PartitionSpec as P

epsilon = 1e-05
LANES = 128
GROUP = 8
AXES = ("half", "quad", "col")
VMEM = pl.BlockSpec(memory_space=pltpu.VMEM)
HBM = pl.BlockSpec(memory_space=pltpu.HBM)
LIMIT = pltpu.CompilerParams(vmem_limit_bytes=32 * 1024 * 1024)


def sigmoid(x):
    return 0.5 * jnp.tanh(0.5 * x) + 0.5


def layer_norm(values, gain, bias, axis):
    mean = jnp.mean(values, axis=axis, keepdims=True)
    centred = values - mean
    variance = jnp.mean(centred * centred, axis=axis, keepdims=True)
    return centred * lax.rsqrt(variance + epsilon) * gain + bias


def column(row):
    n = row.shape[1]
    eye = lax.broadcasted_iota(jnp.int32, (n, n), 0) == lax.broadcasted_iota(jnp.int32, (n, n), 1)
    return jnp.sum(jnp.where(eye, row, 0.0), axis=1, keepdims=True)


def pack(x):
    rows, tokens = x.shape[-2:]
    whole, rest = divmod(tokens, LANES)
    blocks = [x[..., t * LANES : (t + 1) * LANES] for t in range(whole)]
    if rest:
        tail = x[..., whole * LANES :]
        blocks.append(jnp.concatenate([tail[..., : rows // 2, :], tail[..., rows // 2 :, :]], axis=-1))
    return jnp.concatenate(blocks, axis=-2)


def unpack(x, rows):
    whole, rest = divmod(x.shape[-2], rows)
    blocks = [x[..., t * rows : (t + 1) * rows, :] for t in range(whole)]
    if rest:
        tail = x[..., whole * rows :, :]
        blocks.append(jnp.concatenate([tail[..., : LANES // 2], tail[..., LANES // 2 :]], axis=-2))
    return jnp.concatenate(blocks, axis=-1)


def arrange(x):
    row_count, col_count, _ = x.shape
    whole, spare = row_count // 3, LANES - 2 * col_count
    blocks = []
    for t in range(whole):
        blocks += [x[2 * t], x[2 * t + 1], x[2 * whole + t, :spare]]
    return jnp.concatenate(blocks + [x[2 * whole + t, spare:] for t in range(whole)], axis=0)


def restore(x, row_count, col_count):
    whole, spare = row_count // 3, LANES - 2 * col_count
    rest = col_count - spare
    rows = []
    for t in range(whole):
        rows += [x[t * LANES : t * LANES + col_count], x[t * LANES + col_count : t * LANES + 2 * col_count]]
    for t in range(whole):
        tail = whole * LANES + t * rest
        rows += [x[t * LANES + 2 * col_count : (t + 1) * LANES], x[tail : tail + rest]]
    return jnp.concatenate(rows, axis=0)


def normalise(flat, gain, bias):
    return layer_norm(flat.astype(jnp.float32), gain, bias, -1).astype(jnp.bfloat16)


def project(normed, w, shape, quads):
    ours = w.shape[1] // 4
    tokens = normed.shape[0]
    projected = lax.dot_general(w, arrange(normed.reshape(shape)), (((0,), (1,)), ((), ())), preferred_element_type=jnp.float32)
    left = sigmoid(projected[:ours]) * projected[ours : 2 * ours]
    right = sigmoid(projected[2 * ours : 3 * ours]) * projected[3 * ours :]
    sides = jnp.concatenate([left.reshape(quads, -1, tokens), right.reshape(quads, -1, tokens)], axis=1)
    return pack(sides).astype(jnp.bfloat16)


def own_kernel(pair_hbm, gain_hbm, bias_hbm, normed_ref, gain_ref, bias_ref, pair_ref, sems):
    moves = [(pair_hbm, pair_ref), (gain_hbm, gain_ref), (bias_hbm, bias_ref)]
    copies = [pltpu.make_async_copy(source, target, sems.at[n]) for n, (source, target) in enumerate(moves)]
    for copy in copies:
        copy.start()
    for copy in copies:
        copy.wait()
    normed_ref[...] = normalise(pair_ref[...].reshape(normed_ref.shape), gain_ref[...], bias_ref[...])


def mask_kernel(quads, row_count, mask_ref, after_ref, spread_ref, column_mask_ref):
    del after_ref
    group, lanes = spread_ref.shape
    mask_row = mask_ref[...].astype(jnp.float32)
    column_mask_ref[...] = column(mask_row)
    start = lax.axis_index("half") * (lanes // group)
    token = lax.broadcasted_iota(jnp.int32, (mask_row.shape[1], lanes), 0)
    lane = lax.broadcasted_iota(jnp.int32, (mask_row.shape[1], lanes), 1)
    whole = row_count // 3
    block, t, row = lane // LANES, lane // (quads * group) % whole, lane // group % quads
    k = (row ^ lax.axis_index("quad")) * row_count + jnp.where(block < 2, 2 * t + block, 2 * whole + t)
    pick = jnp.where(k + start == token, 1.0, 0.0)
    kept = jnp.dot(mask_row.astype(jnp.bfloat16), pick.astype(jnp.bfloat16), preferred_element_type=jnp.float32)
    channel = lax.broadcasted_iota(jnp.int32, (group, lanes), 0)
    lane = lax.broadcasted_iota(jnp.int32, (group, lanes), 1)
    spread_ref[...] = jnp.where(lane % group == channel, kept, 0.0)


def project_kernel(pair_ref, normed_ref, gain_ref, bias_ref, w_ref, *refs):
    *piece_refs, own_ref, other_ref = refs
    my_quad, my_col = lax.axis_index("quad"), lax.axis_index("col")
    quads = own_ref.shape[0]
    hidden = w_ref.shape[1] // 4
    ours = hidden // piece_refs[0].shape[0]
    parts = [w_ref[:, at : at + hidden] for at in range(0, 4 * hidden, hidden)]
    w = jnp.concatenate([jnp.where(my_col == 0, part[:, :ours], part[:, ours:]) for part in parts], axis=1)
    own_ref[...] = project(normed_ref[...], w, pair_ref.shape, quads)
    normed = normalise(pair_ref[...].reshape(normed_ref.shape), gain_ref[...], bias_ref[...])
    other_ref[...] = project(normed, w, pair_ref.shape, quads)
    for step, piece_ref in enumerate(piece_refs):
        piece_ref[my_col] = own_ref[my_quad ^ step]
        piece_ref[1 - my_col] = other_ref[my_quad ^ step]


def triangle_kernel(far_order, steps, cols, row_count, col_count, share, *refs):
    *got_refs, spread_ref, mask_ref, total_ref = refs
    got_refs = {step: ref for step, ref in zip(steps, got_refs)}
    both = 2 * share
    group, lanes = spread_ref.shape
    length = mask_ref.shape[0]
    rows, quads, parts = length // row_count, len(steps), share // group
    whole, spare = row_count // 3, LANES - 2 * col_count
    rest = col_count - spare
    blocks = [[got_refs[row][col].astype(jnp.float32) for row in range(quads)] for col in range(cols)]

    def turned(picks):
        return jnp.concatenate([blocks[col][row][at : at + group] for col, row, at in picks], axis=0).T

    tail = turned([(col, row, whole * both + part * group) for col in range(cols) for part in range(parts) for row in range(quads)])

    def side(which, part):
        even, odd, third = [], [], []
        for col in range(cols):
            at = which * share + part * group
            block = turned([(col, row, t * both + at) for t in range(whole) for row in range(quads)])
            even.append(block[:col_count])
            odd.append(block[col_count : 2 * col_count])
            lane = (col * parts + part) * quads * group
            at = which * LANES // 2
            last = [tail[at + t * rest : at + (t + 1) * rest, lane : lane + quads * group] for t in range(whole)]
            third += [block[2 * col_count :], jnp.concatenate(last, axis=1)]
        tokens = [jnp.concatenate(pieces, axis=0) for pieces in (even, odd, third)]
        return jnp.concatenate(tokens, axis=1) * mask_ref[...]

    def placed(pieces):
        return jnp.concatenate([jnp.zeros((piece, lanes), jnp.bfloat16) if isinstance(piece, int) else piece for piece in pieces], axis=0)

    contract = (((1,), (1,)), ((), ()))
    mains, lasts = [], []
    for part in range(parts):
        left, right = side(0, part), side(1, part).astype(jnp.bfloat16)
        left = (left[:, None, :] * spread_ref[...][None]).reshape(rows, row_count, group, lanes)
        pairs = left[:, : 2 * whole].reshape(rows, whole, 2, group, lanes)
        left = jnp.concatenate([pairs[:, :, 0], pairs[:, :, 1], left[:, 2 * whole :]], axis=-1)
        left = left.reshape(rows * whole * group, 3 * lanes).astype(jnp.bfloat16)
        ours = [right[col * col_count : (col + 1) * col_count] for col in range(cols)]
        weights = [
            placed([p for mine in ours for p in (mine, LANES - col_count)]),
            placed([p for mine in ours for p in (col_count, mine, spare)]),
            placed([p for mine in ours for p in (2 * col_count, mine[:spare])]),
        ]
        weights = jnp.concatenate(weights, axis=1)
        mains.append(lax.dot_general(left, weights, contract, preferred_element_type=jnp.float32))
        weights = jnp.concatenate([mine[spare:] for mine in ours], axis=0)
        lasts.append(lax.dot_general(left[:, 2 * lanes :], weights, contract, preferred_element_type=jnp.float32))
    for target, device in enumerate(far_order):
        row, col = divmod(device, cols)
        spots = [(row * whole + t) * group for t in range(whole)]
        tiles = [main[at : at + group, col * LANES : (col + 1) * LANES] for at in spots for main in mains]
        last = [part[at : at + group, col * rest : (col + 1) * rest] for part in lasts for at in spots]
        tiles.append(jnp.concatenate(last, axis=1))
        total_ref[target] = jnp.concatenate(tiles, axis=0).astype(jnp.bfloat16)


def gate_kernel(normed_ref, w_ref, gain_ref, bias_ref, gate_ref, gain_out_ref, bias_out_ref):
    gate_ref[...] = sigmoid(jnp.dot(normed_ref[...], w_ref[...], preferred_element_type=jnp.float32))
    gain_out_ref[...] = column(gain_ref[...])
    bias_out_ref[...] = column(bias_ref[...])


def output_kernel(far_order, near_order, total_ref, gate_ref, gain_ref, bias_ref, w_ref, out_ref):
    tokens = gate_ref.shape[0]
    hidden = w_ref.shape[0]
    near = len(near_order)
    share = hidden // near
    blocks = []
    for index in near_order:
        parts = [total_ref[source].astype(jnp.float32) for source, device in enumerate(far_order) if device % near == index]
        blocks.append(unpack(sum(parts[1:], parts[0]), share))
    total = jnp.concatenate(blocks, axis=0)
    normed = layer_norm(total, gain_ref[...], bias_ref[...], 0).astype(jnp.bfloat16)
    output = lax.dot_general(normed, w_ref[...], (((0,), (0,)), ((), ())), preferred_element_type=jnp.float32)
    output = restore(output, out_ref.shape[0], out_ref.shape[1])
    out_ref[...] = (gate_ref[...] * output).astype(jnp.bfloat16).reshape(out_ref.shape)


def per_device(rows, cols, halves, pair, token_mask, gain_in, bias_in, w_in, w_gate, gain_out, bias_out, w_out):
    row_count, col_count, channels = pair.shape
    hidden = w_out.shape[0]
    devices = rows * cols
    near = devices // halves
    quads = rows // halves
    far_order = []
    for col in reversed(range(cols)):
        ahead = list(range(quads)) if col else list(range(1, quads)) + [0]
        behind = [0] + list(reversed(range(1, quads))) if col else list(reversed(range(quads)))
        for quad, other in zip(ahead, behind):
            far_order += [near + other * cols + col, quad * cols + col]
    share = hidden // near
    tokens = row_count * col_count
    length = rows * row_count
    depth = length // halves
    token_mask = token_mask.reshape(1, length)
    near_order = [quad * cols + col for col in range(cols) for quad in range(quads)]
    packed = 2 * share * tokens // LANES
    cost = pl.CostEstimate(flops=2 * tokens * channels * 4 * hidden, bytes_accessed=16 * tokens * channels, transcendentals=0)
    other_pair = lax.ppermute(pair, "col", [(i, (i + 1) % cols) for i in range(cols)])
    arguments = (pair, gain_in.reshape(1, channels), bias_in.reshape(1, channels))
    normed, gain_in, bias_in = pl.pallas_call(
        own_kernel,
        out_shape=(
            jax.ShapeDtypeStruct((tokens, channels), jnp.bfloat16),
            jax.ShapeDtypeStruct((1, channels), jnp.float32),
            jax.ShapeDtypeStruct((1, channels), jnp.float32),
        ),
        in_specs=[HBM] * 3,
        out_specs=(VMEM,) * 3,
        scratch_shapes=[pltpu.VMEM(pair.shape, pair.dtype), pltpu.SemaphoreType.DMA((3,))],
        compiler_params=LIMIT,
        cost_estimate=cost,
    )(*(pltpu.with_memory_space_constraint(x, pltpu.HBM) for x in arguments))
    pieces = pl.pallas_call(
        project_kernel,
        out_shape=[jax.ShapeDtypeStruct((cols, packed, LANES), jnp.bfloat16)] * quads,
        in_specs=[VMEM] * 5,
        out_specs=[VMEM] * quads,
        scratch_shapes=[pltpu.VMEM((quads, packed, LANES), jnp.bfloat16)] * 2,
        compiler_params=LIMIT,
        cost_estimate=cost,
    )(other_pair, normed, gain_in, bias_in, w_in)
    spread, mask = pl.pallas_call(
        functools.partial(mask_kernel, quads, row_count),
        out_shape=(
            jax.ShapeDtypeStruct((GROUP, GROUP * depth), jnp.float32),
            jax.ShapeDtypeStruct((length, 1), jnp.float32),
        ),
        in_specs=[VMEM, VMEM],
        out_specs=(VMEM, VMEM),
        compiler_params=LIMIT,
    )(token_mask, pieces[0])
    steps = [3, 1, 2, 0]
    got = [lax.ppermute(pieces[step], "quad", [(i, i ^ step) for i in range(quads)]) if step else pieces[0] for step in steps]
    total = pl.pallas_call(
        functools.partial(triangle_kernel, far_order, steps, cols, row_count, col_count, share),
        out_shape=jax.ShapeDtypeStruct((devices, share * tokens // LANES, LANES), jnp.bfloat16),
        in_specs=[VMEM] * (quads + 2),
        out_specs=VMEM,
        compiler_params=LIMIT,
    )(*got, spread, mask)
    gate, gain_out, bias_out = pl.pallas_call(
        gate_kernel,
        out_shape=(
            jax.ShapeDtypeStruct((tokens, channels), jnp.float32),
            jax.ShapeDtypeStruct((hidden, 1), jnp.float32),
            jax.ShapeDtypeStruct((hidden, 1), jnp.float32),
        ),
        in_specs=[VMEM] * 4,
        out_specs=(VMEM, VMEM, VMEM),
        compiler_params=LIMIT,
        cost_estimate=pl.CostEstimate(flops=2 * tokens * channels * channels, bytes_accessed=4 * tokens * channels, transcendentals=0),
    )(normed, w_gate, gain_out.reshape(1, hidden), bias_out.reshape(1, hidden))
    total = lax.all_to_all(total, ("half", "quad", "col"), split_axis=0, concat_axis=0, tiled=True, axis_index_groups=[far_order])
    return pl.pallas_call(
        functools.partial(output_kernel, far_order, near_order),
        out_shape=jax.ShapeDtypeStruct(pair.shape, jnp.bfloat16),
        in_specs=[VMEM] * 5,
        out_specs=VMEM,
        compiler_params=LIMIT,
    )(total, gate, gain_out, bias_out, w_out)


def plain_per_device(rows, cols, pair, token_mask, gain_in, bias_in, w_in, w_gate, gain_out, bias_out, w_out):
    row_count, col_count, channels = pair.shape
    hidden = w_out.shape[0]
    devices = rows * cols
    share = hidden // devices
    tokens = row_count * col_count
    row_start = lax.axis_index(("half", "quad")) * row_count
    col_start = lax.axis_index("col") * col_count
    mask_float = token_mask.astype(jnp.float32)
    mask_rows = lax.dynamic_slice_in_dim(mask_float, row_start, row_count)
    mask_cols = lax.dynamic_slice_in_dim(mask_float, col_start, col_count)
    pair_mask = (mask_rows[:, None] * mask_cols[None, :]).reshape(1, tokens)
    flat = pair.reshape(tokens, channels).astype(jnp.float32)
    normed = layer_norm(flat, gain_in, bias_in, -1).astype(jnp.bfloat16)
    projected = lax.dot_general(w_in, normed, (((0,), (1,)), ((), ())), preferred_element_type=jnp.float32)
    projected = projected.reshape(2, 2, hidden, tokens)
    sides = (pair_mask * jax.nn.sigmoid(projected[:, 0]) * projected[:, 1]).astype(jnp.bfloat16)
    sides = sides.reshape(2, devices, share, tokens).transpose(1, 0, 2, 3)
    gate = jax.nn.sigmoid(jnp.dot(normed, w_gate, preferred_element_type=jnp.float32))
    got = lax.all_to_all(sides, AXES, split_axis=0, concat_axis=0, tiled=True)
    got = got.reshape(rows, cols, 2, share, row_count, col_count).transpose(2, 3, 0, 4, 1, 5)
    got = got.reshape(2, share, rows * row_count, cols * col_count)
    total = jnp.einsum("cki,ckj->cij", got[0], got[1], preferred_element_type=jnp.float32).astype(jnp.bfloat16)
    total = total.reshape(share, rows, row_count, cols, col_count).transpose(1, 3, 0, 2, 4)
    total = total.reshape(devices, share, tokens)
    total = lax.all_to_all(total, AXES, split_axis=0, concat_axis=0, tiled=True)
    total = total.reshape(hidden, tokens).astype(jnp.float32)
    summed_norm = layer_norm(total, gain_out[:, None], bias_out[:, None], 0).astype(jnp.bfloat16)
    output = lax.dot_general(summed_norm, w_out, (((0,), (0,)), ((), ())), preferred_element_type=jnp.float32)
    return (gate * output).astype(jnp.bfloat16).reshape(row_count, col_count, channels)


def solution(mesh):
    rows, cols = mesh.shape["row"], mesh.shape["col"]
    halves = 2
    parts = (mesh.shape["groups"], halves, rows // halves, cols)
    finer = jax.sharding.Mesh(mesh.devices.reshape(parts), ("groups", "half", "quad", "col"))

    def per_shard(*args):
        near, hidden, length = rows * cols // halves, args[-1].shape[0], args[1].shape[0]
        row_count, col_count, _ = args[0].shape
        spare = LANES - 2 * col_count
        fits = hidden % (2 * GROUP * near) == 0 and cols == 2 and rows // halves == 4 and length <= LANES and row_count % 3 == 0
        fits = fits and 0 < spare < col_count and row_count // 3 * (col_count - spare) * 2 == LANES
        fits = fits and row_count // 3 * (rows // halves) * GROUP == LANES
        return per_device(rows, cols, halves, *args) if fits else plain_per_device(rows, cols, *args)

    tokens = P(("groups", "half", "quad"), "col", None)
    in_specs = (tokens, P("groups"), P(), P(), P(), P(), P(), P(), P())
    return jax.shard_map(per_shard, mesh=finer, in_specs=in_specs, out_specs=tokens, check_vma=False)
```

```python
import functools

import jax
import jax.numpy as jnp
from jax import lax
from jax.experimental import pallas as pl
from jax.experimental.pallas import tpu as pltpu
from jax.sharding import PartitionSpec as P

epsilon = 1e-05
LANES = 128
GROUP = 8
AXES = ("half", "quad", "col")
VMEM = pl.BlockSpec(memory_space=pltpu.VMEM)
HBM = pl.BlockSpec(memory_space=pltpu.HBM)
LIMIT = pltpu.CompilerParams(vmem_limit_bytes=32 * 1024 * 1024)


def sigmoid(x):
    return 0.5 * jnp.tanh(0.5 * x) + 0.5


def layer_norm(values, gain, bias, axis):
    mean = jnp.mean(values, axis=axis, keepdims=True)
    centred = values - mean
    variance = jnp.mean(centred * centred, axis=axis, keepdims=True)
    return centred * lax.rsqrt(variance + epsilon) * gain + bias


def column(row):
    n = row.shape[1]
    eye = lax.broadcasted_iota(jnp.int32, (n, n), 0) == lax.broadcasted_iota(jnp.int32, (n, n), 1)
    return jnp.sum(jnp.where(eye, row, 0.0), axis=1, keepdims=True)


def pack(x):
    rows, tokens = x.shape[-2:]
    whole, rest = divmod(tokens, LANES)
    blocks = [x[..., t * LANES : (t + 1) * LANES] for t in range(whole)]
    if rest:
        tail = x[..., whole * LANES :]
        blocks.append(jnp.concatenate([tail[..., : rows // 2, :], tail[..., rows // 2 :, :]], axis=-1))
    return jnp.concatenate(blocks, axis=-2)


def unpack(x, rows):
    whole, rest = divmod(x.shape[-2], rows)
    blocks = [x[..., t * rows : (t + 1) * rows, :] for t in range(whole)]
    if rest:
        tail = x[..., whole * rows :, :]
        blocks.append(jnp.concatenate([tail[..., : LANES // 2], tail[..., LANES // 2 :]], axis=-2))
    return jnp.concatenate(blocks, axis=-1)


def arrange(x):
    row_count, col_count, _ = x.shape
    whole, spare = row_count // 3, LANES - 2 * col_count
    blocks = []
    for t in range(whole):
        blocks += [x[2 * t], x[2 * t + 1], x[2 * whole + t, :spare]]
    return jnp.concatenate(blocks + [x[2 * whole + t, spare:] for t in range(whole)], axis=0)


def restore(x, row_count, col_count):
    whole, spare = row_count // 3, LANES - 2 * col_count
    rest = col_count - spare
    rows = []
    for t in range(whole):
        rows += [x[t * LANES : t * LANES + col_count], x[t * LANES + col_count : t * LANES + 2 * col_count]]
    for t in range(whole):
        tail = whole * LANES + t * rest
        rows += [x[t * LANES + 2 * col_count : (t + 1) * LANES], x[tail : tail + rest]]
    return jnp.concatenate(rows, axis=0)


def normalise(flat, gain, bias):
    return layer_norm(flat.astype(jnp.float32), gain, bias, -1).astype(jnp.bfloat16)


def project(normed, w, shape, quads):
    ours = w.shape[1] // 4
    tokens = normed.shape[0]
    projected = lax.dot_general(w, arrange(normed.reshape(shape)), (((0,), (1,)), ((), ())), preferred_element_type=jnp.float32)
    left = sigmoid(projected[:ours]) * projected[ours : 2 * ours]
    right = sigmoid(projected[2 * ours : 3 * ours]) * projected[3 * ours :]
    sides = jnp.concatenate([left.reshape(quads, -1, tokens), right.reshape(quads, -1, tokens)], axis=1)
    return pack(sides).astype(jnp.bfloat16)


def own_kernel(quads, cols, pair_hbm, gain_hbm, bias_hbm, w_hbm, mask_hbm, sides_ref, normed_ref, spread_ref, column_mask_ref, w_ref, gain_ref, bias_ref, pair_ref, all_w_ref, mask_ref, sems):
    moves = [(mask_hbm, mask_ref), (pair_hbm, pair_ref), (gain_hbm, gain_ref), (bias_hbm, bias_ref), (w_hbm, all_w_ref)]
    copies = [pltpu.make_async_copy(source, target, sems.at[n]) for n, (source, target) in enumerate(moves)]
    for copy in copies:
        copy.start()
    my_quad, my_col = lax.axis_index("quad"), lax.axis_index("col")
    row_count, _, channels = pair_ref.shape
    tokens = normed_ref.shape[0]
    hidden = all_w_ref.shape[1] // 4
    ours = hidden // cols
    group, lanes = spread_ref.shape
    copies[0].wait()
    mask_row = mask_ref[...].astype(jnp.float32)
    column_mask_ref[...] = column(mask_row)
    start = lax.axis_index("half") * (lanes // group)
    token = lax.broadcasted_iota(jnp.int32, (mask_row.shape[1], lanes), 0)
    lane = lax.broadcasted_iota(jnp.int32, (mask_row.shape[1], lanes), 1)
    whole = row_count // 3
    block, t, row = lane // LANES, lane // (quads * group) % whole, lane // group % quads
    k = (row ^ my_quad) * row_count + jnp.where(block < 2, 2 * t + block, 2 * whole + t)
    pick = jnp.where(k + start == token, 1.0, 0.0)
    kept = jnp.dot(mask_row.astype(jnp.bfloat16), pick.astype(jnp.bfloat16), preferred_element_type=jnp.float32)
    channel = lax.broadcasted_iota(jnp.int32, (group, lanes), 0)
    lane = lax.broadcasted_iota(jnp.int32, (group, lanes), 1)
    spread_ref[...] = jnp.where(lane % group == channel, kept, 0.0)
    for copy in copies[1:4]:
        copy.wait()
    normed = normalise(pair_ref[...].reshape(tokens, channels), gain_ref[...], bias_ref[...])
    normed_ref[...] = normed
    copies[4].wait()
    parts = [all_w_ref[:, at : at + hidden] for at in range(0, 4 * hidden, hidden)]
    w = jnp.concatenate([jnp.where(my_col == 0, part[:, :ours], part[:, ours:]) for part in parts], axis=1)
    w_ref[...] = w
    sides_ref[...] = project(normed, w, pair_ref.shape, quads)


def other_kernel(pair_ref, sides_ref, gain_ref, bias_ref, w_ref, *refs):
    *piece_refs, others_ref = refs
    my_quad, my_col = lax.axis_index("quad"), lax.axis_index("col")
    quads = sides_ref.shape[0]
    normed = normalise(pair_ref[...].reshape(-1, pair_ref.shape[2]), gain_ref[...], bias_ref[...])
    others_ref[...] = project(normed, w_ref[...], pair_ref.shape, quads)
    for step, piece_ref in enumerate(piece_refs):
        piece_ref[my_col] = sides_ref[my_quad ^ step]
        piece_ref[1 - my_col] = others_ref[my_quad ^ step]


def triangle_kernel(far_order, steps, cols, row_count, col_count, share, *refs):
    *got_refs, spread_ref, mask_ref, total_ref = refs
    got_refs = {step: ref for step, ref in zip(steps, got_refs)}
    both = 2 * share
    group, lanes = spread_ref.shape
    length = mask_ref.shape[0]
    rows, quads, parts = length // row_count, len(steps), share // group
    whole, spare = row_count // 3, LANES - 2 * col_count
    rest = col_count - spare
    blocks = [[got_refs[row][col].astype(jnp.float32) for row in range(quads)] for col in range(cols)]

    def turned(picks):
        return jnp.concatenate([blocks[col][row][at : at + group] for col, row, at in picks], axis=0).T

    tail = turned([(col, row, whole * both + part * group) for col in range(cols) for part in range(parts) for row in range(quads)])

    def side(which, part):
        even, odd, third = [], [], []
        for col in range(cols):
            at = which * share + part * group
            block = turned([(col, row, t * both + at) for t in range(whole) for row in range(quads)])
            even.append(block[:col_count])
            odd.append(block[col_count : 2 * col_count])
            lane = (col * parts + part) * quads * group
            at = which * LANES // 2
            last = [tail[at + t * rest : at + (t + 1) * rest, lane : lane + quads * group] for t in range(whole)]
            third += [block[2 * col_count :], jnp.concatenate(last, axis=1)]
        tokens = [jnp.concatenate(pieces, axis=0) for pieces in (even, odd, third)]
        return jnp.concatenate(tokens, axis=1) * mask_ref[...]

    def placed(pieces):
        return jnp.concatenate([jnp.zeros((piece, lanes), jnp.bfloat16) if isinstance(piece, int) else piece for piece in pieces], axis=0)

    contract = (((1,), (1,)), ((), ()))
    lane_block = lax.broadcasted_iota(jnp.int32, (group, LANES), 1) // rest
    mains, lasts = [], []
    for part in range(parts):
        left, right = side(0, part), side(1, part).astype(jnp.bfloat16)
        left = (left[:, None, :] * spread_ref[...][None]).reshape(rows, row_count, group, lanes)
        pairs = left[:, : 2 * whole].reshape(rows, whole, 2, group, lanes)
        left = jnp.concatenate([pairs[:, :, 0], pairs[:, :, 1], left[:, 2 * whole :]], axis=-1)
        left = left.reshape(rows * whole * group, 3 * lanes).astype(jnp.bfloat16)
        ours = [right[col * col_count : (col + 1) * col_count] for col in range(cols)]
        weights = [
            placed([p for mine in ours for p in (mine, LANES - col_count)]),
            placed([p for mine in ours for p in (col_count, mine, spare)]),
            placed([p for mine in ours for p in (2 * col_count, mine[:spare])]),
        ]
        weights = jnp.concatenate(weights, axis=1)
        mains.append(lax.dot_general(left, weights, contract, preferred_element_type=jnp.float32))
        gap = LANES // parts
        pieces = [[gap * part] + [mine[spare:]] * whole + [LANES - gap * (part + 1)] for mine in ours]
        weights = placed([p for piece in pieces for p in piece if not isinstance(p, int) or p])
        lasts.append(lax.dot_general(left[:, 2 * lanes :], weights, contract, preferred_element_type=jnp.float32))
    for target, device in enumerate(far_order):
        row, col = divmod(device, cols)
        spots = [(row * whole + t) * group for t in range(whole)]
        tiles = [main[at : at + group, col * LANES : (col + 1) * LANES] for at in spots for main in mains]
        last = [part[at : at + group, col * LANES : (col + 1) * LANES] for part in lasts for at in spots]
        tile = last[0]
        for n in range(1, len(last)):
            tile = jnp.where(lane_block >= n, last[n], tile)
        tiles.append(tile)
        total_ref[target] = jnp.concatenate(tiles, axis=0).astype(jnp.bfloat16)


def gate_kernel(normed_ref, w_ref, gain_ref, bias_ref, gate_ref, gain_out_ref, bias_out_ref):
    gate_ref[...] = sigmoid(jnp.dot(normed_ref[...], w_ref[...], preferred_element_type=jnp.float32))
    gain_out_ref[...] = column(gain_ref[...])
    bias_out_ref[...] = column(bias_ref[...])


def output_kernel(far_order, near_order, total_ref, gate_ref, gain_ref, bias_ref, w_ref, out_ref):
    tokens = gate_ref.shape[0]
    hidden = w_ref.shape[0]
    near = len(near_order)
    share = hidden // near
    blocks = []
    for index in near_order:
        parts = [total_ref[source].astype(jnp.float32) for source, device in enumerate(far_order) if device % near == index]
        blocks.append(unpack(sum(parts[1:], parts[0]), share))
    total = jnp.concatenate(blocks, axis=0)
    normed = layer_norm(total, gain_ref[...], bias_ref[...], 0).astype(jnp.bfloat16)
    output = lax.dot_general(normed, w_ref[...], (((0,), (0,)), ((), ())), preferred_element_type=jnp.float32)
    output = restore(output, out_ref.shape[0], out_ref.shape[1])
    out_ref[...] = (gate_ref[...] * output).astype(jnp.bfloat16).reshape(out_ref.shape)


def per_device(rows, cols, halves, pair, token_mask, gain_in, bias_in, w_in, w_gate, gain_out, bias_out, w_out):
    row_count, col_count, channels = pair.shape
    hidden = w_out.shape[0]
    devices = rows * cols
    near = devices // halves
    quads = rows // halves
    far_order = []
    for col in reversed(range(cols)):
        ahead = list(range(quads)) if col else list(range(1, quads)) + [0]
        behind = [0] + list(reversed(range(1, quads))) if col else list(reversed(range(quads)))
        for quad, other in zip(ahead, behind):
            far_order += [near + other * cols + col, quad * cols + col]
    share = hidden // near
    tokens = row_count * col_count
    length = rows * row_count
    depth = length // halves
    token_mask = token_mask.reshape(1, length)
    near_order = [quad * cols + col for col in range(cols) for quad in range(quads)]
    packed = 2 * share * tokens // LANES
    cost = pl.CostEstimate(flops=2 * tokens * channels * 4 * hidden, bytes_accessed=16 * tokens * channels, transcendentals=0)
    other_pair = lax.ppermute(pair, "col", [(i, (i + 1) % cols) for i in range(cols)])
    arguments = (pair, gain_in.reshape(1, channels), bias_in.reshape(1, channels), w_in, token_mask)
    sides, normed, spread, mask, *weights = pl.pallas_call(
        functools.partial(own_kernel, quads, cols),
        out_shape=(
            jax.ShapeDtypeStruct((quads, packed, LANES), jnp.bfloat16),
            jax.ShapeDtypeStruct((tokens, channels), jnp.bfloat16),
            jax.ShapeDtypeStruct((GROUP, GROUP * depth), jnp.float32),
            jax.ShapeDtypeStruct((length, 1), jnp.float32),
            jax.ShapeDtypeStruct((channels, 4 * hidden // cols), jnp.bfloat16),
            jax.ShapeDtypeStruct((1, channels), jnp.float32),
            jax.ShapeDtypeStruct((1, channels), jnp.float32),
        ),
        in_specs=[HBM] * 5,
        out_specs=(VMEM,) * 7,
        scratch_shapes=[
            pltpu.VMEM(pair.shape, pair.dtype),
            pltpu.VMEM(w_in.shape, w_in.dtype),
            pltpu.VMEM((1, length), jnp.int32),
            pltpu.SemaphoreType.DMA((5,)),
        ],
        compiler_params=LIMIT,
        cost_estimate=cost,
    )(*(pltpu.with_memory_space_constraint(x, pltpu.HBM) for x in arguments))
    w_ours, gain_in, bias_in = weights
    pieces = pl.pallas_call(
        other_kernel,
        out_shape=[jax.ShapeDtypeStruct((cols, packed, LANES), jnp.bfloat16)] * quads,
        in_specs=[VMEM] * 5,
        out_specs=[VMEM] * quads,
        scratch_shapes=[pltpu.VMEM((quads, packed, LANES), jnp.bfloat16)],
        compiler_params=LIMIT,
        cost_estimate=cost,
    )(other_pair, sides, gain_in, bias_in, w_ours)
    steps = [3, 2, 1, 0]
    got = [lax.ppermute(pieces[step], "quad", [(i, i ^ step) for i in range(quads)]) if step else pieces[0] for step in steps]
    total = pl.pallas_call(
        functools.partial(triangle_kernel, far_order, steps, cols, row_count, col_count, share),
        out_shape=jax.ShapeDtypeStruct((devices, share * tokens // LANES, LANES), jnp.bfloat16),
        in_specs=[VMEM] * (quads + 2),
        out_specs=VMEM,
        compiler_params=LIMIT,
    )(*got, spread, mask)
    gate, gain_out, bias_out = pl.pallas_call(
        gate_kernel,
        out_shape=(
            jax.ShapeDtypeStruct((tokens, channels), jnp.float32),
            jax.ShapeDtypeStruct((hidden, 1), jnp.float32),
            jax.ShapeDtypeStruct((hidden, 1), jnp.float32),
        ),
        in_specs=[VMEM] * 4,
        out_specs=(VMEM, VMEM, VMEM),
        compiler_params=LIMIT,
        cost_estimate=pl.CostEstimate(flops=2 * tokens * channels * channels, bytes_accessed=4 * tokens * channels, transcendentals=0),
    )(normed, w_gate, gain_out.reshape(1, hidden), bias_out.reshape(1, hidden))
    total = lax.all_to_all(total, ("half", "quad", "col"), split_axis=0, concat_axis=0, tiled=True, axis_index_groups=[far_order])
    return pl.pallas_call(
        functools.partial(output_kernel, far_order, near_order),
        out_shape=jax.ShapeDtypeStruct(pair.shape, jnp.bfloat16),
        in_specs=[VMEM] * 5,
        out_specs=VMEM,
        compiler_params=LIMIT,
    )(total, gate, gain_out, bias_out, w_out)


def plain_per_device(rows, cols, pair, token_mask, gain_in, bias_in, w_in, w_gate, gain_out, bias_out, w_out):
    row_count, col_count, channels = pair.shape
    hidden = w_out.shape[0]
    devices = rows * cols
    share = hidden // devices
    tokens = row_count * col_count
    row_start = lax.axis_index(("half", "quad")) * row_count
    col_start = lax.axis_index("col") * col_count
    mask_float = token_mask.astype(jnp.float32)
    mask_rows = lax.dynamic_slice_in_dim(mask_float, row_start, row_count)
    mask_cols = lax.dynamic_slice_in_dim(mask_float, col_start, col_count)
    pair_mask = (mask_rows[:, None] * mask_cols[None, :]).reshape(1, tokens)
    flat = pair.reshape(tokens, channels).astype(jnp.float32)
    normed = layer_norm(flat, gain_in, bias_in, -1).astype(jnp.bfloat16)
    projected = lax.dot_general(w_in, normed, (((0,), (1,)), ((), ())), preferred_element_type=jnp.float32)
    projected = projected.reshape(2, 2, hidden, tokens)
    sides = (pair_mask * jax.nn.sigmoid(projected[:, 0]) * projected[:, 1]).astype(jnp.bfloat16)
    sides = sides.reshape(2, devices, share, tokens).transpose(1, 0, 2, 3)
    gate = jax.nn.sigmoid(jnp.dot(normed, w_gate, preferred_element_type=jnp.float32))
    got = lax.all_to_all(sides, AXES, split_axis=0, concat_axis=0, tiled=True)
    got = got.reshape(rows, cols, 2, share, row_count, col_count).transpose(2, 3, 0, 4, 1, 5)
    got = got.reshape(2, share, rows * row_count, cols * col_count)
    total = jnp.einsum("cki,ckj->cij", got[0], got[1], preferred_element_type=jnp.float32).astype(jnp.bfloat16)
    total = total.reshape(share, rows, row_count, cols, col_count).transpose(1, 3, 0, 2, 4)
    total = total.reshape(devices, share, tokens)
    total = lax.all_to_all(total, AXES, split_axis=0, concat_axis=0, tiled=True)
    total = total.reshape(hidden, tokens).astype(jnp.float32)
    summed_norm = layer_norm(total, gain_out[:, None], bias_out[:, None], 0).astype(jnp.bfloat16)
    output = lax.dot_general(summed_norm, w_out, (((0,), (0,)), ((), ())), preferred_element_type=jnp.float32)
    return (gate * output).astype(jnp.bfloat16).reshape(row_count, col_count, channels)


def solution(mesh):
    rows, cols = mesh.shape["row"], mesh.shape["col"]
    halves = 2
    parts = (mesh.shape["groups"], halves, rows // halves, cols)
    finer = jax.sharding.Mesh(mesh.devices.reshape(parts), ("groups", "half", "quad", "col"))

    def per_shard(*args):
        near, hidden, length = rows * cols // halves, args[-1].shape[0], args[1].shape[0]
        row_count, col_count, _ = args[0].shape
        spare = LANES - 2 * col_count
        fits = hidden % (2 * GROUP * near) == 0 and cols == 2 and rows // halves == 4 and length <= LANES and row_count % 3 == 0
        fits = fits and 0 < spare < col_count and row_count // 3 * (col_count - spare) * 2 == LANES
        fits = fits and row_count // 3 * (rows // halves) * GROUP == LANES
        return per_device(rows, cols, halves, *args) if fits else plain_per_device(rows, cols, *args)

    tokens = P(("groups", "half", "quad"), "col", None)
    in_specs = (tokens, P("groups"), P(), P(), P(), P(), P(), P(), P())
    return jax.shard_map(per_shard, mesh=finer, in_specs=in_specs, out_specs=tokens, check_vma=False)
```

```python
import functools

import jax
import jax.numpy as jnp
from jax import lax
from jax.experimental import pallas as pl
from jax.experimental.pallas import tpu as pltpu
from jax.sharding import PartitionSpec as P

epsilon = 1e-05
LANES = 128
GROUP = 8
AXES = ("half", "quad", "col")
VMEM = pl.BlockSpec(memory_space=pltpu.VMEM)
HBM = pl.BlockSpec(memory_space=pltpu.HBM)
LIMIT = pltpu.CompilerParams(vmem_limit_bytes=32 * 1024 * 1024)


def sigmoid(x):
    return 0.5 * jnp.tanh(0.5 * x) + 0.5


def layer_norm(values, gain, bias, axis):
    mean = jnp.mean(values, axis=axis, keepdims=True)
    centred = values - mean
    variance = jnp.mean(centred * centred, axis=axis, keepdims=True)
    return centred * lax.rsqrt(variance + epsilon) * gain + bias


def column(row):
    n = row.shape[1]
    eye = lax.broadcasted_iota(jnp.int32, (n, n), 0) == lax.broadcasted_iota(jnp.int32, (n, n), 1)
    return jnp.sum(jnp.where(eye, row, 0.0), axis=1, keepdims=True)


def pack(x):
    rows, tokens = x.shape[-2:]
    whole, rest = divmod(tokens, LANES)
    blocks = [x[..., t * LANES : (t + 1) * LANES] for t in range(whole)]
    if rest:
        tail = x[..., whole * LANES :]
        blocks.append(jnp.concatenate([tail[..., : rows // 2, :], tail[..., rows // 2 :, :]], axis=-1))
    return jnp.concatenate(blocks, axis=-2)


def unpack(x, rows):
    whole, rest = divmod(x.shape[-2], rows)
    blocks = [x[..., t * rows : (t + 1) * rows, :] for t in range(whole)]
    if rest:
        tail = x[..., whole * rows :, :]
        blocks.append(jnp.concatenate([tail[..., : LANES // 2], tail[..., LANES // 2 :]], axis=-2))
    return jnp.concatenate(blocks, axis=-1)


def arrange(x):
    row_count, col_count, _ = x.shape
    whole, spare = row_count // 3, LANES - 2 * col_count
    blocks = []
    for t in range(whole):
        blocks += [x[2 * t], x[2 * t + 1], x[2 * whole + t, :spare]]
    return jnp.concatenate(blocks + [x[2 * whole + t, spare:] for t in range(whole)], axis=0)


def restore(x, row_count, col_count):
    whole, spare = row_count // 3, LANES - 2 * col_count
    rest = col_count - spare
    rows = []
    for t in range(whole):
        rows += [x[t * LANES : t * LANES + col_count], x[t * LANES + col_count : t * LANES + 2 * col_count]]
    for t in range(whole):
        tail = whole * LANES + t * rest
        rows += [x[t * LANES + 2 * col_count : (t + 1) * LANES], x[tail : tail + rest]]
    return jnp.concatenate(rows, axis=0)


def normalise(flat, gain, bias):
    return layer_norm(flat.astype(jnp.float32), gain, bias, -1).astype(jnp.bfloat16)


def project(normed, w, shape, quads):
    ours = w.shape[1] // 4
    tokens = normed.shape[0]
    projected = lax.dot_general(w, arrange(normed.reshape(shape)), (((0,), (1,)), ((), ())), preferred_element_type=jnp.float32)
    left = sigmoid(projected[:ours]) * projected[ours : 2 * ours]
    right = sigmoid(projected[2 * ours : 3 * ours]) * projected[3 * ours :]
    sides = jnp.concatenate([left.reshape(quads, -1, tokens), right.reshape(quads, -1, tokens)], axis=1)
    return pack(sides).astype(jnp.bfloat16)


def own_kernel(quads, cols, pair_hbm, gain_hbm, bias_hbm, w_hbm, mask_hbm, sides_ref, normed_ref, spread_ref, column_mask_ref, w_ref, gain_ref, bias_ref, pair_ref, all_w_ref, mask_ref, sems):
    moves = [(mask_hbm, mask_ref), (pair_hbm, pair_ref), (gain_hbm, gain_ref), (bias_hbm, bias_ref), (w_hbm, all_w_ref)]
    copies = [pltpu.make_async_copy(source, target, sems.at[n]) for n, (source, target) in enumerate(moves)]
    for copy in copies:
        copy.start()
    my_quad, my_col = lax.axis_index("quad"), lax.axis_index("col")
    row_count, _, channels = pair_ref.shape
    tokens = normed_ref.shape[0]
    hidden = all_w_ref.shape[1] // 4
    ours = hidden // cols
    group, lanes = spread_ref.shape
    copies[0].wait()
    mask_row = mask_ref[...].astype(jnp.float32)
    column_mask_ref[...] = column(mask_row)
    start = lax.axis_index("half") * (lanes // group)
    token = lax.broadcasted_iota(jnp.int32, (mask_row.shape[1], lanes), 0)
    lane = lax.broadcasted_iota(jnp.int32, (mask_row.shape[1], lanes), 1)
    whole = row_count // 3
    block, t, row = lane // LANES, lane // (quads * group) % whole, lane // group % quads
    k = (row ^ my_quad) * row_count + jnp.where(block < 2, 2 * t + block, 2 * whole + t)
    pick = jnp.where(k + start == token, 1.0, 0.0)
    kept = jnp.dot(mask_row.astype(jnp.bfloat16), pick.astype(jnp.bfloat16), preferred_element_type=jnp.float32)
    channel = lax.broadcasted_iota(jnp.int32, (group, lanes), 0)
    lane = lax.broadcasted_iota(jnp.int32, (group, lanes), 1)
    spread_ref[...] = jnp.where(lane % group == channel, kept, 0.0)
    for copy in copies[1:4]:
        copy.wait()
    normed = normalise(pair_ref[...].reshape(tokens, channels), gain_ref[...], bias_ref[...])
    normed_ref[...] = normed
    copies[4].wait()
    parts = [all_w_ref[:, at : at + hidden] for at in range(0, 4 * hidden, hidden)]
    w = jnp.concatenate([jnp.where(my_col == 0, part[:, :ours], part[:, ours:]) for part in parts], axis=1)
    w_ref[...] = w
    sides_ref[...] = project(normed, w, pair_ref.shape, quads)


def other_kernel(pair_ref, sides_ref, gain_ref, bias_ref, w_ref, *refs):
    *piece_refs, others_ref = refs
    my_quad, my_col = lax.axis_index("quad"), lax.axis_index("col")
    quads = sides_ref.shape[0]
    normed = normalise(pair_ref[...].reshape(-1, pair_ref.shape[2]), gain_ref[...], bias_ref[...])
    others_ref[...] = project(normed, w_ref[...], pair_ref.shape, quads)
    for step, piece_ref in enumerate(piece_refs):
        piece_ref[my_col] = sides_ref[my_quad ^ step]
        piece_ref[1 - my_col] = others_ref[my_quad ^ step]


def triangle_kernel(far_order, steps, cols, row_count, col_count, share, *refs):
    *got_refs, spread_ref, mask_ref, total_ref = refs
    got_refs = {step: ref for step, ref in zip(steps, got_refs)}
    both = 2 * share
    group, lanes = spread_ref.shape
    length = mask_ref.shape[0]
    rows, quads, parts = length // row_count, len(steps), share // group
    whole, spare = row_count // 3, LANES - 2 * col_count
    rest = col_count - spare
    blocks = [[got_refs[row][col].astype(jnp.float32) for row in range(quads)] for col in range(cols)]

    def turned(picks):
        return jnp.concatenate([blocks[col][row][at : at + group] for col, row, at in picks], axis=0).T

    tail = turned([(col, row, whole * both + part * group) for col in range(cols) for part in range(parts) for row in range(quads)])

    def side(which, part):
        even, odd, third = [], [], []
        for col in range(cols):
            at = which * share + part * group
            block = turned([(col, row, t * both + at) for t in range(whole) for row in range(quads)])
            even.append(block[:col_count])
            odd.append(block[col_count : 2 * col_count])
            lane = (col * parts + part) * quads * group
            at = which * LANES // 2
            last = [tail[at + t * rest : at + (t + 1) * rest, lane : lane + quads * group] for t in range(whole)]
            third += [block[2 * col_count :], jnp.concatenate(last, axis=1)]
        tokens = [jnp.concatenate(pieces, axis=0) for pieces in (even, odd, third)]
        return jnp.concatenate(tokens, axis=1) * mask_ref[...]

    def placed(pieces):
        return jnp.concatenate([jnp.zeros((piece, lanes), jnp.bfloat16) if isinstance(piece, int) else piece for piece in pieces], axis=0)

    contract = (((1,), (1,)), ((), ()))
    lane_block = lax.broadcasted_iota(jnp.int32, (group, LANES), 1) // rest
    mains, lasts = [], []
    for part in range(parts):
        left, right = side(0, part), side(1, part).astype(jnp.bfloat16)
        left = (left[:, None, :] * spread_ref[...][None]).reshape(rows, row_count, group, lanes)
        pairs = left[:, : 2 * whole].reshape(rows, whole, 2, group, lanes)
        left = jnp.concatenate([pairs[:, :, 0], pairs[:, :, 1], left[:, 2 * whole :]], axis=-1)
        left = left.reshape(rows * whole * group, 3 * lanes).astype(jnp.bfloat16)
        ours = [right[col * col_count : (col + 1) * col_count] for col in range(cols)]
        weights = [
            placed([p for mine in ours for p in (mine, LANES - col_count)]),
            placed([p for mine in ours for p in (col_count, mine, spare)]),
            placed([p for mine in ours for p in (2 * col_count, mine[:spare])]),
        ]
        weights = jnp.concatenate(weights, axis=1)
        mains.append(lax.dot_general(left, weights, contract, preferred_element_type=jnp.float32))
        gap = LANES // parts
        pieces = [[gap * part] + [mine[spare:]] * whole + [LANES - gap * (part + 1)] for mine in ours]
        weights = placed([p for piece in pieces for p in piece if not isinstance(p, int) or p])
        lasts.append(lax.dot_general(left[:, 2 * lanes :], weights, contract, preferred_element_type=jnp.float32))
    for target, device in enumerate(far_order):
        row, col = divmod(device, cols)
        spots = [(row * whole + t) * group for t in range(whole)]
        tiles = [main[at : at + group, col * LANES : (col + 1) * LANES] for at in spots for main in mains]
        last = [part[at : at + group, col * LANES : (col + 1) * LANES] for part in lasts for at in spots]
        tile = last[0]
        for n in range(1, len(last)):
            tile = jnp.where(lane_block >= n, last[n], tile)
        tiles.append(tile)
        total_ref[target] = jnp.concatenate(tiles, axis=0).astype(jnp.bfloat16)


def gate_kernel(normed_ref, w_ref, gain_ref, bias_ref, gate_ref, gain_out_ref, bias_out_ref):
    gate_ref[...] = sigmoid(jnp.dot(normed_ref[...], w_ref[...], preferred_element_type=jnp.float32))
    gain_out_ref[...] = column(gain_ref[...])
    bias_out_ref[...] = column(bias_ref[...])


def output_kernel(far_order, near_order, total_ref, gate_ref, gain_ref, bias_ref, w_ref, out_ref):
    tokens = gate_ref.shape[0]
    hidden = w_ref.shape[0]
    near = len(near_order)
    share = hidden // near
    blocks = []
    for index in near_order:
        parts = [total_ref[source].astype(jnp.float32) for source, device in enumerate(far_order) if device % near == index]
        blocks.append(unpack(sum(parts[1:], parts[0]), share))
    total = jnp.concatenate(blocks, axis=0)
    normed = layer_norm(total, gain_ref[...], bias_ref[...], 0).astype(jnp.bfloat16)
    output = lax.dot_general(normed, w_ref[...], (((0,), (0,)), ((), ())), preferred_element_type=jnp.float32)
    output = restore(output, out_ref.shape[0], out_ref.shape[1])
    out_ref[...] = (gate_ref[...] * output).astype(jnp.bfloat16).reshape(out_ref.shape)


def per_device(rows, cols, halves, pair, token_mask, gain_in, bias_in, w_in, w_gate, gain_out, bias_out, w_out):
    row_count, col_count, channels = pair.shape
    hidden = w_out.shape[0]
    devices = rows * cols
    near = devices // halves
    quads = rows // halves
    far_order = []
    for col in reversed(range(cols)):
        ahead = list(range(quads)) if col else list(range(1, quads)) + [0]
        behind = [0] + list(reversed(range(1, quads))) if col else list(reversed(range(quads)))
        for quad, other in zip(ahead, behind):
            far_order += [near + other * cols + col, quad * cols + col]
    share = hidden // near
    tokens = row_count * col_count
    length = rows * row_count
    depth = length // halves
    token_mask = token_mask.reshape(1, length)
    near_order = [quad * cols + col for col in range(cols) for quad in range(quads)]
    packed = 2 * share * tokens // LANES
    cost = pl.CostEstimate(flops=2 * tokens * channels * 4 * hidden, bytes_accessed=16 * tokens * channels, transcendentals=0)
    other_pair = lax.ppermute(pair, "col", [(i, (i + 1) % cols) for i in range(cols)])
    arguments = (pair, gain_in.reshape(1, channels), bias_in.reshape(1, channels), w_in, token_mask)
    sides, normed, spread, mask, *weights = pl.pallas_call(
        functools.partial(own_kernel, quads, cols),
        out_shape=(
            jax.ShapeDtypeStruct((quads, packed, LANES), jnp.bfloat16),
            jax.ShapeDtypeStruct((tokens, channels), jnp.bfloat16),
            jax.ShapeDtypeStruct((GROUP, GROUP * depth), jnp.float32),
            jax.ShapeDtypeStruct((length, 1), jnp.float32),
            jax.ShapeDtypeStruct((channels, 4 * hidden // cols), jnp.bfloat16),
            jax.ShapeDtypeStruct((1, channels), jnp.float32),
            jax.ShapeDtypeStruct((1, channels), jnp.float32),
        ),
        in_specs=[HBM] * 5,
        out_specs=(VMEM,) * 7,
        scratch_shapes=[
            pltpu.VMEM(pair.shape, pair.dtype),
            pltpu.VMEM(w_in.shape, w_in.dtype),
            pltpu.VMEM((1, length), jnp.int32),
            pltpu.SemaphoreType.DMA((5,)),
        ],
        compiler_params=LIMIT,
        cost_estimate=cost,
    )(*(pltpu.with_memory_space_constraint(x, pltpu.HBM) for x in arguments))
    w_ours, gain_in, bias_in = weights
    pieces = pl.pallas_call(
        other_kernel,
        out_shape=[jax.ShapeDtypeStruct((cols, packed, LANES), jnp.bfloat16)] * quads,
        in_specs=[VMEM] * 5,
        out_specs=[VMEM] * quads,
        scratch_shapes=[pltpu.VMEM((quads, packed, LANES), jnp.bfloat16)],
        compiler_params=LIMIT,
        cost_estimate=cost,
    )(other_pair, sides, gain_in, bias_in, w_ours)
    steps = [3, 1, 2, 0]
    got = [lax.ppermute(pieces[step], "quad", [(i, i ^ step) for i in range(quads)]) if step else pieces[0] for step in steps]
    total = pl.pallas_call(
        functools.partial(triangle_kernel, far_order, steps, cols, row_count, col_count, share),
        out_shape=jax.ShapeDtypeStruct((devices, share * tokens // LANES, LANES), jnp.bfloat16),
        in_specs=[VMEM] * (quads + 2),
        out_specs=VMEM,
        compiler_params=LIMIT,
    )(*got, spread, mask)
    gate, gain_out, bias_out = pl.pallas_call(
        gate_kernel,
        out_shape=(
            jax.ShapeDtypeStruct((tokens, channels), jnp.float32),
            jax.ShapeDtypeStruct((hidden, 1), jnp.float32),
            jax.ShapeDtypeStruct((hidden, 1), jnp.float32),
        ),
        in_specs=[VMEM] * 4,
        out_specs=(VMEM, VMEM, VMEM),
        compiler_params=LIMIT,
        cost_estimate=pl.CostEstimate(flops=2 * tokens * channels * channels, bytes_accessed=4 * tokens * channels, transcendentals=0),
    )(normed, w_gate, gain_out.reshape(1, hidden), bias_out.reshape(1, hidden))
    total = lax.all_to_all(total, ("half", "quad", "col"), split_axis=0, concat_axis=0, tiled=True, axis_index_groups=[far_order])
    return pl.pallas_call(
        functools.partial(output_kernel, far_order, near_order),
        out_shape=jax.ShapeDtypeStruct(pair.shape, jnp.bfloat16),
        in_specs=[VMEM] * 5,
        out_specs=VMEM,
        compiler_params=LIMIT,
    )(total, gate, gain_out, bias_out, w_out)


def plain_per_device(rows, cols, pair, token_mask, gain_in, bias_in, w_in, w_gate, gain_out, bias_out, w_out):
    row_count, col_count, channels = pair.shape
    hidden = w_out.shape[0]
    devices = rows * cols
    share = hidden // devices
    tokens = row_count * col_count
    row_start = lax.axis_index(("half", "quad")) * row_count
    col_start = lax.axis_index("col") * col_count
    mask_float = token_mask.astype(jnp.float32)
    mask_rows = lax.dynamic_slice_in_dim(mask_float, row_start, row_count)
    mask_cols = lax.dynamic_slice_in_dim(mask_float, col_start, col_count)
    pair_mask = (mask_rows[:, None] * mask_cols[None, :]).reshape(1, tokens)
    flat = pair.reshape(tokens, channels).astype(jnp.float32)
    normed = layer_norm(flat, gain_in, bias_in, -1).astype(jnp.bfloat16)
    projected = lax.dot_general(w_in, normed, (((0,), (1,)), ((), ())), preferred_element_type=jnp.float32)
    projected = projected.reshape(2, 2, hidden, tokens)
    sides = (pair_mask * jax.nn.sigmoid(projected[:, 0]) * projected[:, 1]).astype(jnp.bfloat16)
    sides = sides.reshape(2, devices, share, tokens).transpose(1, 0, 2, 3)
    gate = jax.nn.sigmoid(jnp.dot(normed, w_gate, preferred_element_type=jnp.float32))
    got = lax.all_to_all(sides, AXES, split_axis=0, concat_axis=0, tiled=True)
    got = got.reshape(rows, cols, 2, share, row_count, col_count).transpose(2, 3, 0, 4, 1, 5)
    got = got.reshape(2, share, rows * row_count, cols * col_count)
    total = jnp.einsum("cki,ckj->cij", got[0], got[1], preferred_element_type=jnp.float32).astype(jnp.bfloat16)
    total = total.reshape(share, rows, row_count, cols, col_count).transpose(1, 3, 0, 2, 4)
    total = total.reshape(devices, share, tokens)
    total = lax.all_to_all(total, AXES, split_axis=0, concat_axis=0, tiled=True)
    total = total.reshape(hidden, tokens).astype(jnp.float32)
    summed_norm = layer_norm(total, gain_out[:, None], bias_out[:, None], 0).astype(jnp.bfloat16)
    output = lax.dot_general(summed_norm, w_out, (((0,), (0,)), ((), ())), preferred_element_type=jnp.float32)
    return (gate * output).astype(jnp.bfloat16).reshape(row_count, col_count, channels)


def solution(mesh):
    rows, cols = mesh.shape["row"], mesh.shape["col"]
    halves = 2
    parts = (mesh.shape["groups"], halves, rows // halves, cols)
    finer = jax.sharding.Mesh(mesh.devices.reshape(parts), ("groups", "half", "quad", "col"))

    def per_shard(*args):
        near, hidden, length = rows * cols // halves, args[-1].shape[0], args[1].shape[0]
        row_count, col_count, _ = args[0].shape
        spare = LANES - 2 * col_count
        fits = hidden % (2 * GROUP * near) == 0 and cols == 2 and rows // halves == 4 and length <= LANES and row_count % 3 == 0
        fits = fits and 0 < spare < col_count and row_count // 3 * (col_count - spare) * 2 == LANES
        fits = fits and row_count // 3 * (rows // halves) * GROUP == LANES
        return per_device(rows, cols, halves, *args) if fits else plain_per_device(rows, cols, *args)

    tokens = P(("groups", "half", "quad"), "col", None)
    in_specs = (tokens, P("groups"), P(), P(), P(), P(), P(), P(), P())
    return jax.shard_map(per_shard, mesh=finer, in_specs=in_specs, out_specs=tokens, check_vma=False)
```

```python
import functools

import jax
import jax.numpy as jnp
from jax import lax
from jax.experimental import pallas as pl
from jax.experimental.pallas import tpu as pltpu
from jax.sharding import PartitionSpec as P

epsilon = 1e-05
LANES = 128
GROUP = 8
AXES = ("half", "quad", "col")
VMEM = pl.BlockSpec(memory_space=pltpu.VMEM)
HBM = pl.BlockSpec(memory_space=pltpu.HBM)
LIMIT = pltpu.CompilerParams(vmem_limit_bytes=32 * 1024 * 1024)


def sigmoid(x):
    return 0.5 * jnp.tanh(0.5 * x) + 0.5


def layer_norm(values, gain, bias, axis):
    mean = jnp.mean(values, axis=axis, keepdims=True)
    centred = values - mean
    variance = jnp.mean(centred * centred, axis=axis, keepdims=True)
    return centred * lax.rsqrt(variance + epsilon) * gain + bias


def column(row):
    n = row.shape[1]
    eye = lax.broadcasted_iota(jnp.int32, (n, n), 0) == lax.broadcasted_iota(jnp.int32, (n, n), 1)
    return jnp.sum(jnp.where(eye, row, 0.0), axis=1, keepdims=True)


def pack(x):
    rows, tokens = x.shape[-2:]
    whole, rest = divmod(tokens, LANES)
    blocks = [x[..., t * LANES : (t + 1) * LANES] for t in range(whole)]
    if rest:
        tail = x[..., whole * LANES :]
        blocks.append(jnp.concatenate([tail[..., : rows // 2, :], tail[..., rows // 2 :, :]], axis=-1))
    return jnp.concatenate(blocks, axis=-2)


def unpack(x, rows):
    whole, rest = divmod(x.shape[-2], rows)
    blocks = [x[..., t * rows : (t + 1) * rows, :] for t in range(whole)]
    if rest:
        tail = x[..., whole * rows :, :]
        blocks.append(jnp.concatenate([tail[..., : LANES // 2], tail[..., LANES // 2 :]], axis=-2))
    return jnp.concatenate(blocks, axis=-1)


def arrange(x):
    row_count, col_count, _ = x.shape
    whole, spare = row_count // 3, LANES - 2 * col_count
    blocks = []
    for t in range(whole):
        blocks += [x[2 * t], x[2 * t + 1], x[2 * whole + t, :spare]]
    return jnp.concatenate(blocks + [x[2 * whole + t, spare:] for t in range(whole)], axis=0)


def restore(x, row_count, col_count):
    whole, spare = row_count // 3, LANES - 2 * col_count
    rest = col_count - spare
    rows = []
    for t in range(whole):
        rows += [x[t * LANES : t * LANES + col_count], x[t * LANES + col_count : t * LANES + 2 * col_count]]
    for t in range(whole):
        tail = whole * LANES + t * rest
        rows += [x[t * LANES + 2 * col_count : (t + 1) * LANES], x[tail : tail + rest]]
    return jnp.concatenate(rows, axis=0)


def normalise(flat, gain, bias):
    return layer_norm(flat.astype(jnp.float32), gain, bias, -1).astype(jnp.bfloat16)


def project(normed, w, shape, quads):
    ours = w.shape[1] // 4
    tokens = normed.shape[0]
    projected = lax.dot_general(w, arrange(normed.reshape(shape)), (((0,), (1,)), ((), ())), preferred_element_type=jnp.float32)
    left = sigmoid(projected[:ours]) * projected[ours : 2 * ours]
    right = sigmoid(projected[2 * ours : 3 * ours]) * projected[3 * ours :]
    sides = jnp.concatenate([left.reshape(quads, -1, tokens), right.reshape(quads, -1, tokens)], axis=1)
    return pack(sides).astype(jnp.bfloat16)


def own_kernel(quads, cols, pair_hbm, gain_hbm, bias_hbm, w_hbm, mask_hbm, sides_ref, normed_ref, spread_ref, column_mask_ref, w_ref, gain_ref, bias_ref, pair_ref, all_w_ref, mask_ref, sems):
    moves = [(mask_hbm, mask_ref), (pair_hbm, pair_ref), (gain_hbm, gain_ref), (bias_hbm, bias_ref), (w_hbm, all_w_ref)]
    copies = [pltpu.make_async_copy(source, target, sems.at[n]) for n, (source, target) in enumerate(moves)]
    for copy in copies:
        copy.start()
    my_quad, my_col = lax.axis_index("quad"), lax.axis_index("col")
    row_count, _, channels = pair_ref.shape
    tokens = normed_ref.shape[0]
    hidden = all_w_ref.shape[1] // 4
    ours = hidden // cols
    group, lanes = spread_ref.shape
    copies[0].wait()
    mask_row = mask_ref[...].astype(jnp.float32)
    column_mask_ref[...] = column(mask_row)
    start = lax.axis_index("half") * (lanes // group)
    token = lax.broadcasted_iota(jnp.int32, (mask_row.shape[1], lanes), 0)
    lane = lax.broadcasted_iota(jnp.int32, (mask_row.shape[1], lanes), 1)
    whole = row_count // 3
    block, t, row = lane // LANES, lane // (quads * group) % whole, lane // group % quads
    k = (row ^ my_quad) * row_count + jnp.where(block < 2, 2 * t + block, 2 * whole + t)
    pick = jnp.where(k + start == token, 1.0, 0.0)
    kept = jnp.dot(mask_row.astype(jnp.bfloat16), pick.astype(jnp.bfloat16), preferred_element_type=jnp.float32)
    channel = lax.broadcasted_iota(jnp.int32, (group, lanes), 0)
    lane = lax.broadcasted_iota(jnp.int32, (group, lanes), 1)
    spread_ref[...] = jnp.where(lane % group == channel, kept, 0.0)
    for copy in copies[1:4]:
        copy.wait()
    normed = normalise(pair_ref[...].reshape(tokens, channels), gain_ref[...], bias_ref[...])
    normed_ref[...] = normed
    copies[4].wait()
    parts = [all_w_ref[:, at : at + hidden] for at in range(0, 4 * hidden, hidden)]
    w = jnp.concatenate([jnp.where(my_col == 0, part[:, :ours], part[:, ours:]) for part in parts], axis=1)
    w_ref[...] = w
    sides_ref[...] = project(normed, w, pair_ref.shape, quads)


def other_kernel(pair_ref, sides_ref, gain_ref, bias_ref, w_ref, *refs):
    *piece_refs, others_ref = refs
    my_quad, my_col = lax.axis_index("quad"), lax.axis_index("col")
    quads = sides_ref.shape[0]
    normed = normalise(pair_ref[...].reshape(-1, pair_ref.shape[2]), gain_ref[...], bias_ref[...])
    others_ref[...] = project(normed, w_ref[...], pair_ref.shape, quads)
    for step, piece_ref in enumerate(piece_refs):
        piece_ref[my_col] = sides_ref[my_quad ^ step]
        piece_ref[1 - my_col] = others_ref[my_quad ^ step]


def triangle_kernel(far_order, steps, cols, row_count, col_count, share, *refs):
    *got_refs, spread_ref, mask_ref, total_ref = refs
    got_refs = {step: ref for step, ref in zip(steps, got_refs)}
    both = 2 * share
    group, lanes = spread_ref.shape
    length = mask_ref.shape[0]
    rows, quads, parts = length // row_count, len(steps), share // group
    whole, spare = row_count // 3, LANES - 2 * col_count
    rest = col_count - spare
    blocks = [[got_refs[row][col].astype(jnp.float32) for row in range(quads)] for col in range(cols)]

    def turned(picks):
        return jnp.concatenate([blocks[col][row][at : at + group] for col, row, at in picks], axis=0).T

    tail = turned([(col, row, whole * both + part * group) for col in range(cols) for part in range(parts) for row in range(quads)])

    def side(which, part):
        even, odd, third = [], [], []
        for col in range(cols):
            at = which * share + part * group
            block = turned([(col, row, t * both + at) for t in range(whole) for row in range(quads)])
            even.append(block[:col_count])
            odd.append(block[col_count : 2 * col_count])
            lane = (col * parts + part) * quads * group
            at = which * LANES // 2
            last = [tail[at + t * rest : at + (t + 1) * rest, lane : lane + quads * group] for t in range(whole)]
            third += [block[2 * col_count :], jnp.concatenate(last, axis=1)]
        tokens = [jnp.concatenate(pieces, axis=0) for pieces in (even, odd, third)]
        return jnp.concatenate(tokens, axis=1) * mask_ref[...]

    def placed(pieces):
        return jnp.concatenate([jnp.zeros((piece, lanes), jnp.bfloat16) if isinstance(piece, int) else piece for piece in pieces], axis=0)

    contract = (((1,), (1,)), ((), ()))
    lane_block = lax.broadcasted_iota(jnp.int32, (group, LANES), 1) // rest
    mains, lasts = [], []
    for part in range(parts):
        left, right = side(0, part), side(1, part).astype(jnp.bfloat16)
        left = (left[:, None, :] * spread_ref[...][None]).reshape(rows, row_count, group, lanes)
        pairs = left[:, : 2 * whole].reshape(rows, whole, 2, group, lanes)
        left = jnp.concatenate([pairs[:, :, 0], pairs[:, :, 1], left[:, 2 * whole :]], axis=-1)
        left = left.reshape(rows * whole * group, 3 * lanes).astype(jnp.bfloat16)
        ours = [right[col * col_count : (col + 1) * col_count] for col in range(cols)]
        weights = [
            placed([p for mine in ours for p in (mine, LANES - col_count)]),
            placed([p for mine in ours for p in (col_count, mine, spare)]),
            placed([p for mine in ours for p in (2 * col_count, mine[:spare])]),
        ]
        weights = jnp.concatenate(weights, axis=1)
        mains.append(lax.dot_general(left, weights, contract, preferred_element_type=jnp.float32))
        gap = LANES // parts
        pieces = [[gap * part] + [mine[spare:]] * whole + [LANES - gap * (part + 1)] for mine in ours]
        weights = placed([p for piece in pieces for p in piece if not isinstance(p, int) or p])
        lasts.append(lax.dot_general(left[:, 2 * lanes :], weights, contract, preferred_element_type=jnp.float32))
    for target, device in enumerate(far_order):
        row, col = divmod(device, cols)
        spots = [(row * whole + t) * group for t in range(whole)]
        tiles = [main[at : at + group, col * LANES : (col + 1) * LANES] for at in spots for main in mains]
        last = [part[at : at + group, col * LANES : (col + 1) * LANES] for part in lasts for at in spots]
        tile = last[0]
        for n in range(1, len(last)):
            tile = jnp.where(lane_block >= n, last[n], tile)
        tiles.append(tile)
        total_ref[target] = jnp.concatenate(tiles, axis=0).astype(jnp.bfloat16)


def gate_kernel(normed_ref, w_ref, gain_ref, bias_ref, gate_ref, gain_out_ref, bias_out_ref):
    gate_ref[...] = sigmoid(jnp.dot(normed_ref[...], w_ref[...], preferred_element_type=jnp.float32))
    gain_out_ref[...] = column(gain_ref[...])
    bias_out_ref[...] = column(bias_ref[...])


def output_kernel(far_order, near_order, total_ref, gate_ref, gain_ref, bias_ref, w_ref, out_ref):
    tokens = gate_ref.shape[0]
    hidden = w_ref.shape[0]
    near = len(near_order)
    share = hidden // near
    blocks = []
    for index in near_order:
        parts = [total_ref[source].astype(jnp.float32) for source, device in enumerate(far_order) if device % near == index]
        blocks.append(unpack(sum(parts[1:], parts[0]), share))
    total = jnp.concatenate(blocks, axis=0)
    normed = layer_norm(total, gain_ref[...], bias_ref[...], 0).astype(jnp.bfloat16)
    output = lax.dot_general(normed, w_ref[...], (((0,), (0,)), ((), ())), preferred_element_type=jnp.float32)
    output = restore(output, out_ref.shape[0], out_ref.shape[1])
    out_ref[...] = (gate_ref[...] * output).astype(jnp.bfloat16).reshape(out_ref.shape)


def per_device(rows, cols, halves, pair, token_mask, gain_in, bias_in, w_in, w_gate, gain_out, bias_out, w_out):
    row_count, col_count, channels = pair.shape
    hidden = w_out.shape[0]
    devices = rows * cols
    near = devices // halves
    quads = rows // halves
    far_order = []
    for col in reversed(range(cols)):
        ahead = list(range(quads)) if col else list(range(1, quads)) + [0]
        behind = [0] + list(reversed(range(1, quads))) if col else list(reversed(range(quads)))
        for quad, other in zip(ahead, behind):
            far_order += [near + other * cols + col, quad * cols + col]
    share = hidden // near
    tokens = row_count * col_count
    length = rows * row_count
    depth = length // halves
    token_mask = token_mask.reshape(1, length)
    near_order = [quad * cols + col for col in range(cols) for quad in range(quads)]
    packed = 2 * share * tokens // LANES
    cost = pl.CostEstimate(flops=2 * tokens * channels * 4 * hidden, bytes_accessed=16 * tokens * channels, transcendentals=0)
    other_pair = lax.ppermute(pair, "col", [(i, (i + 1) % cols) for i in range(cols)])
    arguments = (pair, gain_in.reshape(1, channels), bias_in.reshape(1, channels), w_in, token_mask)
    sides, normed, spread, mask, *weights = pl.pallas_call(
        functools.partial(own_kernel, quads, cols),
        out_shape=(
            jax.ShapeDtypeStruct((quads, packed, LANES), jnp.bfloat16),
            jax.ShapeDtypeStruct((tokens, channels), jnp.bfloat16),
            jax.ShapeDtypeStruct((GROUP, GROUP * depth), jnp.float32),
            jax.ShapeDtypeStruct((length, 1), jnp.float32),
            jax.ShapeDtypeStruct((channels, 4 * hidden // cols), jnp.bfloat16),
            jax.ShapeDtypeStruct((1, channels), jnp.float32),
            jax.ShapeDtypeStruct((1, channels), jnp.float32),
        ),
        in_specs=[HBM] * 5,
        out_specs=(VMEM,) * 7,
        scratch_shapes=[
            pltpu.VMEM(pair.shape, pair.dtype),
            pltpu.VMEM(w_in.shape, w_in.dtype),
            pltpu.VMEM((1, length), jnp.int32),
            pltpu.SemaphoreType.DMA((5,)),
        ],
        compiler_params=LIMIT,
        cost_estimate=cost,
    )(*(pltpu.with_memory_space_constraint(x, pltpu.HBM) for x in arguments))
    w_ours, gain_in, bias_in = weights
    pieces = pl.pallas_call(
        other_kernel,
        out_shape=[jax.ShapeDtypeStruct((cols, packed, LANES), jnp.bfloat16)] * quads,
        in_specs=[VMEM] * 5,
        out_specs=[VMEM] * quads,
        scratch_shapes=[pltpu.VMEM((quads, packed, LANES), jnp.bfloat16)],
        compiler_params=LIMIT,
        cost_estimate=cost,
    )(other_pair, sides, gain_in, bias_in, w_ours)
    steps = [1, 3, 2, 0]
    got = [lax.ppermute(pieces[step], "quad", [(i, i ^ step) for i in range(quads)]) if step else pieces[0] for step in steps]
    total = pl.pallas_call(
        functools.partial(triangle_kernel, far_order, steps, cols, row_count, col_count, share),
        out_shape=jax.ShapeDtypeStruct((devices, share * tokens // LANES, LANES), jnp.bfloat16),
        in_specs=[VMEM] * (quads + 2),
        out_specs=VMEM,
        compiler_params=LIMIT,
    )(*got, spread, mask)
    gate, gain_out, bias_out = pl.pallas_call(
        gate_kernel,
        out_shape=(
            jax.ShapeDtypeStruct((tokens, channels), jnp.float32),
            jax.ShapeDtypeStruct((hidden, 1), jnp.float32),
            jax.ShapeDtypeStruct((hidden, 1), jnp.float32),
        ),
        in_specs=[VMEM] * 4,
        out_specs=(VMEM, VMEM, VMEM),
        compiler_params=LIMIT,
        cost_estimate=pl.CostEstimate(flops=2 * tokens * channels * channels, bytes_accessed=4 * tokens * channels, transcendentals=0),
    )(normed, w_gate, gain_out.reshape(1, hidden), bias_out.reshape(1, hidden))
    total = lax.all_to_all(total, ("half", "quad", "col"), split_axis=0, concat_axis=0, tiled=True, axis_index_groups=[far_order])
    return pl.pallas_call(
        functools.partial(output_kernel, far_order, near_order),
        out_shape=jax.ShapeDtypeStruct(pair.shape, jnp.bfloat16),
        in_specs=[VMEM] * 5,
        out_specs=VMEM,
        compiler_params=LIMIT,
    )(total, gate, gain_out, bias_out, w_out)


def plain_per_device(rows, cols, pair, token_mask, gain_in, bias_in, w_in, w_gate, gain_out, bias_out, w_out):
    row_count, col_count, channels = pair.shape
    hidden = w_out.shape[0]
    devices = rows * cols
    share = hidden // devices
    tokens = row_count * col_count
    row_start = lax.axis_index(("half", "quad")) * row_count
    col_start = lax.axis_index("col") * col_count
    mask_float = token_mask.astype(jnp.float32)
    mask_rows = lax.dynamic_slice_in_dim(mask_float, row_start, row_count)
    mask_cols = lax.dynamic_slice_in_dim(mask_float, col_start, col_count)
    pair_mask = (mask_rows[:, None] * mask_cols[None, :]).reshape(1, tokens)
    flat = pair.reshape(tokens, channels).astype(jnp.float32)
    normed = layer_norm(flat, gain_in, bias_in, -1).astype(jnp.bfloat16)
    projected = lax.dot_general(w_in, normed, (((0,), (1,)), ((), ())), preferred_element_type=jnp.float32)
    projected = projected.reshape(2, 2, hidden, tokens)
    sides = (pair_mask * jax.nn.sigmoid(projected[:, 0]) * projected[:, 1]).astype(jnp.bfloat16)
    sides = sides.reshape(2, devices, share, tokens).transpose(1, 0, 2, 3)
    gate = jax.nn.sigmoid(jnp.dot(normed, w_gate, preferred_element_type=jnp.float32))
    got = lax.all_to_all(sides, AXES, split_axis=0, concat_axis=0, tiled=True)
    got = got.reshape(rows, cols, 2, share, row_count, col_count).transpose(2, 3, 0, 4, 1, 5)
    got = got.reshape(2, share, rows * row_count, cols * col_count)
    total = jnp.einsum("cki,ckj->cij", got[0], got[1], preferred_element_type=jnp.float32).astype(jnp.bfloat16)
    total = total.reshape(share, rows, row_count, cols, col_count).transpose(1, 3, 0, 2, 4)
    total = total.reshape(devices, share, tokens)
    total = lax.all_to_all(total, AXES, split_axis=0, concat_axis=0, tiled=True)
    total = total.reshape(hidden, tokens).astype(jnp.float32)
    summed_norm = layer_norm(total, gain_out[:, None], bias_out[:, None], 0).astype(jnp.bfloat16)
    output = lax.dot_general(summed_norm, w_out, (((0,), (0,)), ((), ())), preferred_element_type=jnp.float32)
    return (gate * output).astype(jnp.bfloat16).reshape(row_count, col_count, channels)


def solution(mesh):
    rows, cols = mesh.shape["row"], mesh.shape["col"]
    halves = 2
    parts = (mesh.shape["groups"], halves, rows // halves, cols)
    finer = jax.sharding.Mesh(mesh.devices.reshape(parts), ("groups", "half", "quad", "col"))

    def per_shard(*args):
        near, hidden, length = rows * cols // halves, args[-1].shape[0], args[1].shape[0]
        row_count, col_count, _ = args[0].shape
        spare = LANES - 2 * col_count
        fits = hidden % (2 * GROUP * near) == 0 and cols == 2 and rows // halves == 4 and length <= LANES and row_count % 3 == 0
        fits = fits and 0 < spare < col_count and row_count // 3 * (col_count - spare) * 2 == LANES
        fits = fits and row_count // 3 * (rows // halves) * GROUP == LANES
        return per_device(rows, cols, halves, *args) if fits else plain_per_device(rows, cols, *args)

    tokens = P(("groups", "half", "quad"), "col", None)
    in_specs = (tokens, P("groups"), P(), P(), P(), P(), P(), P(), P())
    return jax.shard_map(per_shard, mesh=finer, in_specs=in_specs, out_specs=tokens, check_vma=False)
```

```python
import functools

import jax
import jax.numpy as jnp
from jax import lax
from jax.experimental import pallas as pl
from jax.experimental.pallas import tpu as pltpu
from jax.sharding import PartitionSpec as P

epsilon = 1e-05
LANES = 128
GROUP = 8
AXES = ("half", "quad", "col")
VMEM = pl.BlockSpec(memory_space=pltpu.VMEM)
HBM = pl.BlockSpec(memory_space=pltpu.HBM)
LIMIT = pltpu.CompilerParams(vmem_limit_bytes=32 * 1024 * 1024)


def sigmoid(x):
    return 0.5 * jnp.tanh(0.5 * x) + 0.5


def layer_norm(values, gain, bias, axis):
    mean = jnp.mean(values, axis=axis, keepdims=True)
    centred = values - mean
    variance = jnp.mean(centred * centred, axis=axis, keepdims=True)
    return centred * lax.rsqrt(variance + epsilon) * gain + bias


def column(row):
    n = row.shape[1]
    eye = lax.broadcasted_iota(jnp.int32, (n, n), 0) == lax.broadcasted_iota(jnp.int32, (n, n), 1)
    return jnp.sum(jnp.where(eye, row, 0.0), axis=1, keepdims=True)


def pack(x):
    rows, tokens = x.shape[-2:]
    whole, rest = divmod(tokens, LANES)
    blocks = [x[..., t * LANES : (t + 1) * LANES] for t in range(whole)]
    if rest:
        tail = x[..., whole * LANES :]
        blocks.append(jnp.concatenate([tail[..., : rows // 2, :], tail[..., rows // 2 :, :]], axis=-1))
    return jnp.concatenate(blocks, axis=-2)


def unpack(x, rows):
    whole, rest = divmod(x.shape[-2], rows)
    blocks = [x[..., t * rows : (t + 1) * rows, :] for t in range(whole)]
    if rest:
        tail = x[..., whole * rows :, :]
        blocks.append(jnp.concatenate([tail[..., : LANES // 2], tail[..., LANES // 2 :]], axis=-2))
    return jnp.concatenate(blocks, axis=-1)


def arrange(x):
    row_count, col_count, _ = x.shape
    whole, spare = row_count // 3, LANES - 2 * col_count
    blocks = []
    for t in range(whole):
        blocks += [x[2 * t], x[2 * t + 1], x[2 * whole + t, :spare]]
    return jnp.concatenate(blocks + [x[2 * whole + t, spare:] for t in range(whole)], axis=0)


def restore(x, row_count, col_count):
    whole, spare = row_count // 3, LANES - 2 * col_count
    rest = col_count - spare
    rows = []
    for t in range(whole):
        rows += [x[t * LANES : t * LANES + col_count], x[t * LANES + col_count : t * LANES + 2 * col_count]]
    for t in range(whole):
        tail = whole * LANES + t * rest
        rows += [x[t * LANES + 2 * col_count : (t + 1) * LANES], x[tail : tail + rest]]
    return jnp.concatenate(rows, axis=0)


def normalise(flat, gain, bias):
    return layer_norm(flat.astype(jnp.float32), gain, bias, -1).astype(jnp.bfloat16)


def project(normed, w, shape, quads):
    ours = w.shape[1] // 4
    tokens = normed.shape[0]
    projected = lax.dot_general(w, arrange(normed.reshape(shape)), (((0,), (1,)), ((), ())), preferred_element_type=jnp.float32)
    left = sigmoid(projected[:ours]) * projected[ours : 2 * ours]
    right = sigmoid(projected[2 * ours : 3 * ours]) * projected[3 * ours :]
    sides = jnp.concatenate([left.reshape(quads, -1, tokens), right.reshape(quads, -1, tokens)], axis=1)
    return pack(sides).astype(jnp.bfloat16)


def own_kernel(quads, cols, pair_hbm, gain_hbm, bias_hbm, w_hbm, mask_hbm, sides_ref, normed_ref, spread_ref, column_mask_ref, w_ref, gain_ref, bias_ref, pair_ref, all_w_ref, mask_ref, sems):
    moves = [(mask_hbm, mask_ref), (pair_hbm, pair_ref), (gain_hbm, gain_ref), (bias_hbm, bias_ref), (w_hbm, all_w_ref)]
    copies = [pltpu.make_async_copy(source, target, sems.at[n]) for n, (source, target) in enumerate(moves)]
    for copy in copies:
        copy.start()
    my_quad, my_col = lax.axis_index("quad"), lax.axis_index("col")
    row_count, _, channels = pair_ref.shape
    tokens = normed_ref.shape[0]
    hidden = all_w_ref.shape[1] // 4
    ours = hidden // cols
    group, lanes = spread_ref.shape
    copies[0].wait()
    mask_row = mask_ref[...].astype(jnp.float32)
    column_mask_ref[...] = column(mask_row)
    start = lax.axis_index("half") * (lanes // group)
    token = lax.broadcasted_iota(jnp.int32, (mask_row.shape[1], lanes), 0)
    lane = lax.broadcasted_iota(jnp.int32, (mask_row.shape[1], lanes), 1)
    whole = row_count // 3
    block, t, row = lane // LANES, lane // (quads * group) % whole, lane // group % quads
    k = (row ^ my_quad) * row_count + jnp.where(block < 2, 2 * t + block, 2 * whole + t)
    pick = jnp.where(k + start == token, 1.0, 0.0)
    kept = jnp.dot(mask_row.astype(jnp.bfloat16), pick.astype(jnp.bfloat16), preferred_element_type=jnp.float32)
    channel = lax.broadcasted_iota(jnp.int32, (group, lanes), 0)
    lane = lax.broadcasted_iota(jnp.int32, (group, lanes), 1)
    spread_ref[...] = jnp.where(lane % group == channel, kept, 0.0)
    for copy in copies[1:4]:
        copy.wait()
    normed = normalise(pair_ref[...].reshape(tokens, channels), gain_ref[...], bias_ref[...])
    normed_ref[...] = normed
    copies[4].wait()
    parts = [all_w_ref[:, at : at + hidden] for at in range(0, 4 * hidden, hidden)]
    w = jnp.concatenate([jnp.where(my_col == 0, part[:, :ours], part[:, ours:]) for part in parts], axis=1)
    w_ref[...] = w
    sides_ref[...] = project(normed, w, pair_ref.shape, quads)


def other_kernel(pair_ref, sides_ref, gain_ref, bias_ref, w_ref, *refs):
    *piece_refs, others_ref = refs
    my_quad, my_col = lax.axis_index("quad"), lax.axis_index("col")
    quads = sides_ref.shape[0]
    normed = normalise(pair_ref[...].reshape(-1, pair_ref.shape[2]), gain_ref[...], bias_ref[...])
    others_ref[...] = project(normed, w_ref[...], pair_ref.shape, quads)
    for step, piece_ref in enumerate(piece_refs):
        piece_ref[my_col] = sides_ref[my_quad ^ step]
        piece_ref[1 - my_col] = others_ref[my_quad ^ step]


def triangle_kernel(far_order, steps, cols, row_count, col_count, share, *refs):
    *got_refs, spread_ref, mask_ref, total_ref, left_ref, wide_ref = refs
    got_refs = {step: ref for step, ref in zip(steps, got_refs)}
    both = 2 * share
    group, lanes = spread_ref.shape
    length = mask_ref.shape[0]
    rows, quads, parts = length // row_count, len(steps), share // group
    whole, spare = row_count // 3, LANES - 2 * col_count
    rest = col_count - spare
    blocks = [[got_refs[row][col].astype(jnp.float32) for row in range(quads)] for col in range(cols)]

    def turned(picks):
        return jnp.concatenate([blocks[col][row][at : at + group] for col, row, at in picks], axis=0).T

    tail = turned([(col, row, whole * both + part * group) for col in range(cols) for part in range(parts) for row in range(quads)])

    def side(which, part):
        even, odd, third = [], [], []
        for col in range(cols):
            at = which * share + part * group
            block = turned([(col, row, t * both + at) for t in range(whole) for row in range(quads)])
            even.append(block[:col_count])
            odd.append(block[col_count : 2 * col_count])
            lane = (col * parts + part) * quads * group
            at = which * LANES // 2
            last = [tail[at + t * rest : at + (t + 1) * rest, lane : lane + quads * group] for t in range(whole)]
            third += [block[2 * col_count :], jnp.concatenate(last, axis=1)]
        tokens = [jnp.concatenate(pieces, axis=0) for pieces in (even, odd, third)]
        return jnp.concatenate(tokens, axis=1) * mask_ref[...]

    def placed(pieces):
        return jnp.concatenate([jnp.zeros((piece, lanes), jnp.bfloat16) if isinstance(piece, int) else piece for piece in pieces], axis=0)

    contract = (((1,), (1,)), ((), ()))
    lane_block = lax.broadcasted_iota(jnp.int32, (group, LANES), 1) // rest
    mains, lasts = [], []
    for part in range(parts):
        left_ref[part] = side(0, part)
        right = side(1, part).astype(jnp.bfloat16)
        for row in range(rows):
            for t in range(0, whole, 2):
                pair = []
                for at in (row * row_count, row * row_count + 2):
                    picks = [at + 2 * t, at + 2 * t + 1, row * row_count + 2 * whole + t + len(pair)]
                    copies = [jnp.broadcast_to(left_ref[part, i : i + 1, :], (group, lanes)) for i in picks]
                    pair.append(jnp.concatenate([copy * spread_ref[...] for copy in copies], axis=1))
                at = (row * whole + t) * group
                wide_ref[part, at : at + 2 * group, :] = jnp.concatenate(pair, axis=0).astype(jnp.bfloat16)
        ours = [right[col * col_count : (col + 1) * col_count] for col in range(cols)]
        weights = [
            placed([p for mine in ours for p in (mine, LANES - col_count)]),
            placed([p for mine in ours for p in (col_count, mine, spare)]),
            placed([p for mine in ours for p in (2 * col_count, mine[:spare])]),
        ]
        weights = jnp.concatenate(weights, axis=1)
        mains.append(lax.dot_general(wide_ref[part], weights, contract, preferred_element_type=jnp.float32))
        gap = LANES // parts
        pieces = [[gap * part] + [mine[spare:]] * whole + [LANES - gap * (part + 1)] for mine in ours]
        weights = placed([p for piece in pieces for p in piece if not isinstance(p, int) or p])
        lasts.append(lax.dot_general(wide_ref[part, :, 2 * lanes :], weights, contract, preferred_element_type=jnp.float32))
    for target, device in enumerate(far_order):
        row, col = divmod(device, cols)
        spots = [(row * whole + t) * group for t in range(whole)]
        tiles = [main[at : at + group, col * LANES : (col + 1) * LANES] for at in spots for main in mains]
        last = [part[at : at + group, col * LANES : (col + 1) * LANES] for part in lasts for at in spots]
        tile = last[0]
        for n in range(1, len(last)):
            tile = jnp.where(lane_block >= n, last[n], tile)
        tiles.append(tile)
        total_ref[target] = jnp.concatenate(tiles, axis=0).astype(jnp.bfloat16)


def gate_kernel(normed_ref, w_ref, gain_ref, bias_ref, gate_ref, gain_out_ref, bias_out_ref):
    gate_ref[...] = sigmoid(jnp.dot(normed_ref[...], w_ref[...], preferred_element_type=jnp.float32))
    gain_out_ref[...] = column(gain_ref[...])
    bias_out_ref[...] = column(bias_ref[...])


def output_kernel(far_order, near_order, total_ref, gate_ref, gain_ref, bias_ref, w_ref, out_ref):
    tokens = gate_ref.shape[0]
    hidden = w_ref.shape[0]
    near = len(near_order)
    share = hidden // near
    blocks = []
    for index in near_order:
        parts = [total_ref[source].astype(jnp.float32) for source, device in enumerate(far_order) if device % near == index]
        blocks.append(unpack(sum(parts[1:], parts[0]), share))
    total = jnp.concatenate(blocks, axis=0)
    normed = layer_norm(total, gain_ref[...], bias_ref[...], 0).astype(jnp.bfloat16)
    output = lax.dot_general(normed, w_ref[...], (((0,), (0,)), ((), ())), preferred_element_type=jnp.float32)
    output = restore(output, out_ref.shape[0], out_ref.shape[1])
    out_ref[...] = (gate_ref[...] * output).astype(jnp.bfloat16).reshape(out_ref.shape)


def per_device(rows, cols, halves, pair, token_mask, gain_in, bias_in, w_in, w_gate, gain_out, bias_out, w_out):
    row_count, col_count, channels = pair.shape
    hidden = w_out.shape[0]
    devices = rows * cols
    near = devices // halves
    quads = rows // halves
    far_order = []
    for col in reversed(range(cols)):
        ahead = list(range(quads)) if col else list(range(1, quads)) + [0]
        behind = [0] + list(reversed(range(1, quads))) if col else list(reversed(range(quads)))
        for quad, other in zip(ahead, behind):
            far_order += [near + other * cols + col, quad * cols + col]
    share = hidden // near
    tokens = row_count * col_count
    length = rows * row_count
    depth = length // halves
    token_mask = token_mask.reshape(1, length)
    near_order = [quad * cols + col for col in range(cols) for quad in range(quads)]
    packed = 2 * share * tokens // LANES
    cost = pl.CostEstimate(flops=2 * tokens * channels * 4 * hidden, bytes_accessed=16 * tokens * channels, transcendentals=0)
    other_pair = lax.ppermute(pair, "col", [(i, (i + 1) % cols) for i in range(cols)])
    arguments = (pair, gain_in.reshape(1, channels), bias_in.reshape(1, channels), w_in, token_mask)
    sides, normed, spread, mask, *weights = pl.pallas_call(
        functools.partial(own_kernel, quads, cols),
        out_shape=(
            jax.ShapeDtypeStruct((quads, packed, LANES), jnp.bfloat16),
            jax.ShapeDtypeStruct((tokens, channels), jnp.bfloat16),
            jax.ShapeDtypeStruct((GROUP, GROUP * depth), jnp.float32),
            jax.ShapeDtypeStruct((length, 1), jnp.float32),
            jax.ShapeDtypeStruct((channels, 4 * hidden // cols), jnp.bfloat16),
            jax.ShapeDtypeStruct((1, channels), jnp.float32),
            jax.ShapeDtypeStruct((1, channels), jnp.float32),
        ),
        in_specs=[HBM] * 5,
        out_specs=(VMEM,) * 7,
        scratch_shapes=[
            pltpu.VMEM(pair.shape, pair.dtype),
            pltpu.VMEM(w_in.shape, w_in.dtype),
            pltpu.VMEM((1, length), jnp.int32),
            pltpu.SemaphoreType.DMA((5,)),
        ],
        compiler_params=LIMIT,
        cost_estimate=cost,
    )(*(pltpu.with_memory_space_constraint(x, pltpu.HBM) for x in arguments))
    w_ours, gain_in, bias_in = weights
    pieces = pl.pallas_call(
        other_kernel,
        out_shape=[jax.ShapeDtypeStruct((cols, packed, LANES), jnp.bfloat16)] * quads,
        in_specs=[VMEM] * 5,
        out_specs=[VMEM] * quads,
        scratch_shapes=[pltpu.VMEM((quads, packed, LANES), jnp.bfloat16)],
        compiler_params=LIMIT,
        cost_estimate=cost,
    )(other_pair, sides, gain_in, bias_in, w_ours)
    steps = [3, 1, 2, 0]
    got = [lax.ppermute(pieces[step], "quad", [(i, i ^ step) for i in range(quads)]) if step else pieces[0] for step in steps]
    total = pl.pallas_call(
        functools.partial(triangle_kernel, far_order, steps, cols, row_count, col_count, share),
        out_shape=jax.ShapeDtypeStruct((devices, share * tokens // LANES, LANES), jnp.bfloat16),
        in_specs=[VMEM] * (quads + 2),
        out_specs=VMEM,
        scratch_shapes=[
            pltpu.VMEM((share // GROUP, length, GROUP * depth), jnp.float32),
            pltpu.VMEM((share // GROUP, length // 3 * GROUP, 3 * GROUP * depth), jnp.bfloat16),
        ],
        compiler_params=LIMIT,
    )(*got, spread, mask)
    gate, gain_out, bias_out = pl.pallas_call(
        gate_kernel,
        out_shape=(
            jax.ShapeDtypeStruct((tokens, channels), jnp.float32),
            jax.ShapeDtypeStruct((hidden, 1), jnp.float32),
            jax.ShapeDtypeStruct((hidden, 1), jnp.float32),
        ),
        in_specs=[VMEM] * 4,
        out_specs=(VMEM, VMEM, VMEM),
        compiler_params=LIMIT,
        cost_estimate=pl.CostEstimate(flops=2 * tokens * channels * channels, bytes_accessed=4 * tokens * channels, transcendentals=0),
    )(normed, w_gate, gain_out.reshape(1, hidden), bias_out.reshape(1, hidden))
    total = lax.all_to_all(total, ("half", "quad", "col"), split_axis=0, concat_axis=0, tiled=True, axis_index_groups=[far_order])
    return pl.pallas_call(
        functools.partial(output_kernel, far_order, near_order),
        out_shape=jax.ShapeDtypeStruct(pair.shape, jnp.bfloat16),
        in_specs=[VMEM] * 5,
        out_specs=VMEM,
        compiler_params=LIMIT,
    )(total, gate, gain_out, bias_out, w_out)


def plain_per_device(rows, cols, pair, token_mask, gain_in, bias_in, w_in, w_gate, gain_out, bias_out, w_out):
    row_count, col_count, channels = pair.shape
    hidden = w_out.shape[0]
    devices = rows * cols
    share = hidden // devices
    tokens = row_count * col_count
    row_start = lax.axis_index(("half", "quad")) * row_count
    col_start = lax.axis_index("col") * col_count
    mask_float = token_mask.astype(jnp.float32)
    mask_rows = lax.dynamic_slice_in_dim(mask_float, row_start, row_count)
    mask_cols = lax.dynamic_slice_in_dim(mask_float, col_start, col_count)
    pair_mask = (mask_rows[:, None] * mask_cols[None, :]).reshape(1, tokens)
    flat = pair.reshape(tokens, channels).astype(jnp.float32)
    normed = layer_norm(flat, gain_in, bias_in, -1).astype(jnp.bfloat16)
    projected = lax.dot_general(w_in, normed, (((0,), (1,)), ((), ())), preferred_element_type=jnp.float32)
    projected = projected.reshape(2, 2, hidden, tokens)
    sides = (pair_mask * jax.nn.sigmoid(projected[:, 0]) * projected[:, 1]).astype(jnp.bfloat16)
    sides = sides.reshape(2, devices, share, tokens).transpose(1, 0, 2, 3)
    gate = jax.nn.sigmoid(jnp.dot(normed, w_gate, preferred_element_type=jnp.float32))
    got = lax.all_to_all(sides, AXES, split_axis=0, concat_axis=0, tiled=True)
    got = got.reshape(rows, cols, 2, share, row_count, col_count).transpose(2, 3, 0, 4, 1, 5)
    got = got.reshape(2, share, rows * row_count, cols * col_count)
    total = jnp.einsum("cki,ckj->cij", got[0], got[1], preferred_element_type=jnp.float32).astype(jnp.bfloat16)
    total = total.reshape(share, rows, row_count, cols, col_count).transpose(1, 3, 0, 2, 4)
    total = total.reshape(devices, share, tokens)
    total = lax.all_to_all(total, AXES, split_axis=0, concat_axis=0, tiled=True)
    total = total.reshape(hidden, tokens).astype(jnp.float32)
    summed_norm = layer_norm(total, gain_out[:, None], bias_out[:, None], 0).astype(jnp.bfloat16)
    output = lax.dot_general(summed_norm, w_out, (((0,), (0,)), ((), ())), preferred_element_type=jnp.float32)
    return (gate * output).astype(jnp.bfloat16).reshape(row_count, col_count, channels)


def solution(mesh):
    rows, cols = mesh.shape["row"], mesh.shape["col"]
    halves = 2
    parts = (mesh.shape["groups"], halves, rows // halves, cols)
    finer = jax.sharding.Mesh(mesh.devices.reshape(parts), ("groups", "half", "quad", "col"))

    def per_shard(*args):
        near, hidden, length = rows * cols // halves, args[-1].shape[0], args[1].shape[0]
        row_count, col_count, _ = args[0].shape
        spare = LANES - 2 * col_count
        fits = hidden % (2 * GROUP * near) == 0 and cols == 2 and rows // halves == 4 and length <= LANES and row_count % 3 == 0
        fits = fits and 0 < spare < col_count and row_count // 3 * (col_count - spare) * 2 == LANES
        fits = fits and row_count // 3 * (rows // halves) * GROUP == LANES
        return per_device(rows, cols, halves, *args) if fits else plain_per_device(rows, cols, *args)

    tokens = P(("groups", "half", "quad"), "col", None)
    in_specs = (tokens, P("groups"), P(), P(), P(), P(), P(), P(), P())
    return jax.shard_map(per_shard, mesh=finer, in_specs=in_specs, out_specs=tokens, check_vma=False)
```

```python
import functools

import jax
import jax.numpy as jnp
from jax import lax
from jax.experimental import pallas as pl
from jax.experimental.pallas import tpu as pltpu
from jax.sharding import PartitionSpec as P

epsilon = 1e-05
LANES = 128
GROUP = 8
AXES = ("half", "quad", "col")
VMEM = pl.BlockSpec(memory_space=pltpu.VMEM)
HBM = pl.BlockSpec(memory_space=pltpu.HBM)
LIMIT = pltpu.CompilerParams(vmem_limit_bytes=32 * 1024 * 1024)


def sigmoid(x):
    return 0.5 * jnp.tanh(0.5 * x) + 0.5


def layer_norm(values, gain, bias, axis):
    mean = jnp.mean(values, axis=axis, keepdims=True)
    centred = values - mean
    variance = jnp.mean(centred * centred, axis=axis, keepdims=True)
    return centred * lax.rsqrt(variance + epsilon) * gain + bias


def column(row):
    n = row.shape[1]
    eye = lax.broadcasted_iota(jnp.int32, (n, n), 0) == lax.broadcasted_iota(jnp.int32, (n, n), 1)
    return jnp.sum(jnp.where(eye, row, 0.0), axis=1, keepdims=True)


def pack(x):
    rows, tokens = x.shape[-2:]
    whole, rest = divmod(tokens, LANES)
    blocks = [x[..., t * LANES : (t + 1) * LANES] for t in range(whole)]
    if rest:
        tail = x[..., whole * LANES :]
        blocks.append(jnp.concatenate([tail[..., : rows // 2, :], tail[..., rows // 2 :, :]], axis=-1))
    return jnp.concatenate(blocks, axis=-2)


def unpack(x, rows):
    whole, rest = divmod(x.shape[-2], rows)
    blocks = [x[..., t * rows : (t + 1) * rows, :] for t in range(whole)]
    if rest:
        tail = x[..., whole * rows :, :]
        blocks.append(jnp.concatenate([tail[..., : LANES // 2], tail[..., LANES // 2 :]], axis=-2))
    return jnp.concatenate(blocks, axis=-1)


def arrange(x):
    row_count, col_count, _ = x.shape
    whole, spare = row_count // 3, LANES - 2 * col_count
    blocks = []
    for t in range(whole):
        blocks += [x[2 * t], x[2 * t + 1], x[2 * whole + t, :spare]]
    return jnp.concatenate(blocks + [x[2 * whole + t, spare:] for t in range(whole)], axis=0)


def restore(x, row_count, col_count):
    whole, spare = row_count // 3, LANES - 2 * col_count
    rest = col_count - spare
    rows = []
    for t in range(whole):
        rows += [x[t * LANES : t * LANES + col_count], x[t * LANES + col_count : t * LANES + 2 * col_count]]
    for t in range(whole):
        tail = whole * LANES + t * rest
        rows += [x[t * LANES + 2 * col_count : (t + 1) * LANES], x[tail : tail + rest]]
    return jnp.concatenate(rows, axis=0)


def normalise(flat, gain, bias):
    return layer_norm(flat.astype(jnp.float32), gain, bias, -1).astype(jnp.bfloat16)


def project(normed, w, shape, quads):
    ours = w.shape[1] // 4
    tokens = normed.shape[0]
    projected = lax.dot_general(w, arrange(normed.reshape(shape)), (((0,), (1,)), ((), ())), preferred_element_type=jnp.float32)
    left = sigmoid(projected[:ours]) * projected[ours : 2 * ours]
    right = sigmoid(projected[2 * ours : 3 * ours]) * projected[3 * ours :]
    sides = jnp.concatenate([left.reshape(quads, -1, tokens), right.reshape(quads, -1, tokens)], axis=1)
    return pack(sides).astype(jnp.bfloat16)


def own_kernel(quads, cols, pair_hbm, gain_hbm, bias_hbm, w_hbm, mask_hbm, sides_ref, normed_ref, spread_ref, column_mask_ref, w_ref, gain_ref, bias_ref, pair_ref, all_w_ref, mask_ref, sems):
    moves = [(mask_hbm, mask_ref), (pair_hbm, pair_ref), (gain_hbm, gain_ref), (bias_hbm, bias_ref), (w_hbm, all_w_ref)]
    copies = [pltpu.make_async_copy(source, target, sems.at[n]) for n, (source, target) in enumerate(moves)]
    for copy in copies:
        copy.start()
    my_quad, my_col = lax.axis_index("quad"), lax.axis_index("col")
    row_count, _, channels = pair_ref.shape
    tokens = normed_ref.shape[0]
    hidden = all_w_ref.shape[1] // 4
    ours = hidden // cols
    group, lanes = spread_ref.shape
    copies[0].wait()
    mask_row = mask_ref[...].astype(jnp.float32)
    column_mask_ref[...] = column(mask_row)
    start = lax.axis_index("half") * (lanes // group)
    token = lax.broadcasted_iota(jnp.int32, (mask_row.shape[1], lanes), 0)
    lane = lax.broadcasted_iota(jnp.int32, (mask_row.shape[1], lanes), 1)
    whole = row_count // 3
    block, t, row = lane // LANES, lane // (quads * group) % whole, lane // group % quads
    k = (row ^ my_quad) * row_count + jnp.where(block < 2, 2 * t + block, 2 * whole + t)
    pick = jnp.where(k + start == token, 1.0, 0.0)
    kept = jnp.dot(mask_row.astype(jnp.bfloat16), pick.astype(jnp.bfloat16), preferred_element_type=jnp.float32)
    channel = lax.broadcasted_iota(jnp.int32, (group, lanes), 0)
    lane = lax.broadcasted_iota(jnp.int32, (group, lanes), 1)
    spread_ref[...] = jnp.where(lane % group == channel, kept, 0.0)
    for copy in copies[1:4]:
        copy.wait()
    normed = normalise(pair_ref[...].reshape(tokens, channels), gain_ref[...], bias_ref[...])
    normed_ref[...] = normed
    copies[4].wait()
    parts = [all_w_ref[:, at : at + hidden] for at in range(0, 4 * hidden, hidden)]
    w = jnp.concatenate([jnp.where(my_col == 0, part[:, :ours], part[:, ours:]) for part in parts], axis=1)
    w_ref[...] = w
    sides_ref[...] = project(normed, w, pair_ref.shape, quads)


def other_kernel(pair_ref, sides_ref, gain_ref, bias_ref, w_ref, *refs):
    *piece_refs, others_ref = refs
    my_quad, my_col = lax.axis_index("quad"), lax.axis_index("col")
    quads = sides_ref.shape[0]
    normed = normalise(pair_ref[...].reshape(-1, pair_ref.shape[2]), gain_ref[...], bias_ref[...])
    others_ref[...] = project(normed, w_ref[...], pair_ref.shape, quads)
    for step, piece_ref in enumerate(piece_refs):
        piece_ref[my_col] = sides_ref[my_quad ^ step]
        piece_ref[1 - my_col] = others_ref[my_quad ^ step]


def triangle_kernel(far_order, steps, cols, row_count, col_count, share, *refs):
    *got_refs, spread_ref, mask_ref, total_ref, left_ref, wide_ref = refs
    got_refs = {step: ref for step, ref in zip(steps, got_refs)}
    both = 2 * share
    group, lanes = spread_ref.shape
    length = mask_ref.shape[0]
    rows, quads, parts = length // row_count, len(steps), share // group
    whole, spare = row_count // 3, LANES - 2 * col_count
    rest = col_count - spare
    blocks = [[got_refs[row][col].astype(jnp.float32) for row in range(quads)] for col in range(cols)]

    contract = (((1,), (1,)), ((), ()))
    unit = lax.broadcasted_iota(jnp.int32, (LANES, LANES), 0) == lax.broadcasted_iota(jnp.int32, (LANES, LANES), 1)
    unit = jnp.where(unit, 1.0, 0.0).astype(jnp.bfloat16)

    def turned(picks):
        block = jnp.concatenate([blocks[col][row][at : at + group] for col, row, at in picks], axis=0).astype(jnp.bfloat16)
        return lax.dot_general(unit, block, contract, preferred_element_type=jnp.float32)

    tail = turned([(col, row, whole * both + part * group) for col in range(cols) for part in range(parts) for row in range(quads)])

    def side(which, part):
        even, odd, third = [], [], []
        for col in range(cols):
            at = which * share + part * group
            block = turned([(col, row, t * both + at) for t in range(whole) for row in range(quads)])
            even.append(block[:col_count])
            odd.append(block[col_count : 2 * col_count])
            lane = (col * parts + part) * quads * group
            at = which * LANES // 2
            last = [tail[at + t * rest : at + (t + 1) * rest, lane : lane + quads * group] for t in range(whole)]
            third += [block[2 * col_count :], jnp.concatenate(last, axis=1)]
        tokens = [jnp.concatenate(pieces, axis=0) for pieces in (even, odd, third)]
        return jnp.concatenate(tokens, axis=1) * mask_ref[...]

    def placed(pieces):
        return jnp.concatenate([jnp.zeros((piece, lanes), jnp.bfloat16) if isinstance(piece, int) else piece for piece in pieces], axis=0)

    lane_block = lax.broadcasted_iota(jnp.int32, (group, LANES), 1) // rest
    mains, lasts = [], []
    for part in range(parts):
        left_ref[part] = side(0, part)
        right = side(1, part).astype(jnp.bfloat16)
        for row in range(rows):
            for t in range(0, whole, 2):
                pair = []
                for at in (row * row_count, row * row_count + 2):
                    picks = [at + 2 * t, at + 2 * t + 1, row * row_count + 2 * whole + t + len(pair)]
                    copies = [jnp.broadcast_to(left_ref[part, i : i + 1, :], (group, lanes)) for i in picks]
                    pair.append(jnp.concatenate([copy * spread_ref[...] for copy in copies], axis=1))
                at = (row * whole + t) * group
                wide_ref[part, at : at + 2 * group, :] = jnp.concatenate(pair, axis=0).astype(jnp.bfloat16)
        ours = [right[col * col_count : (col + 1) * col_count] for col in range(cols)]
        weights = [
            placed([p for mine in ours for p in (mine, LANES - col_count)]),
            placed([p for mine in ours for p in (col_count, mine, spare)]),
            placed([p for mine in ours for p in (2 * col_count, mine[:spare])]),
        ]
        weights = jnp.concatenate(weights, axis=1)
        mains.append(lax.dot_general(wide_ref[part], weights, contract, preferred_element_type=jnp.float32))
        gap = LANES // parts
        pieces = [[gap * part] + [mine[spare:]] * whole + [LANES - gap * (part + 1)] for mine in ours]
        weights = placed([p for piece in pieces for p in piece if not isinstance(p, int) or p])
        lasts.append(lax.dot_general(wide_ref[part, :, 2 * lanes :], weights, contract, preferred_element_type=jnp.float32))
    for target, device in enumerate(far_order):
        row, col = divmod(device, cols)
        spots = [(row * whole + t) * group for t in range(whole)]
        tiles = [main[at : at + group, col * LANES : (col + 1) * LANES] for at in spots for main in mains]
        last = [part[at : at + group, col * LANES : (col + 1) * LANES] for part in lasts for at in spots]
        tile = last[0]
        for n in range(1, len(last)):
            tile = jnp.where(lane_block >= n, last[n], tile)
        tiles.append(tile)
        total_ref[target] = jnp.concatenate(tiles, axis=0).astype(jnp.bfloat16)


def gate_kernel(normed_ref, w_ref, gain_ref, bias_ref, gate_ref, gain_out_ref, bias_out_ref):
    gate_ref[...] = sigmoid(jnp.dot(normed_ref[...], w_ref[...], preferred_element_type=jnp.float32))
    gain_out_ref[...] = column(gain_ref[...])
    bias_out_ref[...] = column(bias_ref[...])


def output_kernel(far_order, near_order, total_ref, gate_ref, gain_ref, bias_ref, w_ref, out_ref):
    tokens = gate_ref.shape[0]
    hidden = w_ref.shape[0]
    near = len(near_order)
    share = hidden // near
    blocks = []
    for index in near_order:
        parts = [total_ref[source].astype(jnp.float32) for source, device in enumerate(far_order) if device % near == index]
        blocks.append(unpack(sum(parts[1:], parts[0]), share))
    total = jnp.concatenate(blocks, axis=0)
    normed = layer_norm(total, gain_ref[...], bias_ref[...], 0).astype(jnp.bfloat16)
    output = lax.dot_general(normed, w_ref[...], (((0,), (0,)), ((), ())), preferred_element_type=jnp.float32)
    output = restore(output, out_ref.shape[0], out_ref.shape[1])
    out_ref[...] = (gate_ref[...] * output).astype(jnp.bfloat16).reshape(out_ref.shape)


def per_device(rows, cols, halves, pair, token_mask, gain_in, bias_in, w_in, w_gate, gain_out, bias_out, w_out):
    row_count, col_count, channels = pair.shape
    hidden = w_out.shape[0]
    devices = rows * cols
    near = devices // halves
    quads = rows // halves
    far_order = []
    for col in reversed(range(cols)):
        ahead = list(range(quads)) if col else list(range(1, quads)) + [0]
        behind = [0] + list(reversed(range(1, quads))) if col else list(reversed(range(quads)))
        for quad, other in zip(ahead, behind):
            far_order += [near + other * cols + col, quad * cols + col]
    share = hidden // near
    tokens = row_count * col_count
    length = rows * row_count
    depth = length // halves
    token_mask = token_mask.reshape(1, length)
    near_order = [quad * cols + col for col in range(cols) for quad in range(quads)]
    packed = 2 * share * tokens // LANES
    cost = pl.CostEstimate(flops=2 * tokens * channels * 4 * hidden, bytes_accessed=16 * tokens * channels, transcendentals=0)
    other_pair = lax.ppermute(pair, "col", [(i, (i + 1) % cols) for i in range(cols)])
    arguments = (pair, gain_in.reshape(1, channels), bias_in.reshape(1, channels), w_in, token_mask)
    sides, normed, spread, mask, *weights = pl.pallas_call(
        functools.partial(own_kernel, quads, cols),
        out_shape=(
            jax.ShapeDtypeStruct((quads, packed, LANES), jnp.bfloat16),
            jax.ShapeDtypeStruct((tokens, channels), jnp.bfloat16),
            jax.ShapeDtypeStruct((GROUP, GROUP * depth), jnp.float32),
            jax.ShapeDtypeStruct((length, 1), jnp.float32),
            jax.ShapeDtypeStruct((channels, 4 * hidden // cols), jnp.bfloat16),
            jax.ShapeDtypeStruct((1, channels), jnp.float32),
            jax.ShapeDtypeStruct((1, channels), jnp.float32),
        ),
        in_specs=[HBM] * 5,
        out_specs=(VMEM,) * 7,
        scratch_shapes=[
            pltpu.VMEM(pair.shape, pair.dtype),
            pltpu.VMEM(w_in.shape, w_in.dtype),
            pltpu.VMEM((1, length), jnp.int32),
            pltpu.SemaphoreType.DMA((5,)),
        ],
        compiler_params=LIMIT,
        cost_estimate=cost,
    )(*(pltpu.with_memory_space_constraint(x, pltpu.HBM) for x in arguments))
    w_ours, gain_in, bias_in = weights
    pieces = pl.pallas_call(
        other_kernel,
        out_shape=[jax.ShapeDtypeStruct((cols, packed, LANES), jnp.bfloat16)] * quads,
        in_specs=[VMEM] * 5,
        out_specs=[VMEM] * quads,
        scratch_shapes=[pltpu.VMEM((quads, packed, LANES), jnp.bfloat16)],
        compiler_params=LIMIT,
        cost_estimate=cost,
    )(other_pair, sides, gain_in, bias_in, w_ours)
    steps = [3, 1, 2, 0]
    got = [lax.ppermute(pieces[step], "quad", [(i, i ^ step) for i in range(quads)]) if step else pieces[0] for step in steps]
    total = pl.pallas_call(
        functools.partial(triangle_kernel, far_order, steps, cols, row_count, col_count, share),
        out_shape=jax.ShapeDtypeStruct((devices, share * tokens // LANES, LANES), jnp.bfloat16),
        in_specs=[VMEM] * (quads + 2),
        out_specs=VMEM,
        scratch_shapes=[
            pltpu.VMEM((share // GROUP, length, GROUP * depth), jnp.float32),
            pltpu.VMEM((share // GROUP, length // 3 * GROUP, 3 * GROUP * depth), jnp.bfloat16),
        ],
        compiler_params=LIMIT,
    )(*got, spread, mask)
    gate, gain_out, bias_out = pl.pallas_call(
        gate_kernel,
        out_shape=(
            jax.ShapeDtypeStruct((tokens, channels), jnp.float32),
            jax.ShapeDtypeStruct((hidden, 1), jnp.float32),
            jax.ShapeDtypeStruct((hidden, 1), jnp.float32),
        ),
        in_specs=[VMEM] * 4,
        out_specs=(VMEM, VMEM, VMEM),
        compiler_params=LIMIT,
        cost_estimate=pl.CostEstimate(flops=2 * tokens * channels * channels, bytes_accessed=4 * tokens * channels, transcendentals=0),
    )(normed, w_gate, gain_out.reshape(1, hidden), bias_out.reshape(1, hidden))
    total = lax.all_to_all(total, ("half", "quad", "col"), split_axis=0, concat_axis=0, tiled=True, axis_index_groups=[far_order])
    return pl.pallas_call(
        functools.partial(output_kernel, far_order, near_order),
        out_shape=jax.ShapeDtypeStruct(pair.shape, jnp.bfloat16),
        in_specs=[VMEM] * 5,
        out_specs=VMEM,
        compiler_params=LIMIT,
    )(total, gate, gain_out, bias_out, w_out)


def plain_per_device(rows, cols, pair, token_mask, gain_in, bias_in, w_in, w_gate, gain_out, bias_out, w_out):
    row_count, col_count, channels = pair.shape
    hidden = w_out.shape[0]
    devices = rows * cols
    share = hidden // devices
    tokens = row_count * col_count
    row_start = lax.axis_index(("half", "quad")) * row_count
    col_start = lax.axis_index("col") * col_count
    mask_float = token_mask.astype(jnp.float32)
    mask_rows = lax.dynamic_slice_in_dim(mask_float, row_start, row_count)
    mask_cols = lax.dynamic_slice_in_dim(mask_float, col_start, col_count)
    pair_mask = (mask_rows[:, None] * mask_cols[None, :]).reshape(1, tokens)
    flat = pair.reshape(tokens, channels).astype(jnp.float32)
    normed = layer_norm(flat, gain_in, bias_in, -1).astype(jnp.bfloat16)
    projected = lax.dot_general(w_in, normed, (((0,), (1,)), ((), ())), preferred_element_type=jnp.float32)
    projected = projected.reshape(2, 2, hidden, tokens)
    sides = (pair_mask * jax.nn.sigmoid(projected[:, 0]) * projected[:, 1]).astype(jnp.bfloat16)
    sides = sides.reshape(2, devices, share, tokens).transpose(1, 0, 2, 3)
    gate = jax.nn.sigmoid(jnp.dot(normed, w_gate, preferred_element_type=jnp.float32))
    got = lax.all_to_all(sides, AXES, split_axis=0, concat_axis=0, tiled=True)
    got = got.reshape(rows, cols, 2, share, row_count, col_count).transpose(2, 3, 0, 4, 1, 5)
    got = got.reshape(2, share, rows * row_count, cols * col_count)
    total = jnp.einsum("cki,ckj->cij", got[0], got[1], preferred_element_type=jnp.float32).astype(jnp.bfloat16)
    total = total.reshape(share, rows, row_count, cols, col_count).transpose(1, 3, 0, 2, 4)
    total = total.reshape(devices, share, tokens)
    total = lax.all_to_all(total, AXES, split_axis=0, concat_axis=0, tiled=True)
    total = total.reshape(hidden, tokens).astype(jnp.float32)
    summed_norm = layer_norm(total, gain_out[:, None], bias_out[:, None], 0).astype(jnp.bfloat16)
    output = lax.dot_general(summed_norm, w_out, (((0,), (0,)), ((), ())), preferred_element_type=jnp.float32)
    return (gate * output).astype(jnp.bfloat16).reshape(row_count, col_count, channels)


def solution(mesh):
    rows, cols = mesh.shape["row"], mesh.shape["col"]
    halves = 2
    parts = (mesh.shape["groups"], halves, rows // halves, cols)
    finer = jax.sharding.Mesh(mesh.devices.reshape(parts), ("groups", "half", "quad", "col"))

    def per_shard(*args):
        near, hidden, length = rows * cols // halves, args[-1].shape[0], args[1].shape[0]
        row_count, col_count, _ = args[0].shape
        spare = LANES - 2 * col_count
        fits = hidden % (2 * GROUP * near) == 0 and cols == 2 and rows // halves == 4 and length <= LANES and row_count % 3 == 0
        fits = fits and 0 < spare < col_count and row_count // 3 * (col_count - spare) * 2 == LANES
        fits = fits and row_count // 3 * (rows // halves) * GROUP == LANES
        return per_device(rows, cols, halves, *args) if fits else plain_per_device(rows, cols, *args)

    tokens = P(("groups", "half", "quad"), "col", None)
    in_specs = (tokens, P("groups"), P(), P(), P(), P(), P(), P(), P())
    return jax.shard_map(per_shard, mesh=finer, in_specs=in_specs, out_specs=tokens, check_vma=False)
```

```python
import functools

import jax
import jax.numpy as jnp
from jax import lax
from jax.experimental import pallas as pl
from jax.experimental.pallas import tpu as pltpu
from jax.sharding import PartitionSpec as P

epsilon = 1e-05
LANES = 128
GROUP = 8
AXES = ("half", "quad", "col")
VMEM = pl.BlockSpec(memory_space=pltpu.VMEM)
HBM = pl.BlockSpec(memory_space=pltpu.HBM)
LIMIT = pltpu.CompilerParams(vmem_limit_bytes=32 * 1024 * 1024)


def sigmoid(x):
    return 0.5 * jnp.tanh(0.5 * x) + 0.5


def layer_norm(values, gain, bias, axis):
    mean = jnp.mean(values, axis=axis, keepdims=True)
    centred = values - mean
    variance = jnp.mean(centred * centred, axis=axis, keepdims=True)
    return centred * lax.rsqrt(variance + epsilon) * gain + bias


def column(row):
    n = row.shape[1]
    eye = lax.broadcasted_iota(jnp.int32, (n, n), 0) == lax.broadcasted_iota(jnp.int32, (n, n), 1)
    return jnp.sum(jnp.where(eye, row, 0.0), axis=1, keepdims=True)


def pack(x):
    rows, tokens = x.shape[-2:]
    whole, rest = divmod(tokens, LANES)
    blocks = [x[..., t * LANES : (t + 1) * LANES] for t in range(whole)]
    if rest:
        tail = x[..., whole * LANES :]
        blocks.append(jnp.concatenate([tail[..., : rows // 2, :], tail[..., rows // 2 :, :]], axis=-1))
    return jnp.concatenate(blocks, axis=-2)


def arrange(x):
    row_count, col_count, _ = x.shape
    whole, spare = row_count // 3, LANES - 2 * col_count
    blocks = []
    for t in range(whole):
        blocks += [x[2 * t], x[2 * t + 1], x[2 * whole + t, :spare]]
    return jnp.concatenate(blocks + [x[2 * whole + t, spare:] for t in range(whole)], axis=0)


def normalise(flat, gain, bias):
    return layer_norm(flat.astype(jnp.float32), gain, bias, -1).astype(jnp.bfloat16)


def project(normed, w, shape, quads):
    ours = w.shape[1] // 4
    tokens = normed.shape[0]
    projected = lax.dot_general(w, arrange(normed.reshape(shape)), (((0,), (1,)), ((), ())), preferred_element_type=jnp.float32)
    left = sigmoid(projected[:ours]) * projected[ours : 2 * ours]
    right = sigmoid(projected[2 * ours : 3 * ours]) * projected[3 * ours :]
    sides = jnp.concatenate([left.reshape(quads, -1, tokens), right.reshape(quads, -1, tokens)], axis=1)
    return pack(sides).astype(jnp.bfloat16)


def own_kernel(quads, cols, pair_hbm, gain_hbm, bias_hbm, w_hbm, mask_hbm, sides_ref, normed_ref, spread_ref, column_mask_ref, w_ref, gain_ref, bias_ref, pair_ref, all_w_ref, mask_ref, sems):
    moves = [(mask_hbm, mask_ref), (pair_hbm, pair_ref), (gain_hbm, gain_ref), (bias_hbm, bias_ref), (w_hbm, all_w_ref)]
    copies = [pltpu.make_async_copy(source, target, sems.at[n]) for n, (source, target) in enumerate(moves)]
    for copy in copies:
        copy.start()
    my_quad, my_col = lax.axis_index("quad"), lax.axis_index("col")
    row_count, _, channels = pair_ref.shape
    tokens = normed_ref.shape[0]
    hidden = all_w_ref.shape[1] // 4
    ours = hidden // cols
    group, lanes = spread_ref.shape
    copies[0].wait()
    mask_row = mask_ref[...].astype(jnp.float32)
    column_mask_ref[...] = column(mask_row)
    start = lax.axis_index("half") * (lanes // group)
    token = lax.broadcasted_iota(jnp.int32, (mask_row.shape[1], lanes), 0)
    lane = lax.broadcasted_iota(jnp.int32, (mask_row.shape[1], lanes), 1)
    whole = row_count // 3
    block, t, row = lane // LANES, lane // (quads * group) % whole, lane // group % quads
    k = (row ^ my_quad) * row_count + jnp.where(block < 2, 2 * t + block, 2 * whole + t)
    pick = jnp.where(k + start == token, 1.0, 0.0)
    kept = jnp.dot(mask_row.astype(jnp.bfloat16), pick.astype(jnp.bfloat16), preferred_element_type=jnp.float32)
    channel = lax.broadcasted_iota(jnp.int32, (group, lanes), 0)
    lane = lax.broadcasted_iota(jnp.int32, (group, lanes), 1)
    spread_ref[...] = jnp.where(lane % group == channel, kept, 0.0)
    for copy in copies[1:4]:
        copy.wait()
    normed = normalise(pair_ref[...].reshape(tokens, channels), gain_ref[...], bias_ref[...])
    normed_ref[...] = normed
    copies[4].wait()
    parts = [all_w_ref[:, at : at + hidden] for at in range(0, 4 * hidden, hidden)]
    w = jnp.concatenate([jnp.where(my_col == 0, part[:, :ours], part[:, ours:]) for part in parts], axis=1)
    w_ref[...] = w
    sides_ref[...] = project(normed, w, pair_ref.shape, quads)


def other_kernel(pair_ref, sides_ref, gain_ref, bias_ref, w_ref, *refs):
    *piece_refs, others_ref = refs
    my_quad, my_col = lax.axis_index("quad"), lax.axis_index("col")
    quads = sides_ref.shape[0]
    normed = normalise(pair_ref[...].reshape(-1, pair_ref.shape[2]), gain_ref[...], bias_ref[...])
    others_ref[...] = project(normed, w_ref[...], pair_ref.shape, quads)
    for step, piece_ref in enumerate(piece_refs):
        piece_ref[my_col] = sides_ref[my_quad ^ step]
        piece_ref[1 - my_col] = others_ref[my_quad ^ step]


def triangle_kernel(far_order, steps, cols, row_count, col_count, share, *refs):
    *got_refs, spread_ref, mask_ref, total_ref, left_ref, wide_ref = refs
    got_refs = {step: ref for step, ref in zip(steps, got_refs)}
    both = 2 * share
    group, lanes = spread_ref.shape
    length = mask_ref.shape[0]
    rows, quads, parts = length // row_count, len(steps), share // group
    whole, spare = row_count // 3, LANES - 2 * col_count
    rest = col_count - spare
    blocks = [[got_refs[row][col].astype(jnp.float32) for row in range(quads)] for col in range(cols)]

    def turned(picks):
        return jnp.concatenate([blocks[col][row][at : at + group] for col, row, at in picks], axis=0).T

    tail = turned([(col, row, whole * both + part * group) for col in range(cols) for part in range(parts) for row in range(quads)])

    def side(which, part):
        even, odd, third = [], [], []
        for col in range(cols):
            at = which * share + part * group
            block = turned([(col, row, t * both + at) for t in range(whole) for row in range(quads)])
            even.append(block[:col_count])
            odd.append(block[col_count : 2 * col_count])
            lane = (col * parts + part) * quads * group
            at = which * LANES // 2
            last = [tail[at + t * rest : at + (t + 1) * rest, lane : lane + quads * group] for t in range(whole)]
            third += [block[2 * col_count :], jnp.concatenate(last, axis=1)]
        tokens = [jnp.concatenate(pieces, axis=0) for pieces in (even, odd, third)]
        return jnp.concatenate(tokens, axis=1) * mask_ref[...]

    def placed(pieces):
        return jnp.concatenate([jnp.zeros((piece, lanes), jnp.bfloat16) if isinstance(piece, int) else piece for piece in pieces], axis=0)

    contract = (((1,), (1,)), ((), ()))
    lane_block = lax.broadcasted_iota(jnp.int32, (group, LANES), 1) // rest
    mains, lasts = [], []
    for part in range(parts):
        left_ref[part] = side(0, part)
        right = side(1, part).astype(jnp.bfloat16)
        for row in range(rows):
            for t in range(0, whole, 2):
                pair = []
                for at in (row * row_count, row * row_count + 2):
                    picks = [at + 2 * t, at + 2 * t + 1, row * row_count + 2 * whole + t + len(pair)]
                    copies = [jnp.broadcast_to(left_ref[part, i : i + 1, :], (group, lanes)) for i in picks]
                    pair.append(jnp.concatenate([copy * spread_ref[...] for copy in copies], axis=1))
                at = (row * whole + t) * group
                wide_ref[part, at : at + 2 * group, :] = jnp.concatenate(pair, axis=0).astype(jnp.bfloat16)
        ours = [right[col * col_count : (col + 1) * col_count] for col in range(cols)]
        weights = [
            placed([p for mine in ours for p in (mine, LANES - col_count)]),
            placed([p for mine in ours for p in (col_count, mine, spare)]),
            placed([p for mine in ours for p in (2 * col_count, mine[:spare])]),
        ]
        weights = jnp.concatenate(weights, axis=1)
        mains.append(lax.dot_general(wide_ref[part], weights, contract, preferred_element_type=jnp.float32))
        gap = LANES // parts
        pieces = [[gap * part] + [mine[spare:]] * whole + [LANES - gap * (part + 1)] for mine in ours]
        weights = placed([p for piece in pieces for p in piece if not isinstance(p, int) or p])
        lasts.append(lax.dot_general(wide_ref[part, :, 2 * lanes :], weights, contract, preferred_element_type=jnp.float32))
    for target, device in enumerate(far_order):
        row, col = divmod(device, cols)
        spots = [(row * whole + t) * group for t in range(whole)]
        tiles = [main[at : at + group, col * LANES : (col + 1) * LANES] for at in spots for main in mains]
        last = [part[at : at + group, col * LANES : (col + 1) * LANES] for part in lasts for at in spots]
        tile = last[0]
        for n in range(1, len(last)):
            tile = jnp.where(lane_block >= n, last[n], tile)
        tiles.append(tile)
        total_ref[target] = jnp.concatenate(tiles, axis=0).astype(jnp.bfloat16)


def gate_kernel(normed_ref, w_ref, gain_ref, bias_ref, gate_ref, gain_out_ref, bias_out_ref):
    gate_ref[...] = sigmoid(jnp.dot(normed_ref[...], w_ref[...], preferred_element_type=jnp.float32))
    gain_out_ref[...] = column(gain_ref[...])
    bias_out_ref[...] = column(bias_ref[...])


def output_kernel(far_order, near_order, total_ref, gate_ref, gain_ref, bias_ref, w_ref, out_hbm, out_ref, sems):
    row_count, col_count, _ = out_ref.shape
    near = len(near_order)
    share = w_ref.shape[0] // near
    whole, spare = row_count // 3, LANES - 2 * col_count
    rest = col_count - spare
    blocks = []
    for index in near_order:
        parts = [total_ref[source].astype(jnp.float32) for source, device in enumerate(far_order) if device % near == index]
        blocks.append(sum(parts[1:], parts[0]))
    tails = [block[whole * share :] for block in blocks]
    tails = [jnp.concatenate([tail[:, : LANES // 2], tail[:, LANES // 2 :]], axis=0) for tail in tails]
    columns = [jnp.concatenate([block[t * share : (t + 1) * share] for block in blocks], axis=0) for t in range(whole)]
    columns.append(jnp.concatenate(tails, axis=0))

    def project(picks):
        total = jnp.concatenate([columns[pick] for pick in picks], axis=1)
        normed = layer_norm(total, gain_ref[...], bias_ref[...], 0).astype(jnp.bfloat16)
        return lax.dot_general(normed, w_ref[...], (((0,), (0,)), ((), ())), preferred_element_type=jnp.float32)

    def store(row, at, values):
        spot = pl.ds(row * col_count + at, values.shape[0])
        out_ref[row, pl.ds(at, values.shape[0])] = (gate_ref[spot] * values).astype(jnp.bfloat16)

    copies = []
    half = whole // 2
    for first in (0, half):
        values = project(list(range(first, first + half)) + ([whole] if first == 0 else []))
        if first == 0:
            for t in range(whole):
                at = half * LANES + t * rest
                store(2 * whole + t, spare, values[at : at + rest])
        for n in range(half):
            t = first + n
            tile = values[n * LANES : (n + 1) * LANES]
            store(2 * t, 0, tile[:col_count])
            store(2 * t + 1, 0, tile[col_count : 2 * col_count])
            store(2 * whole + t, 0, tile[2 * col_count :])
        for rows in (pl.ds(2 * first, 2 * half), pl.ds(2 * whole + first, half)):
            copy = pltpu.make_async_copy(out_ref.at[rows], out_hbm.at[rows], sems.at[len(copies)])
            copy.start()
            copies.append(copy)
    for copy in copies:
        copy.wait()


def per_device(rows, cols, halves, pair, token_mask, gain_in, bias_in, w_in, w_gate, gain_out, bias_out, w_out):
    row_count, col_count, channels = pair.shape
    hidden = w_out.shape[0]
    devices = rows * cols
    near = devices // halves
    quads = rows // halves
    far_order = []
    for col in reversed(range(cols)):
        ahead = list(range(quads)) if col else list(range(1, quads)) + [0]
        behind = [0] + list(reversed(range(1, quads))) if col else list(reversed(range(quads)))
        for quad, other in zip(ahead, behind):
            far_order += [near + other * cols + col, quad * cols + col]
    share = hidden // near
    tokens = row_count * col_count
    length = rows * row_count
    depth = length // halves
    token_mask = token_mask.reshape(1, length)
    near_order = [quad * cols + col for col in range(cols) for quad in range(quads)]
    packed = 2 * share * tokens // LANES
    cost = pl.CostEstimate(flops=2 * tokens * channels * 4 * hidden, bytes_accessed=16 * tokens * channels, transcendentals=0)
    other_pair = lax.ppermute(pair, "col", [(i, (i + 1) % cols) for i in range(cols)])
    arguments = (pair, gain_in.reshape(1, channels), bias_in.reshape(1, channels), w_in, token_mask)
    sides, normed, spread, mask, *weights = pl.pallas_call(
        functools.partial(own_kernel, quads, cols),
        out_shape=(
            jax.ShapeDtypeStruct((quads, packed, LANES), jnp.bfloat16),
            jax.ShapeDtypeStruct((tokens, channels), jnp.bfloat16),
            jax.ShapeDtypeStruct((GROUP, GROUP * depth), jnp.float32),
            jax.ShapeDtypeStruct((length, 1), jnp.float32),
            jax.ShapeDtypeStruct((channels, 4 * hidden // cols), jnp.bfloat16),
            jax.ShapeDtypeStruct((1, channels), jnp.float32),
            jax.ShapeDtypeStruct((1, channels), jnp.float32),
        ),
        in_specs=[HBM] * 5,
        out_specs=(VMEM,) * 7,
        scratch_shapes=[
            pltpu.VMEM(pair.shape, pair.dtype),
            pltpu.VMEM(w_in.shape, w_in.dtype),
            pltpu.VMEM((1, length), jnp.int32),
            pltpu.SemaphoreType.DMA((5,)),
        ],
        compiler_params=LIMIT,
        cost_estimate=cost,
    )(*(pltpu.with_memory_space_constraint(x, pltpu.HBM) for x in arguments))
    w_ours, gain_in, bias_in = weights
    pieces = pl.pallas_call(
        other_kernel,
        out_shape=[jax.ShapeDtypeStruct((cols, packed, LANES), jnp.bfloat16)] * quads,
        in_specs=[VMEM] * 5,
        out_specs=[VMEM] * quads,
        scratch_shapes=[pltpu.VMEM((quads, packed, LANES), jnp.bfloat16)],
        compiler_params=LIMIT,
        cost_estimate=cost,
    )(other_pair, sides, gain_in, bias_in, w_ours)
    steps = [3, 1, 2, 0]
    got = [lax.ppermute(pieces[step], "quad", [(i, i ^ step) for i in range(quads)]) if step else pieces[0] for step in steps]
    total = pl.pallas_call(
        functools.partial(triangle_kernel, far_order, steps, cols, row_count, col_count, share),
        out_shape=jax.ShapeDtypeStruct((devices, share * tokens // LANES, LANES), jnp.bfloat16),
        in_specs=[VMEM] * (quads + 2),
        out_specs=VMEM,
        scratch_shapes=[
            pltpu.VMEM((share // GROUP, length, GROUP * depth), jnp.float32),
            pltpu.VMEM((share // GROUP, length // 3 * GROUP, 3 * GROUP * depth), jnp.bfloat16),
        ],
        compiler_params=LIMIT,
    )(*got, spread, mask)
    gate, gain_out, bias_out = pl.pallas_call(
        gate_kernel,
        out_shape=(
            jax.ShapeDtypeStruct((tokens, channels), jnp.float32),
            jax.ShapeDtypeStruct((hidden, 1), jnp.float32),
            jax.ShapeDtypeStruct((hidden, 1), jnp.float32),
        ),
        in_specs=[VMEM] * 4,
        out_specs=(VMEM, VMEM, VMEM),
        compiler_params=LIMIT,
        cost_estimate=pl.CostEstimate(flops=2 * tokens * channels * channels, bytes_accessed=4 * tokens * channels, transcendentals=0),
    )(normed, w_gate, gain_out.reshape(1, hidden), bias_out.reshape(1, hidden))
    total = lax.all_to_all(total, ("half", "quad", "col"), split_axis=0, concat_axis=0, tiled=True, axis_index_groups=[far_order])
    return pl.pallas_call(
        functools.partial(output_kernel, far_order, near_order),
        out_shape=jax.ShapeDtypeStruct(pair.shape, jnp.bfloat16),
        in_specs=[VMEM] * 5,
        out_specs=HBM,
        scratch_shapes=[pltpu.VMEM(pair.shape, jnp.bfloat16), pltpu.SemaphoreType.DMA((4,))],
        compiler_params=LIMIT,
    )(total, gate, gain_out, bias_out, w_out)


def plain_per_device(rows, cols, pair, token_mask, gain_in, bias_in, w_in, w_gate, gain_out, bias_out, w_out):
    row_count, col_count, channels = pair.shape
    hidden = w_out.shape[0]
    devices = rows * cols
    share = hidden // devices
    tokens = row_count * col_count
    row_start = lax.axis_index(("half", "quad")) * row_count
    col_start = lax.axis_index("col") * col_count
    mask_float = token_mask.astype(jnp.float32)
    mask_rows = lax.dynamic_slice_in_dim(mask_float, row_start, row_count)
    mask_cols = lax.dynamic_slice_in_dim(mask_float, col_start, col_count)
    pair_mask = (mask_rows[:, None] * mask_cols[None, :]).reshape(1, tokens)
    flat = pair.reshape(tokens, channels).astype(jnp.float32)
    normed = layer_norm(flat, gain_in, bias_in, -1).astype(jnp.bfloat16)
    projected = lax.dot_general(w_in, normed, (((0,), (1,)), ((), ())), preferred_element_type=jnp.float32)
    projected = projected.reshape(2, 2, hidden, tokens)
    sides = (pair_mask * jax.nn.sigmoid(projected[:, 0]) * projected[:, 1]).astype(jnp.bfloat16)
    sides = sides.reshape(2, devices, share, tokens).transpose(1, 0, 2, 3)
    gate = jax.nn.sigmoid(jnp.dot(normed, w_gate, preferred_element_type=jnp.float32))
    got = lax.all_to_all(sides, AXES, split_axis=0, concat_axis=0, tiled=True)
    got = got.reshape(rows, cols, 2, share, row_count, col_count).transpose(2, 3, 0, 4, 1, 5)
    got = got.reshape(2, share, rows * row_count, cols * col_count)
    total = jnp.einsum("cki,ckj->cij", got[0], got[1], preferred_element_type=jnp.float32).astype(jnp.bfloat16)
    total = total.reshape(share, rows, row_count, cols, col_count).transpose(1, 3, 0, 2, 4)
    total = total.reshape(devices, share, tokens)
    total = lax.all_to_all(total, AXES, split_axis=0, concat_axis=0, tiled=True)
    total = total.reshape(hidden, tokens).astype(jnp.float32)
    summed_norm = layer_norm(total, gain_out[:, None], bias_out[:, None], 0).astype(jnp.bfloat16)
    output = lax.dot_general(summed_norm, w_out, (((0,), (0,)), ((), ())), preferred_element_type=jnp.float32)
    return (gate * output).astype(jnp.bfloat16).reshape(row_count, col_count, channels)


def solution(mesh):
    rows, cols = mesh.shape["row"], mesh.shape["col"]
    halves = 2
    parts = (mesh.shape["groups"], halves, rows // halves, cols)
    finer = jax.sharding.Mesh(mesh.devices.reshape(parts), ("groups", "half", "quad", "col"))

    def per_shard(*args):
        near, hidden, length = rows * cols // halves, args[-1].shape[0], args[1].shape[0]
        row_count, col_count, _ = args[0].shape
        spare = LANES - 2 * col_count
        fits = hidden % (2 * GROUP * near) == 0 and cols == 2 and rows // halves == 4 and length <= LANES and row_count % 3 == 0
        fits = fits and 0 < spare < col_count and row_count // 3 * (col_count - spare) * 2 == LANES
        fits = fits and row_count // 3 * (rows // halves) * GROUP == LANES and row_count % 6 == 0
        return per_device(rows, cols, halves, *args) if fits else plain_per_device(rows, cols, *args)

    tokens = P(("groups", "half", "quad"), "col", None)
    in_specs = (tokens, P("groups"), P(), P(), P(), P(), P(), P(), P())
    return jax.shard_map(per_shard, mesh=finer, in_specs=in_specs, out_specs=tokens, check_vma=False)
```

```python
import functools

import jax
import jax.numpy as jnp
from jax import lax
from jax.experimental import pallas as pl
from jax.experimental.pallas import tpu as pltpu
from jax.sharding import PartitionSpec as P

epsilon = 1e-05
LANES = 128
GROUP = 8
AXES = ("half", "quad", "col")
VMEM = pl.BlockSpec(memory_space=pltpu.VMEM)
HBM = pl.BlockSpec(memory_space=pltpu.HBM)
LIMIT = pltpu.CompilerParams(vmem_limit_bytes=32 * 1024 * 1024)


def sigmoid(x):
    return 0.5 * jnp.tanh(0.5 * x) + 0.5


def layer_norm(values, gain, bias, axis):
    mean = jnp.mean(values, axis=axis, keepdims=True)
    centred = values - mean
    variance = jnp.mean(centred * centred, axis=axis, keepdims=True)
    return centred * lax.rsqrt(variance + epsilon) * gain + bias


def column(row):
    n = row.shape[1]
    eye = lax.broadcasted_iota(jnp.int32, (n, n), 0) == lax.broadcasted_iota(jnp.int32, (n, n), 1)
    return jnp.sum(jnp.where(eye, row, 0.0), axis=1, keepdims=True)


def pack(x):
    rows, tokens = x.shape[-2:]
    whole, rest = divmod(tokens, LANES)
    blocks = [x[..., t * LANES : (t + 1) * LANES] for t in range(whole)]
    if rest:
        tail = x[..., whole * LANES :]
        blocks.append(jnp.concatenate([tail[..., : rows // 2, :], tail[..., rows // 2 :, :]], axis=-1))
    return jnp.concatenate(blocks, axis=-2)


def unpack(x, rows):
    whole, rest = divmod(x.shape[-2], rows)
    blocks = [x[..., t * rows : (t + 1) * rows, :] for t in range(whole)]
    if rest:
        tail = x[..., whole * rows :, :]
        blocks.append(jnp.concatenate([tail[..., : LANES // 2], tail[..., LANES // 2 :]], axis=-2))
    return jnp.concatenate(blocks, axis=-1)


def arrange(x):
    row_count, col_count, _ = x.shape
    whole, spare = row_count // 3, LANES - 2 * col_count
    blocks = []
    for t in range(whole):
        blocks += [x[2 * t], x[2 * t + 1], x[2 * whole + t, :spare]]
    return jnp.concatenate(blocks + [x[2 * whole + t, spare:] for t in range(whole)], axis=0)


def restore(x, row_count, col_count):
    whole, spare = row_count // 3, LANES - 2 * col_count
    rest = col_count - spare
    rows = []
    for t in range(whole):
        rows += [x[t * LANES : t * LANES + col_count], x[t * LANES + col_count : t * LANES + 2 * col_count]]
    for t in range(whole):
        tail = whole * LANES + t * rest
        rows += [x[t * LANES + 2 * col_count : (t + 1) * LANES], x[tail : tail + rest]]
    return jnp.concatenate(rows, axis=0)


def normalise(flat, gain, bias):
    return layer_norm(flat.astype(jnp.float32), gain, bias, -1).astype(jnp.bfloat16)


def project(normed, w, shape, quads):
    ours = w.shape[0] // 4
    tokens = normed.shape[0]
    projected = lax.dot_general(w, arrange(normed.reshape(shape)), (((1,), (1,)), ((), ())), preferred_element_type=jnp.float32)
    left = sigmoid(projected[:ours]) * projected[ours : 2 * ours]
    right = sigmoid(projected[2 * ours : 3 * ours]) * projected[3 * ours :]
    sides = jnp.concatenate([left.reshape(quads, -1, tokens), right.reshape(quads, -1, tokens)], axis=1)
    return pack(sides).astype(jnp.bfloat16)


def own_kernel(quads, cols, pair_hbm, gain_hbm, bias_hbm, w_hbm, mask_hbm, sides_ref, normed_ref, spread_ref, column_mask_ref, w_ref, gain_ref, bias_ref, pair_ref, all_w_ref, mask_ref, sems):
    moves = [(mask_hbm, mask_ref), (pair_hbm, pair_ref), (gain_hbm, gain_ref), (bias_hbm, bias_ref), (w_hbm, all_w_ref)]
    copies = [pltpu.make_async_copy(source, target, sems.at[n]) for n, (source, target) in enumerate(moves)]
    for copy in copies:
        copy.start()
    my_quad, my_col = lax.axis_index("quad"), lax.axis_index("col")
    row_count, _, channels = pair_ref.shape
    tokens = normed_ref.shape[0]
    hidden = all_w_ref.shape[1] // 4
    ours = hidden // cols
    group, lanes = spread_ref.shape
    copies[0].wait()
    mask_row = mask_ref[...].astype(jnp.float32)
    column_mask_ref[...] = column(mask_row)
    start = lax.axis_index("half") * (lanes // group)
    token = lax.broadcasted_iota(jnp.int32, (mask_row.shape[1], lanes), 0)
    lane = lax.broadcasted_iota(jnp.int32, (mask_row.shape[1], lanes), 1)
    whole = row_count // 3
    block, t, row = lane // LANES, lane // (quads * group) % whole, lane // group % quads
    k = (row ^ my_quad) * row_count + jnp.where(block < 2, 2 * t + block, 2 * whole + t)
    pick = jnp.where(k + start == token, 1.0, 0.0)
    kept = jnp.dot(mask_row.astype(jnp.bfloat16), pick.astype(jnp.bfloat16), preferred_element_type=jnp.float32)
    channel = lax.broadcasted_iota(jnp.int32, (group, lanes), 0)
    lane = lax.broadcasted_iota(jnp.int32, (group, lanes), 1)
    spread_ref[...] = jnp.where(lane % group == channel, kept, 0.0)
    for copy in copies[1:4]:
        copy.wait()
    normed = normalise(pair_ref[...].reshape(tokens, channels), gain_ref[...], bias_ref[...])
    normed_ref[...] = normed
    copies[4].wait()
    parts = [all_w_ref[:, at : at + hidden] for at in range(0, 4 * hidden, hidden)]
    w = jnp.concatenate([jnp.where(my_col == 0, part[:, :ours], part[:, ours:]) for part in parts], axis=1).T
    w_ref[...] = w
    sides_ref[...] = project(normed, w, pair_ref.shape, quads)


def other_kernel(pair_ref, sides_ref, gain_ref, bias_ref, w_ref, *refs):
    *piece_refs, others_ref = refs
    my_quad, my_col = lax.axis_index("quad"), lax.axis_index("col")
    quads = sides_ref.shape[0]
    normed = normalise(pair_ref[...].reshape(-1, pair_ref.shape[2]), gain_ref[...], bias_ref[...])
    others_ref[...] = project(normed, w_ref[...], pair_ref.shape, quads)
    for step, piece_ref in enumerate(piece_refs):
        piece_ref[my_col] = sides_ref[my_quad ^ step]
        piece_ref[1 - my_col] = others_ref[my_quad ^ step]


def triangle_kernel(far_order, steps, cols, row_count, col_count, share, *refs):
    *got_refs, spread_ref, mask_ref, total_ref, left_ref, wide_ref = refs
    got_refs = {step: ref for step, ref in zip(steps, got_refs)}
    both = 2 * share
    group, lanes = spread_ref.shape
    length = mask_ref.shape[0]
    rows, quads, parts = length // row_count, len(steps), share // group
    whole, spare = row_count // 3, LANES - 2 * col_count
    rest = col_count - spare
    blocks = [[got_refs[row][col].astype(jnp.float32) for row in range(quads)] for col in range(cols)]

    def turned(picks):
        return jnp.concatenate([blocks[col][row][at : at + group] for col, row, at in picks], axis=0).T

    tail = turned([(col, row, whole * both + part * group) for col in range(cols) for part in range(parts) for row in range(quads)])

    def side(which, part):
        even, odd, third = [], [], []
        for col in range(cols):
            at = which * share + part * group
            block = turned([(col, row, t * both + at) for t in range(whole) for row in range(quads)])
            even.append(block[:col_count])
            odd.append(block[col_count : 2 * col_count])
            lane = (col * parts + part) * quads * group
            at = which * LANES // 2
            last = [tail[at + t * rest : at + (t + 1) * rest, lane : lane + quads * group] for t in range(whole)]
            third += [block[2 * col_count :], jnp.concatenate(last, axis=1)]
        tokens = [jnp.concatenate(pieces, axis=0) for pieces in (even, odd, third)]
        return jnp.concatenate(tokens, axis=1) * mask_ref[...]

    def placed(pieces):
        return jnp.concatenate([jnp.zeros((piece, lanes), jnp.bfloat16) if isinstance(piece, int) else piece for piece in pieces], axis=0)

    contract = (((1,), (1,)), ((), ()))
    lane_block = lax.broadcasted_iota(jnp.int32, (group, LANES), 1) // rest
    mains, lasts = [], []
    for part in range(parts):
        left_ref[part] = side(0, part)
        right = side(1, part).astype(jnp.bfloat16)
        for row in range(rows):
            for t in range(0, whole, 2):
                pair = []
                for at in (row * row_count, row * row_count + 2):
                    picks = [at + 2 * t, at + 2 * t + 1, row * row_count + 2 * whole + t + len(pair)]
                    copies = [jnp.broadcast_to(left_ref[part, i : i + 1, :], (group, lanes)) for i in picks]
                    pair.append(jnp.concatenate([copy * spread_ref[...] for copy in copies], axis=1))
                at = (row * whole + t) * group
                wide_ref[part, at : at + 2 * group, :] = jnp.concatenate(pair, axis=0).astype(jnp.bfloat16)
        ours = [right[col * col_count : (col + 1) * col_count] for col in range(cols)]
        weights = [
            placed([p for mine in ours for p in (mine, LANES - col_count)]),
            placed([p for mine in ours for p in (col_count, mine, spare)]),
            placed([p for mine in ours for p in (2 * col_count, mine[:spare])]),
        ]
        weights = jnp.concatenate(weights, axis=1)
        mains.append(lax.dot_general(wide_ref[part], weights, contract, preferred_element_type=jnp.float32))
        gap = LANES // parts
        pieces = [[gap * part] + [mine[spare:]] * whole + [LANES - gap * (part + 1)] for mine in ours]
        weights = placed([p for piece in pieces for p in piece if not isinstance(p, int) or p])
        lasts.append(lax.dot_general(wide_ref[part, :, 2 * lanes :], weights, contract, preferred_element_type=jnp.float32))
    for target, device in enumerate(far_order):
        row, col = divmod(device, cols)
        spots = [(row * whole + t) * group for t in range(whole)]
        tiles = [main[at : at + group, col * LANES : (col + 1) * LANES] for at in spots for main in mains]
        last = [part[at : at + group, col * LANES : (col + 1) * LANES] for part in lasts for at in spots]
        tile = last[0]
        for n in range(1, len(last)):
            tile = jnp.where(lane_block >= n, last[n], tile)
        tiles.append(tile)
        total_ref[target] = jnp.concatenate(tiles, axis=0).astype(jnp.bfloat16)


def gate_kernel(normed_ref, w_ref, gain_ref, bias_ref, gate_ref, gain_out_ref, bias_out_ref):
    gate_ref[...] = sigmoid(jnp.dot(normed_ref[...], w_ref[...], preferred_element_type=jnp.float32))
    gain_out_ref[...] = column(gain_ref[...])
    bias_out_ref[...] = column(bias_ref[...])


def output_kernel(far_order, near_order, total_ref, gate_ref, gain_ref, bias_ref, w_ref, out_ref):
    tokens = gate_ref.shape[0]
    hidden = w_ref.shape[0]
    near = len(near_order)
    share = hidden // near
    blocks = []
    for index in near_order:
        parts = [total_ref[source].astype(jnp.float32) for source, device in enumerate(far_order) if device % near == index]
        blocks.append(unpack(sum(parts[1:], parts[0]), share))
    total = jnp.concatenate(blocks, axis=0)
    normed = layer_norm(total, gain_ref[...], bias_ref[...], 0).astype(jnp.bfloat16)
    output = lax.dot_general(normed, w_ref[...], (((0,), (0,)), ((), ())), preferred_element_type=jnp.float32)
    output = restore(output, out_ref.shape[0], out_ref.shape[1])
    out_ref[...] = (gate_ref[...] * output).astype(jnp.bfloat16).reshape(out_ref.shape)


def per_device(rows, cols, halves, pair, token_mask, gain_in, bias_in, w_in, w_gate, gain_out, bias_out, w_out):
    row_count, col_count, channels = pair.shape
    hidden = w_out.shape[0]
    devices = rows * cols
    near = devices // halves
    quads = rows // halves
    far_order = []
    for col in reversed(range(cols)):
        ahead = list(range(quads)) if col else list(range(1, quads)) + [0]
        behind = [0] + list(reversed(range(1, quads))) if col else list(reversed(range(quads)))
        for quad, other in zip(ahead, behind):
            far_order += [near + other * cols + col, quad * cols + col]
    share = hidden // near
    tokens = row_count * col_count
    length = rows * row_count
    depth = length // halves
    token_mask = token_mask.reshape(1, length)
    near_order = [quad * cols + col for col in range(cols) for quad in range(quads)]
    packed = 2 * share * tokens // LANES
    cost = pl.CostEstimate(flops=2 * tokens * channels * 4 * hidden, bytes_accessed=16 * tokens * channels, transcendentals=0)
    other_pair = lax.ppermute(pair, "col", [(i, (i + 1) % cols) for i in range(cols)])
    arguments = (pair, gain_in.reshape(1, channels), bias_in.reshape(1, channels), w_in, token_mask)
    sides, normed, spread, mask, *weights = pl.pallas_call(
        functools.partial(own_kernel, quads, cols),
        out_shape=(
            jax.ShapeDtypeStruct((quads, packed, LANES), jnp.bfloat16),
            jax.ShapeDtypeStruct((tokens, channels), jnp.bfloat16),
            jax.ShapeDtypeStruct((GROUP, GROUP * depth), jnp.float32),
            jax.ShapeDtypeStruct((length, 1), jnp.float32),
            jax.ShapeDtypeStruct((4 * hidden // cols, channels), jnp.bfloat16),
            jax.ShapeDtypeStruct((1, channels), jnp.float32),
            jax.ShapeDtypeStruct((1, channels), jnp.float32),
        ),
        in_specs=[HBM] * 5,
        out_specs=(VMEM,) * 7,
        scratch_shapes=[
            pltpu.VMEM(pair.shape, pair.dtype),
            pltpu.VMEM(w_in.shape, w_in.dtype),
            pltpu.VMEM((1, length), jnp.int32),
            pltpu.SemaphoreType.DMA((5,)),
        ],
        compiler_params=LIMIT,
        cost_estimate=cost,
    )(*(pltpu.with_memory_space_constraint(x, pltpu.HBM) for x in arguments))
    w_ours, gain_in, bias_in = weights
    pieces = pl.pallas_call(
        other_kernel,
        out_shape=[jax.ShapeDtypeStruct((cols, packed, LANES), jnp.bfloat16)] * quads,
        in_specs=[VMEM] * 5,
        out_specs=[VMEM] * quads,
        scratch_shapes=[pltpu.VMEM((quads, packed, LANES), jnp.bfloat16)],
        compiler_params=LIMIT,
        cost_estimate=cost,
    )(other_pair, sides, gain_in, bias_in, w_ours)
    steps = [3, 1, 2, 0]
    got = [lax.ppermute(pieces[step], "quad", [(i, i ^ step) for i in range(quads)]) if step else pieces[0] for step in steps]
    total = pl.pallas_call(
        functools.partial(triangle_kernel, far_order, steps, cols, row_count, col_count, share),
        out_shape=jax.ShapeDtypeStruct((devices, share * tokens // LANES, LANES), jnp.bfloat16),
        in_specs=[VMEM] * (quads + 2),
        out_specs=VMEM,
        scratch_shapes=[
            pltpu.VMEM((share // GROUP, length, GROUP * depth), jnp.float32),
            pltpu.VMEM((share // GROUP, length // 3 * GROUP, 3 * GROUP * depth), jnp.bfloat16),
        ],
        compiler_params=LIMIT,
    )(*got, spread, mask)
    gate, gain_out, bias_out = pl.pallas_call(
        gate_kernel,
        out_shape=(
            jax.ShapeDtypeStruct((tokens, channels), jnp.float32),
            jax.ShapeDtypeStruct((hidden, 1), jnp.float32),
            jax.ShapeDtypeStruct((hidden, 1), jnp.float32),
        ),
        in_specs=[VMEM] * 4,
        out_specs=(VMEM, VMEM, VMEM),
        compiler_params=LIMIT,
        cost_estimate=pl.CostEstimate(flops=2 * tokens * channels * channels, bytes_accessed=4 * tokens * channels, transcendentals=0),
    )(normed, w_gate, gain_out.reshape(1, hidden), bias_out.reshape(1, hidden))
    total = lax.all_to_all(total, ("half", "quad", "col"), split_axis=0, concat_axis=0, tiled=True, axis_index_groups=[far_order])
    return pl.pallas_call(
        functools.partial(output_kernel, far_order, near_order),
        out_shape=jax.ShapeDtypeStruct(pair.shape, jnp.bfloat16),
        in_specs=[VMEM] * 5,
        out_specs=VMEM,
        compiler_params=LIMIT,
    )(total, gate, gain_out, bias_out, w_out)


def plain_per_device(rows, cols, pair, token_mask, gain_in, bias_in, w_in, w_gate, gain_out, bias_out, w_out):
    row_count, col_count, channels = pair.shape
    hidden = w_out.shape[0]
    devices = rows * cols
    share = hidden // devices
    tokens = row_count * col_count
    row_start = lax.axis_index(("half", "quad")) * row_count
    col_start = lax.axis_index("col") * col_count
    mask_float = token_mask.astype(jnp.float32)
    mask_rows = lax.dynamic_slice_in_dim(mask_float, row_start, row_count)
    mask_cols = lax.dynamic_slice_in_dim(mask_float, col_start, col_count)
    pair_mask = (mask_rows[:, None] * mask_cols[None, :]).reshape(1, tokens)
    flat = pair.reshape(tokens, channels).astype(jnp.float32)
    normed = layer_norm(flat, gain_in, bias_in, -1).astype(jnp.bfloat16)
    projected = lax.dot_general(w_in, normed, (((0,), (1,)), ((), ())), preferred_element_type=jnp.float32)
    projected = projected.reshape(2, 2, hidden, tokens)
    sides = (pair_mask * jax.nn.sigmoid(projected[:, 0]) * projected[:, 1]).astype(jnp.bfloat16)
    sides = sides.reshape(2, devices, share, tokens).transpose(1, 0, 2, 3)
    gate = jax.nn.sigmoid(jnp.dot(normed, w_gate, preferred_element_type=jnp.float32))
    got = lax.all_to_all(sides, AXES, split_axis=0, concat_axis=0, tiled=True)
    got = got.reshape(rows, cols, 2, share, row_count, col_count).transpose(2, 3, 0, 4, 1, 5)
    got = got.reshape(2, share, rows * row_count, cols * col_count)
    total = jnp.einsum("cki,ckj->cij", got[0], got[1], preferred_element_type=jnp.float32).astype(jnp.bfloat16)
    total = total.reshape(share, rows, row_count, cols, col_count).transpose(1, 3, 0, 2, 4)
    total = total.reshape(devices, share, tokens)
    total = lax.all_to_all(total, AXES, split_axis=0, concat_axis=0, tiled=True)
    total = total.reshape(hidden, tokens).astype(jnp.float32)
    summed_norm = layer_norm(total, gain_out[:, None], bias_out[:, None], 0).astype(jnp.bfloat16)
    output = lax.dot_general(summed_norm, w_out, (((0,), (0,)), ((), ())), preferred_element_type=jnp.float32)
    return (gate * output).astype(jnp.bfloat16).reshape(row_count, col_count, channels)


def solution(mesh):
    rows, cols = mesh.shape["row"], mesh.shape["col"]
    halves = 2
    parts = (mesh.shape["groups"], halves, rows // halves, cols)
    finer = jax.sharding.Mesh(mesh.devices.reshape(parts), ("groups", "half", "quad", "col"))

    def per_shard(*args):
        near, hidden, length = rows * cols // halves, args[-1].shape[0], args[1].shape[0]
        row_count, col_count, _ = args[0].shape
        spare = LANES - 2 * col_count
        fits = hidden % (2 * GROUP * near) == 0 and cols == 2 and rows // halves == 4 and length <= LANES and row_count % 3 == 0
        fits = fits and 0 < spare < col_count and row_count // 3 * (col_count - spare) * 2 == LANES
        fits = fits and row_count // 3 * (rows // halves) * GROUP == LANES
        return per_device(rows, cols, halves, *args) if fits else plain_per_device(rows, cols, *args)

    tokens = P(("groups", "half", "quad"), "col", None)
    in_specs = (tokens, P("groups"), P(), P(), P(), P(), P(), P(), P())
    return jax.shard_map(per_shard, mesh=finer, in_specs=in_specs, out_specs=tokens, check_vma=False)
```

```python
import functools

import jax
import jax.numpy as jnp
from jax import lax
from jax.experimental import pallas as pl
from jax.experimental.pallas import tpu as pltpu
from jax.sharding import PartitionSpec as P

epsilon = 1e-05
LANES = 128
GROUP = 8
AXES = ("half", "quad", "col")
VMEM = pl.BlockSpec(memory_space=pltpu.VMEM)
HBM = pl.BlockSpec(memory_space=pltpu.HBM)
LIMIT = pltpu.CompilerParams(vmem_limit_bytes=32 * 1024 * 1024)


def sigmoid(x):
    return 0.5 * jnp.tanh(0.5 * x) + 0.5


def layer_norm(values, gain, bias, axis):
    mean = jnp.mean(values, axis=axis, keepdims=True)
    centred = values - mean
    variance = jnp.mean(centred * centred, axis=axis, keepdims=True)
    return centred * lax.rsqrt(variance + epsilon) * gain + bias


def column(row):
    n = row.shape[1]
    eye = lax.broadcasted_iota(jnp.int32, (n, n), 0) == lax.broadcasted_iota(jnp.int32, (n, n), 1)
    return jnp.sum(jnp.where(eye, row, 0.0), axis=1, keepdims=True)


def pack(x):
    rows, tokens = x.shape[-2:]
    whole, rest = divmod(tokens, LANES)
    blocks = [x[..., t * LANES : (t + 1) * LANES] for t in range(whole)]
    if rest:
        tail = x[..., whole * LANES :]
        blocks.append(jnp.concatenate([tail[..., : rows // 2, :], tail[..., rows // 2 :, :]], axis=-1))
    return jnp.concatenate(blocks, axis=-2)


def unpack(x, rows):
    whole, rest = divmod(x.shape[-2], rows)
    blocks = [x[..., t * rows : (t + 1) * rows, :] for t in range(whole)]
    if rest:
        tail = x[..., whole * rows :, :]
        blocks.append(jnp.concatenate([tail[..., : LANES // 2], tail[..., LANES // 2 :]], axis=-2))
    return jnp.concatenate(blocks, axis=-1)


def arrange(x):
    row_count, col_count, _ = x.shape
    whole, spare = row_count // 3, LANES - 2 * col_count
    blocks = []
    for t in range(whole):
        blocks += [x[2 * t], x[2 * t + 1], x[2 * whole + t, :spare]]
    return jnp.concatenate(blocks + [x[2 * whole + t, spare:] for t in range(whole)], axis=0)


def restore(x, row_count, col_count):
    whole, spare = row_count // 3, LANES - 2 * col_count
    rest = col_count - spare
    rows = []
    for t in range(whole):
        rows += [x[t * LANES : t * LANES + col_count], x[t * LANES + col_count : t * LANES + 2 * col_count]]
    for t in range(whole):
        tail = whole * LANES + t * rest
        rows += [x[t * LANES + 2 * col_count : (t + 1) * LANES], x[tail : tail + rest]]
    return jnp.concatenate(rows, axis=0)


def normalise(flat, gain, bias):
    return layer_norm(flat.astype(jnp.float32), gain, bias, -1).astype(jnp.bfloat16)


def project(normed, w, shape, quads):
    ours = w.shape[0] // 4
    tokens = normed.shape[0]
    projected = lax.dot_general(w, arrange(normed.reshape(shape)), (((1,), (1,)), ((), ())), preferred_element_type=jnp.float32)
    left = sigmoid(projected[:ours]) * projected[ours : 2 * ours]
    right = sigmoid(projected[2 * ours : 3 * ours]) * projected[3 * ours :]
    sides = jnp.concatenate([left.reshape(quads, -1, tokens), right.reshape(quads, -1, tokens)], axis=1)
    return pack(sides).astype(jnp.bfloat16)


def my_steps(steps):
    my_col = lax.axis_index("col")
    return [jnp.where(my_col == 0, first, second) for first, second in steps]


def own_kernel(steps, quads, cols, pair_hbm, gain_hbm, bias_hbm, w_hbm, mask_hbm, sides_ref, normed_ref, spread_ref, column_mask_ref, w_ref, gain_ref, bias_ref, pair_ref, all_w_ref, mask_ref, sems):
    moves = [(mask_hbm, mask_ref), (pair_hbm, pair_ref), (gain_hbm, gain_ref), (bias_hbm, bias_ref), (w_hbm, all_w_ref)]
    copies = [pltpu.make_async_copy(source, target, sems.at[n]) for n, (source, target) in enumerate(moves)]
    for copy in copies:
        copy.start()
    my_quad, my_col = lax.axis_index("quad"), lax.axis_index("col")
    row_count, _, channels = pair_ref.shape
    tokens = normed_ref.shape[0]
    hidden = all_w_ref.shape[1] // 4
    ours = hidden // cols
    group, lanes = spread_ref.shape
    copies[0].wait()
    mask_row = mask_ref[...].astype(jnp.float32)
    column_mask_ref[...] = column(mask_row)
    start = lax.axis_index("half") * (lanes // group)
    token = lax.broadcasted_iota(jnp.int32, (mask_row.shape[1], lanes), 0)
    lane = lax.broadcasted_iota(jnp.int32, (mask_row.shape[1], lanes), 1)
    whole = row_count // 3
    block, t, slot = lane // LANES, lane // (quads * group) % whole, lane // group % quads
    row = my_quad ^ sum(jnp.where(slot == n, step, 0) for n, step in enumerate(my_steps(steps)))
    k = row * row_count + jnp.where(block < 2, 2 * t + block, 2 * whole + t)
    pick = jnp.where(k + start == token, 1.0, 0.0)
    kept = jnp.dot(mask_row.astype(jnp.bfloat16), pick.astype(jnp.bfloat16), preferred_element_type=jnp.float32)
    channel = lax.broadcasted_iota(jnp.int32, (group, lanes), 0)
    lane = lax.broadcasted_iota(jnp.int32, (group, lanes), 1)
    spread_ref[...] = jnp.where(lane % group == channel, kept, 0.0)
    for copy in copies[1:4]:
        copy.wait()
    normed = normalise(pair_ref[...].reshape(tokens, channels), gain_ref[...], bias_ref[...])
    normed_ref[...] = normed
    copies[4].wait()
    parts = [all_w_ref[:, at : at + hidden] for at in range(0, 4 * hidden, hidden)]
    w = jnp.concatenate([jnp.where(my_col == 0, part[:, :ours], part[:, ours:]) for part in parts], axis=1).T
    w_ref[...] = w
    sides_ref[...] = project(normed, w, pair_ref.shape, quads)


def other_kernel(steps, pair_ref, sides_ref, gain_ref, bias_ref, w_ref, *refs):
    *piece_refs, others_ref = refs
    my_quad, my_col = lax.axis_index("quad"), lax.axis_index("col")
    quads = sides_ref.shape[0]
    normed = normalise(pair_ref[...].reshape(-1, pair_ref.shape[2]), gain_ref[...], bias_ref[...])
    others_ref[...] = project(normed, w_ref[...], pair_ref.shape, quads)
    for step, piece_ref in zip(my_steps(steps), piece_refs):
        piece_ref[my_col] = sides_ref[my_quad ^ step]
        piece_ref[1 - my_col] = others_ref[my_quad ^ step]


def triangle_kernel(far_order, cols, row_count, col_count, share, *refs):
    *got_refs, spread_ref, mask_ref, total_ref, left_ref, wide_ref = refs
    both = 2 * share
    group, lanes = spread_ref.shape
    length = mask_ref.shape[0]
    rows, quads, parts = length // row_count, len(got_refs), share // group
    whole, spare = row_count // 3, LANES - 2 * col_count
    rest = col_count - spare
    blocks = [[got_refs[row][col].astype(jnp.float32) for row in range(quads)] for col in range(cols)]

    def turned(picks):
        return jnp.concatenate([blocks[col][row][at : at + group] for col, row, at in picks], axis=0).T

    tail = turned([(col, row, whole * both + part * group) for col in range(cols) for part in range(parts) for row in range(quads)])

    def side(which, part):
        even, odd, third = [], [], []
        for col in range(cols):
            at = which * share + part * group
            block = turned([(col, row, t * both + at) for t in range(whole) for row in range(quads)])
            even.append(block[:col_count])
            odd.append(block[col_count : 2 * col_count])
            lane = (col * parts + part) * quads * group
            at = which * LANES // 2
            last = [tail[at + t * rest : at + (t + 1) * rest, lane : lane + quads * group] for t in range(whole)]
            third += [block[2 * col_count :], jnp.concatenate(last, axis=1)]
        tokens = [jnp.concatenate(pieces, axis=0) for pieces in (even, odd, third)]
        return jnp.concatenate(tokens, axis=1) * mask_ref[...]

    def placed(pieces):
        return jnp.concatenate([jnp.zeros((piece, lanes), jnp.bfloat16) if isinstance(piece, int) else piece for piece in pieces], axis=0)

    contract = (((1,), (1,)), ((), ()))
    lane_block = lax.broadcasted_iota(jnp.int32, (group, LANES), 1) // rest
    mains, lasts = [], []
    for part in range(parts):
        left_ref[part] = side(0, part)
        right = side(1, part).astype(jnp.bfloat16)
        for row in range(rows):
            for t in range(0, whole, 2):
                pair = []
                for at in (row * row_count, row * row_count + 2):
                    picks = [at + 2 * t, at + 2 * t + 1, row * row_count + 2 * whole + t + len(pair)]
                    copies = [jnp.broadcast_to(left_ref[part, i : i + 1, :], (group, lanes)) for i in picks]
                    pair.append(jnp.concatenate([copy * spread_ref[...] for copy in copies], axis=1))
                at = (row * whole + t) * group
                wide_ref[part, at : at + 2 * group, :] = jnp.concatenate(pair, axis=0).astype(jnp.bfloat16)
        ours = [right[col * col_count : (col + 1) * col_count] for col in range(cols)]
        weights = [
            placed([p for mine in ours for p in (mine, LANES - col_count)]),
            placed([p for mine in ours for p in (col_count, mine, spare)]),
            placed([p for mine in ours for p in (2 * col_count, mine[:spare])]),
        ]
        weights = jnp.concatenate(weights, axis=1)
        mains.append(lax.dot_general(wide_ref[part], weights, contract, preferred_element_type=jnp.float32))
        gap = LANES // parts
        pieces = [[gap * part] + [mine[spare:]] * whole + [LANES - gap * (part + 1)] for mine in ours]
        weights = placed([p for piece in pieces for p in piece if not isinstance(p, int) or p])
        lasts.append(lax.dot_general(wide_ref[part, :, 2 * lanes :], weights, contract, preferred_element_type=jnp.float32))
    for target, device in enumerate(far_order):
        row, col = divmod(device, cols)
        spots = [(row * whole + t) * group for t in range(whole)]
        tiles = [main[at : at + group, col * LANES : (col + 1) * LANES] for at in spots for main in mains]
        last = [part[at : at + group, col * LANES : (col + 1) * LANES] for part in lasts for at in spots]
        tile = last[0]
        for n in range(1, len(last)):
            tile = jnp.where(lane_block >= n, last[n], tile)
        tiles.append(tile)
        total_ref[target] = jnp.concatenate(tiles, axis=0).astype(jnp.bfloat16)


def gate_kernel(normed_ref, w_ref, gain_ref, bias_ref, gate_ref, gain_out_ref, bias_out_ref):
    gate_ref[...] = sigmoid(jnp.dot(normed_ref[...], w_ref[...], preferred_element_type=jnp.float32))
    gain_out_ref[...] = column(gain_ref[...])
    bias_out_ref[...] = column(bias_ref[...])


def output_kernel(far_order, near_order, total_ref, gate_ref, gain_ref, bias_ref, w_ref, out_ref):
    tokens = gate_ref.shape[0]
    hidden = w_ref.shape[0]
    near = len(near_order)
    share = hidden // near
    blocks = []
    for index in near_order:
        parts = [total_ref[source].astype(jnp.float32) for source, device in enumerate(far_order) if device % near == index]
        blocks.append(unpack(sum(parts[1:], parts[0]), share))
    total = jnp.concatenate(blocks, axis=0)
    normed = layer_norm(total, gain_ref[...], bias_ref[...], 0).astype(jnp.bfloat16)
    output = lax.dot_general(normed, w_ref[...], (((0,), (0,)), ((), ())), preferred_element_type=jnp.float32)
    output = restore(output, out_ref.shape[0], out_ref.shape[1])
    out_ref[...] = (gate_ref[...] * output).astype(jnp.bfloat16).reshape(out_ref.shape)


def per_device(rows, cols, halves, pair, token_mask, gain_in, bias_in, w_in, w_gate, gain_out, bias_out, w_out):
    row_count, col_count, channels = pair.shape
    hidden = w_out.shape[0]
    devices = rows * cols
    near = devices // halves
    quads = rows // halves
    far_order = []
    for col in reversed(range(cols)):
        ahead = list(range(quads)) if col else list(range(1, quads)) + [0]
        behind = [0] + list(reversed(range(1, quads))) if col else list(reversed(range(quads)))
        for quad, other in zip(ahead, behind):
            far_order += [near + other * cols + col, quad * cols + col]
    share = hidden // near
    tokens = row_count * col_count
    length = rows * row_count
    depth = length // halves
    token_mask = token_mask.reshape(1, length)
    near_order = [quad * cols + col for col in range(cols) for quad in range(quads)]
    packed = 2 * share * tokens // LANES
    cost = pl.CostEstimate(flops=2 * tokens * channels * 4 * hidden, bytes_accessed=16 * tokens * channels, transcendentals=0)
    steps = [(3, 1), (1, 2), (2, 3), (0, 0)]
    other_pair = lax.ppermute(pair, "col", [(i, (i + 1) % cols) for i in range(cols)])
    arguments = (pair, gain_in.reshape(1, channels), bias_in.reshape(1, channels), w_in, token_mask)
    sides, normed, spread, mask, *weights = pl.pallas_call(
        functools.partial(own_kernel, steps, quads, cols),
        out_shape=(
            jax.ShapeDtypeStruct((quads, packed, LANES), jnp.bfloat16),
            jax.ShapeDtypeStruct((tokens, channels), jnp.bfloat16),
            jax.ShapeDtypeStruct((GROUP, GROUP * depth), jnp.float32),
            jax.ShapeDtypeStruct((length, 1), jnp.float32),
            jax.ShapeDtypeStruct((4 * hidden // cols, channels), jnp.bfloat16),
            jax.ShapeDtypeStruct((1, channels), jnp.float32),
            jax.ShapeDtypeStruct((1, channels), jnp.float32),
        ),
        in_specs=[HBM] * 5,
        out_specs=(VMEM,) * 7,
        scratch_shapes=[
            pltpu.VMEM(pair.shape, pair.dtype),
            pltpu.VMEM(w_in.shape, w_in.dtype),
            pltpu.VMEM((1, length), jnp.int32),
            pltpu.SemaphoreType.DMA((5,)),
        ],
        compiler_params=LIMIT,
        cost_estimate=cost,
    )(*(pltpu.with_memory_space_constraint(x, pltpu.HBM) for x in arguments))
    w_ours, gain_in, bias_in = weights
    pieces = pl.pallas_call(
        functools.partial(other_kernel, steps),
        out_shape=[jax.ShapeDtypeStruct((cols, packed, LANES), jnp.bfloat16)] * quads,
        in_specs=[VMEM] * 5,
        out_specs=[VMEM] * quads,
        scratch_shapes=[pltpu.VMEM((quads, packed, LANES), jnp.bfloat16)],
        compiler_params=LIMIT,
        cost_estimate=cost,
    )(other_pair, sides, gain_in, bias_in, w_ours)
    got = []
    for piece, step in zip(pieces, steps):
        moves = [(quad * cols + col, (quad ^ step[col]) * cols + col) for quad in range(quads) for col in range(cols)]
        got.append(lax.ppermute(piece, ("quad", "col"), moves) if any(step) else piece)
    total = pl.pallas_call(
        functools.partial(triangle_kernel, far_order, cols, row_count, col_count, share),
        out_shape=jax.ShapeDtypeStruct((devices, share * tokens // LANES, LANES), jnp.bfloat16),
        in_specs=[VMEM] * (quads + 2),
        out_specs=VMEM,
        scratch_shapes=[
            pltpu.VMEM((share // GROUP, length, GROUP * depth), jnp.float32),
            pltpu.VMEM((share // GROUP, length // 3 * GROUP, 3 * GROUP * depth), jnp.bfloat16),
        ],
        compiler_params=LIMIT,
    )(*got, spread, mask)
    gate, gain_out, bias_out = pl.pallas_call(
        gate_kernel,
        out_shape=(
            jax.ShapeDtypeStruct((tokens, channels), jnp.float32),
            jax.ShapeDtypeStruct((hidden, 1), jnp.float32),
            jax.ShapeDtypeStruct((hidden, 1), jnp.float32),
        ),
        in_specs=[VMEM] * 4,
        out_specs=(VMEM, VMEM, VMEM),
        compiler_params=LIMIT,
        cost_estimate=pl.CostEstimate(flops=2 * tokens * channels * channels, bytes_accessed=4 * tokens * channels, transcendentals=0),
    )(normed, w_gate, gain_out.reshape(1, hidden), bias_out.reshape(1, hidden))
    total = lax.all_to_all(total, ("half", "quad", "col"), split_axis=0, concat_axis=0, tiled=True, axis_index_groups=[far_order])
    return pl.pallas_call(
        functools.partial(output_kernel, far_order, near_order),
        out_shape=jax.ShapeDtypeStruct(pair.shape, jnp.bfloat16),
        in_specs=[VMEM] * 5,
        out_specs=VMEM,
        compiler_params=LIMIT,
    )(total, gate, gain_out, bias_out, w_out)


def plain_per_device(rows, cols, pair, token_mask, gain_in, bias_in, w_in, w_gate, gain_out, bias_out, w_out):
    row_count, col_count, channels = pair.shape
    hidden = w_out.shape[0]
    devices = rows * cols
    share = hidden // devices
    tokens = row_count * col_count
    row_start = lax.axis_index(("half", "quad")) * row_count
    col_start = lax.axis_index("col") * col_count
    mask_float = token_mask.astype(jnp.float32)
    mask_rows = lax.dynamic_slice_in_dim(mask_float, row_start, row_count)
    mask_cols = lax.dynamic_slice_in_dim(mask_float, col_start, col_count)
    pair_mask = (mask_rows[:, None] * mask_cols[None, :]).reshape(1, tokens)
    flat = pair.reshape(tokens, channels).astype(jnp.float32)
    normed = layer_norm(flat, gain_in, bias_in, -1).astype(jnp.bfloat16)
    projected = lax.dot_general(w_in, normed, (((0,), (1,)), ((), ())), preferred_element_type=jnp.float32)
    projected = projected.reshape(2, 2, hidden, tokens)
    sides = (pair_mask * jax.nn.sigmoid(projected[:, 0]) * projected[:, 1]).astype(jnp.bfloat16)
    sides = sides.reshape(2, devices, share, tokens).transpose(1, 0, 2, 3)
    gate = jax.nn.sigmoid(jnp.dot(normed, w_gate, preferred_element_type=jnp.float32))
    got = lax.all_to_all(sides, AXES, split_axis=0, concat_axis=0, tiled=True)
    got = got.reshape(rows, cols, 2, share, row_count, col_count).transpose(2, 3, 0, 4, 1, 5)
    got = got.reshape(2, share, rows * row_count, cols * col_count)
    total = jnp.einsum("cki,ckj->cij", got[0], got[1], preferred_element_type=jnp.float32).astype(jnp.bfloat16)
    total = total.reshape(share, rows, row_count, cols, col_count).transpose(1, 3, 0, 2, 4)
    total = total.reshape(devices, share, tokens)
    total = lax.all_to_all(total, AXES, split_axis=0, concat_axis=0, tiled=True)
    total = total.reshape(hidden, tokens).astype(jnp.float32)
    summed_norm = layer_norm(total, gain_out[:, None], bias_out[:, None], 0).astype(jnp.bfloat16)
    output = lax.dot_general(summed_norm, w_out, (((0,), (0,)), ((), ())), preferred_element_type=jnp.float32)
    return (gate * output).astype(jnp.bfloat16).reshape(row_count, col_count, channels)


def solution(mesh):
    rows, cols = mesh.shape["row"], mesh.shape["col"]
    halves = 2
    parts = (mesh.shape["groups"], halves, rows // halves, cols)
    finer = jax.sharding.Mesh(mesh.devices.reshape(parts), ("groups", "half", "quad", "col"))

    def per_shard(*args):
        near, hidden, length = rows * cols // halves, args[-1].shape[0], args[1].shape[0]
        row_count, col_count, _ = args[0].shape
        spare = LANES - 2 * col_count
        fits = hidden % (2 * GROUP * near) == 0 and cols == 2 and rows // halves == 4 and length <= LANES and row_count % 3 == 0
        fits = fits and 0 < spare < col_count and row_count // 3 * (col_count - spare) * 2 == LANES
        fits = fits and row_count // 3 * (rows // halves) * GROUP == LANES
        return per_device(rows, cols, halves, *args) if fits else plain_per_device(rows, cols, *args)

    tokens = P(("groups", "half", "quad"), "col", None)
    in_specs = (tokens, P("groups"), P(), P(), P(), P(), P(), P(), P())
    return jax.shard_map(per_shard, mesh=finer, in_specs=in_specs, out_specs=tokens, check_vma=False)
```

```python
import functools

import jax
import jax.numpy as jnp
from jax import lax
from jax.experimental import pallas as pl
from jax.experimental.pallas import tpu as pltpu
from jax.sharding import PartitionSpec as P

epsilon = 1e-05
LANES = 128
GROUP = 8
AXES = ("half", "quad", "col")
VMEM = pl.BlockSpec(memory_space=pltpu.VMEM)
HBM = pl.BlockSpec(memory_space=pltpu.HBM)
LIMIT = pltpu.CompilerParams(vmem_limit_bytes=32 * 1024 * 1024)


def sigmoid(x):
    return 0.5 * jnp.tanh(0.5 * x) + 0.5


def layer_norm(values, gain, bias, axis):
    mean = jnp.mean(values, axis=axis, keepdims=True)
    centred = values - mean
    variance = jnp.mean(centred * centred, axis=axis, keepdims=True)
    return centred * lax.rsqrt(variance + epsilon) * gain + bias


def column(row):
    n = row.shape[1]
    eye = lax.broadcasted_iota(jnp.int32, (n, n), 0) == lax.broadcasted_iota(jnp.int32, (n, n), 1)
    return jnp.sum(jnp.where(eye, row, 0.0), axis=1, keepdims=True)


def pack(x):
    rows, tokens = x.shape[-2:]
    whole, rest = divmod(tokens, LANES)
    blocks = [x[..., t * LANES : (t + 1) * LANES] for t in range(whole)]
    if rest:
        tail = x[..., whole * LANES :]
        blocks.append(jnp.concatenate([tail[..., : rows // 2, :], tail[..., rows // 2 :, :]], axis=-1))
    return jnp.concatenate(blocks, axis=-2)


def unpack(x, rows):
    whole, rest = divmod(x.shape[-2], rows)
    blocks = [x[..., t * rows : (t + 1) * rows, :] for t in range(whole)]
    if rest:
        tail = x[..., whole * rows :, :]
        blocks.append(jnp.concatenate([tail[..., : LANES // 2], tail[..., LANES // 2 :]], axis=-2))
    return jnp.concatenate(blocks, axis=-1)


def arrange(x):
    row_count, col_count, _ = x.shape
    whole, spare = row_count // 3, LANES - 2 * col_count
    blocks = []
    for t in range(whole):
        blocks += [x[2 * t], x[2 * t + 1], x[2 * whole + t, :spare]]
    return jnp.concatenate(blocks + [x[2 * whole + t, spare:] for t in range(whole)], axis=0)


def restore(x, row_count, col_count):
    whole, spare = row_count // 3, LANES - 2 * col_count
    rest = col_count - spare
    rows = []
    for t in range(whole):
        rows += [x[t * LANES : t * LANES + col_count], x[t * LANES + col_count : t * LANES + 2 * col_count]]
    for t in range(whole):
        tail = whole * LANES + t * rest
        rows += [x[t * LANES + 2 * col_count : (t + 1) * LANES], x[tail : tail + rest]]
    return jnp.concatenate(rows, axis=0)


def normalise(flat, gain, bias):
    return layer_norm(flat.astype(jnp.float32), gain, bias, -1).astype(jnp.bfloat16)


def project(normed, w, shape, quads):
    ours = w.shape[0] // 4
    tokens = normed.shape[0]
    projected = lax.dot_general(w, arrange(normed.reshape(shape)), (((1,), (1,)), ((), ())), preferred_element_type=jnp.float32)
    left = sigmoid(projected[:ours]) * projected[ours : 2 * ours]
    right = sigmoid(projected[2 * ours : 3 * ours]) * projected[3 * ours :]
    sides = jnp.concatenate([left.reshape(quads, -1, tokens), right.reshape(quads, -1, tokens)], axis=1)
    return pack(sides).astype(jnp.bfloat16)


def own_kernel(quads, cols, pair_hbm, gain_hbm, bias_hbm, w_hbm, mask_hbm, sides_ref, normed_ref, spread_ref, column_mask_ref, w_ref, gain_ref, bias_ref, pair_ref, all_w_ref, mask_ref, sems):
    moves = [(mask_hbm, mask_ref), (pair_hbm, pair_ref), (gain_hbm, gain_ref), (bias_hbm, bias_ref), (w_hbm, all_w_ref)]
    copies = [pltpu.make_async_copy(source, target, sems.at[n]) for n, (source, target) in enumerate(moves)]
    for copy in copies:
        copy.start()
    my_quad, my_col = lax.axis_index("quad"), lax.axis_index("col")
    row_count, _, channels = pair_ref.shape
    tokens = normed_ref.shape[0]
    hidden = all_w_ref.shape[1] // 4
    ours = hidden // cols
    group, lanes = spread_ref.shape
    copies[0].wait()
    mask_row = mask_ref[...].astype(jnp.float32)
    column_mask_ref[...] = column(mask_row)
    start = lax.axis_index("half") * (lanes // group)
    token = lax.broadcasted_iota(jnp.int32, (mask_row.shape[1], lanes), 0)
    lane = lax.broadcasted_iota(jnp.int32, (mask_row.shape[1], lanes), 1)
    whole = row_count // 3
    block, t, row = lane // LANES, lane // (quads * group) % whole, lane // group % quads
    k = (row ^ my_quad) * row_count + jnp.where(block < 2, 2 * t + block, 2 * whole + t)
    pick = jnp.where(k + start == token, 1.0, 0.0)
    kept = jnp.dot(mask_row.astype(jnp.bfloat16), pick.astype(jnp.bfloat16), preferred_element_type=jnp.float32)
    channel = lax.broadcasted_iota(jnp.int32, (group, lanes), 0)
    lane = lax.broadcasted_iota(jnp.int32, (group, lanes), 1)
    spread_ref[...] = jnp.where(lane % group == channel, kept, 0.0)
    for copy in copies[1:4]:
        copy.wait()
    normed = normalise(pair_ref[...].reshape(tokens, channels), gain_ref[...], bias_ref[...])
    normed_ref[...] = normed
    copies[4].wait()
    parts = [all_w_ref[:, at : at + hidden] for at in range(0, 4 * hidden, hidden)]
    w = jnp.concatenate([jnp.where(my_col == 0, part[:, :ours], part[:, ours:]) for part in parts], axis=1).T
    w_ref[...] = w
    sides_ref[...] = project(normed, w, pair_ref.shape, quads)


def other_kernel(pair_ref, sides_ref, gain_ref, bias_ref, w_ref, *refs):
    *piece_refs, others_ref = refs
    my_quad, my_col = lax.axis_index("quad"), lax.axis_index("col")
    quads = sides_ref.shape[0]
    normed = normalise(pair_ref[...].reshape(-1, pair_ref.shape[2]), gain_ref[...], bias_ref[...])
    others_ref[...] = project(normed, w_ref[...], pair_ref.shape, quads)
    for step, piece_ref in enumerate(piece_refs):
        piece_ref[my_col] = sides_ref[my_quad ^ step]
        piece_ref[1 - my_col] = others_ref[my_quad ^ step]


def triangle_kernel(far_order, steps, cols, row_count, col_count, share, *refs):
    *got_refs, spread_ref, mask_ref, total_ref, left_ref, wide_ref = refs
    got_refs = {step: ref for step, ref in zip(steps, got_refs)}
    both = 2 * share
    group, lanes = spread_ref.shape
    length = mask_ref.shape[0]
    rows, quads, parts = length // row_count, len(steps), share // group
    whole, spare = row_count // 3, LANES - 2 * col_count
    rest = col_count - spare
    blocks = [[got_refs[row][col].astype(jnp.float32) for row in range(quads)] for col in range(cols)]

    def turned(picks):
        return jnp.concatenate([blocks[col][row][at : at + group] for col, row, at in picks], axis=0).T

    tail = turned([(col, row, whole * both + part * group) for col in range(cols) for part in range(parts) for row in range(quads)])

    def side(which, part):
        even, odd, third = [], [], []
        for col in range(cols):
            at = which * share + part * group
            block = turned([(col, row, t * both + at) for t in range(whole) for row in range(quads)])
            even.append(block[:col_count])
            odd.append(block[col_count : 2 * col_count])
            lane = (col * parts + part) * quads * group
            at = which * LANES // 2
            last = [tail[at + t * rest : at + (t + 1) * rest, lane : lane + quads * group] for t in range(whole)]
            third += [block[2 * col_count :], jnp.concatenate(last, axis=1)]
        tokens = [jnp.concatenate(pieces, axis=0) for pieces in (even, odd, third)]
        return jnp.concatenate(tokens, axis=1) * mask_ref[...]

    def placed(pieces):
        return jnp.concatenate([jnp.zeros((piece, lanes), jnp.bfloat16) if isinstance(piece, int) else piece for piece in pieces], axis=0)

    contract = (((1,), (1,)), ((), ()))
    lane_block = lax.broadcasted_iota(jnp.int32, (group, LANES), 1) // rest
    mains, lasts = [], []
    for part in range(parts):
        left_ref[part] = side(0, part)
        right = side(1, part).astype(jnp.bfloat16)
        for row in range(rows):
            for t in range(0, whole, 2):
                pair = []
                for at in (row * row_count, row * row_count + 2):
                    picks = [at + 2 * t, at + 2 * t + 1, row * row_count + 2 * whole + t + len(pair)]
                    copies = [jnp.broadcast_to(left_ref[part, i : i + 1, :], (group, lanes)) for i in picks]
                    pair.append(jnp.concatenate([copy * spread_ref[...] for copy in copies], axis=1))
                at = (row * whole + t) * group
                wide_ref[part, at : at + 2 * group, :] = jnp.concatenate(pair, axis=0).astype(jnp.bfloat16)
        ours = [right[col * col_count : (col + 1) * col_count] for col in range(cols)]
        weights = [
            placed([p for mine in ours for p in (mine, LANES - col_count)]),
            placed([p for mine in ours for p in (col_count, mine, spare)]),
            placed([p for mine in ours for p in (2 * col_count, mine[:spare])]),
        ]
        weights = jnp.concatenate(weights, axis=1)
        mains.append(lax.dot_general(wide_ref[part], weights, contract, preferred_element_type=jnp.float32))
        gap = LANES // parts
        pieces = [[gap * part] + [mine[spare:]] * whole + [LANES - gap * (part + 1)] for mine in ours]
        weights = placed([p for piece in pieces for p in piece if not isinstance(p, int) or p])
        lasts.append(lax.dot_general(wide_ref[part, :, 2 * lanes :], weights, contract, preferred_element_type=jnp.float32))
    for target, device in enumerate(far_order):
        row, col = divmod(device, cols)
        spots = [(row * whole + t) * group for t in range(whole)]
        tiles = [main[at : at + group, col * LANES : (col + 1) * LANES] for at in spots for main in mains]
        last = [part[at : at + group, col * LANES : (col + 1) * LANES] for part in lasts for at in spots]
        tile = last[0]
        for n in range(1, len(last)):
            tile = jnp.where(lane_block >= n, last[n], tile)
        tiles.append(tile)
        total_ref[target] = jnp.concatenate(tiles, axis=0).astype(jnp.bfloat16)


def gate_kernel(normed_ref, w_ref, gain_ref, bias_ref, gate_ref, gain_out_ref, bias_out_ref):
    gate_ref[...] = sigmoid(jnp.dot(normed_ref[...], w_ref[...], preferred_element_type=jnp.float32))
    gain_out_ref[...] = column(gain_ref[...])
    bias_out_ref[...] = column(bias_ref[...])


def output_kernel(far_order, near_order, total_ref, gate_ref, gain_ref, bias_ref, w_ref, out_ref):
    tokens = gate_ref.shape[0]
    hidden = w_ref.shape[0]
    near = len(near_order)
    share = hidden // near
    blocks = []
    for index in near_order:
        parts = [total_ref[source].astype(jnp.float32) for source, device in enumerate(far_order) if device % near == index]
        blocks.append(unpack(sum(parts[1:], parts[0]), share))
    total = jnp.concatenate(blocks, axis=0)
    normed = layer_norm(total, gain_ref[...], bias_ref[...], 0).astype(jnp.bfloat16)
    output = lax.dot_general(normed, w_ref[...], (((0,), (0,)), ((), ())), preferred_element_type=jnp.float32)
    output = restore(output, out_ref.shape[0], out_ref.shape[1])
    out_ref[...] = (gate_ref[...] * output).astype(jnp.bfloat16).reshape(out_ref.shape)


def per_device(rows, cols, halves, pair, token_mask, gain_in, bias_in, w_in, w_gate, gain_out, bias_out, w_out):
    row_count, col_count, channels = pair.shape
    hidden = w_out.shape[0]
    devices = rows * cols
    near = devices // halves
    quads = rows // halves
    far_order = []
    for col in reversed(range(cols)):
        ahead = list(range(1, quads)) + [0]
        behind = [0] + list(reversed(range(1, quads))) if col else list(reversed(range(quads)))
        for quad, other in zip(ahead, behind):
            far_order += [near + other * cols + col, quad * cols + col]
    first, last = far_order.index(cols - 1), len(far_order) - cols
    far_order[first], far_order[last] = far_order[last], far_order[first]
    share = hidden // near
    tokens = row_count * col_count
    length = rows * row_count
    depth = length // halves
    token_mask = token_mask.reshape(1, length)
    near_order = [quad * cols + col for col in range(cols) for quad in range(quads)]
    packed = 2 * share * tokens // LANES
    cost = pl.CostEstimate(flops=2 * tokens * channels * 4 * hidden, bytes_accessed=16 * tokens * channels, transcendentals=0)
    other_pair = lax.ppermute(pair, "col", [(i, (i + 1) % cols) for i in range(cols)])
    arguments = (pair, gain_in.reshape(1, channels), bias_in.reshape(1, channels), w_in, token_mask)
    sides, normed, spread, mask, *weights = pl.pallas_call(
        functools.partial(own_kernel, quads, cols),
        out_shape=(
            jax.ShapeDtypeStruct((quads, packed, LANES), jnp.bfloat16),
            jax.ShapeDtypeStruct((tokens, channels), jnp.bfloat16),
            jax.ShapeDtypeStruct((GROUP, GROUP * depth), jnp.float32),
            jax.ShapeDtypeStruct((length, 1), jnp.float32),
            jax.ShapeDtypeStruct((4 * hidden // cols, channels), jnp.bfloat16),
            jax.ShapeDtypeStruct((1, channels), jnp.float32),
            jax.ShapeDtypeStruct((1, channels), jnp.float32),
        ),
        in_specs=[HBM] * 5,
        out_specs=(VMEM,) * 7,
        scratch_shapes=[
            pltpu.VMEM(pair.shape, pair.dtype),
            pltpu.VMEM(w_in.shape, w_in.dtype),
            pltpu.VMEM((1, length), jnp.int32),
            pltpu.SemaphoreType.DMA((5,)),
        ],
        compiler_params=LIMIT,
        cost_estimate=cost,
    )(*(pltpu.with_memory_space_constraint(x, pltpu.HBM) for x in arguments))
    w_ours, gain_in, bias_in = weights
    pieces = pl.pallas_call(
        other_kernel,
        out_shape=[jax.ShapeDtypeStruct((cols, packed, LANES), jnp.bfloat16)] * quads,
        in_specs=[VMEM] * 5,
        out_specs=[VMEM] * quads,
        scratch_shapes=[pltpu.VMEM((quads, packed, LANES), jnp.bfloat16)],
        compiler_params=LIMIT,
        cost_estimate=cost,
    )(other_pair, sides, gain_in, bias_in, w_ours)
    steps = [3, 1, 2, 0]
    got = [lax.ppermute(pieces[step], "quad", [(i, i ^ step) for i in range(quads)]) if step else pieces[0] for step in steps]
    total = pl.pallas_call(
        functools.partial(triangle_kernel, far_order, steps, cols, row_count, col_count, share),
        out_shape=jax.ShapeDtypeStruct((devices, share * tokens // LANES, LANES), jnp.bfloat16),
        in_specs=[VMEM] * (quads + 2),
        out_specs=VMEM,
        scratch_shapes=[
            pltpu.VMEM((share // GROUP, length, GROUP * depth), jnp.float32),
            pltpu.VMEM((share // GROUP, length // 3 * GROUP, 3 * GROUP * depth), jnp.bfloat16),
        ],
        compiler_params=LIMIT,
    )(*got, spread, mask)
    gate, gain_out, bias_out = pl.pallas_call(
        gate_kernel,
        out_shape=(
            jax.ShapeDtypeStruct((tokens, channels), jnp.float32),
            jax.ShapeDtypeStruct((hidden, 1), jnp.float32),
            jax.ShapeDtypeStruct((hidden, 1), jnp.float32),
        ),
        in_specs=[VMEM] * 4,
        out_specs=(VMEM, VMEM, VMEM),
        compiler_params=LIMIT,
        cost_estimate=pl.CostEstimate(flops=2 * tokens * channels * channels, bytes_accessed=4 * tokens * channels, transcendentals=0),
    )(normed, w_gate, gain_out.reshape(1, hidden), bias_out.reshape(1, hidden))
    total = lax.all_to_all(total, ("half", "quad", "col"), split_axis=0, concat_axis=0, tiled=True, axis_index_groups=[far_order])
    return pl.pallas_call(
        functools.partial(output_kernel, far_order, near_order),
        out_shape=jax.ShapeDtypeStruct(pair.shape, jnp.bfloat16),
        in_specs=[VMEM] * 5,
        out_specs=VMEM,
        compiler_params=LIMIT,
    )(total, gate, gain_out, bias_out, w_out)


def plain_per_device(rows, cols, pair, token_mask, gain_in, bias_in, w_in, w_gate, gain_out, bias_out, w_out):
    row_count, col_count, channels = pair.shape
    hidden = w_out.shape[0]
    devices = rows * cols
    share = hidden // devices
    tokens = row_count * col_count
    row_start = lax.axis_index(("half", "quad")) * row_count
    col_start = lax.axis_index("col") * col_count
    mask_float = token_mask.astype(jnp.float32)
    mask_rows = lax.dynamic_slice_in_dim(mask_float, row_start, row_count)
    mask_cols = lax.dynamic_slice_in_dim(mask_float, col_start, col_count)
    pair_mask = (mask_rows[:, None] * mask_cols[None, :]).reshape(1, tokens)
    flat = pair.reshape(tokens, channels).astype(jnp.float32)
    normed = layer_norm(flat, gain_in, bias_in, -1).astype(jnp.bfloat16)
    projected = lax.dot_general(w_in, normed, (((0,), (1,)), ((), ())), preferred_element_type=jnp.float32)
    projected = projected.reshape(2, 2, hidden, tokens)
    sides = (pair_mask * jax.nn.sigmoid(projected[:, 0]) * projected[:, 1]).astype(jnp.bfloat16)
    sides = sides.reshape(2, devices, share, tokens).transpose(1, 0, 2, 3)
    gate = jax.nn.sigmoid(jnp.dot(normed, w_gate, preferred_element_type=jnp.float32))
    got = lax.all_to_all(sides, AXES, split_axis=0, concat_axis=0, tiled=True)
    got = got.reshape(rows, cols, 2, share, row_count, col_count).transpose(2, 3, 0, 4, 1, 5)
    got = got.reshape(2, share, rows * row_count, cols * col_count)
    total = jnp.einsum("cki,ckj->cij", got[0], got[1], preferred_element_type=jnp.float32).astype(jnp.bfloat16)
    total = total.reshape(share, rows, row_count, cols, col_count).transpose(1, 3, 0, 2, 4)
    total = total.reshape(devices, share, tokens)
    total = lax.all_to_all(total, AXES, split_axis=0, concat_axis=0, tiled=True)
    total = total.reshape(hidden, tokens).astype(jnp.float32)
    summed_norm = layer_norm(total, gain_out[:, None], bias_out[:, None], 0).astype(jnp.bfloat16)
    output = lax.dot_general(summed_norm, w_out, (((0,), (0,)), ((), ())), preferred_element_type=jnp.float32)
    return (gate * output).astype(jnp.bfloat16).reshape(row_count, col_count, channels)


def solution(mesh):
    rows, cols = mesh.shape["row"], mesh.shape["col"]
    halves = 2
    parts = (mesh.shape["groups"], halves, rows // halves, cols)
    finer = jax.sharding.Mesh(mesh.devices.reshape(parts), ("groups", "half", "quad", "col"))

    def per_shard(*args):
        near, hidden, length = rows * cols // halves, args[-1].shape[0], args[1].shape[0]
        row_count, col_count, _ = args[0].shape
        spare = LANES - 2 * col_count
        fits = hidden % (2 * GROUP * near) == 0 and cols == 2 and rows // halves == 4 and length <= LANES and row_count % 3 == 0
        fits = fits and 0 < spare < col_count and row_count // 3 * (col_count - spare) * 2 == LANES
        fits = fits and row_count // 3 * (rows // halves) * GROUP == LANES
        return per_device(rows, cols, halves, *args) if fits else plain_per_device(rows, cols, *args)

    tokens = P(("groups", "half", "quad"), "col", None)
    in_specs = (tokens, P("groups"), P(), P(), P(), P(), P(), P(), P())
    return jax.shard_map(per_shard, mesh=finer, in_specs=in_specs, out_specs=tokens, check_vma=False)
```

```python
import functools

import jax
import jax.numpy as jnp
from jax import lax
from jax.experimental import pallas as pl
from jax.experimental.pallas import tpu as pltpu
from jax.sharding import PartitionSpec as P

epsilon = 1e-05
LANES = 128
GROUP = 8
AXES = ("half", "quad", "col")
VMEM = pl.BlockSpec(memory_space=pltpu.VMEM)
HBM = pl.BlockSpec(memory_space=pltpu.HBM)
LIMIT = pltpu.CompilerParams(vmem_limit_bytes=32 * 1024 * 1024)


def sigmoid(x):
    return 0.5 * jnp.tanh(0.5 * x) + 0.5


def layer_norm(values, gain, bias, axis):
    mean = jnp.mean(values, axis=axis, keepdims=True)
    centred = values - mean
    variance = jnp.mean(centred * centred, axis=axis, keepdims=True)
    return centred * lax.rsqrt(variance + epsilon) * gain + bias


def column(row):
    n = row.shape[1]
    eye = lax.broadcasted_iota(jnp.int32, (n, n), 0) == lax.broadcasted_iota(jnp.int32, (n, n), 1)
    return jnp.sum(jnp.where(eye, row, 0.0), axis=1, keepdims=True)


def pack(x):
    rows, tokens = x.shape[-2:]
    whole, rest = divmod(tokens, LANES)
    blocks = [x[..., t * LANES : (t + 1) * LANES] for t in range(whole)]
    if rest:
        tail = x[..., whole * LANES :]
        blocks.append(jnp.concatenate([tail[..., : rows // 2, :], tail[..., rows // 2 :, :]], axis=-1))
    return jnp.concatenate(blocks, axis=-2)


def unpack(x, rows):
    whole, rest = divmod(x.shape[-2], rows)
    blocks = [x[..., t * rows : (t + 1) * rows, :] for t in range(whole)]
    if rest:
        tail = x[..., whole * rows :, :]
        blocks.append(jnp.concatenate([tail[..., : LANES // 2], tail[..., LANES // 2 :]], axis=-2))
    return jnp.concatenate(blocks, axis=-1)


def arrange(x):
    row_count, col_count, _ = x.shape
    whole, spare = row_count // 3, LANES - 2 * col_count
    blocks = []
    for t in range(whole):
        blocks += [x[2 * t], x[2 * t + 1], x[2 * whole + t, :spare]]
    return jnp.concatenate(blocks + [x[2 * whole + t, spare:] for t in range(whole)], axis=0)


def restore(x, row_count, col_count):
    whole, spare = row_count // 3, LANES - 2 * col_count
    rest = col_count - spare
    rows = []
    for t in range(whole):
        rows += [x[t * LANES : t * LANES + col_count], x[t * LANES + col_count : t * LANES + 2 * col_count]]
    for t in range(whole):
        tail = whole * LANES + t * rest
        rows += [x[t * LANES + 2 * col_count : (t + 1) * LANES], x[tail : tail + rest]]
    return jnp.concatenate(rows, axis=0)


def normalise(flat, gain, bias):
    return layer_norm(flat.astype(jnp.float32), gain, bias, -1).astype(jnp.bfloat16)


def project(normed, w, shape, quads):
    ours = w.shape[0] // 4
    tokens = normed.shape[0]
    projected = lax.dot_general(w, arrange(normed.reshape(shape)), (((1,), (1,)), ((), ())), preferred_element_type=jnp.float32)
    left = sigmoid(projected[:ours]) * projected[ours : 2 * ours]
    right = sigmoid(projected[2 * ours : 3 * ours]) * projected[3 * ours :]
    sides = jnp.concatenate([left.reshape(quads, -1, tokens), right.reshape(quads, -1, tokens)], axis=1)
    return pack(sides).astype(jnp.bfloat16)


def own_kernel(quads, cols, pair_hbm, gain_hbm, bias_hbm, w_hbm, mask_hbm, sides_ref, normed_ref, spread_ref, column_mask_ref, w_ref, gain_ref, bias_ref, pair_ref, all_w_ref, mask_ref, sems):
    moves = [(mask_hbm, mask_ref), (pair_hbm, pair_ref), (gain_hbm, gain_ref), (bias_hbm, bias_ref), (w_hbm, all_w_ref)]
    copies = [pltpu.make_async_copy(source, target, sems.at[n]) for n, (source, target) in enumerate(moves)]
    for copy in copies:
        copy.start()
    my_quad, my_col = lax.axis_index("quad"), lax.axis_index("col")
    row_count, _, channels = pair_ref.shape
    tokens = normed_ref.shape[0]
    hidden = all_w_ref.shape[1] // 4
    ours = hidden // cols
    group, lanes = spread_ref.shape
    copies[0].wait()
    mask_row = mask_ref[...].astype(jnp.float32)
    column_mask_ref[...] = column(mask_row)
    start = lax.axis_index("half") * (lanes // group)
    token = lax.broadcasted_iota(jnp.int32, (mask_row.shape[1], lanes), 0)
    lane = lax.broadcasted_iota(jnp.int32, (mask_row.shape[1], lanes), 1)
    whole = row_count // 3
    block, t, row = lane // LANES, lane // (quads * group) % whole, lane // group % quads
    k = (row ^ my_quad) * row_count + jnp.where(block < 2, 2 * t + block, 2 * whole + t)
    pick = jnp.where(k + start == token, 1.0, 0.0)
    kept = jnp.dot(mask_row.astype(jnp.bfloat16), pick.astype(jnp.bfloat16), preferred_element_type=jnp.float32)
    channel = lax.broadcasted_iota(jnp.int32, (group, lanes), 0)
    lane = lax.broadcasted_iota(jnp.int32, (group, lanes), 1)
    spread_ref[...] = jnp.where(lane % group == channel, kept, 0.0)
    for copy in copies[1:4]:
        copy.wait()
    normed = normalise(pair_ref[...].reshape(tokens, channels), gain_ref[...], bias_ref[...])
    normed_ref[...] = normed
    copies[4].wait()
    parts = [all_w_ref[:, at : at + hidden] for at in range(0, 4 * hidden, hidden)]
    w = jnp.concatenate([jnp.where(my_col == 0, part[:, :ours], part[:, ours:]) for part in parts], axis=1).T
    w_ref[...] = w
    sides_ref[...] = project(normed, w, pair_ref.shape, quads)


def other_kernel(pair_ref, sides_ref, gain_ref, bias_ref, w_ref, *refs):
    *piece_refs, others_ref = refs
    my_quad, my_col = lax.axis_index("quad"), lax.axis_index("col")
    quads = sides_ref.shape[0]
    normed = normalise(pair_ref[...].reshape(-1, pair_ref.shape[2]), gain_ref[...], bias_ref[...])
    others_ref[...] = project(normed, w_ref[...], pair_ref.shape, quads)
    for step, piece_ref in enumerate(piece_refs):
        piece_ref[my_col] = sides_ref[my_quad ^ step]
        piece_ref[1 - my_col] = others_ref[my_quad ^ step]


def triangle_kernel(far_order, steps, cols, row_count, col_count, share, *refs):
    *got_refs, spread_ref, mask_ref, total_ref, left_ref, wide_ref = refs
    got_refs = {step: ref for step, ref in zip(steps, got_refs)}
    both = 2 * share
    group, lanes = spread_ref.shape
    length = mask_ref.shape[0]
    rows, quads, parts = length // row_count, len(steps), share // group
    whole, spare = row_count // 3, LANES - 2 * col_count
    rest = col_count - spare
    blocks = [[got_refs[row][col].astype(jnp.float32) for row in range(quads)] for col in range(cols)]

    def turned(picks):
        return jnp.concatenate([blocks[col][row][at : at + group] for col, row, at in picks], axis=0).T

    tail = turned([(col, row, whole * both + part * group) for col in range(cols) for part in range(parts) for row in range(quads)])

    def side(which, part):
        even, odd, third = [], [], []
        for col in range(cols):
            at = which * share + part * group
            block = turned([(col, row, t * both + at) for t in range(whole) for row in range(quads)])
            even.append(block[:col_count])
            odd.append(block[col_count : 2 * col_count])
            lane = (col * parts + part) * quads * group
            at = which * LANES // 2
            last = [tail[at + t * rest : at + (t + 1) * rest, lane : lane + quads * group] for t in range(whole)]
            third += [block[2 * col_count :], jnp.concatenate(last, axis=1)]
        tokens = [jnp.concatenate(pieces, axis=0) for pieces in (even, odd, third)]
        return jnp.concatenate(tokens, axis=1) * mask_ref[...]

    def placed(pieces):
        return jnp.concatenate([jnp.zeros((piece, lanes), jnp.bfloat16) if isinstance(piece, int) else piece for piece in pieces], axis=0)

    contract = (((1,), (1,)), ((), ()))
    lane_block = lax.broadcasted_iota(jnp.int32, (group, LANES), 1) // rest
    mains, lasts = [], []
    for part in range(parts):
        left_ref[part] = side(0, part)
        right = side(1, part).astype(jnp.bfloat16)
        for row in range(rows):
            for t in range(0, whole, 2):
                pair = []
                for at in (row * row_count, row * row_count + 2):
                    picks = [at + 2 * t, at + 2 * t + 1, row * row_count + 2 * whole + t + len(pair)]
                    copies = [jnp.broadcast_to(left_ref[part, i : i + 1, :], (group, lanes)) for i in picks]
                    pair.append(jnp.concatenate([copy * spread_ref[...] for copy in copies], axis=1))
                at = (row * whole + t) * group
                wide_ref[part, at : at + 2 * group, :] = jnp.concatenate(pair, axis=0).astype(jnp.bfloat16)
        ours = [right[col * col_count : (col + 1) * col_count] for col in range(cols)]
        weights = [
            placed([p for mine in ours for p in (mine, LANES - col_count)]),
            placed([p for mine in ours for p in (col_count, mine, spare)]),
            placed([p for mine in ours for p in (2 * col_count, mine[:spare])]),
        ]
        weights = jnp.concatenate(weights, axis=1)
        mains.append(lax.dot_general(wide_ref[part], weights, contract, preferred_element_type=jnp.float32))
        gap = LANES // parts
        pieces = [[gap * part] + [mine[spare:]] * whole + [LANES - gap * (part + 1)] for mine in ours]
        weights = placed([p for piece in pieces for p in piece if not isinstance(p, int) or p])
        lasts.append(lax.dot_general(wide_ref[part, :, 2 * lanes :], weights, contract, preferred_element_type=jnp.float32))
    for target, device in enumerate(far_order):
        row, col = divmod(device, cols)
        spots = [(row * whole + t) * group for t in range(whole)]
        tiles = [main[at : at + group, col * LANES : (col + 1) * LANES] for at in spots for main in mains]
        last = [part[at : at + group, col * LANES : (col + 1) * LANES] for part in lasts for at in spots]
        tile = last[0]
        for n in range(1, len(last)):
            tile = jnp.where(lane_block >= n, last[n], tile)
        tiles.append(tile)
        total_ref[target] = jnp.concatenate(tiles, axis=0).astype(jnp.bfloat16)


def gate_kernel(normed_ref, w_ref, gain_ref, bias_ref, gate_ref, gain_out_ref, bias_out_ref):
    gate_ref[...] = sigmoid(jnp.dot(normed_ref[...], w_ref[...], preferred_element_type=jnp.float32))
    gain_out_ref[...] = column(gain_ref[...])
    bias_out_ref[...] = column(bias_ref[...])


def output_kernel(far_order, near_order, total_ref, gate_ref, gain_ref, bias_ref, w_ref, out_ref):
    tokens = gate_ref.shape[0]
    hidden = w_ref.shape[0]
    near = len(near_order)
    share = hidden // near
    blocks = []
    for index in near_order:
        parts = [total_ref[source].astype(jnp.float32) for source, device in enumerate(far_order) if device % near == index]
        blocks.append(unpack(sum(parts[1:], parts[0]), share))
    total = jnp.concatenate(blocks, axis=0)
    normed = layer_norm(total, gain_ref[...], bias_ref[...], 0).astype(jnp.bfloat16)
    output = lax.dot_general(normed, w_ref[...], (((0,), (0,)), ((), ())), preferred_element_type=jnp.float32)
    output = restore(output, out_ref.shape[0], out_ref.shape[1])
    out_ref[...] = (gate_ref[...] * output).astype(jnp.bfloat16).reshape(out_ref.shape)


def per_device(rows, cols, halves, pair, token_mask, gain_in, bias_in, w_in, w_gate, gain_out, bias_out, w_out):
    row_count, col_count, channels = pair.shape
    hidden = w_out.shape[0]
    devices = rows * cols
    near = devices // halves
    quads = rows // halves
    far_order = []
    for col in reversed(range(cols)):
        ahead = list(range(quads)) if col else list(range(1, quads)) + [0]
        behind = [0] + list(reversed(range(1, quads))) if col else list(range(quads))
        for quad, other in zip(ahead, behind):
            far_order += [near + other * cols + col, quad * cols + col]
    share = hidden // near
    tokens = row_count * col_count
    length = rows * row_count
    depth = length // halves
    token_mask = token_mask.reshape(1, length)
    near_order = [quad * cols + col for col in range(cols) for quad in range(quads)]
    packed = 2 * share * tokens // LANES
    cost = pl.CostEstimate(flops=2 * tokens * channels * 4 * hidden, bytes_accessed=16 * tokens * channels, transcendentals=0)
    other_pair = lax.ppermute(pair, "col", [(i, (i + 1) % cols) for i in range(cols)])
    arguments = (pair, gain_in.reshape(1, channels), bias_in.reshape(1, channels), w_in, token_mask)
    sides, normed, spread, mask, *weights = pl.pallas_call(
        functools.partial(own_kernel, quads, cols),
        out_shape=(
            jax.ShapeDtypeStruct((quads, packed, LANES), jnp.bfloat16),
            jax.ShapeDtypeStruct((tokens, channels), jnp.bfloat16),
            jax.ShapeDtypeStruct((GROUP, GROUP * depth), jnp.float32),
            jax.ShapeDtypeStruct((length, 1), jnp.float32),
            jax.ShapeDtypeStruct((4 * hidden // cols, channels), jnp.bfloat16),
            jax.ShapeDtypeStruct((1, channels), jnp.float32),
            jax.ShapeDtypeStruct((1, channels), jnp.float32),
        ),
        in_specs=[HBM] * 5,
        out_specs=(VMEM,) * 7,
        scratch_shapes=[
            pltpu.VMEM(pair.shape, pair.dtype),
            pltpu.VMEM(w_in.shape, w_in.dtype),
            pltpu.VMEM((1, length), jnp.int32),
            pltpu.SemaphoreType.DMA((5,)),
        ],
        compiler_params=LIMIT,
        cost_estimate=cost,
    )(*(pltpu.with_memory_space_constraint(x, pltpu.HBM) for x in arguments))
    w_ours, gain_in, bias_in = weights
    pieces = pl.pallas_call(
        other_kernel,
        out_shape=[jax.ShapeDtypeStruct((cols, packed, LANES), jnp.bfloat16)] * quads,
        in_specs=[VMEM] * 5,
        out_specs=[VMEM] * quads,
        scratch_shapes=[pltpu.VMEM((quads, packed, LANES), jnp.bfloat16)],
        compiler_params=LIMIT,
        cost_estimate=cost,
    )(other_pair, sides, gain_in, bias_in, w_ours)
    steps = [3, 1, 2, 0]
    got = [lax.ppermute(pieces[step], "quad", [(i, i ^ step) for i in range(quads)]) if step else pieces[0] for step in steps]
    total = pl.pallas_call(
        functools.partial(triangle_kernel, far_order, steps, cols, row_count, col_count, share),
        out_shape=jax.ShapeDtypeStruct((devices, share * tokens // LANES, LANES), jnp.bfloat16),
        in_specs=[VMEM] * (quads + 2),
        out_specs=VMEM,
        scratch_shapes=[
            pltpu.VMEM((share // GROUP, length, GROUP * depth), jnp.float32),
            pltpu.VMEM((share // GROUP, length // 3 * GROUP, 3 * GROUP * depth), jnp.bfloat16),
        ],
        compiler_params=LIMIT,
    )(*got, spread, mask)
    gate, gain_out, bias_out = pl.pallas_call(
        gate_kernel,
        out_shape=(
            jax.ShapeDtypeStruct((tokens, channels), jnp.float32),
            jax.ShapeDtypeStruct((hidden, 1), jnp.float32),
            jax.ShapeDtypeStruct((hidden, 1), jnp.float32),
        ),
        in_specs=[VMEM] * 4,
        out_specs=(VMEM, VMEM, VMEM),
        compiler_params=LIMIT,
        cost_estimate=pl.CostEstimate(flops=2 * tokens * channels * channels, bytes_accessed=4 * tokens * channels, transcendentals=0),
    )(normed, w_gate, gain_out.reshape(1, hidden), bias_out.reshape(1, hidden))
    total = lax.all_to_all(total, ("half", "quad", "col"), split_axis=0, concat_axis=0, tiled=True, axis_index_groups=[far_order])
    return pl.pallas_call(
        functools.partial(output_kernel, far_order, near_order),
        out_shape=jax.ShapeDtypeStruct(pair.shape, jnp.bfloat16),
        in_specs=[VMEM] * 5,
        out_specs=VMEM,
        compiler_params=LIMIT,
    )(total, gate, gain_out, bias_out, w_out)


def plain_per_device(rows, cols, pair, token_mask, gain_in, bias_in, w_in, w_gate, gain_out, bias_out, w_out):
    row_count, col_count, channels = pair.shape
    hidden = w_out.shape[0]
    devices = rows * cols
    share = hidden // devices
    tokens = row_count * col_count
    row_start = lax.axis_index(("half", "quad")) * row_count
    col_start = lax.axis_index("col") * col_count
    mask_float = token_mask.astype(jnp.float32)
    mask_rows = lax.dynamic_slice_in_dim(mask_float, row_start, row_count)
    mask_cols = lax.dynamic_slice_in_dim(mask_float, col_start, col_count)
    pair_mask = (mask_rows[:, None] * mask_cols[None, :]).reshape(1, tokens)
    flat = pair.reshape(tokens, channels).astype(jnp.float32)
    normed = layer_norm(flat, gain_in, bias_in, -1).astype(jnp.bfloat16)
    projected = lax.dot_general(w_in, normed, (((0,), (1,)), ((), ())), preferred_element_type=jnp.float32)
    projected = projected.reshape(2, 2, hidden, tokens)
    sides = (pair_mask * jax.nn.sigmoid(projected[:, 0]) * projected[:, 1]).astype(jnp.bfloat16)
    sides = sides.reshape(2, devices, share, tokens).transpose(1, 0, 2, 3)
    gate = jax.nn.sigmoid(jnp.dot(normed, w_gate, preferred_element_type=jnp.float32))
    got = lax.all_to_all(sides, AXES, split_axis=0, concat_axis=0, tiled=True)
    got = got.reshape(rows, cols, 2, share, row_count, col_count).transpose(2, 3, 0, 4, 1, 5)
    got = got.reshape(2, share, rows * row_count, cols * col_count)
    total = jnp.einsum("cki,ckj->cij", got[0], got[1], preferred_element_type=jnp.float32).astype(jnp.bfloat16)
    total = total.reshape(share, rows, row_count, cols, col_count).transpose(1, 3, 0, 2, 4)
    total = total.reshape(devices, share, tokens)
    total = lax.all_to_all(total, AXES, split_axis=0, concat_axis=0, tiled=True)
    total = total.reshape(hidden, tokens).astype(jnp.float32)
    summed_norm = layer_norm(total, gain_out[:, None], bias_out[:, None], 0).astype(jnp.bfloat16)
    output = lax.dot_general(summed_norm, w_out, (((0,), (0,)), ((), ())), preferred_element_type=jnp.float32)
    return (gate * output).astype(jnp.bfloat16).reshape(row_count, col_count, channels)


def solution(mesh):
    rows, cols = mesh.shape["row"], mesh.shape["col"]
    halves = 2
    parts = (mesh.shape["groups"], halves, rows // halves, cols)
    finer = jax.sharding.Mesh(mesh.devices.reshape(parts), ("groups", "half", "quad", "col"))

    def per_shard(*args):
        near, hidden, length = rows * cols // halves, args[-1].shape[0], args[1].shape[0]
        row_count, col_count, _ = args[0].shape
        spare = LANES - 2 * col_count
        fits = hidden % (2 * GROUP * near) == 0 and cols == 2 and rows // halves == 4 and length <= LANES and row_count % 3 == 0
        fits = fits and 0 < spare < col_count and row_count // 3 * (col_count - spare) * 2 == LANES
        fits = fits and row_count // 3 * (rows // halves) * GROUP == LANES
        return per_device(rows, cols, halves, *args) if fits else plain_per_device(rows, cols, *args)

    tokens = P(("groups", "half", "quad"), "col", None)
    in_specs = (tokens, P("groups"), P(), P(), P(), P(), P(), P(), P())
    return jax.shard_map(per_shard, mesh=finer, in_specs=in_specs, out_specs=tokens, check_vma=False)
```

```python
import functools

import jax
import jax.numpy as jnp
from jax import lax
from jax.experimental import pallas as pl
from jax.experimental.pallas import tpu as pltpu
from jax.sharding import PartitionSpec as P

epsilon = 1e-05
LANES = 128
GROUP = 8
AXES = ("half", "quad", "col")
VMEM = pl.BlockSpec(memory_space=pltpu.VMEM)
HBM = pl.BlockSpec(memory_space=pltpu.HBM)
LIMIT = pltpu.CompilerParams(vmem_limit_bytes=32 * 1024 * 1024)


def sigmoid(x):
    return 0.5 * jnp.tanh(0.5 * x) + 0.5


def layer_norm(values, gain, bias, axis):
    mean = jnp.mean(values, axis=axis, keepdims=True)
    centred = values - mean
    variance = jnp.mean(centred * centred, axis=axis, keepdims=True)
    return centred * lax.rsqrt(variance + epsilon) * gain + bias


def column(row):
    n = row.shape[1]
    eye = lax.broadcasted_iota(jnp.int32, (n, n), 0) == lax.broadcasted_iota(jnp.int32, (n, n), 1)
    return jnp.sum(jnp.where(eye, row, 0.0), axis=1, keepdims=True)


def pack(x):
    rows, tokens = x.shape[-2:]
    whole, rest = divmod(tokens, LANES)
    blocks = [x[..., t * LANES : (t + 1) * LANES] for t in range(whole)]
    if rest:
        tail = x[..., whole * LANES :]
        blocks.append(jnp.concatenate([tail[..., : rows // 2, :], tail[..., rows // 2 :, :]], axis=-1))
    return jnp.concatenate(blocks, axis=-2)


def unpack(x, rows):
    whole, rest = divmod(x.shape[-2], rows)
    blocks = [x[..., t * rows : (t + 1) * rows, :] for t in range(whole)]
    if rest:
        tail = x[..., whole * rows :, :]
        blocks.append(jnp.concatenate([tail[..., : LANES // 2], tail[..., LANES // 2 :]], axis=-2))
    return jnp.concatenate(blocks, axis=-1)


def arrange(x):
    row_count, col_count, _ = x.shape
    whole, spare = row_count // 3, LANES - 2 * col_count
    blocks = []
    for t in range(whole):
        blocks += [x[2 * t], x[2 * t + 1], x[2 * whole + t, :spare]]
    return jnp.concatenate(blocks + [x[2 * whole + t, spare:] for t in range(whole)], axis=0)


def restore(x, row_count, col_count):
    whole, spare = row_count // 3, LANES - 2 * col_count
    rest = col_count - spare
    rows = []
    for t in range(whole):
        rows += [x[t * LANES : t * LANES + col_count], x[t * LANES + col_count : t * LANES + 2 * col_count]]
    for t in range(whole):
        tail = whole * LANES + t * rest
        rows += [x[t * LANES + 2 * col_count : (t + 1) * LANES], x[tail : tail + rest]]
    return jnp.concatenate(rows, axis=0)


def normalise(flat, gain, bias):
    return layer_norm(flat.astype(jnp.float32), gain, bias, -1).astype(jnp.bfloat16)


def project(normed, w, shape, quads):
    ours = w.shape[0] // 4
    tokens = normed.shape[0]
    projected = lax.dot_general(w, arrange(normed.reshape(shape)), (((1,), (1,)), ((), ())), preferred_element_type=jnp.float32)
    left = sigmoid(projected[:ours]) * projected[ours : 2 * ours]
    right = sigmoid(projected[2 * ours : 3 * ours]) * projected[3 * ours :]
    sides = jnp.concatenate([left.reshape(quads, -1, tokens), right.reshape(quads, -1, tokens)], axis=1)
    return pack(sides).astype(jnp.bfloat16)


def own_kernel(quads, cols, pair_hbm, gain_hbm, bias_hbm, w_hbm, mask_hbm, sides_ref, normed_ref, spread_ref, column_mask_ref, w_ref, gain_ref, bias_ref, pair_ref, all_w_ref, mask_ref, sems):
    moves = [(mask_hbm, mask_ref), (pair_hbm, pair_ref), (gain_hbm, gain_ref), (bias_hbm, bias_ref), (w_hbm, all_w_ref)]
    copies = [pltpu.make_async_copy(source, target, sems.at[n]) for n, (source, target) in enumerate(moves)]
    for copy in copies:
        copy.start()
    my_quad, my_col = lax.axis_index("quad"), lax.axis_index("col")
    row_count, _, channels = pair_ref.shape
    tokens = normed_ref.shape[0]
    hidden = all_w_ref.shape[1] // 4
    ours = hidden // cols
    group, lanes = spread_ref.shape
    copies[0].wait()
    mask_row = mask_ref[...].astype(jnp.float32)
    column_mask_ref[...] = column(mask_row)
    start = lax.axis_index("half") * (lanes // group)
    token = lax.broadcasted_iota(jnp.int32, (mask_row.shape[1], lanes), 0)
    lane = lax.broadcasted_iota(jnp.int32, (mask_row.shape[1], lanes), 1)
    whole = row_count // 3
    block, t, row = lane // LANES, lane // (quads * group) % whole, lane // group % quads
    k = (row ^ my_quad) * row_count + jnp.where(block < 2, 2 * t + block, 2 * whole + t)
    pick = jnp.where(k + start == token, 1.0, 0.0)
    kept = jnp.dot(mask_row.astype(jnp.bfloat16), pick.astype(jnp.bfloat16), preferred_element_type=jnp.float32)
    channel = lax.broadcasted_iota(jnp.int32, (group, lanes), 0)
    lane = lax.broadcasted_iota(jnp.int32, (group, lanes), 1)
    spread_ref[...] = jnp.where(lane % group == channel, kept, 0.0)
    for copy in copies[1:4]:
        copy.wait()
    normed = normalise(pair_ref[...].reshape(tokens, channels), gain_ref[...], bias_ref[...])
    normed_ref[...] = normed
    copies[4].wait()
    parts = [all_w_ref[:, at : at + hidden] for at in range(0, 4 * hidden, hidden)]
    w = jnp.concatenate([jnp.where(my_col == 0, part[:, :ours], part[:, ours:]) for part in parts], axis=1).T
    w_ref[...] = w
    sides_ref[...] = project(normed, w, pair_ref.shape, quads)


def other_kernel(pair_ref, sides_ref, gain_ref, bias_ref, w_ref, *refs):
    *piece_refs, others_ref = refs
    my_quad, my_col = lax.axis_index("quad"), lax.axis_index("col")
    quads = sides_ref.shape[0]
    normed = normalise(pair_ref[...].reshape(-1, pair_ref.shape[2]), gain_ref[...], bias_ref[...])
    others_ref[...] = project(normed, w_ref[...], pair_ref.shape, quads)
    for step, piece_ref in enumerate(piece_refs):
        piece_ref[my_col] = sides_ref[my_quad ^ step]
        piece_ref[1 - my_col] = others_ref[my_quad ^ step]


def triangle_kernel(far_order, steps, cols, row_count, col_count, share, *refs):
    *got_refs, spread_ref, mask_ref, total_ref, left_ref, wide_ref = refs
    got_refs = {step: ref for step, ref in zip(steps, got_refs)}
    both = 2 * share
    group, lanes = spread_ref.shape
    length = mask_ref.shape[0]
    rows, quads, parts = length // row_count, len(steps), share // group
    whole, spare = row_count // 3, LANES - 2 * col_count
    rest = col_count - spare
    blocks = [[got_refs[row][col].astype(jnp.float32) for row in range(quads)] for col in range(cols)]

    def turned(picks):
        return jnp.concatenate([blocks[col][row][at : at + group] for col, row, at in picks], axis=0).T

    tail = turned([(col, row, whole * both + part * group) for col in range(cols) for part in range(parts) for row in range(quads)])

    def side(which, part):
        even, odd, third = [], [], []
        for col in range(cols):
            at = which * share + part * group
            block = turned([(col, row, t * both + at) for t in range(whole) for row in range(quads)])
            even.append(block[:col_count])
            odd.append(block[col_count : 2 * col_count])
            lane = (col * parts + part) * quads * group
            at = which * LANES // 2
            last = [tail[at + t * rest : at + (t + 1) * rest, lane : lane + quads * group] for t in range(whole)]
            third += [block[2 * col_count :], jnp.concatenate(last, axis=1)]
        tokens = [jnp.concatenate(pieces, axis=0) for pieces in (even, odd, third)]
        return jnp.concatenate(tokens, axis=1) * mask_ref[...]

    def placed(pieces):
        return jnp.concatenate([jnp.zeros((piece, lanes), jnp.bfloat16) if isinstance(piece, int) else piece for piece in pieces], axis=0)

    contract = (((1,), (1,)), ((), ()))
    lane_block = lax.broadcasted_iota(jnp.int32, (group, LANES), 1) // rest
    mains, lasts = [], []
    for part in range(parts):
        left_ref[part] = side(0, part)
        right = side(1, part).astype(jnp.bfloat16)
        for row in range(rows):
            for t in range(0, whole, 2):
                pair = []
                for at in (row * row_count, row * row_count + 2):
                    picks = [at + 2 * t, at + 2 * t + 1, row * row_count + 2 * whole + t + len(pair)]
                    copies = [jnp.broadcast_to(left_ref[part, i : i + 1, :], (group, lanes)) for i in picks]
                    pair.append(jnp.concatenate([copy * spread_ref[...] for copy in copies], axis=1))
                at = (row * whole + t) * group
                wide_ref[part, at : at + 2 * group, :] = jnp.concatenate(pair, axis=0).astype(jnp.bfloat16)
        ours = [right[col * col_count : (col + 1) * col_count] for col in range(cols)]
        weights = [
            placed([p for mine in ours for p in (mine, LANES - col_count)]),
            placed([p for mine in ours for p in (col_count, mine, spare)]),
            placed([p for mine in ours for p in (2 * col_count, mine[:spare])]),
        ]
        weights = jnp.concatenate(weights, axis=1)
        mains.append(lax.dot_general(wide_ref[part], weights, contract, preferred_element_type=jnp.float32))
        gap = LANES // parts
        pieces = [[gap * part] + [mine[spare:]] * whole + [LANES - gap * (part + 1)] for mine in ours]
        weights = placed([p for piece in pieces for p in piece if not isinstance(p, int) or p])
        lasts.append(lax.dot_general(wide_ref[part, :, 2 * lanes :], weights, contract, preferred_element_type=jnp.float32))
    for target, device in enumerate(far_order):
        row, col = divmod(device, cols)
        spots = [(row * whole + t) * group for t in range(whole)]
        tiles = [main[at : at + group, col * LANES : (col + 1) * LANES] for at in spots for main in mains]
        last = [part[at : at + group, col * LANES : (col + 1) * LANES] for part in lasts for at in spots]
        tile = last[0]
        for n in range(1, len(last)):
            tile = jnp.where(lane_block >= n, last[n], tile)
        tiles.append(tile)
        total_ref[target] = jnp.concatenate(tiles, axis=0).astype(jnp.bfloat16)


def gate_kernel(normed_ref, w_ref, gain_ref, bias_ref, gate_ref, gain_out_ref, bias_out_ref):
    gate_ref[...] = sigmoid(jnp.dot(normed_ref[...], w_ref[...], preferred_element_type=jnp.float32))
    gain_out_ref[...] = column(gain_ref[...])
    bias_out_ref[...] = column(bias_ref[...])


def output_kernel(far_order, near_order, total_ref, gate_ref, gain_ref, bias_ref, w_ref, out_ref):
    tokens = gate_ref.shape[0]
    hidden = w_ref.shape[0]
    near = len(near_order)
    share = hidden // near
    blocks = []
    for index in near_order:
        parts = [total_ref[source].astype(jnp.float32) for source, device in enumerate(far_order) if device % near == index]
        blocks.append(unpack(sum(parts[1:], parts[0]), share))
    total = jnp.concatenate(blocks, axis=0)
    normed = layer_norm(total, gain_ref[...], bias_ref[...], 0).astype(jnp.bfloat16)
    output = jnp.dot(normed.T, w_ref[...], preferred_element_type=jnp.float32)
    output = restore(output, out_ref.shape[0], out_ref.shape[1])
    out_ref[...] = (gate_ref[...] * output).astype(jnp.bfloat16).reshape(out_ref.shape)


def per_device(rows, cols, halves, pair, token_mask, gain_in, bias_in, w_in, w_gate, gain_out, bias_out, w_out):
    row_count, col_count, channels = pair.shape
    hidden = w_out.shape[0]
    devices = rows * cols
    near = devices // halves
    quads = rows // halves
    far_order = []
    for col in reversed(range(cols)):
        ahead = list(range(quads)) if col else list(range(1, quads)) + [0]
        behind = [0] + list(reversed(range(1, quads))) if col else list(reversed(range(quads)))
        for quad, other in zip(ahead, behind):
            far_order += [near + other * cols + col, quad * cols + col]
    share = hidden // near
    tokens = row_count * col_count
    length = rows * row_count
    depth = length // halves
    token_mask = token_mask.reshape(1, length)
    near_order = [quad * cols + col for col in range(cols) for quad in range(quads)]
    packed = 2 * share * tokens // LANES
    cost = pl.CostEstimate(flops=2 * tokens * channels * 4 * hidden, bytes_accessed=16 * tokens * channels, transcendentals=0)
    other_pair = lax.ppermute(pair, "col", [(i, (i + 1) % cols) for i in range(cols)])
    arguments = (pair, gain_in.reshape(1, channels), bias_in.reshape(1, channels), w_in, token_mask)
    sides, normed, spread, mask, *weights = pl.pallas_call(
        functools.partial(own_kernel, quads, cols),
        out_shape=(
            jax.ShapeDtypeStruct((quads, packed, LANES), jnp.bfloat16),
            jax.ShapeDtypeStruct((tokens, channels), jnp.bfloat16),
            jax.ShapeDtypeStruct((GROUP, GROUP * depth), jnp.float32),
            jax.ShapeDtypeStruct((length, 1), jnp.float32),
            jax.ShapeDtypeStruct((4 * hidden // cols, channels), jnp.bfloat16),
            jax.ShapeDtypeStruct((1, channels), jnp.float32),
            jax.ShapeDtypeStruct((1, channels), jnp.float32),
        ),
        in_specs=[HBM] * 5,
        out_specs=(VMEM,) * 7,
        scratch_shapes=[
            pltpu.VMEM(pair.shape, pair.dtype),
            pltpu.VMEM(w_in.shape, w_in.dtype),
            pltpu.VMEM((1, length), jnp.int32),
            pltpu.SemaphoreType.DMA((5,)),
        ],
        compiler_params=LIMIT,
        cost_estimate=cost,
    )(*(pltpu.with_memory_space_constraint(x, pltpu.HBM) for x in arguments))
    w_ours, gain_in, bias_in = weights
    pieces = pl.pallas_call(
        other_kernel,
        out_shape=[jax.ShapeDtypeStruct((cols, packed, LANES), jnp.bfloat16)] * quads,
        in_specs=[VMEM] * 5,
        out_specs=[VMEM] * quads,
        scratch_shapes=[pltpu.VMEM((quads, packed, LANES), jnp.bfloat16)],
        compiler_params=LIMIT,
        cost_estimate=cost,
    )(other_pair, sides, gain_in, bias_in, w_ours)
    steps = [3, 1, 2, 0]
    got = [lax.ppermute(pieces[step], "quad", [(i, i ^ step) for i in range(quads)]) if step else pieces[0] for step in steps]
    total = pl.pallas_call(
        functools.partial(triangle_kernel, far_order, steps, cols, row_count, col_count, share),
        out_shape=jax.ShapeDtypeStruct((devices, share * tokens // LANES, LANES), jnp.bfloat16),
        in_specs=[VMEM] * (quads + 2),
        out_specs=VMEM,
        scratch_shapes=[
            pltpu.VMEM((share // GROUP, length, GROUP * depth), jnp.float32),
            pltpu.VMEM((share // GROUP, length // 3 * GROUP, 3 * GROUP * depth), jnp.bfloat16),
        ],
        compiler_params=LIMIT,
    )(*got, spread, mask)
    gate, gain_out, bias_out = pl.pallas_call(
        gate_kernel,
        out_shape=(
            jax.ShapeDtypeStruct((tokens, channels), jnp.float32),
            jax.ShapeDtypeStruct((hidden, 1), jnp.float32),
            jax.ShapeDtypeStruct((hidden, 1), jnp.float32),
        ),
        in_specs=[VMEM] * 4,
        out_specs=(VMEM, VMEM, VMEM),
        compiler_params=LIMIT,
        cost_estimate=pl.CostEstimate(flops=2 * tokens * channels * channels, bytes_accessed=4 * tokens * channels, transcendentals=0),
    )(normed, w_gate, gain_out.reshape(1, hidden), bias_out.reshape(1, hidden))
    total = lax.all_to_all(total, ("half", "quad", "col"), split_axis=0, concat_axis=0, tiled=True, axis_index_groups=[far_order])
    return pl.pallas_call(
        functools.partial(output_kernel, far_order, near_order),
        out_shape=jax.ShapeDtypeStruct(pair.shape, jnp.bfloat16),
        in_specs=[VMEM] * 5,
        out_specs=VMEM,
        compiler_params=LIMIT,
    )(total, gate, gain_out, bias_out, w_out)


def plain_per_device(rows, cols, pair, token_mask, gain_in, bias_in, w_in, w_gate, gain_out, bias_out, w_out):
    row_count, col_count, channels = pair.shape
    hidden = w_out.shape[0]
    devices = rows * cols
    share = hidden // devices
    tokens = row_count * col_count
    row_start = lax.axis_index(("half", "quad")) * row_count
    col_start = lax.axis_index("col") * col_count
    mask_float = token_mask.astype(jnp.float32)
    mask_rows = lax.dynamic_slice_in_dim(mask_float, row_start, row_count)
    mask_cols = lax.dynamic_slice_in_dim(mask_float, col_start, col_count)
    pair_mask = (mask_rows[:, None] * mask_cols[None, :]).reshape(1, tokens)
    flat = pair.reshape(tokens, channels).astype(jnp.float32)
    normed = layer_norm(flat, gain_in, bias_in, -1).astype(jnp.bfloat16)
    projected = lax.dot_general(w_in, normed, (((0,), (1,)), ((), ())), preferred_element_type=jnp.float32)
    projected = projected.reshape(2, 2, hidden, tokens)
    sides = (pair_mask * jax.nn.sigmoid(projected[:, 0]) * projected[:, 1]).astype(jnp.bfloat16)
    sides = sides.reshape(2, devices, share, tokens).transpose(1, 0, 2, 3)
    gate = jax.nn.sigmoid(jnp.dot(normed, w_gate, preferred_element_type=jnp.float32))
    got = lax.all_to_all(sides, AXES, split_axis=0, concat_axis=0, tiled=True)
    got = got.reshape(rows, cols, 2, share, row_count, col_count).transpose(2, 3, 0, 4, 1, 5)
    got = got.reshape(2, share, rows * row_count, cols * col_count)
    total = jnp.einsum("cki,ckj->cij", got[0], got[1], preferred_element_type=jnp.float32).astype(jnp.bfloat16)
    total = total.reshape(share, rows, row_count, cols, col_count).transpose(1, 3, 0, 2, 4)
    total = total.reshape(devices, share, tokens)
    total = lax.all_to_all(total, AXES, split_axis=0, concat_axis=0, tiled=True)
    total = total.reshape(hidden, tokens).astype(jnp.float32)
    summed_norm = layer_norm(total, gain_out[:, None], bias_out[:, None], 0).astype(jnp.bfloat16)
    output = lax.dot_general(summed_norm, w_out, (((0,), (0,)), ((), ())), preferred_element_type=jnp.float32)
    return (gate * output).astype(jnp.bfloat16).reshape(row_count, col_count, channels)


def solution(mesh):
    rows, cols = mesh.shape["row"], mesh.shape["col"]
    halves = 2
    parts = (mesh.shape["groups"], halves, rows // halves, cols)
    finer = jax.sharding.Mesh(mesh.devices.reshape(parts), ("groups", "half", "quad", "col"))

    def per_shard(*args):
        near, hidden, length = rows * cols // halves, args[-1].shape[0], args[1].shape[0]
        row_count, col_count, _ = args[0].shape
        spare = LANES - 2 * col_count
        fits = hidden % (2 * GROUP * near) == 0 and cols == 2 and rows // halves == 4 and length <= LANES and row_count % 3 == 0
        fits = fits and 0 < spare < col_count and row_count // 3 * (col_count - spare) * 2 == LANES
        fits = fits and row_count // 3 * (rows // halves) * GROUP == LANES
        return per_device(rows, cols, halves, *args) if fits else plain_per_device(rows, cols, *args)

    tokens = P(("groups", "half", "quad"), "col", None)
    in_specs = (tokens, P("groups"), P(), P(), P(), P(), P(), P(), P())
    return jax.shard_map(per_shard, mesh=finer, in_specs=in_specs, out_specs=tokens, check_vma=False)
```

```python
import functools

import jax
import jax.numpy as jnp
from jax import lax
from jax.experimental import pallas as pl
from jax.experimental.pallas import tpu as pltpu
from jax.sharding import PartitionSpec as P

epsilon = 1e-05
LANES = 128
GROUP = 8
AXES = ("half", "quad", "col")
VMEM = pl.BlockSpec(memory_space=pltpu.VMEM)
HBM = pl.BlockSpec(memory_space=pltpu.HBM)
LIMIT = pltpu.CompilerParams(vmem_limit_bytes=32 * 1024 * 1024)


def sigmoid(x):
    return 0.5 * jnp.tanh(0.5 * x) + 0.5


def layer_norm(values, gain, bias, axis):
    mean = jnp.mean(values, axis=axis, keepdims=True)
    centred = values - mean
    variance = jnp.mean(centred * centred, axis=axis, keepdims=True)
    return centred * lax.rsqrt(variance + epsilon) * gain + bias


def column(row):
    n = row.shape[1]
    eye = lax.broadcasted_iota(jnp.int32, (n, n), 0) == lax.broadcasted_iota(jnp.int32, (n, n), 1)
    return jnp.sum(jnp.where(eye, row, 0.0), axis=1, keepdims=True)


def pack(x):
    rows, tokens = x.shape[-2:]
    whole, rest = divmod(tokens, LANES)
    blocks = [x[..., t * LANES : (t + 1) * LANES] for t in range(whole)]
    if rest:
        tail = x[..., whole * LANES :]
        blocks.append(jnp.concatenate([tail[..., : rows // 2, :], tail[..., rows // 2 :, :]], axis=-1))
    return jnp.concatenate(blocks, axis=-2)


def unpack(x, rows):
    whole, rest = divmod(x.shape[-2], rows)
    blocks = [x[..., t * rows : (t + 1) * rows, :] for t in range(whole)]
    if rest:
        tail = x[..., whole * rows :, :]
        blocks.append(jnp.concatenate([tail[..., : LANES // 2], tail[..., LANES // 2 :]], axis=-2))
    return jnp.concatenate(blocks, axis=-1)


def arrange(x):
    row_count, col_count, _ = x.shape
    whole, spare = row_count // 3, LANES - 2 * col_count
    blocks = []
    for t in range(whole):
        blocks += [x[2 * t], x[2 * t + 1], x[2 * whole + t, :spare]]
    return jnp.concatenate(blocks + [x[2 * whole + t, spare:] for t in range(whole)], axis=0)


def restore(x, row_count, col_count):
    whole, spare = row_count // 3, LANES - 2 * col_count
    rest = col_count - spare
    rows = []
    for t in range(whole):
        rows += [x[t * LANES : t * LANES + col_count], x[t * LANES + col_count : t * LANES + 2 * col_count]]
    for t in range(whole):
        tail = whole * LANES + t * rest
        rows += [x[t * LANES + 2 * col_count : (t + 1) * LANES], x[tail : tail + rest]]
    return jnp.concatenate(rows, axis=0)


def normalise(flat, gain, bias):
    return layer_norm(flat.astype(jnp.float32), gain, bias, -1).astype(jnp.bfloat16)


def project(normed, w, shape, quads):
    ours = w.shape[0] // 4
    tokens = normed.shape[0]
    projected = lax.dot_general(w, arrange(normed.reshape(shape)), (((1,), (1,)), ((), ())), preferred_element_type=jnp.float32)
    left = sigmoid(projected[:ours]) * projected[ours : 2 * ours]
    right = sigmoid(projected[2 * ours : 3 * ours]) * projected[3 * ours :]
    sides = jnp.concatenate([left.reshape(quads, -1, tokens), right.reshape(quads, -1, tokens)], axis=1)
    return pack(sides).astype(jnp.bfloat16)


def own_kernel(quads, cols, pair_hbm, gain_hbm, bias_hbm, w_hbm, mask_hbm, sides_ref, normed_ref, spread_ref, column_mask_ref, w_ref, gain_ref, bias_ref, pair_ref, all_w_ref, mask_ref, sems):
    step = pair_ref.shape[0] // 2
    halves = [pl.ds(0, step), pl.ds(step, step)]
    moves = [(mask_hbm, mask_ref), (gain_hbm, gain_ref), (bias_hbm, bias_ref)]
    moves += [(pair_hbm.at[half], pair_ref.at[half]) for half in halves] + [(w_hbm, all_w_ref)]
    copies = [pltpu.make_async_copy(source, target, sems.at[n]) for n, (source, target) in enumerate(moves)]
    for copy in copies:
        copy.start()
    my_quad, my_col = lax.axis_index("quad"), lax.axis_index("col")
    row_count, _, channels = pair_ref.shape
    tokens = normed_ref.shape[0]
    hidden = all_w_ref.shape[1] // 4
    ours = hidden // cols
    group, lanes = spread_ref.shape
    copies[0].wait()
    mask_row = mask_ref[...].astype(jnp.float32)
    column_mask_ref[...] = column(mask_row)
    start = lax.axis_index("half") * (lanes // group)
    token = lax.broadcasted_iota(jnp.int32, (mask_row.shape[1], lanes), 0)
    lane = lax.broadcasted_iota(jnp.int32, (mask_row.shape[1], lanes), 1)
    whole = row_count // 3
    block, t, row = lane // LANES, lane // (quads * group) % whole, lane // group % quads
    k = (row ^ my_quad) * row_count + jnp.where(block < 2, 2 * t + block, 2 * whole + t)
    pick = jnp.where(k + start == token, 1.0, 0.0)
    kept = jnp.dot(mask_row.astype(jnp.bfloat16), pick.astype(jnp.bfloat16), preferred_element_type=jnp.float32)
    channel = lax.broadcasted_iota(jnp.int32, (group, lanes), 0)
    lane = lax.broadcasted_iota(jnp.int32, (group, lanes), 1)
    spread_ref[...] = jnp.where(lane % group == channel, kept, 0.0)
    for copy in copies[1:3]:
        copy.wait()
    parts = []
    for half, copy in zip(halves, copies[3:5]):
        copy.wait()
        parts.append(normalise(pair_ref[half].reshape(tokens // 2, channels), gain_ref[...], bias_ref[...]))
    normed = jnp.concatenate(parts, axis=0)
    normed_ref[...] = normed
    copies[5].wait()
    parts = [all_w_ref[:, at : at + hidden] for at in range(0, 4 * hidden, hidden)]
    w = jnp.concatenate([jnp.where(my_col == 0, part[:, :ours], part[:, ours:]) for part in parts], axis=1).T
    w_ref[...] = w
    sides_ref[...] = project(normed, w, pair_ref.shape, quads)


def other_kernel(pair_ref, sides_ref, gain_ref, bias_ref, w_ref, *refs):
    *piece_refs, others_ref = refs
    my_quad, my_col = lax.axis_index("quad"), lax.axis_index("col")
    quads = sides_ref.shape[0]
    normed = normalise(pair_ref[...].reshape(-1, pair_ref.shape[2]), gain_ref[...], bias_ref[...])
    others_ref[...] = project(normed, w_ref[...], pair_ref.shape, quads)
    for step, piece_ref in enumerate(piece_refs):
        piece_ref[my_col] = sides_ref[my_quad ^ step]
        piece_ref[1 - my_col] = others_ref[my_quad ^ step]


def triangle_kernel(far_order, steps, cols, row_count, col_count, share, *refs):
    *got_refs, spread_ref, mask_ref, total_ref, left_ref, wide_ref = refs
    got_refs = {step: ref for step, ref in zip(steps, got_refs)}
    both = 2 * share
    group, lanes = spread_ref.shape
    length = mask_ref.shape[0]
    rows, quads, parts = length // row_count, len(steps), share // group
    whole, spare = row_count // 3, LANES - 2 * col_count
    rest = col_count - spare
    blocks = [[got_refs[row][col].astype(jnp.float32) for row in range(quads)] for col in range(cols)]

    def turned(picks):
        return jnp.concatenate([blocks[col][row][at : at + group] for col, row, at in picks], axis=0).T

    tail = turned([(col, row, whole * both + part * group) for col in range(cols) for part in range(parts) for row in range(quads)])

    def side(which, part):
        even, odd, third = [], [], []
        for col in range(cols):
            at = which * share + part * group
            block = turned([(col, row, t * both + at) for t in range(whole) for row in range(quads)])
            even.append(block[:col_count])
            odd.append(block[col_count : 2 * col_count])
            lane = (col * parts + part) * quads * group
            at = which * LANES // 2
            last = [tail[at + t * rest : at + (t + 1) * rest, lane : lane + quads * group] for t in range(whole)]
            third += [block[2 * col_count :], jnp.concatenate(last, axis=1)]
        tokens = [jnp.concatenate(pieces, axis=0) for pieces in (even, odd, third)]
        return jnp.concatenate(tokens, axis=1) * mask_ref[...]

    def placed(pieces):
        return jnp.concatenate([jnp.zeros((piece, lanes), jnp.bfloat16) if isinstance(piece, int) else piece for piece in pieces], axis=0)

    contract = (((1,), (1,)), ((), ()))
    lane_block = lax.broadcasted_iota(jnp.int32, (group, LANES), 1) // rest
    mains, lasts = [], []
    for part in range(parts):
        left_ref[part] = side(0, part)
        right = side(1, part).astype(jnp.bfloat16)
        for row in range(rows):
            for t in range(0, whole, 2):
                pair = []
                for at in (row * row_count, row * row_count + 2):
                    picks = [at + 2 * t, at + 2 * t + 1, row * row_count + 2 * whole + t + len(pair)]
                    copies = [jnp.broadcast_to(left_ref[part, i : i + 1, :], (group, lanes)) for i in picks]
                    pair.append(jnp.concatenate([copy * spread_ref[...] for copy in copies], axis=1))
                at = (row * whole + t) * group
                wide_ref[part, at : at + 2 * group, :] = jnp.concatenate(pair, axis=0).astype(jnp.bfloat16)
        ours = [right[col * col_count : (col + 1) * col_count] for col in range(cols)]
        weights = [
            placed([p for mine in ours for p in (mine, LANES - col_count)]),
            placed([p for mine in ours for p in (col_count, mine, spare)]),
            placed([p for mine in ours for p in (2 * col_count, mine[:spare])]),
        ]
        weights = jnp.concatenate(weights, axis=1)
        mains.append(lax.dot_general(wide_ref[part], weights, contract, preferred_element_type=jnp.float32))
        gap = LANES // parts
        pieces = [[gap * part] + [mine[spare:]] * whole + [LANES - gap * (part + 1)] for mine in ours]
        weights = placed([p for piece in pieces for p in piece if not isinstance(p, int) or p])
        lasts.append(lax.dot_general(wide_ref[part, :, 2 * lanes :], weights, contract, preferred_element_type=jnp.float32))
    for target, device in enumerate(far_order):
        row, col = divmod(device, cols)
        spots = [(row * whole + t) * group for t in range(whole)]
        tiles = [main[at : at + group, col * LANES : (col + 1) * LANES] for at in spots for main in mains]
        last = [part[at : at + group, col * LANES : (col + 1) * LANES] for part in lasts for at in spots]
        tile = last[0]
        for n in range(1, len(last)):
            tile = jnp.where(lane_block >= n, last[n], tile)
        tiles.append(tile)
        total_ref[target] = jnp.concatenate(tiles, axis=0).astype(jnp.bfloat16)


def gate_kernel(normed_ref, w_ref, gain_ref, bias_ref, gate_ref, gain_out_ref, bias_out_ref):
    gate_ref[...] = sigmoid(jnp.dot(normed_ref[...], w_ref[...], preferred_element_type=jnp.float32))
    gain_out_ref[...] = column(gain_ref[...])
    bias_out_ref[...] = column(bias_ref[...])


def output_kernel(far_order, near_order, total_ref, gate_ref, gain_ref, bias_ref, w_ref, out_ref):
    tokens = gate_ref.shape[0]
    hidden = w_ref.shape[0]
    near = len(near_order)
    share = hidden // near
    blocks = []
    for index in near_order:
        parts = [total_ref[source].astype(jnp.float32) for source, device in enumerate(far_order) if device % near == index]
        blocks.append(unpack(sum(parts[1:], parts[0]), share))
    total = jnp.concatenate(blocks, axis=0)
    normed = layer_norm(total, gain_ref[...], bias_ref[...], 0).astype(jnp.bfloat16)
    output = lax.dot_general(normed, w_ref[...], (((0,), (0,)), ((), ())), preferred_element_type=jnp.float32)
    output = restore(output, out_ref.shape[0], out_ref.shape[1])
    out_ref[...] = (gate_ref[...] * output).astype(jnp.bfloat16).reshape(out_ref.shape)


def per_device(rows, cols, halves, pair, token_mask, gain_in, bias_in, w_in, w_gate, gain_out, bias_out, w_out):
    row_count, col_count, channels = pair.shape
    hidden = w_out.shape[0]
    devices = rows * cols
    near = devices // halves
    quads = rows // halves
    far_order = []
    for col in reversed(range(cols)):
        ahead = list(range(quads)) if col else list(range(1, quads)) + [0]
        behind = [0] + list(reversed(range(1, quads))) if col else list(reversed(range(quads)))
        for quad, other in zip(ahead, behind):
            far_order += [near + other * cols + col, quad * cols + col]
    share = hidden // near
    tokens = row_count * col_count
    length = rows * row_count
    depth = length // halves
    token_mask = token_mask.reshape(1, length)
    near_order = [quad * cols + col for col in range(cols) for quad in range(quads)]
    packed = 2 * share * tokens // LANES
    cost = pl.CostEstimate(flops=2 * tokens * channels * 4 * hidden, bytes_accessed=16 * tokens * channels, transcendentals=0)
    other_pair = lax.ppermute(pair, "col", [(i, (i + 1) % cols) for i in range(cols)])
    arguments = (pair, gain_in.reshape(1, channels), bias_in.reshape(1, channels), w_in, token_mask)
    sides, normed, spread, mask, *weights = pl.pallas_call(
        functools.partial(own_kernel, quads, cols),
        out_shape=(
            jax.ShapeDtypeStruct((quads, packed, LANES), jnp.bfloat16),
            jax.ShapeDtypeStruct((tokens, channels), jnp.bfloat16),
            jax.ShapeDtypeStruct((GROUP, GROUP * depth), jnp.float32),
            jax.ShapeDtypeStruct((length, 1), jnp.float32),
            jax.ShapeDtypeStruct((4 * hidden // cols, channels), jnp.bfloat16),
            jax.ShapeDtypeStruct((1, channels), jnp.float32),
            jax.ShapeDtypeStruct((1, channels), jnp.float32),
        ),
        in_specs=[HBM] * 5,
        out_specs=(VMEM,) * 7,
        scratch_shapes=[
            pltpu.VMEM(pair.shape, pair.dtype),
            pltpu.VMEM(w_in.shape, w_in.dtype),
            pltpu.VMEM((1, length), jnp.int32),
            pltpu.SemaphoreType.DMA((6,)),
        ],
        compiler_params=LIMIT,
        cost_estimate=cost,
    )(*(pltpu.with_memory_space_constraint(x, pltpu.HBM) for x in arguments))
    w_ours, gain_in, bias_in = weights
    pieces = pl.pallas_call(
        other_kernel,
        out_shape=[jax.ShapeDtypeStruct((cols, packed, LANES), jnp.bfloat16)] * quads,
        in_specs=[VMEM] * 5,
        out_specs=[VMEM] * quads,
        scratch_shapes=[pltpu.VMEM((quads, packed, LANES), jnp.bfloat16)],
        compiler_params=LIMIT,
        cost_estimate=cost,
    )(other_pair, sides, gain_in, bias_in, w_ours)
    steps = [3, 1, 2, 0]
    got = [lax.ppermute(pieces[step], "quad", [(i, i ^ step) for i in range(quads)]) if step else pieces[0] for step in steps]
    total = pl.pallas_call(
        functools.partial(triangle_kernel, far_order, steps, cols, row_count, col_count, share),
        out_shape=jax.ShapeDtypeStruct((devices, share * tokens // LANES, LANES), jnp.bfloat16),
        in_specs=[VMEM] * (quads + 2),
        out_specs=VMEM,
        scratch_shapes=[
            pltpu.VMEM((share // GROUP, length, GROUP * depth), jnp.float32),
            pltpu.VMEM((share // GROUP, length // 3 * GROUP, 3 * GROUP * depth), jnp.bfloat16),
        ],
        compiler_params=LIMIT,
    )(*got, spread, mask)
    gate, gain_out, bias_out = pl.pallas_call(
        gate_kernel,
        out_shape=(
            jax.ShapeDtypeStruct((tokens, channels), jnp.float32),
            jax.ShapeDtypeStruct((hidden, 1), jnp.float32),
            jax.ShapeDtypeStruct((hidden, 1), jnp.float32),
        ),
        in_specs=[VMEM] * 4,
        out_specs=(VMEM, VMEM, VMEM),
        compiler_params=LIMIT,
        cost_estimate=pl.CostEstimate(flops=2 * tokens * channels * channels, bytes_accessed=4 * tokens * channels, transcendentals=0),
    )(normed, w_gate, gain_out.reshape(1, hidden), bias_out.reshape(1, hidden))
    total = lax.all_to_all(total, ("half", "quad", "col"), split_axis=0, concat_axis=0, tiled=True, axis_index_groups=[far_order])
    return pl.pallas_call(
        functools.partial(output_kernel, far_order, near_order),
        out_shape=jax.ShapeDtypeStruct(pair.shape, jnp.bfloat16),
        in_specs=[VMEM] * 5,
        out_specs=VMEM,
        compiler_params=LIMIT,
    )(total, gate, gain_out, bias_out, w_out)


def plain_per_device(rows, cols, pair, token_mask, gain_in, bias_in, w_in, w_gate, gain_out, bias_out, w_out):
    row_count, col_count, channels = pair.shape
    hidden = w_out.shape[0]
    devices = rows * cols
    share = hidden // devices
    tokens = row_count * col_count
    row_start = lax.axis_index(("half", "quad")) * row_count
    col_start = lax.axis_index("col") * col_count
    mask_float = token_mask.astype(jnp.float32)
    mask_rows = lax.dynamic_slice_in_dim(mask_float, row_start, row_count)
    mask_cols = lax.dynamic_slice_in_dim(mask_float, col_start, col_count)
    pair_mask = (mask_rows[:, None] * mask_cols[None, :]).reshape(1, tokens)
    flat = pair.reshape(tokens, channels).astype(jnp.float32)
    normed = layer_norm(flat, gain_in, bias_in, -1).astype(jnp.bfloat16)
    projected = lax.dot_general(w_in, normed, (((0,), (1,)), ((), ())), preferred_element_type=jnp.float32)
    projected = projected.reshape(2, 2, hidden, tokens)
    sides = (pair_mask * jax.nn.sigmoid(projected[:, 0]) * projected[:, 1]).astype(jnp.bfloat16)
    sides = sides.reshape(2, devices, share, tokens).transpose(1, 0, 2, 3)
    gate = jax.nn.sigmoid(jnp.dot(normed, w_gate, preferred_element_type=jnp.float32))
    got = lax.all_to_all(sides, AXES, split_axis=0, concat_axis=0, tiled=True)
    got = got.reshape(rows, cols, 2, share, row_count, col_count).transpose(2, 3, 0, 4, 1, 5)
    got = got.reshape(2, share, rows * row_count, cols * col_count)
    total = jnp.einsum("cki,ckj->cij", got[0], got[1], preferred_element_type=jnp.float32).astype(jnp.bfloat16)
    total = total.reshape(share, rows, row_count, cols, col_count).transpose(1, 3, 0, 2, 4)
    total = total.reshape(devices, share, tokens)
    total = lax.all_to_all(total, AXES, split_axis=0, concat_axis=0, tiled=True)
    total = total.reshape(hidden, tokens).astype(jnp.float32)
    summed_norm = layer_norm(total, gain_out[:, None], bias_out[:, None], 0).astype(jnp.bfloat16)
    output = lax.dot_general(summed_norm, w_out, (((0,), (0,)), ((), ())), preferred_element_type=jnp.float32)
    return (gate * output).astype(jnp.bfloat16).reshape(row_count, col_count, channels)


def solution(mesh):
    rows, cols = mesh.shape["row"], mesh.shape["col"]
    halves = 2
    parts = (mesh.shape["groups"], halves, rows // halves, cols)
    finer = jax.sharding.Mesh(mesh.devices.reshape(parts), ("groups", "half", "quad", "col"))

    def per_shard(*args):
        near, hidden, length = rows * cols // halves, args[-1].shape[0], args[1].shape[0]
        row_count, col_count, _ = args[0].shape
        spare = LANES - 2 * col_count
        fits = hidden % (2 * GROUP * near) == 0 and cols == 2 and rows // halves == 4 and length <= LANES and row_count % 3 == 0
        fits = fits and 0 < spare < col_count and row_count // 3 * (col_count - spare) * 2 == LANES
        fits = fits and row_count // 3 * (rows // halves) * GROUP == LANES
        return per_device(rows, cols, halves, *args) if fits else plain_per_device(rows, cols, *args)

    tokens = P(("groups", "half", "quad"), "col", None)
    in_specs = (tokens, P("groups"), P(), P(), P(), P(), P(), P(), P())
    return jax.shard_map(per_shard, mesh=finer, in_specs=in_specs, out_specs=tokens, check_vma=False)
```

```python
import functools

import jax
import jax.numpy as jnp
from jax import lax
from jax.experimental import pallas as pl
from jax.experimental.pallas import tpu as pltpu
from jax.sharding import PartitionSpec as P

epsilon = 1e-05
LANES = 128
GROUP = 8
AXES = ("half", "quad", "col")
VMEM = pl.BlockSpec(memory_space=pltpu.VMEM)
HBM = pl.BlockSpec(memory_space=pltpu.HBM)
LIMIT = pltpu.CompilerParams(vmem_limit_bytes=32 * 1024 * 1024)


def sigmoid(x):
    return 0.5 * jnp.tanh(0.5 * x) + 0.5


def layer_norm(values, gain, bias, axis):
    mean = jnp.mean(values, axis=axis, keepdims=True)
    centred = values - mean
    variance = jnp.mean(centred * centred, axis=axis, keepdims=True)
    return centred * lax.rsqrt(variance + epsilon) * gain + bias


def column(row):
    n = row.shape[1]
    eye = lax.broadcasted_iota(jnp.int32, (n, n), 0) == lax.broadcasted_iota(jnp.int32, (n, n), 1)
    return jnp.sum(jnp.where(eye, row, 0.0), axis=1, keepdims=True)


def pack(x):
    rows, tokens = x.shape[-2:]
    whole, rest = divmod(tokens, LANES)
    blocks = [x[..., t * LANES : (t + 1) * LANES] for t in range(whole)]
    if rest:
        tail = x[..., whole * LANES :]
        blocks.append(jnp.concatenate([tail[..., : rows // 2, :], tail[..., rows // 2 :, :]], axis=-1))
    return jnp.concatenate(blocks, axis=-2)


def unpack(x, rows):
    whole, rest = divmod(x.shape[-2], rows)
    blocks = [x[..., t * rows : (t + 1) * rows, :] for t in range(whole)]
    if rest:
        tail = x[..., whole * rows :, :]
        blocks.append(jnp.concatenate([tail[..., : LANES // 2], tail[..., LANES // 2 :]], axis=-2))
    return jnp.concatenate(blocks, axis=-1)


def arrange(x):
    row_count, col_count, _ = x.shape
    whole, spare = row_count // 3, LANES - 2 * col_count
    blocks = []
    for t in range(whole):
        blocks += [x[2 * t], x[2 * t + 1], x[2 * whole + t, :spare]]
    return jnp.concatenate(blocks + [x[2 * whole + t, spare:] for t in range(whole)], axis=0)


def restore(x, row_count, col_count):
    whole, spare = row_count // 3, LANES - 2 * col_count
    rest = col_count - spare
    rows = []
    for t in range(whole):
        rows += [x[t * LANES : t * LANES + col_count], x[t * LANES + col_count : t * LANES + 2 * col_count]]
    for t in range(whole):
        tail = whole * LANES + t * rest
        rows += [x[t * LANES + 2 * col_count : (t + 1) * LANES], x[tail : tail + rest]]
    return jnp.concatenate(rows, axis=0)


def normalise(flat, gain, bias):
    return layer_norm(flat.astype(jnp.float32), gain, bias, -1).astype(jnp.bfloat16)


def project(normed, w, shape, quads):
    ours = w.shape[0] // 4
    tokens = normed.shape[0]
    projected = lax.dot_general(w, arrange(normed.reshape(shape)), (((1,), (1,)), ((), ())), preferred_element_type=jnp.float32)
    left = sigmoid(projected[:ours]) * projected[ours : 2 * ours]
    right = sigmoid(projected[2 * ours : 3 * ours]) * projected[3 * ours :]
    sides = jnp.concatenate([left.reshape(quads, -1, tokens), right.reshape(quads, -1, tokens)], axis=1)
    return pack(sides).astype(jnp.bfloat16)


def own_kernel(quads, cols, pair_hbm, gain_hbm, bias_hbm, w_hbm, mask_hbm, sides_ref, normed_ref, spread_ref, column_mask_ref, w_ref, gain_ref, bias_ref, pair_ref, all_w_ref, mask_ref, sems):
    moves = [(mask_hbm, mask_ref), (pair_hbm, pair_ref), (gain_hbm, gain_ref), (bias_hbm, bias_ref), (w_hbm, all_w_ref)]
    copies = [pltpu.make_async_copy(source, target, sems.at[n]) for n, (source, target) in enumerate(moves)]
    for copy in copies:
        copy.start()
    my_quad, my_col = lax.axis_index("quad"), lax.axis_index("col")
    row_count, _, channels = pair_ref.shape
    tokens = normed_ref.shape[0]
    hidden = all_w_ref.shape[1] // 4
    ours = hidden // cols
    group, lanes = spread_ref.shape
    copies[0].wait()
    mask_row = mask_ref[...].astype(jnp.float32)
    column_mask_ref[...] = column(mask_row)
    start = lax.axis_index("half") * (lanes // group)
    token = lax.broadcasted_iota(jnp.int32, (mask_row.shape[1], lanes), 0)
    lane = lax.broadcasted_iota(jnp.int32, (mask_row.shape[1], lanes), 1)
    whole = row_count // 3
    block, t, row = lane // LANES, lane // (quads * group) % whole, lane // group % quads
    k = (row ^ my_quad) * row_count + jnp.where(block < 2, 2 * t + block, 2 * whole + t)
    pick = jnp.where(k + start == token, 1.0, 0.0)
    kept = jnp.dot(mask_row.astype(jnp.bfloat16), pick.astype(jnp.bfloat16), preferred_element_type=jnp.float32)
    channel = lax.broadcasted_iota(jnp.int32, (group, lanes), 0)
    lane = lax.broadcasted_iota(jnp.int32, (group, lanes), 1)
    spread_ref[...] = jnp.where(lane % group == channel, kept, 0.0)
    for copy in copies[1:4]:
        copy.wait()
    normed = normalise(pair_ref[...].reshape(tokens, channels), gain_ref[...], bias_ref[...])
    normed_ref[...] = normed
    copies[4].wait()
    parts = [all_w_ref[:, at : at + hidden] for at in range(0, 4 * hidden, hidden)]
    w = jnp.concatenate([jnp.where(my_col == 0, part[:, :ours], part[:, ours:]) for part in parts], axis=1).T
    w_ref[...] = w
    sides_ref[...] = project(normed, w, pair_ref.shape, quads)


def other_kernel(pair_ref, sides_ref, gain_ref, bias_ref, w_ref, *refs):
    *piece_refs, others_ref = refs
    my_quad, my_col = lax.axis_index("quad"), lax.axis_index("col")
    quads = sides_ref.shape[0]
    normed = normalise(pair_ref[...].reshape(-1, pair_ref.shape[2]), gain_ref[...], bias_ref[...])
    others_ref[...] = project(normed, w_ref[...], pair_ref.shape, quads)
    for step, piece_ref in enumerate(piece_refs):
        piece_ref[my_col] = sides_ref[my_quad ^ step]
        piece_ref[1 - my_col] = others_ref[my_quad ^ step]


def triangle_kernel(far_order, steps, cols, row_count, col_count, share, *refs):
    *got_refs, spread_ref, mask_ref, total_ref, left_ref, wide_ref = refs
    got_refs = {step: ref for step, ref in zip(steps, got_refs)}
    both = 2 * share
    group, lanes = spread_ref.shape
    length = mask_ref.shape[0]
    rows, quads, parts = length // row_count, len(steps), share // group
    whole, spare = row_count // 3, LANES - 2 * col_count
    rest = col_count - spare
    blocks = [[got_refs[row][col].astype(jnp.float32) for row in range(quads)] for col in range(cols)]

    def turned(picks):
        return jnp.concatenate([blocks[col][row][at : at + group] for col, row, at in picks], axis=0).T

    tail = turned([(col, row, whole * both + part * group) for col in range(cols) for part in range(parts) for row in range(quads)])

    def side(which, part):
        even, odd, third = [], [], []
        for col in range(cols):
            at = which * share + part * group
            block = turned([(col, row, t * both + at) for t in range(whole) for row in range(quads)])
            even.append(block[:col_count])
            odd.append(block[col_count : 2 * col_count])
            lane = (col * parts + part) * quads * group
            at = which * LANES // 2
            last = [tail[at + t * rest : at + (t + 1) * rest, lane : lane + quads * group] for t in range(whole)]
            third += [block[2 * col_count :], jnp.concatenate(last, axis=1)]
        tokens = [jnp.concatenate(pieces, axis=0) for pieces in (even, odd, third)]
        return jnp.concatenate(tokens, axis=1) * mask_ref[...]

    def placed(pieces):
        return jnp.concatenate([jnp.zeros((piece, lanes), jnp.bfloat16) if isinstance(piece, int) else piece for piece in pieces], axis=0)

    contract = (((1,), (1,)), ((), ()))
    lane_block = lax.broadcasted_iota(jnp.int32, (group, LANES), 1) // rest
    gap = LANES // parts
    weights = []
    for part in range(parts):
        right = side(1, part).astype(jnp.bfloat16)
        ours = [right[col * col_count : (col + 1) * col_count] for col in range(cols)]
        main = [
            placed([p for mine in ours for p in (mine, LANES - col_count)]),
            placed([p for mine in ours for p in (col_count, mine, spare)]),
            placed([p for mine in ours for p in (2 * col_count, mine[:spare])]),
        ]
        pieces = [[gap * part] + [mine[spare:]] * whole + [LANES - gap * (part + 1)] for mine in ours]
        last = placed([p for piece in pieces for p in piece if not isinstance(p, int) or p])
        weights.append((jnp.concatenate(main, axis=1), last))
    for part in range(parts):
        left_ref[part] = side(0, part)
    for row in range(rows):
        for part in range(parts):
            for t in range(0, whole, 2):
                pair = []
                for at in (row * row_count, row * row_count + 2):
                    picks = [at + 2 * t, at + 2 * t + 1, row * row_count + 2 * whole + t + len(pair)]
                    copies = [jnp.broadcast_to(left_ref[part, i : i + 1, :], (group, lanes)) for i in picks]
                    pair.append(jnp.concatenate([copy * spread_ref[...] for copy in copies], axis=1))
                at = (row * whole + t) * group
                wide_ref[part, at : at + 2 * group, :] = jnp.concatenate(pair, axis=0).astype(jnp.bfloat16)
    mains, lasts = [], []
    for part, (main, last) in enumerate(weights):
        mains.append(lax.dot_general(wide_ref[part], main, contract, preferred_element_type=jnp.float32))
        lasts.append(lax.dot_general(wide_ref[part, :, 2 * lanes :], last, contract, preferred_element_type=jnp.float32))
    for target, device in enumerate(far_order):
        row, col = divmod(device, cols)
        spots = [(row * whole + t) * group for t in range(whole)]
        tiles = [main[at : at + group, col * LANES : (col + 1) * LANES] for at in spots for main in mains]
        last = [part[at : at + group, col * LANES : (col + 1) * LANES] for part in lasts for at in spots]
        tile = last[0]
        for n in range(1, len(last)):
            tile = jnp.where(lane_block >= n, last[n], tile)
        tiles.append(tile)
        total_ref[target] = jnp.concatenate(tiles, axis=0).astype(jnp.bfloat16)


def gate_kernel(normed_ref, w_ref, gain_ref, bias_ref, gate_ref, gain_out_ref, bias_out_ref):
    gate_ref[...] = sigmoid(jnp.dot(normed_ref[...], w_ref[...], preferred_element_type=jnp.float32))
    gain_out_ref[...] = column(gain_ref[...])
    bias_out_ref[...] = column(bias_ref[...])


def output_kernel(far_order, near_order, total_ref, gate_ref, gain_ref, bias_ref, w_ref, out_ref):
    tokens = gate_ref.shape[0]
    hidden = w_ref.shape[0]
    near = len(near_order)
    share = hidden // near
    blocks = []
    for index in near_order:
        parts = [total_ref[source].astype(jnp.float32) for source, device in enumerate(far_order) if device % near == index]
        blocks.append(unpack(sum(parts[1:], parts[0]), share))
    total = jnp.concatenate(blocks, axis=0)
    normed = layer_norm(total, gain_ref[...], bias_ref[...], 0).astype(jnp.bfloat16)
    output = lax.dot_general(normed, w_ref[...], (((0,), (0,)), ((), ())), preferred_element_type=jnp.float32)
    output = restore(output, out_ref.shape[0], out_ref.shape[1])
    out_ref[...] = (gate_ref[...] * output).astype(jnp.bfloat16).reshape(out_ref.shape)


def per_device(rows, cols, halves, pair, token_mask, gain_in, bias_in, w_in, w_gate, gain_out, bias_out, w_out):
    row_count, col_count, channels = pair.shape
    hidden = w_out.shape[0]
    devices = rows * cols
    near = devices // halves
    quads = rows // halves
    far_order = []
    for col in reversed(range(cols)):
        ahead = list(range(quads)) if col else list(range(1, quads)) + [0]
        behind = [0] + list(reversed(range(1, quads))) if col else list(reversed(range(quads)))
        for quad, other in zip(ahead, behind):
            far_order += [near + other * cols + col, quad * cols + col]
    share = hidden // near
    tokens = row_count * col_count
    length = rows * row_count
    depth = length // halves
    token_mask = token_mask.reshape(1, length)
    near_order = [quad * cols + col for col in range(cols) for quad in range(quads)]
    packed = 2 * share * tokens // LANES
    cost = pl.CostEstimate(flops=2 * tokens * channels * 4 * hidden, bytes_accessed=16 * tokens * channels, transcendentals=0)
    other_pair = lax.ppermute(pair, "col", [(i, (i + 1) % cols) for i in range(cols)])
    arguments = (pair, gain_in.reshape(1, channels), bias_in.reshape(1, channels), w_in, token_mask)
    sides, normed, spread, mask, *weights = pl.pallas_call(
        functools.partial(own_kernel, quads, cols),
        out_shape=(
            jax.ShapeDtypeStruct((quads, packed, LANES), jnp.bfloat16),
            jax.ShapeDtypeStruct((tokens, channels), jnp.bfloat16),
            jax.ShapeDtypeStruct((GROUP, GROUP * depth), jnp.float32),
            jax.ShapeDtypeStruct((length, 1), jnp.float32),
            jax.ShapeDtypeStruct((4 * hidden // cols, channels), jnp.bfloat16),
            jax.ShapeDtypeStruct((1, channels), jnp.float32),
            jax.ShapeDtypeStruct((1, channels), jnp.float32),
        ),
        in_specs=[HBM] * 5,
        out_specs=(VMEM,) * 7,
        scratch_shapes=[
            pltpu.VMEM(pair.shape, pair.dtype),
            pltpu.VMEM(w_in.shape, w_in.dtype),
            pltpu.VMEM((1, length), jnp.int32),
            pltpu.SemaphoreType.DMA((5,)),
        ],
        compiler_params=LIMIT,
        cost_estimate=cost,
    )(*(pltpu.with_memory_space_constraint(x, pltpu.HBM) for x in arguments))
    w_ours, gain_in, bias_in = weights
    pieces = pl.pallas_call(
        other_kernel,
        out_shape=[jax.ShapeDtypeStruct((cols, packed, LANES), jnp.bfloat16)] * quads,
        in_specs=[VMEM] * 5,
        out_specs=[VMEM] * quads,
        scratch_shapes=[pltpu.VMEM((quads, packed, LANES), jnp.bfloat16)],
        compiler_params=LIMIT,
        cost_estimate=cost,
    )(other_pair, sides, gain_in, bias_in, w_ours)
    steps = [3, 1, 2, 0]
    got = [lax.ppermute(pieces[step], "quad", [(i, i ^ step) for i in range(quads)]) if step else pieces[0] for step in steps]
    total = pl.pallas_call(
        functools.partial(triangle_kernel, far_order, steps, cols, row_count, col_count, share),
        out_shape=jax.ShapeDtypeStruct((devices, share * tokens // LANES, LANES), jnp.bfloat16),
        in_specs=[VMEM] * (quads + 2),
        out_specs=VMEM,
        scratch_shapes=[
            pltpu.VMEM((share // GROUP, length, GROUP * depth), jnp.float32),
            pltpu.VMEM((share // GROUP, length // 3 * GROUP, 3 * GROUP * depth), jnp.bfloat16),
        ],
        compiler_params=LIMIT,
    )(*got, spread, mask)
    gate, gain_out, bias_out = pl.pallas_call(
        gate_kernel,
        out_shape=(
            jax.ShapeDtypeStruct((tokens, channels), jnp.float32),
            jax.ShapeDtypeStruct((hidden, 1), jnp.float32),
            jax.ShapeDtypeStruct((hidden, 1), jnp.float32),
        ),
        in_specs=[VMEM] * 4,
        out_specs=(VMEM, VMEM, VMEM),
        compiler_params=LIMIT,
        cost_estimate=pl.CostEstimate(flops=2 * tokens * channels * channels, bytes_accessed=4 * tokens * channels, transcendentals=0),
    )(normed, w_gate, gain_out.reshape(1, hidden), bias_out.reshape(1, hidden))
    total = lax.all_to_all(total, ("half", "quad", "col"), split_axis=0, concat_axis=0, tiled=True, axis_index_groups=[far_order])
    return pl.pallas_call(
        functools.partial(output_kernel, far_order, near_order),
        out_shape=jax.ShapeDtypeStruct(pair.shape, jnp.bfloat16),
        in_specs=[VMEM] * 5,
        out_specs=VMEM,
        compiler_params=LIMIT,
    )(total, gate, gain_out, bias_out, w_out)


def plain_per_device(rows, cols, pair, token_mask, gain_in, bias_in, w_in, w_gate, gain_out, bias_out, w_out):
    row_count, col_count, channels = pair.shape
    hidden = w_out.shape[0]
    devices = rows * cols
    share = hidden // devices
    tokens = row_count * col_count
    row_start = lax.axis_index(("half", "quad")) * row_count
    col_start = lax.axis_index("col") * col_count
    mask_float = token_mask.astype(jnp.float32)
    mask_rows = lax.dynamic_slice_in_dim(mask_float, row_start, row_count)
    mask_cols = lax.dynamic_slice_in_dim(mask_float, col_start, col_count)
    pair_mask = (mask_rows[:, None] * mask_cols[None, :]).reshape(1, tokens)
    flat = pair.reshape(tokens, channels).astype(jnp.float32)
    normed = layer_norm(flat, gain_in, bias_in, -1).astype(jnp.bfloat16)
    projected = lax.dot_general(w_in, normed, (((0,), (1,)), ((), ())), preferred_element_type=jnp.float32)
    projected = projected.reshape(2, 2, hidden, tokens)
    sides = (pair_mask * jax.nn.sigmoid(projected[:, 0]) * projected[:, 1]).astype(jnp.bfloat16)
    sides = sides.reshape(2, devices, share, tokens).transpose(1, 0, 2, 3)
    gate = jax.nn.sigmoid(jnp.dot(normed, w_gate, preferred_element_type=jnp.float32))
    got = lax.all_to_all(sides, AXES, split_axis=0, concat_axis=0, tiled=True)
    got = got.reshape(rows, cols, 2, share, row_count, col_count).transpose(2, 3, 0, 4, 1, 5)
    got = got.reshape(2, share, rows * row_count, cols * col_count)
    total = jnp.einsum("cki,ckj->cij", got[0], got[1], preferred_element_type=jnp.float32).astype(jnp.bfloat16)
    total = total.reshape(share, rows, row_count, cols, col_count).transpose(1, 3, 0, 2, 4)
    total = total.reshape(devices, share, tokens)
    total = lax.all_to_all(total, AXES, split_axis=0, concat_axis=0, tiled=True)
    total = total.reshape(hidden, tokens).astype(jnp.float32)
    summed_norm = layer_norm(total, gain_out[:, None], bias_out[:, None], 0).astype(jnp.bfloat16)
    output = lax.dot_general(summed_norm, w_out, (((0,), (0,)), ((), ())), preferred_element_type=jnp.float32)
    return (gate * output).astype(jnp.bfloat16).reshape(row_count, col_count, channels)


def solution(mesh):
    rows, cols = mesh.shape["row"], mesh.shape["col"]
    halves = 2
    parts = (mesh.shape["groups"], halves, rows // halves, cols)
    finer = jax.sharding.Mesh(mesh.devices.reshape(parts), ("groups", "half", "quad", "col"))

    def per_shard(*args):
        near, hidden, length = rows * cols // halves, args[-1].shape[0], args[1].shape[0]
        row_count, col_count, _ = args[0].shape
        spare = LANES - 2 * col_count
        fits = hidden % (2 * GROUP * near) == 0 and cols == 2 and rows // halves == 4 and length <= LANES and row_count % 3 == 0
        fits = fits and 0 < spare < col_count and row_count // 3 * (col_count - spare) * 2 == LANES
        fits = fits and row_count // 3 * (rows // halves) * GROUP == LANES
        return per_device(rows, cols, halves, *args) if fits else plain_per_device(rows, cols, *args)

    tokens = P(("groups", "half", "quad"), "col", None)
    in_specs = (tokens, P("groups"), P(), P(), P(), P(), P(), P(), P())
    return jax.shard_map(per_shard, mesh=finer, in_specs=in_specs, out_specs=tokens, check_vma=False)
```

```python
import functools

import jax
import jax.numpy as jnp
from jax import lax
from jax.experimental import pallas as pl
from jax.experimental.pallas import tpu as pltpu
from jax.sharding import PartitionSpec as P

epsilon = 1e-05
LANES = 128
GROUP = 8
AXES = ("half", "quad", "col")
VMEM = pl.BlockSpec(memory_space=pltpu.VMEM)
HBM = pl.BlockSpec(memory_space=pltpu.HBM)
LIMIT = pltpu.CompilerParams(vmem_limit_bytes=32 * 1024 * 1024)


def sigmoid(x):
    return 0.5 * jnp.tanh(0.5 * x) + 0.5


def layer_norm(values, gain, bias, axis):
    mean = jnp.mean(values, axis=axis, keepdims=True)
    centred = values - mean
    variance = jnp.mean(centred * centred, axis=axis, keepdims=True)
    return centred * lax.rsqrt(variance + epsilon) * gain + bias


def column(row):
    n = row.shape[1]
    eye = lax.broadcasted_iota(jnp.int32, (n, n), 0) == lax.broadcasted_iota(jnp.int32, (n, n), 1)
    return jnp.sum(jnp.where(eye, row, 0.0), axis=1, keepdims=True)


def pack(x):
    rows, tokens = x.shape[-2:]
    whole, rest = divmod(tokens, LANES)
    blocks = [x[..., t * LANES : (t + 1) * LANES] for t in range(whole)]
    if rest:
        tail = x[..., whole * LANES :]
        blocks.append(jnp.concatenate([tail[..., : rows // 2, :], tail[..., rows // 2 :, :]], axis=-1))
    return jnp.concatenate(blocks, axis=-2)


def unpack(x, rows):
    whole, rest = divmod(x.shape[-2], rows)
    blocks = [x[..., t * rows : (t + 1) * rows, :] for t in range(whole)]
    if rest:
        tail = x[..., whole * rows :, :]
        blocks.append(jnp.concatenate([tail[..., : LANES // 2], tail[..., LANES // 2 :]], axis=-2))
    return jnp.concatenate(blocks, axis=-1)


def arrange(x):
    row_count, col_count, _ = x.shape
    whole, spare = row_count // 3, LANES - 2 * col_count
    blocks = []
    for t in range(whole):
        blocks += [x[2 * t], x[2 * t + 1], x[2 * whole + t, :spare]]
    return jnp.concatenate(blocks + [x[2 * whole + t, spare:] for t in range(whole)], axis=0)


def restore(x, row_count, col_count):
    whole, spare = row_count // 3, LANES - 2 * col_count
    rest = col_count - spare
    rows = []
    for t in range(whole):
        rows += [x[t * LANES : t * LANES + col_count], x[t * LANES + col_count : t * LANES + 2 * col_count]]
    for t in range(whole):
        tail = whole * LANES + t * rest
        rows += [x[t * LANES + 2 * col_count : (t + 1) * LANES], x[tail : tail + rest]]
    return jnp.concatenate(rows, axis=0)


def normalise(flat, gain, bias):
    return layer_norm(flat.astype(jnp.float32), gain, bias, -1).astype(jnp.bfloat16)


def project(normed, w, shape, quads):
    ours = w.shape[0] // 4
    tokens = normed.shape[0]
    projected = lax.dot_general(w, arrange(normed.reshape(shape)), (((1,), (1,)), ((), ())), preferred_element_type=jnp.float32)
    left = sigmoid(projected[:ours]) * projected[ours : 2 * ours]
    right = sigmoid(projected[2 * ours : 3 * ours]) * projected[3 * ours :]
    sides = jnp.concatenate([left.reshape(quads, -1, tokens), right.reshape(quads, -1, tokens)], axis=1)
    return pack(sides).astype(jnp.bfloat16)


def my_steps(steps):
    my_col = lax.axis_index("col")
    return [jnp.where(my_col == 0, first, second) for first, second in steps]


def own_kernel(steps, quads, cols, pair_hbm, gain_hbm, bias_hbm, w_hbm, mask_hbm, sides_ref, normed_ref, spread_ref, column_mask_ref, w_ref, gain_ref, bias_ref, pair_ref, all_w_ref, mask_ref, sems):
    moves = [(mask_hbm, mask_ref), (pair_hbm, pair_ref), (gain_hbm, gain_ref), (bias_hbm, bias_ref), (w_hbm, all_w_ref)]
    copies = [pltpu.make_async_copy(source, target, sems.at[n]) for n, (source, target) in enumerate(moves)]
    for copy in copies:
        copy.start()
    my_quad, my_col = lax.axis_index("quad"), lax.axis_index("col")
    row_count, _, channels = pair_ref.shape
    tokens = normed_ref.shape[0]
    hidden = all_w_ref.shape[1] // 4
    ours = hidden // cols
    group, lanes = spread_ref.shape
    copies[0].wait()
    mask_row = mask_ref[...].astype(jnp.float32)
    column_mask_ref[...] = column(mask_row)
    start = lax.axis_index("half") * (lanes // group)
    token = lax.broadcasted_iota(jnp.int32, (mask_row.shape[1], lanes), 0)
    lane = lax.broadcasted_iota(jnp.int32, (mask_row.shape[1], lanes), 1)
    whole = row_count // 3
    block, t, slot = lane // LANES, lane // (quads * group) % whole, lane // group % quads
    row = my_quad ^ sum(jnp.where(slot == n, step, 0) for n, step in enumerate(my_steps(steps)))
    k = row * row_count + jnp.where(block < 2, 2 * t + block, 2 * whole + t)
    pick = jnp.where(k + start == token, 1.0, 0.0)
    kept = jnp.dot(mask_row.astype(jnp.bfloat16), pick.astype(jnp.bfloat16), preferred_element_type=jnp.float32)
    channel = lax.broadcasted_iota(jnp.int32, (group, lanes), 0)
    lane = lax.broadcasted_iota(jnp.int32, (group, lanes), 1)
    spread_ref[...] = jnp.where(lane % group == channel, kept, 0.0)
    for copy in copies[1:4]:
        copy.wait()
    normed = normalise(pair_ref[...].reshape(tokens, channels), gain_ref[...], bias_ref[...])
    normed_ref[...] = normed
    copies[4].wait()
    parts = [all_w_ref[:, at : at + hidden] for at in range(0, 4 * hidden, hidden)]
    w = jnp.concatenate([jnp.where(my_col == 0, part[:, :ours], part[:, ours:]) for part in parts], axis=1).T
    w_ref[...] = w
    sides_ref[...] = project(normed, w, pair_ref.shape, quads)


def other_kernel(steps, pair_ref, sides_ref, gain_ref, bias_ref, w_ref, *refs):
    *piece_refs, others_ref = refs
    my_quad, my_col = lax.axis_index("quad"), lax.axis_index("col")
    quads = sides_ref.shape[0]
    normed = normalise(pair_ref[...].reshape(-1, pair_ref.shape[2]), gain_ref[...], bias_ref[...])
    others_ref[...] = project(normed, w_ref[...], pair_ref.shape, quads)
    for step, piece_ref in zip(my_steps(steps), piece_refs):
        piece_ref[my_col] = sides_ref[my_quad ^ step]
        piece_ref[1 - my_col] = others_ref[my_quad ^ step]


def triangle_kernel(far_order, cols, row_count, col_count, share, *refs):
    *got_refs, spread_ref, mask_ref, total_ref, left_ref, wide_ref = refs
    both = 2 * share
    group, lanes = spread_ref.shape
    length = mask_ref.shape[0]
    rows, quads, parts = length // row_count, len(got_refs), share // group
    whole, spare = row_count // 3, LANES - 2 * col_count
    rest = col_count - spare
    blocks = [[got_refs[row][col].astype(jnp.float32) for row in range(quads)] for col in range(cols)]

    def turned(picks):
        return jnp.concatenate([blocks[col][row][at : at + group] for col, row, at in picks], axis=0).T

    tail = turned([(col, row, whole * both + part * group) for col in range(cols) for part in range(parts) for row in range(quads)])

    def side(which, part):
        even, odd, third = [], [], []
        for col in range(cols):
            at = which * share + part * group
            block = turned([(col, row, t * both + at) for t in range(whole) for row in range(quads)])
            even.append(block[:col_count])
            odd.append(block[col_count : 2 * col_count])
            lane = (col * parts + part) * quads * group
            at = which * LANES // 2
            last = [tail[at + t * rest : at + (t + 1) * rest, lane : lane + quads * group] for t in range(whole)]
            third += [block[2 * col_count :], jnp.concatenate(last, axis=1)]
        tokens = [jnp.concatenate(pieces, axis=0) for pieces in (even, odd, third)]
        return jnp.concatenate(tokens, axis=1) * mask_ref[...]

    def placed(pieces):
        return jnp.concatenate([jnp.zeros((piece, lanes), jnp.bfloat16) if isinstance(piece, int) else piece for piece in pieces], axis=0)

    contract = (((1,), (1,)), ((), ()))
    lane_block = lax.broadcasted_iota(jnp.int32, (group, LANES), 1) // rest
    mains, lasts = [], []
    for part in range(parts):
        left_ref[part] = side(0, part)
        right = side(1, part).astype(jnp.bfloat16)
        for row in range(rows):
            for t in range(0, whole, 2):
                pair = []
                for at in (row * row_count, row * row_count + 2):
                    picks = [at + 2 * t, at + 2 * t + 1, row * row_count + 2 * whole + t + len(pair)]
                    copies = [jnp.broadcast_to(left_ref[part, i : i + 1, :], (group, lanes)) for i in picks]
                    pair.append(jnp.concatenate([copy * spread_ref[...] for copy in copies], axis=1))
                at = (row * whole + t) * group
                wide_ref[part, at : at + 2 * group, :] = jnp.concatenate(pair, axis=0).astype(jnp.bfloat16)
        ours = [right[col * col_count : (col + 1) * col_count] for col in range(cols)]
        weights = [
            placed([p for mine in ours for p in (mine, LANES - col_count)]),
            placed([p for mine in ours for p in (col_count, mine, spare)]),
            placed([p for mine in ours for p in (2 * col_count, mine[:spare])]),
        ]
        weights = jnp.concatenate(weights, axis=1)
        mains.append(lax.dot_general(wide_ref[part], weights, contract, preferred_element_type=jnp.float32))
        gap = LANES // parts
        pieces = [[gap * part] + [mine[spare:]] * whole + [LANES - gap * (part + 1)] for mine in ours]
        weights = placed([p for piece in pieces for p in piece if not isinstance(p, int) or p])
        lasts.append(lax.dot_general(wide_ref[part, :, 2 * lanes :], weights, contract, preferred_element_type=jnp.float32))
    for target, device in enumerate(far_order):
        row, col = divmod(device, cols)
        spots = [(row * whole + t) * group for t in range(whole)]
        tiles = [main[at : at + group, col * LANES : (col + 1) * LANES] for at in spots for main in mains]
        last = [part[at : at + group, col * LANES : (col + 1) * LANES] for part in lasts for at in spots]
        tile = last[0]
        for n in range(1, len(last)):
            tile = jnp.where(lane_block >= n, last[n], tile)
        tiles.append(tile)
        total_ref[target] = jnp.concatenate(tiles, axis=0).astype(jnp.bfloat16)


def gate_kernel(normed_ref, w_ref, gain_ref, bias_ref, gate_ref, gain_out_ref, bias_out_ref):
    gate_ref[...] = sigmoid(jnp.dot(normed_ref[...], w_ref[...], preferred_element_type=jnp.float32))
    gain_out_ref[...] = column(gain_ref[...])
    bias_out_ref[...] = column(bias_ref[...])


def output_kernel(far_order, near_order, total_ref, gate_ref, gain_ref, bias_ref, w_ref, out_ref):
    tokens = gate_ref.shape[0]
    hidden = w_ref.shape[0]
    near = len(near_order)
    share = hidden // near
    blocks = []
    for index in near_order:
        parts = [total_ref[source].astype(jnp.float32) for source, device in enumerate(far_order) if device % near == index]
        blocks.append(unpack(sum(parts[1:], parts[0]), share))
    total = jnp.concatenate(blocks, axis=0)
    normed = layer_norm(total, gain_ref[...], bias_ref[...], 0).astype(jnp.bfloat16)
    output = lax.dot_general(normed, w_ref[...], (((0,), (0,)), ((), ())), preferred_element_type=jnp.float32)
    output = restore(output, out_ref.shape[0], out_ref.shape[1])
    out_ref[...] = (gate_ref[...] * output).astype(jnp.bfloat16).reshape(out_ref.shape)


def per_device(rows, cols, halves, pair, token_mask, gain_in, bias_in, w_in, w_gate, gain_out, bias_out, w_out):
    row_count, col_count, channels = pair.shape
    hidden = w_out.shape[0]
    devices = rows * cols
    near = devices // halves
    quads = rows // halves
    far_order = []
    for col in reversed(range(cols)):
        ahead = list(range(quads)) if col else list(range(1, quads)) + [0]
        behind = [0] + list(reversed(range(1, quads))) if col else list(reversed(range(quads)))
        for quad, other in zip(ahead, behind):
            far_order += [near + other * cols + col, quad * cols + col]
    share = hidden // near
    tokens = row_count * col_count
    length = rows * row_count
    depth = length // halves
    token_mask = token_mask.reshape(1, length)
    near_order = [quad * cols + col for col in range(cols) for quad in range(quads)]
    packed = 2 * share * tokens // LANES
    cost = pl.CostEstimate(flops=2 * tokens * channels * 4 * hidden, bytes_accessed=16 * tokens * channels, transcendentals=0)
    steps = [(3, 3), (1, 2), (2, 1), (0, 0)]
    other_pair = lax.ppermute(pair, "col", [(i, (i + 1) % cols) for i in range(cols)])
    arguments = (pair, gain_in.reshape(1, channels), bias_in.reshape(1, channels), w_in, token_mask)
    sides, normed, spread, mask, *weights = pl.pallas_call(
        functools.partial(own_kernel, steps, quads, cols),
        out_shape=(
            jax.ShapeDtypeStruct((quads, packed, LANES), jnp.bfloat16),
            jax.ShapeDtypeStruct((tokens, channels), jnp.bfloat16),
            jax.ShapeDtypeStruct((GROUP, GROUP * depth), jnp.float32),
            jax.ShapeDtypeStruct((length, 1), jnp.float32),
            jax.ShapeDtypeStruct((4 * hidden // cols, channels), jnp.bfloat16),
            jax.ShapeDtypeStruct((1, channels), jnp.float32),
            jax.ShapeDtypeStruct((1, channels), jnp.float32),
        ),
        in_specs=[HBM] * 5,
        out_specs=(VMEM,) * 7,
        scratch_shapes=[
            pltpu.VMEM(pair.shape, pair.dtype),
            pltpu.VMEM(w_in.shape, w_in.dtype),
            pltpu.VMEM((1, length), jnp.int32),
            pltpu.SemaphoreType.DMA((5,)),
        ],
        compiler_params=LIMIT,
        cost_estimate=cost,
    )(*(pltpu.with_memory_space_constraint(x, pltpu.HBM) for x in arguments))
    w_ours, gain_in, bias_in = weights
    pieces = pl.pallas_call(
        functools.partial(other_kernel, steps),
        out_shape=[jax.ShapeDtypeStruct((cols, packed, LANES), jnp.bfloat16)] * quads,
        in_specs=[VMEM] * 5,
        out_specs=[VMEM] * quads,
        scratch_shapes=[pltpu.VMEM((quads, packed, LANES), jnp.bfloat16)],
        compiler_params=LIMIT,
        cost_estimate=cost,
    )(other_pair, sides, gain_in, bias_in, w_ours)
    got = []
    for piece, step in zip(pieces, steps):
        moves = [(quad * cols + col, (quad ^ step[col]) * cols + col) for quad in range(quads) for col in range(cols)]
        got.append(lax.ppermute(piece, ("quad", "col"), moves) if any(step) else piece)
    total = pl.pallas_call(
        functools.partial(triangle_kernel, far_order, cols, row_count, col_count, share),
        out_shape=jax.ShapeDtypeStruct((devices, share * tokens // LANES, LANES), jnp.bfloat16),
        in_specs=[VMEM] * (quads + 2),
        out_specs=VMEM,
        scratch_shapes=[
            pltpu.VMEM((share // GROUP, length, GROUP * depth), jnp.float32),
            pltpu.VMEM((share // GROUP, length // 3 * GROUP, 3 * GROUP * depth), jnp.bfloat16),
        ],
        compiler_params=LIMIT,
    )(*got, spread, mask)
    gate, gain_out, bias_out = pl.pallas_call(
        gate_kernel,
        out_shape=(
            jax.ShapeDtypeStruct((tokens, channels), jnp.float32),
            jax.ShapeDtypeStruct((hidden, 1), jnp.float32),
            jax.ShapeDtypeStruct((hidden, 1), jnp.float32),
        ),
        in_specs=[VMEM] * 4,
        out_specs=(VMEM, VMEM, VMEM),
        compiler_params=LIMIT,
        cost_estimate=pl.CostEstimate(flops=2 * tokens * channels * channels, bytes_accessed=4 * tokens * channels, transcendentals=0),
    )(normed, w_gate, gain_out.reshape(1, hidden), bias_out.reshape(1, hidden))
    total = lax.all_to_all(total, ("half", "quad", "col"), split_axis=0, concat_axis=0, tiled=True, axis_index_groups=[far_order])
    return pl.pallas_call(
        functools.partial(output_kernel, far_order, near_order),
        out_shape=jax.ShapeDtypeStruct(pair.shape, jnp.bfloat16),
        in_specs=[VMEM] * 5,
        out_specs=VMEM,
        compiler_params=LIMIT,
    )(total, gate, gain_out, bias_out, w_out)


def plain_per_device(rows, cols, pair, token_mask, gain_in, bias_in, w_in, w_gate, gain_out, bias_out, w_out):
    row_count, col_count, channels = pair.shape
    hidden = w_out.shape[0]
    devices = rows * cols
    share = hidden // devices
    tokens = row_count * col_count
    row_start = lax.axis_index(("half", "quad")) * row_count
    col_start = lax.axis_index("col") * col_count
    mask_float = token_mask.astype(jnp.float32)
    mask_rows = lax.dynamic_slice_in_dim(mask_float, row_start, row_count)
    mask_cols = lax.dynamic_slice_in_dim(mask_float, col_start, col_count)
    pair_mask = (mask_rows[:, None] * mask_cols[None, :]).reshape(1, tokens)
    flat = pair.reshape(tokens, channels).astype(jnp.float32)
    normed = layer_norm(flat, gain_in, bias_in, -1).astype(jnp.bfloat16)
    projected = lax.dot_general(w_in, normed, (((0,), (1,)), ((), ())), preferred_element_type=jnp.float32)
    projected = projected.reshape(2, 2, hidden, tokens)
    sides = (pair_mask * jax.nn.sigmoid(projected[:, 0]) * projected[:, 1]).astype(jnp.bfloat16)
    sides = sides.reshape(2, devices, share, tokens).transpose(1, 0, 2, 3)
    gate = jax.nn.sigmoid(jnp.dot(normed, w_gate, preferred_element_type=jnp.float32))
    got = lax.all_to_all(sides, AXES, split_axis=0, concat_axis=0, tiled=True)
    got = got.reshape(rows, cols, 2, share, row_count, col_count).transpose(2, 3, 0, 4, 1, 5)
    got = got.reshape(2, share, rows * row_count, cols * col_count)
    total = jnp.einsum("cki,ckj->cij", got[0], got[1], preferred_element_type=jnp.float32).astype(jnp.bfloat16)
    total = total.reshape(share, rows, row_count, cols, col_count).transpose(1, 3, 0, 2, 4)
    total = total.reshape(devices, share, tokens)
    total = lax.all_to_all(total, AXES, split_axis=0, concat_axis=0, tiled=True)
    total = total.reshape(hidden, tokens).astype(jnp.float32)
    summed_norm = layer_norm(total, gain_out[:, None], bias_out[:, None], 0).astype(jnp.bfloat16)
    output = lax.dot_general(summed_norm, w_out, (((0,), (0,)), ((), ())), preferred_element_type=jnp.float32)
    return (gate * output).astype(jnp.bfloat16).reshape(row_count, col_count, channels)


def solution(mesh):
    rows, cols = mesh.shape["row"], mesh.shape["col"]
    halves = 2
    parts = (mesh.shape["groups"], halves, rows // halves, cols)
    finer = jax.sharding.Mesh(mesh.devices.reshape(parts), ("groups", "half", "quad", "col"))

    def per_shard(*args):
        near, hidden, length = rows * cols // halves, args[-1].shape[0], args[1].shape[0]
        row_count, col_count, _ = args[0].shape
        spare = LANES - 2 * col_count
        fits = hidden % (2 * GROUP * near) == 0 and cols == 2 and rows // halves == 4 and length <= LANES and row_count % 3 == 0
        fits = fits and 0 < spare < col_count and row_count // 3 * (col_count - spare) * 2 == LANES
        fits = fits and row_count // 3 * (rows // halves) * GROUP == LANES
        return per_device(rows, cols, halves, *args) if fits else plain_per_device(rows, cols, *args)

    tokens = P(("groups", "half", "quad"), "col", None)
    in_specs = (tokens, P("groups"), P(), P(), P(), P(), P(), P(), P())
    return jax.shard_map(per_shard, mesh=finer, in_specs=in_specs, out_specs=tokens, check_vma=False)
```

```python
import functools

import jax
import jax.numpy as jnp
from jax import lax
from jax.experimental import pallas as pl
from jax.experimental.pallas import tpu as pltpu
from jax.sharding import PartitionSpec as P

epsilon = 1e-05
LANES = 128
GROUP = 8
AXES = ("half", "quad", "col")
VMEM = pl.BlockSpec(memory_space=pltpu.VMEM)
HBM = pl.BlockSpec(memory_space=pltpu.HBM)
LIMIT = pltpu.CompilerParams(vmem_limit_bytes=32 * 1024 * 1024)


def sigmoid(x):
    return 0.5 * jnp.tanh(0.5 * x) + 0.5


def layer_norm(values, gain, bias, axis):
    mean = jnp.mean(values, axis=axis, keepdims=True)
    centred = values - mean
    variance = jnp.mean(centred * centred, axis=axis, keepdims=True)
    return centred * lax.rsqrt(variance + epsilon) * gain + bias


def column(row):
    n = row.shape[1]
    eye = lax.broadcasted_iota(jnp.int32, (n, n), 0) == lax.broadcasted_iota(jnp.int32, (n, n), 1)
    return jnp.sum(jnp.where(eye, row, 0.0), axis=1, keepdims=True)


def pack(x):
    rows, tokens = x.shape[-2:]
    whole, rest = divmod(tokens, LANES)
    blocks = [x[..., t * LANES : (t + 1) * LANES] for t in range(whole)]
    if rest:
        tail = x[..., whole * LANES :]
        blocks.append(jnp.concatenate([tail[..., : rows // 2, :], tail[..., rows // 2 :, :]], axis=-1))
    return jnp.concatenate(blocks, axis=-2)


def unpack(x, rows):
    whole, rest = divmod(x.shape[-2], rows)
    blocks = [x[..., t * rows : (t + 1) * rows, :] for t in range(whole)]
    if rest:
        tail = x[..., whole * rows :, :]
        blocks.append(jnp.concatenate([tail[..., : LANES // 2], tail[..., LANES // 2 :]], axis=-2))
    return jnp.concatenate(blocks, axis=-1)


def arrange(x):
    row_count, col_count, _ = x.shape
    whole, spare = row_count // 3, LANES - 2 * col_count
    blocks = []
    for t in range(whole):
        blocks += [x[2 * t], x[2 * t + 1], x[2 * whole + t, :spare]]
    return jnp.concatenate(blocks + [x[2 * whole + t, spare:] for t in range(whole)], axis=0)


def restore(x, row_count, col_count):
    whole, spare = row_count // 3, LANES - 2 * col_count
    rest = col_count - spare
    rows = []
    for t in range(whole):
        rows += [x[t * LANES : t * LANES + col_count], x[t * LANES + col_count : t * LANES + 2 * col_count]]
    for t in range(whole):
        tail = whole * LANES + t * rest
        rows += [x[t * LANES + 2 * col_count : (t + 1) * LANES], x[tail : tail + rest]]
    return jnp.concatenate(rows, axis=0)


def normalise(flat, gain, bias):
    return layer_norm(flat.astype(jnp.float32), gain, bias, -1).astype(jnp.bfloat16)


def project(normed, w, shape, quads):
    ours = w.shape[0] // 4
    tokens = normed.shape[0]
    projected = lax.dot_general(w, arrange(normed.reshape(shape)), (((1,), (1,)), ((), ())), preferred_element_type=jnp.float32)
    left = sigmoid(projected[:ours]) * projected[ours : 2 * ours]
    right = sigmoid(projected[2 * ours : 3 * ours]) * projected[3 * ours :]
    sides = jnp.concatenate([left.reshape(quads, -1, tokens), right.reshape(quads, -1, tokens)], axis=1)
    return pack(sides).astype(jnp.bfloat16)


def own_kernel(quads, cols, pair_hbm, gain_hbm, bias_hbm, w_hbm, mask_hbm, sides_ref, normed_ref, spread_ref, column_mask_ref, w_ref, gain_ref, bias_ref, pair_ref, all_w_ref, mask_ref, sems):
    moves = [(mask_hbm, mask_ref), (pair_hbm, pair_ref), (gain_hbm, gain_ref), (bias_hbm, bias_ref), (w_hbm, all_w_ref)]
    copies = [pltpu.make_async_copy(source, target, sems.at[n]) for n, (source, target) in enumerate(moves)]
    for copy in copies:
        copy.start()
    my_quad, my_col = lax.axis_index("quad"), lax.axis_index("col")
    row_count, _, channels = pair_ref.shape
    tokens = normed_ref.shape[0]
    hidden = all_w_ref.shape[1] // 4
    ours = hidden // cols
    group, lanes = spread_ref.shape
    copies[0].wait()
    mask_row = mask_ref[...].astype(jnp.float32)
    column_mask_ref[...] = column(mask_row)
    start = lax.axis_index("half") * (lanes // group)
    token = lax.broadcasted_iota(jnp.int32, (mask_row.shape[1], lanes), 0)
    lane = lax.broadcasted_iota(jnp.int32, (mask_row.shape[1], lanes), 1)
    whole = row_count // 3
    block, t, row = lane // LANES, lane // (quads * group) % whole, lane // group % quads
    k = (row ^ my_quad) * row_count + jnp.where(block < 2, 2 * t + block, 2 * whole + t)
    pick = jnp.where(k + start == token, 1.0, 0.0)
    kept = jnp.dot(mask_row.astype(jnp.bfloat16), pick.astype(jnp.bfloat16), preferred_element_type=jnp.float32)
    channel = lax.broadcasted_iota(jnp.int32, (group, lanes), 0)
    lane = lax.broadcasted_iota(jnp.int32, (group, lanes), 1)
    spread_ref[...] = jnp.where(lane % group == channel, kept, 0.0)
    for copy in copies[1:4]:
        copy.wait()
    normed = normalise(pair_ref[...].reshape(tokens, channels), gain_ref[...], bias_ref[...])
    normed_ref[...] = normed
    copies[4].wait()
    parts = [all_w_ref[:, at : at + hidden] for at in range(0, 4 * hidden, hidden)]
    w = jnp.concatenate([jnp.where(my_col == 0, part[:, :ours], part[:, ours:]) for part in parts], axis=1).T
    w_ref[...] = w
    sides_ref[...] = project(normed, w, pair_ref.shape, quads)


def other_kernel(pair_ref, sides_ref, gain_ref, bias_ref, w_ref, *refs):
    *piece_refs, others_ref = refs
    my_quad, my_col = lax.axis_index("quad"), lax.axis_index("col")
    quads = sides_ref.shape[0]
    normed = normalise(pair_ref[...].reshape(-1, pair_ref.shape[2]), gain_ref[...], bias_ref[...])
    others_ref[...] = project(normed, w_ref[...], pair_ref.shape, quads)
    for step, piece_ref in enumerate(piece_refs):
        piece_ref[my_col] = sides_ref[my_quad ^ step]
        piece_ref[1 - my_col] = others_ref[my_quad ^ step]


def triangle_kernel(far_order, steps, cols, row_count, col_count, share, *refs):
    *got_refs, spread_ref, mask_ref, total_ref, left_ref, wide_ref = refs
    got_refs = {step: ref for step, ref in zip(steps, got_refs)}
    both = 2 * share
    group, lanes = spread_ref.shape
    length = mask_ref.shape[0]
    rows, quads, parts = length // row_count, len(steps), share // group
    whole, spare = row_count // 3, LANES - 2 * col_count
    rest = col_count - spare
    blocks = [[got_refs[row][col].astype(jnp.float32) for row in range(quads)] for col in range(cols)]

    def turned(picks):
        return jnp.concatenate([blocks[col][row][at : at + group] for col, row, at in picks], axis=0).T

    tail = turned([(col, row, whole * both + part * group) for col in range(cols) for part in range(parts) for row in range(quads)])

    def side(which, part):
        even, odd, third = [], [], []
        for col in range(cols):
            at = which * share + part * group
            block = turned([(col, row, t * both + at) for t in range(whole) for row in range(quads)])
            even.append(block[:col_count])
            odd.append(block[col_count : 2 * col_count])
            lane = (col * parts + part) * quads * group
            at = which * LANES // 2
            last = [tail[at + t * rest : at + (t + 1) * rest, lane : lane + quads * group] for t in range(whole)]
            third += [block[2 * col_count :], jnp.concatenate(last, axis=1)]
        tokens = [jnp.concatenate(pieces, axis=0) for pieces in (even, odd, third)]
        return jnp.concatenate(tokens, axis=1) * mask_ref[...]

    def placed(pieces):
        return jnp.concatenate([jnp.zeros((piece, lanes), jnp.bfloat16) if isinstance(piece, int) else piece for piece in pieces], axis=0)

    contract = (((1,), (1,)), ((), ()))
    lane_block = lax.broadcasted_iota(jnp.int32, (group, LANES), 1) // rest
    mains, lasts = [], []
    for part in range(parts):
        left_ref[part] = side(0, part)
        right = side(1, part).astype(jnp.bfloat16)
        for row in range(rows):
            for t in range(0, whole, 2):
                pair = []
                for at in (row * row_count, row * row_count + 2):
                    picks = [at + 2 * t, at + 2 * t + 1, row * row_count + 2 * whole + t + len(pair)]
                    copies = [jnp.broadcast_to(left_ref[part, i : i + 1, :], (group, lanes)) for i in picks]
                    pair.append(jnp.concatenate([copy * spread_ref[...] for copy in copies], axis=1))
                at = (row * whole + t) * group
                wide_ref[part, at : at + 2 * group, :] = jnp.concatenate(pair, axis=0).astype(jnp.bfloat16)
        ours = [right[col * col_count : (col + 1) * col_count] for col in range(cols)]
        weights = [
            placed([p for mine in ours for p in (mine, LANES - col_count)]),
            placed([p for mine in ours for p in (col_count, mine, spare)]),
            placed([p for mine in ours for p in (2 * col_count, mine[:spare])]),
        ]
        weights = jnp.concatenate(weights, axis=1)
        mains.append(lax.dot_general(wide_ref[part], weights, contract, preferred_element_type=jnp.float32))
        gap = LANES // parts
        pieces = [[gap * part] + [mine[spare:]] * whole + [LANES - gap * (part + 1)] for mine in ours]
        weights = placed([p for piece in pieces for p in piece if not isinstance(p, int) or p])
        lasts.append(lax.dot_general(wide_ref[part, :, 2 * lanes :], weights, contract, preferred_element_type=jnp.float32))
    for target, device in enumerate(far_order):
        row, col = divmod(device, cols)
        spots = [(row * whole + t) * group for t in range(whole)]
        tiles = [main[at : at + group, col * LANES : (col + 1) * LANES] for at in spots for main in mains]
        last = [part[at : at + group, col * LANES : (col + 1) * LANES] for part in lasts for at in spots]
        tile = last[0]
        for n in range(1, len(last)):
            tile = jnp.where(lane_block >= n, last[n], tile)
        tiles.append(tile)
        total_ref[target] = jnp.concatenate(tiles, axis=0).astype(jnp.bfloat16)


def gate_kernel(normed_ref, w_ref, gain_ref, bias_ref, gate_ref, gain_out_ref, bias_out_ref):
    gate_ref[...] = sigmoid(jnp.dot(normed_ref[...], w_ref[...], preferred_element_type=jnp.float32))
    gain_out_ref[...] = column(gain_ref[...])
    bias_out_ref[...] = column(bias_ref[...])


def output_kernel(far_order, near_order, total_ref, gate_ref, gain_ref, bias_ref, w_ref, out_ref):
    tokens = gate_ref.shape[0]
    hidden = w_ref.shape[0]
    near = len(near_order)
    share = hidden // near
    blocks = []
    for index in near_order:
        parts = [total_ref[source].astype(jnp.float32) for source, device in enumerate(far_order) if device % near == index]
        blocks.append(unpack(sum(parts[1:], parts[0]), share))
    total = jnp.concatenate(blocks, axis=0)
    normed = layer_norm(total, gain_ref[...], bias_ref[...], 0).astype(jnp.bfloat16)
    output = lax.dot_general(normed, w_ref[...], (((0,), (0,)), ((), ())), preferred_element_type=jnp.float32)
    output = restore(output, out_ref.shape[0], out_ref.shape[1])
    out_ref[...] = (gate_ref[...] * output).astype(jnp.bfloat16).reshape(out_ref.shape)


def per_device(rows, cols, halves, pair, token_mask, gain_in, bias_in, w_in, w_gate, gain_out, bias_out, w_out):
    row_count, col_count, channels = pair.shape
    hidden = w_out.shape[0]
    devices = rows * cols
    near = devices // halves
    quads = rows // halves
    far_order = []
    for col in reversed(range(cols)):
        ours = [quad * cols + col for quad in (range(quads) if col else [*range(1, quads), 0])]
        behind = [near + quad * cols + col for quad in reversed(range(quads))]
        far_order += behind[-1:] + ours + behind[:-1] if col else behind + ours
    share = hidden // near
    tokens = row_count * col_count
    length = rows * row_count
    depth = length // halves
    token_mask = token_mask.reshape(1, length)
    near_order = [quad * cols + col for col in range(cols) for quad in range(quads)]
    packed = 2 * share * tokens // LANES
    cost = pl.CostEstimate(flops=2 * tokens * channels * 4 * hidden, bytes_accessed=16 * tokens * channels, transcendentals=0)
    other_pair = lax.ppermute(pair, "col", [(i, (i + 1) % cols) for i in range(cols)])
    arguments = (pair, gain_in.reshape(1, channels), bias_in.reshape(1, channels), w_in, token_mask)
    sides, normed, spread, mask, *weights = pl.pallas_call(
        functools.partial(own_kernel, quads, cols),
        out_shape=(
            jax.ShapeDtypeStruct((quads, packed, LANES), jnp.bfloat16),
            jax.ShapeDtypeStruct((tokens, channels), jnp.bfloat16),
            jax.ShapeDtypeStruct((GROUP, GROUP * depth), jnp.float32),
            jax.ShapeDtypeStruct((length, 1), jnp.float32),
            jax.ShapeDtypeStruct((4 * hidden // cols, channels), jnp.bfloat16),
            jax.ShapeDtypeStruct((1, channels), jnp.float32),
            jax.ShapeDtypeStruct((1, channels), jnp.float32),
        ),
        in_specs=[HBM] * 5,
        out_specs=(VMEM,) * 7,
        scratch_shapes=[
            pltpu.VMEM(pair.shape, pair.dtype),
            pltpu.VMEM(w_in.shape, w_in.dtype),
            pltpu.VMEM((1, length), jnp.int32),
            pltpu.SemaphoreType.DMA((5,)),
        ],
        compiler_params=LIMIT,
        cost_estimate=cost,
    )(*(pltpu.with_memory_space_constraint(x, pltpu.HBM) for x in arguments))
    w_ours, gain_in, bias_in = weights
    pieces = pl.pallas_call(
        other_kernel,
        out_shape=[jax.ShapeDtypeStruct((cols, packed, LANES), jnp.bfloat16)] * quads,
        in_specs=[VMEM] * 5,
        out_specs=[VMEM] * quads,
        scratch_shapes=[pltpu.VMEM((quads, packed, LANES), jnp.bfloat16)],
        compiler_params=LIMIT,
        cost_estimate=cost,
    )(other_pair, sides, gain_in, bias_in, w_ours)
    steps = [3, 1, 2, 0]
    got = [lax.ppermute(pieces[step], "quad", [(i, i ^ step) for i in range(quads)]) if step else pieces[0] for step in steps]
    total = pl.pallas_call(
        functools.partial(triangle_kernel, far_order, steps, cols, row_count, col_count, share),
        out_shape=jax.ShapeDtypeStruct((devices, share * tokens // LANES, LANES), jnp.bfloat16),
        in_specs=[VMEM] * (quads + 2),
        out_specs=VMEM,
        scratch_shapes=[
            pltpu.VMEM((share // GROUP, length, GROUP * depth), jnp.float32),
            pltpu.VMEM((share // GROUP, length // 3 * GROUP, 3 * GROUP * depth), jnp.bfloat16),
        ],
        compiler_params=LIMIT,
    )(*got, spread, mask)
    gate, gain_out, bias_out = pl.pallas_call(
        gate_kernel,
        out_shape=(
            jax.ShapeDtypeStruct((tokens, channels), jnp.float32),
            jax.ShapeDtypeStruct((hidden, 1), jnp.float32),
            jax.ShapeDtypeStruct((hidden, 1), jnp.float32),
        ),
        in_specs=[VMEM] * 4,
        out_specs=(VMEM, VMEM, VMEM),
        compiler_params=LIMIT,
        cost_estimate=pl.CostEstimate(flops=2 * tokens * channels * channels, bytes_accessed=4 * tokens * channels, transcendentals=0),
    )(normed, w_gate, gain_out.reshape(1, hidden), bias_out.reshape(1, hidden))
    total = lax.all_to_all(total, ("half", "quad", "col"), split_axis=0, concat_axis=0, tiled=True, axis_index_groups=[far_order])
    return pl.pallas_call(
        functools.partial(output_kernel, far_order, near_order),
        out_shape=jax.ShapeDtypeStruct(pair.shape, jnp.bfloat16),
        in_specs=[VMEM] * 5,
        out_specs=VMEM,
        compiler_params=LIMIT,
    )(total, gate, gain_out, bias_out, w_out)


def plain_per_device(rows, cols, pair, token_mask, gain_in, bias_in, w_in, w_gate, gain_out, bias_out, w_out):
    row_count, col_count, channels = pair.shape
    hidden = w_out.shape[0]
    devices = rows * cols
    share = hidden // devices
    tokens = row_count * col_count
    row_start = lax.axis_index(("half", "quad")) * row_count
    col_start = lax.axis_index("col") * col_count
    mask_float = token_mask.astype(jnp.float32)
    mask_rows = lax.dynamic_slice_in_dim(mask_float, row_start, row_count)
    mask_cols = lax.dynamic_slice_in_dim(mask_float, col_start, col_count)
    pair_mask = (mask_rows[:, None] * mask_cols[None, :]).reshape(1, tokens)
    flat = pair.reshape(tokens, channels).astype(jnp.float32)
    normed = layer_norm(flat, gain_in, bias_in, -1).astype(jnp.bfloat16)
    projected = lax.dot_general(w_in, normed, (((0,), (1,)), ((), ())), preferred_element_type=jnp.float32)
    projected = projected.reshape(2, 2, hidden, tokens)
    sides = (pair_mask * jax.nn.sigmoid(projected[:, 0]) * projected[:, 1]).astype(jnp.bfloat16)
    sides = sides.reshape(2, devices, share, tokens).transpose(1, 0, 2, 3)
    gate = jax.nn.sigmoid(jnp.dot(normed, w_gate, preferred_element_type=jnp.float32))
    got = lax.all_to_all(sides, AXES, split_axis=0, concat_axis=0, tiled=True)
    got = got.reshape(rows, cols, 2, share, row_count, col_count).transpose(2, 3, 0, 4, 1, 5)
    got = got.reshape(2, share, rows * row_count, cols * col_count)
    total = jnp.einsum("cki,ckj->cij", got[0], got[1], preferred_element_type=jnp.float32).astype(jnp.bfloat16)
    total = total.reshape(share, rows, row_count, cols, col_count).transpose(1, 3, 0, 2, 4)
    total = total.reshape(devices, share, tokens)
    total = lax.all_to_all(total, AXES, split_axis=0, concat_axis=0, tiled=True)
    total = total.reshape(hidden, tokens).astype(jnp.float32)
    summed_norm = layer_norm(total, gain_out[:, None], bias_out[:, None], 0).astype(jnp.bfloat16)
    output = lax.dot_general(summed_norm, w_out, (((0,), (0,)), ((), ())), preferred_element_type=jnp.float32)
    return (gate * output).astype(jnp.bfloat16).reshape(row_count, col_count, channels)


def solution(mesh):
    rows, cols = mesh.shape["row"], mesh.shape["col"]
    halves = 2
    parts = (mesh.shape["groups"], halves, rows // halves, cols)
    finer = jax.sharding.Mesh(mesh.devices.reshape(parts), ("groups", "half", "quad", "col"))

    def per_shard(*args):
        near, hidden, length = rows * cols // halves, args[-1].shape[0], args[1].shape[0]
        row_count, col_count, _ = args[0].shape
        spare = LANES - 2 * col_count
        fits = hidden % (2 * GROUP * near) == 0 and cols == 2 and rows // halves == 4 and length <= LANES and row_count % 3 == 0
        fits = fits and 0 < spare < col_count and row_count // 3 * (col_count - spare) * 2 == LANES
        fits = fits and row_count // 3 * (rows // halves) * GROUP == LANES
        return per_device(rows, cols, halves, *args) if fits else plain_per_device(rows, cols, *args)

    tokens = P(("groups", "half", "quad"), "col", None)
    in_specs = (tokens, P("groups"), P(), P(), P(), P(), P(), P(), P())
    return jax.shard_map(per_shard, mesh=finer, in_specs=in_specs, out_specs=tokens, check_vma=False)
```

```python
import functools

import jax
import jax.numpy as jnp
from jax import lax
from jax.experimental import pallas as pl
from jax.experimental.pallas import tpu as pltpu
from jax.sharding import PartitionSpec as P

epsilon = 1e-05
LANES = 128
GROUP = 8
AXES = ("half", "quad", "col")
VMEM = pl.BlockSpec(memory_space=pltpu.VMEM)
HBM = pl.BlockSpec(memory_space=pltpu.HBM)
LIMIT = pltpu.CompilerParams(vmem_limit_bytes=32 * 1024 * 1024)


def sigmoid(x):
    return 0.5 * jnp.tanh(0.5 * x) + 0.5


def layer_norm(values, gain, bias, axis):
    mean = jnp.mean(values, axis=axis, keepdims=True)
    centred = values - mean
    variance = jnp.mean(centred * centred, axis=axis, keepdims=True)
    return centred * lax.rsqrt(variance + epsilon) * gain + bias


def column(row):
    n = row.shape[1]
    eye = lax.broadcasted_iota(jnp.int32, (n, n), 0) == lax.broadcasted_iota(jnp.int32, (n, n), 1)
    return jnp.sum(jnp.where(eye, row, 0.0), axis=1, keepdims=True)


def pack(x):
    rows, tokens = x.shape[-2:]
    whole, rest = divmod(tokens, LANES)
    blocks = [x[..., t * LANES : (t + 1) * LANES] for t in range(whole)]
    if rest:
        tail = x[..., whole * LANES :]
        blocks.append(jnp.concatenate([tail[..., : rows // 2, :], tail[..., rows // 2 :, :]], axis=-1))
    return jnp.concatenate(blocks, axis=-2)


def unpack(x, rows):
    whole, rest = divmod(x.shape[-2], rows)
    blocks = [x[..., t * rows : (t + 1) * rows, :] for t in range(whole)]
    if rest:
        tail = x[..., whole * rows :, :]
        blocks.append(jnp.concatenate([tail[..., : LANES // 2], tail[..., LANES // 2 :]], axis=-2))
    return jnp.concatenate(blocks, axis=-1)


def arrange(x):
    row_count, col_count, _ = x.shape
    whole, spare = row_count // 3, LANES - 2 * col_count
    blocks = []
    for t in range(whole):
        blocks += [x[2 * t], x[2 * t + 1], x[2 * whole + t, :spare]]
    return jnp.concatenate(blocks + [x[2 * whole + t, spare:] for t in range(whole)], axis=0)


def restore(x, row_count, col_count):
    whole, spare = row_count // 3, LANES - 2 * col_count
    rest = col_count - spare
    rows = []
    for t in range(whole):
        rows += [x[t * LANES : t * LANES + col_count], x[t * LANES + col_count : t * LANES + 2 * col_count]]
    for t in range(whole):
        tail = whole * LANES + t * rest
        rows += [x[t * LANES + 2 * col_count : (t + 1) * LANES], x[tail : tail + rest]]
    return jnp.concatenate(rows, axis=0)


def normalise(flat, gain, bias):
    return layer_norm(flat.astype(jnp.float32), gain, bias, -1).astype(jnp.bfloat16)


def project(normed, w, shape, quads):
    ours = w.shape[0] // 4
    tokens = normed.shape[0]
    projected = lax.dot_general(w, arrange(normed.reshape(shape)), (((1,), (1,)), ((), ())), preferred_element_type=jnp.float32)
    left = sigmoid(projected[:ours]) * projected[ours : 2 * ours]
    right = sigmoid(projected[2 * ours : 3 * ours]) * projected[3 * ours :]
    sides = jnp.concatenate([left.reshape(quads, -1, tokens), right.reshape(quads, -1, tokens)], axis=1)
    return pack(sides).astype(jnp.bfloat16)


def own_kernel(quads, cols, pair_hbm, gain_hbm, bias_hbm, w_hbm, mask_hbm, sides_ref, normed_ref, spread_ref, column_mask_ref, w_ref, gain_ref, bias_ref, pair_ref, all_w_ref, mask_ref, sems):
    moves = [(mask_hbm, mask_ref), (pair_hbm, pair_ref), (gain_hbm, gain_ref), (bias_hbm, bias_ref), (w_hbm, all_w_ref)]
    copies = [pltpu.make_async_copy(source, target, sems.at[n]) for n, (source, target) in enumerate(moves)]
    for copy in copies:
        copy.start()
    my_quad, my_col = lax.axis_index("quad"), lax.axis_index("col")
    row_count, _, channels = pair_ref.shape
    tokens = normed_ref.shape[0]
    hidden = all_w_ref.shape[1] // 4
    ours = hidden // cols
    group, lanes = spread_ref.shape
    copies[0].wait()
    mask_row = mask_ref[...].astype(jnp.float32)
    column_mask_ref[...] = column(mask_row)
    start = lax.axis_index("half") * (lanes // group)
    token = lax.broadcasted_iota(jnp.int32, (mask_row.shape[1], lanes), 0)
    lane = lax.broadcasted_iota(jnp.int32, (mask_row.shape[1], lanes), 1)
    whole = row_count // 3
    block, t, row = lane // LANES, lane // (quads * group) % whole, lane // group % quads
    k = (row ^ my_quad) * row_count + jnp.where(block < 2, 2 * t + block, 2 * whole + t)
    pick = jnp.where(k + start == token, 1.0, 0.0)
    kept = jnp.dot(mask_row.astype(jnp.bfloat16), pick.astype(jnp.bfloat16), preferred_element_type=jnp.float32)
    channel = lax.broadcasted_iota(jnp.int32, (group, lanes), 0)
    lane = lax.broadcasted_iota(jnp.int32, (group, lanes), 1)
    spread_ref[...] = jnp.where(lane % group == channel, kept, 0.0)
    for copy in copies[1:4]:
        copy.wait()
    normed = normalise(pair_ref[...].reshape(tokens, channels), gain_ref[...], bias_ref[...])
    normed_ref[...] = normed
    copies[4].wait()
    parts = [all_w_ref[:, at : at + hidden] for at in range(0, 4 * hidden, hidden)]
    w = jnp.concatenate([jnp.where(my_col == 0, part[:, :ours], part[:, ours:]) for part in parts], axis=1).T
    w_ref[...] = w
    sides_ref[...] = project(normed, w, pair_ref.shape, quads)


def other_kernel(pair_ref, sides_ref, gain_ref, bias_ref, w_ref, *refs):
    *piece_refs, others_ref = refs
    my_quad, my_col = lax.axis_index("quad"), lax.axis_index("col")
    quads = sides_ref.shape[0]
    normed = normalise(pair_ref[...].reshape(-1, pair_ref.shape[2]), gain_ref[...], bias_ref[...])
    others_ref[...] = project(normed, w_ref[...], pair_ref.shape, quads)
    for step, piece_ref in enumerate(piece_refs):
        piece_ref[my_col] = sides_ref[my_quad ^ step]
        piece_ref[1 - my_col] = others_ref[my_quad ^ step]


def triangle_kernel(far_order, steps, cols, row_count, col_count, share, *refs):
    *got_refs, spread_ref, mask_ref, total_ref, left_ref, wide_ref = refs
    got_refs = {step: ref for step, ref in zip(steps, got_refs)}
    both = 2 * share
    group, lanes = spread_ref.shape
    length = mask_ref.shape[0]
    rows, quads, parts = length // row_count, len(steps), share // group
    whole, spare = row_count // 3, LANES - 2 * col_count
    rest = col_count - spare
    blocks = [[got_refs[row][col].astype(jnp.float32) for row in range(quads)] for col in range(cols)]

    def turned(picks):
        return jnp.concatenate([blocks[col][row][at : at + group] for col, row, at in picks], axis=0).T

    tail = turned([(col, row, whole * both + part * group) for col in range(cols) for part in range(parts) for row in range(quads)])

    def side(which, part):
        even, odd, third = [], [], []
        for col in range(cols):
            at = which * share + part * group
            block = turned([(col, row, t * both + at) for t in range(whole) for row in range(quads)])
            even.append(block[:col_count])
            odd.append(block[col_count : 2 * col_count])
            lane = (col * parts + part) * quads * group
            at = which * LANES // 2
            last = [tail[at + t * rest : at + (t + 1) * rest, lane : lane + quads * group] for t in range(whole)]
            third += [block[2 * col_count :], jnp.concatenate(last, axis=1)]
        tokens = [jnp.concatenate(pieces, axis=0) for pieces in (even, odd, third)]
        return jnp.concatenate(tokens, axis=1) * mask_ref[...]

    def placed(pieces):
        return jnp.concatenate([jnp.zeros((piece, lanes), jnp.bfloat16) if isinstance(piece, int) else piece for piece in pieces], axis=0)

    contract = (((1,), (1,)), ((), ()))
    lane_block = lax.broadcasted_iota(jnp.int32, (group, LANES), 1) // rest
    mains, lasts = [], []
    for part in range(parts):
        left_ref[part] = side(0, part)
        right = side(1, part).astype(jnp.bfloat16)
        for row in range(rows):
            for t in range(0, whole, 2):
                pair = []
                for at in (row * row_count, row * row_count + 2):
                    picks = [at + 2 * t, at + 2 * t + 1, row * row_count + 2 * whole + t + len(pair)]
                    copies = [jnp.broadcast_to(left_ref[part, i : i + 1, :], (group, lanes)) for i in picks]
                    pair.append(jnp.concatenate([copy * spread_ref[...] for copy in copies], axis=1))
                at = (row * whole + t) * group
                wide_ref[part, at : at + 2 * group, :] = jnp.concatenate(pair, axis=0).astype(jnp.bfloat16)
        ours = [right[col * col_count : (col + 1) * col_count] for col in range(cols)]
        weights = [
            placed([p for mine in ours for p in (mine, LANES - col_count)]),
            placed([p for mine in ours for p in (col_count, mine, spare)]),
            placed([p for mine in ours for p in (2 * col_count, mine[:spare])]),
        ]
        weights = jnp.concatenate(weights, axis=1)
        mains.append(lax.dot_general(wide_ref[part], weights, contract, preferred_element_type=jnp.float32))
        gap = LANES // parts
        pieces = [[gap * part] + [mine[spare:]] * whole + [LANES - gap * (part + 1)] for mine in ours]
        weights = placed([p for piece in pieces for p in piece if not isinstance(p, int) or p])
        lasts.append(lax.dot_general(wide_ref[part, :, 2 * lanes :], weights, contract, preferred_element_type=jnp.float32))
    for target, device in enumerate(far_order):
        row, col = divmod(device, cols)
        spots = [(row * whole + t) * group for t in range(whole)]
        tiles = [main[at : at + group, col * LANES : (col + 1) * LANES] for at in spots for main in mains]
        last = [part[at : at + group, col * LANES : (col + 1) * LANES] for part in lasts for at in spots]
        tile = last[0]
        for n in range(1, len(last)):
            tile = jnp.where(lane_block >= n, last[n], tile)
        tiles.append(tile)
        total_ref[target] = jnp.concatenate(tiles, axis=0).astype(jnp.bfloat16)


def gate_kernel(normed_ref, w_ref, gain_ref, bias_ref, gate_ref, gain_out_ref, bias_out_ref):
    gate_ref[...] = sigmoid(jnp.dot(normed_ref[...], w_ref[...], preferred_element_type=jnp.float32))
    gain_out_ref[...] = column(gain_ref[...])
    bias_out_ref[...] = column(bias_ref[...])


def output_kernel(far_order, near_order, total_ref, gate_ref, gain_ref, bias_ref, w_ref, out_ref):
    tokens = gate_ref.shape[0]
    hidden = w_ref.shape[0]
    near = len(near_order)
    share = hidden // near
    blocks = []
    for index in near_order:
        parts = [total_ref[source].astype(jnp.float32) for source, device in enumerate(far_order) if device % near == index]
        blocks.append(unpack(sum(parts[1:], parts[0]), share))
    total = jnp.concatenate(blocks, axis=0)
    normed = layer_norm(total, gain_ref[...], bias_ref[...], 0).astype(jnp.bfloat16)
    output = lax.dot_general(normed, w_ref[...], (((0,), (0,)), ((), ())), preferred_element_type=jnp.float32)
    output = restore(output, out_ref.shape[0], out_ref.shape[1])
    out_ref[...] = (gate_ref[...] * output).astype(jnp.bfloat16).reshape(out_ref.shape)


def per_device(rows, cols, halves, pair, token_mask, gain_in, bias_in, w_in, w_gate, gain_out, bias_out, w_out):
    row_count, col_count, channels = pair.shape
    hidden = w_out.shape[0]
    devices = rows * cols
    near = devices // halves
    quads = rows // halves
    far_order = []
    for n in range(quads):
        far, other = [(quads - n) % quads, (n + 1) % quads], [quads - 1 - n, n]
        spots = [near + far[0] * cols + 1, far[1] * cols, near + other[0] * cols, other[1] * cols + 1]
        far_order += spots if n < quads - 1 else [spots[0], spots[3], spots[2], spots[1]]
    share = hidden // near
    tokens = row_count * col_count
    length = rows * row_count
    depth = length // halves
    token_mask = token_mask.reshape(1, length)
    near_order = [quad * cols + col for col in range(cols) for quad in range(quads)]
    packed = 2 * share * tokens // LANES
    cost = pl.CostEstimate(flops=2 * tokens * channels * 4 * hidden, bytes_accessed=16 * tokens * channels, transcendentals=0)
    other_pair = lax.ppermute(pair, "col", [(i, (i + 1) % cols) for i in range(cols)])
    arguments = (pair, gain_in.reshape(1, channels), bias_in.reshape(1, channels), w_in, token_mask)
    sides, normed, spread, mask, *weights = pl.pallas_call(
        functools.partial(own_kernel, quads, cols),
        out_shape=(
            jax.ShapeDtypeStruct((quads, packed, LANES), jnp.bfloat16),
            jax.ShapeDtypeStruct((tokens, channels), jnp.bfloat16),
            jax.ShapeDtypeStruct((GROUP, GROUP * depth), jnp.float32),
            jax.ShapeDtypeStruct((length, 1), jnp.float32),
            jax.ShapeDtypeStruct((4 * hidden // cols, channels), jnp.bfloat16),
            jax.ShapeDtypeStruct((1, channels), jnp.float32),
            jax.ShapeDtypeStruct((1, channels), jnp.float32),
        ),
        in_specs=[HBM] * 5,
        out_specs=(VMEM,) * 7,
        scratch_shapes=[
            pltpu.VMEM(pair.shape, pair.dtype),
            pltpu.VMEM(w_in.shape, w_in.dtype),
            pltpu.VMEM((1, length), jnp.int32),
            pltpu.SemaphoreType.DMA((5,)),
        ],
        compiler_params=LIMIT,
        cost_estimate=cost,
    )(*(pltpu.with_memory_space_constraint(x, pltpu.HBM) for x in arguments))
    w_ours, gain_in, bias_in = weights
    pieces = pl.pallas_call(
        other_kernel,
        out_shape=[jax.ShapeDtypeStruct((cols, packed, LANES), jnp.bfloat16)] * quads,
        in_specs=[VMEM] * 5,
        out_specs=[VMEM] * quads,
        scratch_shapes=[pltpu.VMEM((quads, packed, LANES), jnp.bfloat16)],
        compiler_params=LIMIT,
        cost_estimate=cost,
    )(other_pair, sides, gain_in, bias_in, w_ours)
    steps = [3, 1, 2, 0]
    got = [lax.ppermute(pieces[step], "quad", [(i, i ^ step) for i in range(quads)]) if step else pieces[0] for step in steps]
    total = pl.pallas_call(
        functools.partial(triangle_kernel, far_order, steps, cols, row_count, col_count, share),
        out_shape=jax.ShapeDtypeStruct((devices, share * tokens // LANES, LANES), jnp.bfloat16),
        in_specs=[VMEM] * (quads + 2),
        out_specs=VMEM,
        scratch_shapes=[
            pltpu.VMEM((share // GROUP, length, GROUP * depth), jnp.float32),
            pltpu.VMEM((share // GROUP, length // 3 * GROUP, 3 * GROUP * depth), jnp.bfloat16),
        ],
        compiler_params=LIMIT,
    )(*got, spread, mask)
    gate, gain_out, bias_out = pl.pallas_call(
        gate_kernel,
        out_shape=(
            jax.ShapeDtypeStruct((tokens, channels), jnp.float32),
            jax.ShapeDtypeStruct((hidden, 1), jnp.float32),
            jax.ShapeDtypeStruct((hidden, 1), jnp.float32),
        ),
        in_specs=[VMEM] * 4,
        out_specs=(VMEM, VMEM, VMEM),
        compiler_params=LIMIT,
        cost_estimate=pl.CostEstimate(flops=2 * tokens * channels * channels, bytes_accessed=4 * tokens * channels, transcendentals=0),
    )(normed, w_gate, gain_out.reshape(1, hidden), bias_out.reshape(1, hidden))
    total = lax.all_to_all(total, ("half", "quad", "col"), split_axis=0, concat_axis=0, tiled=True, axis_index_groups=[far_order])
    return pl.pallas_call(
        functools.partial(output_kernel, far_order, near_order),
        out_shape=jax.ShapeDtypeStruct(pair.shape, jnp.bfloat16),
        in_specs=[VMEM] * 5,
        out_specs=VMEM,
        compiler_params=LIMIT,
    )(total, gate, gain_out, bias_out, w_out)


def plain_per_device(rows, cols, pair, token_mask, gain_in, bias_in, w_in, w_gate, gain_out, bias_out, w_out):
    row_count, col_count, channels = pair.shape
    hidden = w_out.shape[0]
    devices = rows * cols
    share = hidden // devices
    tokens = row_count * col_count
    row_start = lax.axis_index(("half", "quad")) * row_count
    col_start = lax.axis_index("col") * col_count
    mask_float = token_mask.astype(jnp.float32)
    mask_rows = lax.dynamic_slice_in_dim(mask_float, row_start, row_count)
    mask_cols = lax.dynamic_slice_in_dim(mask_float, col_start, col_count)
    pair_mask = (mask_rows[:, None] * mask_cols[None, :]).reshape(1, tokens)
    flat = pair.reshape(tokens, channels).astype(jnp.float32)
    normed = layer_norm(flat, gain_in, bias_in, -1).astype(jnp.bfloat16)
    projected = lax.dot_general(w_in, normed, (((0,), (1,)), ((), ())), preferred_element_type=jnp.float32)
    projected = projected.reshape(2, 2, hidden, tokens)
    sides = (pair_mask * jax.nn.sigmoid(projected[:, 0]) * projected[:, 1]).astype(jnp.bfloat16)
    sides = sides.reshape(2, devices, share, tokens).transpose(1, 0, 2, 3)
    gate = jax.nn.sigmoid(jnp.dot(normed, w_gate, preferred_element_type=jnp.float32))
    got = lax.all_to_all(sides, AXES, split_axis=0, concat_axis=0, tiled=True)
    got = got.reshape(rows, cols, 2, share, row_count, col_count).transpose(2, 3, 0, 4, 1, 5)
    got = got.reshape(2, share, rows * row_count, cols * col_count)
    total = jnp.einsum("cki,ckj->cij", got[0], got[1], preferred_element_type=jnp.float32).astype(jnp.bfloat16)
    total = total.reshape(share, rows, row_count, cols, col_count).transpose(1, 3, 0, 2, 4)
    total = total.reshape(devices, share, tokens)
    total = lax.all_to_all(total, AXES, split_axis=0, concat_axis=0, tiled=True)
    total = total.reshape(hidden, tokens).astype(jnp.float32)
    summed_norm = layer_norm(total, gain_out[:, None], bias_out[:, None], 0).astype(jnp.bfloat16)
    output = lax.dot_general(summed_norm, w_out, (((0,), (0,)), ((), ())), preferred_element_type=jnp.float32)
    return (gate * output).astype(jnp.bfloat16).reshape(row_count, col_count, channels)


def solution(mesh):
    rows, cols = mesh.shape["row"], mesh.shape["col"]
    halves = 2
    parts = (mesh.shape["groups"], halves, rows // halves, cols)
    finer = jax.sharding.Mesh(mesh.devices.reshape(parts), ("groups", "half", "quad", "col"))

    def per_shard(*args):
        near, hidden, length = rows * cols // halves, args[-1].shape[0], args[1].shape[0]
        row_count, col_count, _ = args[0].shape
        spare = LANES - 2 * col_count
        fits = hidden % (2 * GROUP * near) == 0 and cols == 2 and rows // halves == 4 and length <= LANES and row_count % 3 == 0
        fits = fits and 0 < spare < col_count and row_count // 3 * (col_count - spare) * 2 == LANES
        fits = fits and row_count // 3 * (rows // halves) * GROUP == LANES
        return per_device(rows, cols, halves, *args) if fits else plain_per_device(rows, cols, *args)

    tokens = P(("groups", "half", "quad"), "col", None)
    in_specs = (tokens, P("groups"), P(), P(), P(), P(), P(), P(), P())
    return jax.shard_map(per_shard, mesh=finer, in_specs=in_specs, out_specs=tokens, check_vma=False)
```

```python
import functools

import jax
import jax.numpy as jnp
from jax import lax
from jax.experimental import pallas as pl
from jax.experimental.pallas import tpu as pltpu
from jax.sharding import PartitionSpec as P

epsilon = 1e-05
LANES = 128
GROUP = 8
AXES = ("half", "quad", "col")
VMEM = pl.BlockSpec(memory_space=pltpu.VMEM)
HBM = pl.BlockSpec(memory_space=pltpu.HBM)
LIMIT = pltpu.CompilerParams(vmem_limit_bytes=32 * 1024 * 1024)


def sigmoid(x):
    return 0.5 * jnp.tanh(0.5 * x) + 0.5


def layer_norm(values, gain, bias, axis):
    mean = jnp.mean(values, axis=axis, keepdims=True)
    centred = values - mean
    variance = jnp.mean(centred * centred, axis=axis, keepdims=True)
    return centred * lax.rsqrt(variance + epsilon) * gain + bias


def column(row):
    n = row.shape[1]
    eye = lax.broadcasted_iota(jnp.int32, (n, n), 0) == lax.broadcasted_iota(jnp.int32, (n, n), 1)
    return jnp.sum(jnp.where(eye, row, 0.0), axis=1, keepdims=True)


def pack(x):
    rows, tokens = x.shape[-2:]
    whole, rest = divmod(tokens, LANES)
    blocks = [x[..., t * LANES : (t + 1) * LANES] for t in range(whole)]
    if rest:
        tail = x[..., whole * LANES :]
        blocks.append(jnp.concatenate([tail[..., : rows // 2, :], tail[..., rows // 2 :, :]], axis=-1))
    return jnp.concatenate(blocks, axis=-2)


def unpack(x, rows):
    whole, rest = divmod(x.shape[-2], rows)
    blocks = [x[..., t * rows : (t + 1) * rows, :] for t in range(whole)]
    if rest:
        tail = x[..., whole * rows :, :]
        blocks.append(jnp.concatenate([tail[..., : LANES // 2], tail[..., LANES // 2 :]], axis=-2))
    return jnp.concatenate(blocks, axis=-1)


def arrange(x):
    row_count, col_count, _ = x.shape
    whole, spare = row_count // 3, LANES - 2 * col_count
    blocks = []
    for t in range(whole):
        blocks += [x[2 * t], x[2 * t + 1], x[2 * whole + t, :spare]]
    return jnp.concatenate(blocks + [x[2 * whole + t, spare:] for t in range(whole)], axis=0)


def restore(x, row_count, col_count):
    whole, spare = row_count // 3, LANES - 2 * col_count
    rest = col_count - spare
    rows = []
    for t in range(whole):
        rows += [x[t * LANES : t * LANES + col_count], x[t * LANES + col_count : t * LANES + 2 * col_count]]
    for t in range(whole):
        tail = whole * LANES + t * rest
        rows += [x[t * LANES + 2 * col_count : (t + 1) * LANES], x[tail : tail + rest]]
    return jnp.concatenate(rows, axis=0)


def normalise(flat, gain, bias):
    return layer_norm(flat.astype(jnp.float32), gain, bias, -1).astype(jnp.bfloat16)


def project(normed, w, shape, quads):
    ours = w.shape[0] // 4
    tokens = normed.shape[0]
    projected = lax.dot_general(w, arrange(normed.reshape(shape)), (((1,), (1,)), ((), ())), preferred_element_type=jnp.float32)
    left = sigmoid(projected[:ours]) * projected[ours : 2 * ours]
    right = sigmoid(projected[2 * ours : 3 * ours]) * projected[3 * ours :]
    sides = jnp.concatenate([left.reshape(quads, -1, tokens), right.reshape(quads, -1, tokens)], axis=1)
    return pack(sides).astype(jnp.bfloat16)


def own_kernel(quads, cols, pair_hbm, gain_hbm, bias_hbm, w_hbm, mask_hbm, sides_ref, normed_ref, spread_ref, column_mask_ref, w_ref, gain_ref, bias_ref, pair_ref, all_w_ref, mask_ref, sems):
    moves = [(mask_hbm, mask_ref), (pair_hbm, pair_ref), (gain_hbm, gain_ref), (bias_hbm, bias_ref), (w_hbm, all_w_ref)]
    copies = [pltpu.make_async_copy(source, target, sems.at[n]) for n, (source, target) in enumerate(moves)]
    for copy in copies:
        copy.start()
    my_quad, my_col = lax.axis_index("quad"), lax.axis_index("col")
    row_count, _, channels = pair_ref.shape
    tokens = normed_ref.shape[0]
    hidden = all_w_ref.shape[1] // 4
    ours = hidden // cols
    group, lanes = spread_ref.shape
    copies[0].wait()
    mask_row = mask_ref[...].astype(jnp.float32)
    column_mask_ref[...] = column(mask_row)
    start = lax.axis_index("half") * (lanes // group)
    token = lax.broadcasted_iota(jnp.int32, (mask_row.shape[1], lanes), 0)
    lane = lax.broadcasted_iota(jnp.int32, (mask_row.shape[1], lanes), 1)
    whole = row_count // 3
    block, t, row = lane // LANES, lane // (quads * group) % whole, lane // group % quads
    k = (row ^ my_quad) * row_count + jnp.where(block < 2, 2 * t + block, 2 * whole + t)
    pick = jnp.where(k + start == token, 1.0, 0.0)
    kept = jnp.dot(mask_row.astype(jnp.bfloat16), pick.astype(jnp.bfloat16), preferred_element_type=jnp.float32)
    channel = lax.broadcasted_iota(jnp.int32, (group, lanes), 0)
    lane = lax.broadcasted_iota(jnp.int32, (group, lanes), 1)
    spread_ref[...] = jnp.where(lane % group == channel, kept, 0.0)
    for copy in copies[1:4]:
        copy.wait()
    normed = normalise(pair_ref[...].reshape(tokens, channels), gain_ref[...], bias_ref[...])
    normed_ref[...] = normed
    copies[4].wait()
    parts = [all_w_ref[:, at : at + hidden] for at in range(0, 4 * hidden, hidden)]
    w = jnp.concatenate([jnp.where(my_col == 0, part[:, :ours], part[:, ours:]) for part in parts], axis=1).T
    w_ref[...] = w
    sides_ref[...] = project(normed, w, pair_ref.shape, quads)


def other_kernel(pair_ref, sides_ref, gain_ref, bias_ref, w_ref, *refs):
    *piece_refs, others_ref = refs
    my_quad, my_col = lax.axis_index("quad"), lax.axis_index("col")
    quads = sides_ref.shape[0]
    normed = normalise(pair_ref[...].reshape(-1, pair_ref.shape[2]), gain_ref[...], bias_ref[...])
    others_ref[...] = project(normed, w_ref[...], pair_ref.shape, quads)
    for step, piece_ref in enumerate(piece_refs):
        piece_ref[my_col] = sides_ref[my_quad ^ step]
        piece_ref[1 - my_col] = others_ref[my_quad ^ step]


def triangle_kernel(far_order, steps, cols, row_count, col_count, share, *refs):
    *got_refs, spread_ref, mask_ref, total_ref, left_ref, wide_ref = refs
    got_refs = {step: ref for step, ref in zip(steps, got_refs)}
    both = 2 * share
    group, lanes = spread_ref.shape
    length = mask_ref.shape[0]
    rows, quads, parts = length // row_count, len(steps), share // group
    whole, spare = row_count // 3, LANES - 2 * col_count
    rest = col_count - spare
    blocks = [[got_refs[row][col].astype(jnp.float32) for row in range(quads)] for col in range(cols)]

    def turned(picks):
        return jnp.concatenate([blocks[col][row][at : at + group] for col, row, at in picks], axis=0).T

    tail = turned([(col, row, whole * both + part * group) for col in range(cols) for part in range(parts) for row in range(quads)])

    def side(which, part):
        even, odd, third = [], [], []
        for col in range(cols):
            at = which * share + part * group
            block = turned([(col, row, t * both + at) for t in range(whole) for row in range(quads)])
            even.append(block[:col_count])
            odd.append(block[col_count : 2 * col_count])
            lane = (col * parts + part) * quads * group
            at = which * LANES // 2
            last = [tail[at + t * rest : at + (t + 1) * rest, lane : lane + quads * group] for t in range(whole)]
            third += [block[2 * col_count :], jnp.concatenate(last, axis=1)]
        tokens = [jnp.concatenate(pieces, axis=0) for pieces in (even, odd, third)]
        return jnp.concatenate(tokens, axis=1) * mask_ref[...]

    def placed(pieces):
        return jnp.concatenate([jnp.zeros((piece, lanes), jnp.bfloat16) if isinstance(piece, int) else piece for piece in pieces], axis=0)

    contract = (((1,), (1,)), ((), ()))
    lane_block = lax.broadcasted_iota(jnp.int32, (group, LANES), 1) // rest
    mains, lasts = [], []
    for part in range(parts):
        left_ref[part] = side(0, part)
        right = side(1, part).astype(jnp.bfloat16)
        for row in range(rows):
            for t in range(0, whole, 2):
                pair = []
                for at in (row * row_count, row * row_count + 2):
                    picks = [at + 2 * t, at + 2 * t + 1, row * row_count + 2 * whole + t + len(pair)]
                    copies = [jnp.broadcast_to(left_ref[part, i : i + 1, :], (group, lanes)) for i in picks]
                    pair.append(jnp.concatenate([copy * spread_ref[...] for copy in copies], axis=1))
                at = (row * whole + t) * group
                wide_ref[part, at : at + 2 * group, :] = jnp.concatenate(pair, axis=0).astype(jnp.bfloat16)
        ours = [right[col * col_count : (col + 1) * col_count] for col in range(cols)]
        weights = [
            placed([p for mine in ours for p in (mine, LANES - col_count)]),
            placed([p for mine in ours for p in (col_count, mine, spare)]),
            placed([p for mine in ours for p in (2 * col_count, mine[:spare])]),
        ]
        weights = jnp.concatenate(weights, axis=1)
        mains.append(lax.dot_general(wide_ref[part], weights, contract, preferred_element_type=jnp.float32))
        gap = LANES // parts
        pieces = [[gap * part] + [mine[spare:]] * whole + [LANES - gap * (part + 1)] for mine in ours]
        weights = placed([p for piece in pieces for p in piece if not isinstance(p, int) or p])
        lasts.append(lax.dot_general(wide_ref[part, :, 2 * lanes :], weights, contract, preferred_element_type=jnp.float32))
    for target, device in enumerate(far_order):
        row, col = divmod(device, cols)
        spots = [(row * whole + t) * group for t in range(whole)]
        tiles = [main[at : at + group, col * LANES : (col + 1) * LANES] for at in spots for main in mains]
        last = [part[at : at + group, col * LANES : (col + 1) * LANES] for part in lasts for at in spots]
        tile = last[0]
        for n in range(1, len(last)):
            tile = jnp.where(lane_block >= n, last[n], tile)
        tiles.append(tile)
        total_ref[target] = jnp.concatenate(tiles, axis=0).astype(jnp.bfloat16)


def gate_kernel(normed_ref, w_ref, gain_ref, bias_ref, gate_ref, gain_out_ref, bias_out_ref):
    gate_ref[...] = sigmoid(jnp.dot(normed_ref[...], w_ref[...], preferred_element_type=jnp.float32))
    gain_out_ref[...] = column(gain_ref[...])
    bias_out_ref[...] = column(bias_ref[...])


def output_kernel(far_order, near_order, total_ref, gate_ref, gain_ref, bias_ref, w_ref, out_ref):
    tokens = gate_ref.shape[0]
    hidden = w_ref.shape[0]
    near = len(near_order)
    share = hidden // near
    blocks = []
    for index in near_order:
        parts = [total_ref[source].astype(jnp.float32) for source, device in enumerate(far_order) if device % near == index]
        blocks.append(unpack(sum(parts[1:], parts[0]), share))
    total = jnp.concatenate(blocks, axis=0)
    normed = layer_norm(total, gain_ref[...], bias_ref[...], 0).astype(jnp.bfloat16)
    output = lax.dot_general(normed, w_ref[...], (((0,), (0,)), ((), ())), preferred_element_type=jnp.float32)
    output = restore(output, out_ref.shape[0], out_ref.shape[1])
    out_ref[...] = (gate_ref[...] * output).astype(jnp.bfloat16).reshape(out_ref.shape)


def per_device(rows, cols, halves, pair, token_mask, gain_in, bias_in, w_in, w_gate, gain_out, bias_out, w_out):
    row_count, col_count, channels = pair.shape
    hidden = w_out.shape[0]
    devices = rows * cols
    near = devices // halves
    quads = rows // halves
    far_order = []
    for col in reversed(range(cols)):
        ahead = list(range(quads)) if col else list(reversed(range(quads)))
        behind = [0] + list(reversed(range(1, quads))) if col else list(reversed(range(quads)))
        for quad, other in zip(ahead, behind):
            far_order += [near + other * cols + col, quad * cols + col]
    share = hidden // near
    tokens = row_count * col_count
    length = rows * row_count
    depth = length // halves
    token_mask = token_mask.reshape(1, length)
    near_order = [quad * cols + col for col in range(cols) for quad in range(quads)]
    packed = 2 * share * tokens // LANES
    cost = pl.CostEstimate(flops=2 * tokens * channels * 4 * hidden, bytes_accessed=16 * tokens * channels, transcendentals=0)
    other_pair = lax.ppermute(pair, "col", [(i, (i + 1) % cols) for i in range(cols)])
    arguments = (pair, gain_in.reshape(1, channels), bias_in.reshape(1, channels), w_in, token_mask)
    sides, normed, spread, mask, *weights = pl.pallas_call(
        functools.partial(own_kernel, quads, cols),
        out_shape=(
            jax.ShapeDtypeStruct((quads, packed, LANES), jnp.bfloat16),
            jax.ShapeDtypeStruct((tokens, channels), jnp.bfloat16),
            jax.ShapeDtypeStruct((GROUP, GROUP * depth), jnp.float32),
            jax.ShapeDtypeStruct((length, 1), jnp.float32),
            jax.ShapeDtypeStruct((4 * hidden // cols, channels), jnp.bfloat16),
            jax.ShapeDtypeStruct((1, channels), jnp.float32),
            jax.ShapeDtypeStruct((1, channels), jnp.float32),
        ),
        in_specs=[HBM] * 5,
        out_specs=(VMEM,) * 7,
        scratch_shapes=[
            pltpu.VMEM(pair.shape, pair.dtype),
            pltpu.VMEM(w_in.shape, w_in.dtype),
            pltpu.VMEM((1, length), jnp.int32),
            pltpu.SemaphoreType.DMA((5,)),
        ],
        compiler_params=LIMIT,
        cost_estimate=cost,
    )(*(pltpu.with_memory_space_constraint(x, pltpu.HBM) for x in arguments))
    w_ours, gain_in, bias_in = weights
    pieces = pl.pallas_call(
        other_kernel,
        out_shape=[jax.ShapeDtypeStruct((cols, packed, LANES), jnp.bfloat16)] * quads,
        in_specs=[VMEM] * 5,
        out_specs=[VMEM] * quads,
        scratch_shapes=[pltpu.VMEM((quads, packed, LANES), jnp.bfloat16)],
        compiler_params=LIMIT,
        cost_estimate=cost,
    )(other_pair, sides, gain_in, bias_in, w_ours)
    steps = [3, 1, 2, 0]
    got = [lax.ppermute(pieces[step], "quad", [(i, i ^ step) for i in range(quads)]) if step else pieces[0] for step in steps]
    total = pl.pallas_call(
        functools.partial(triangle_kernel, far_order, steps, cols, row_count, col_count, share),
        out_shape=jax.ShapeDtypeStruct((devices, share * tokens // LANES, LANES), jnp.bfloat16),
        in_specs=[VMEM] * (quads + 2),
        out_specs=VMEM,
        scratch_shapes=[
            pltpu.VMEM((share // GROUP, length, GROUP * depth), jnp.float32),
            pltpu.VMEM((share // GROUP, length // 3 * GROUP, 3 * GROUP * depth), jnp.bfloat16),
        ],
        compiler_params=LIMIT,
    )(*got, spread, mask)
    gate, gain_out, bias_out = pl.pallas_call(
        gate_kernel,
        out_shape=(
            jax.ShapeDtypeStruct((tokens, channels), jnp.float32),
            jax.ShapeDtypeStruct((hidden, 1), jnp.float32),
            jax.ShapeDtypeStruct((hidden, 1), jnp.float32),
        ),
        in_specs=[VMEM] * 4,
        out_specs=(VMEM, VMEM, VMEM),
        compiler_params=LIMIT,
        cost_estimate=pl.CostEstimate(flops=2 * tokens * channels * channels, bytes_accessed=4 * tokens * channels, transcendentals=0),
    )(normed, w_gate, gain_out.reshape(1, hidden), bias_out.reshape(1, hidden))
    total = lax.all_to_all(total, ("half", "quad", "col"), split_axis=0, concat_axis=0, tiled=True, axis_index_groups=[far_order])
    return pl.pallas_call(
        functools.partial(output_kernel, far_order, near_order),
        out_shape=jax.ShapeDtypeStruct(pair.shape, jnp.bfloat16),
        in_specs=[VMEM] * 5,
        out_specs=VMEM,
        compiler_params=LIMIT,
    )(total, gate, gain_out, bias_out, w_out)


def plain_per_device(rows, cols, pair, token_mask, gain_in, bias_in, w_in, w_gate, gain_out, bias_out, w_out):
    row_count, col_count, channels = pair.shape
    hidden = w_out.shape[0]
    devices = rows * cols
    share = hidden // devices
    tokens = row_count * col_count
    row_start = lax.axis_index(("half", "quad")) * row_count
    col_start = lax.axis_index("col") * col_count
    mask_float = token_mask.astype(jnp.float32)
    mask_rows = lax.dynamic_slice_in_dim(mask_float, row_start, row_count)
    mask_cols = lax.dynamic_slice_in_dim(mask_float, col_start, col_count)
    pair_mask = (mask_rows[:, None] * mask_cols[None, :]).reshape(1, tokens)
    flat = pair.reshape(tokens, channels).astype(jnp.float32)
    normed = layer_norm(flat, gain_in, bias_in, -1).astype(jnp.bfloat16)
    projected = lax.dot_general(w_in, normed, (((0,), (1,)), ((), ())), preferred_element_type=jnp.float32)
    projected = projected.reshape(2, 2, hidden, tokens)
    sides = (pair_mask * jax.nn.sigmoid(projected[:, 0]) * projected[:, 1]).astype(jnp.bfloat16)
    sides = sides.reshape(2, devices, share, tokens).transpose(1, 0, 2, 3)
    gate = jax.nn.sigmoid(jnp.dot(normed, w_gate, preferred_element_type=jnp.float32))
    got = lax.all_to_all(sides, AXES, split_axis=0, concat_axis=0, tiled=True)
    got = got.reshape(rows, cols, 2, share, row_count, col_count).transpose(2, 3, 0, 4, 1, 5)
    got = got.reshape(2, share, rows * row_count, cols * col_count)
    total = jnp.einsum("cki,ckj->cij", got[0], got[1], preferred_element_type=jnp.float32).astype(jnp.bfloat16)
    total = total.reshape(share, rows, row_count, cols, col_count).transpose(1, 3, 0, 2, 4)
    total = total.reshape(devices, share, tokens)
    total = lax.all_to_all(total, AXES, split_axis=0, concat_axis=0, tiled=True)
    total = total.reshape(hidden, tokens).astype(jnp.float32)
    summed_norm = layer_norm(total, gain_out[:, None], bias_out[:, None], 0).astype(jnp.bfloat16)
    output = lax.dot_general(summed_norm, w_out, (((0,), (0,)), ((), ())), preferred_element_type=jnp.float32)
    return (gate * output).astype(jnp.bfloat16).reshape(row_count, col_count, channels)


def solution(mesh):
    rows, cols = mesh.shape["row"], mesh.shape["col"]
    halves = 2
    parts = (mesh.shape["groups"], halves, rows // halves, cols)
    finer = jax.sharding.Mesh(mesh.devices.reshape(parts), ("groups", "half", "quad", "col"))

    def per_shard(*args):
        near, hidden, length = rows * cols // halves, args[-1].shape[0], args[1].shape[0]
        row_count, col_count, _ = args[0].shape
        spare = LANES - 2 * col_count
        fits = hidden % (2 * GROUP * near) == 0 and cols == 2 and rows // halves == 4 and length <= LANES and row_count % 3 == 0
        fits = fits and 0 < spare < col_count and row_count // 3 * (col_count - spare) * 2 == LANES
        fits = fits and row_count // 3 * (rows // halves) * GROUP == LANES
        return per_device(rows, cols, halves, *args) if fits else plain_per_device(rows, cols, *args)

    tokens = P(("groups", "half", "quad"), "col", None)
    in_specs = (tokens, P("groups"), P(), P(), P(), P(), P(), P(), P())
    return jax.shard_map(per_shard, mesh=finer, in_specs=in_specs, out_specs=tokens, check_vma=False)
```
